32 devices in a mesh: task: 4 (over y, x), feat: 8 (over z, core).
Axes of the slice: x: 2, y: 2, z: 4, core: 2. Of those that a mesh axis runs over, the one named last changes fastest.
Arguments:
- tokens_in: bfloat16 [4, 512, 16, 512], P('task', None, 'feat'), may hold values from -6 to 6
- sample_weights: bfloat16 [2, 4, 512, 512], replicated
- feature_weights: bfloat16 [2, 4, 512, 512], replicated
- norm_gain: float32 [2, 3, 512], replicated, may hold values from 0.5 to 1.5
- norm_shift: float32 [2, 3, 512], replicated, may hold values from -1 to 1
- up_weight: bfloat16 [2, 512, 2048], replicated, may hold values from -0.25 to 0.25
- up_bias: float32 [2, 2048], replicated, may hold values from -1 to 1
- down_weight: bfloat16 [2, 2048, 512], replicated, may hold values from -0.125 to 0.125
- down_bias: float32 [2, 512], replicated, may hold values from -1 to 1
- read_weight: bfloat16 [512, 10], replicated, may hold values from -0.125 to 0.125
- output_grad: bfloat16 [4, 512, 16, 512], P('task', None, 'feat'), may hold values from -6 to 6
- task_sizes: int32 [4], P('task'), may hold values from 64 to 512, as said below
- feature_counts: int32 [4], P('task'), may hold values from 2 to 16, as said below
- bin_index: int32 [4, 512, 16], P('task', None, 'feat'), may hold values from 0 to 63
- bin_counts: int32 [4, 16, 64], P('task', 'feat'), may hold values from 1 to 49
- class_labels: int32 [4, 512], P('task'), may hold values from 0 to 9
Outputs:
- tokens_out: float32 [4, 512, 16, 512], P('task', None, 'feat')
- centered_shapes: float32 [4, 16, 64, 10], P('task', 'feat')
- tokens_grad: float32 [4, 512, 16, 512], P('task', None, 'feat')
- task_loss: float32 [4], P('task')
- sample_grad: float32 [2, 4, 512, 512], P(None, 'task', 'feat')
- feature_grad: float32 [2, 4, 512, 512], P(None, 'task', 'feat')
- gain_grad: float32 [2, 3, 512], replicated
- shift_grad: float32 [2, 3, 512], replicated
- up_grad: float32 [2, 512, 2048], P(None, None, ('task', 'feat'))
- up_bias_grad: float32 [2, 2048], replicated
- down_grad: float32 [2, 2048, 512], P(None, ('task', 'feat'))
- down_bias_grad: float32 [2, 512], replicated
- read_grad: float32 [512, 10], replicated
The draws below stay inside these ranges and needn't reach their ends.
Inputs may be any that keep to these rules, and one draw needn't show every extreme that they name: Samples of task t at positions below task_sizes[t] are live, the rest are padding. In every draw one task has all 512. Features of task t at positions below feature_counts[t] are live, the rest are padding. In every draw one task has all 16.
All inputs are finite; a program needn't handle non-finite values.
Results may differ from the reference program's by a relative error of at most 0.018.
Values may be sent and summed in bfloat16 or wider, within the bound.
A program may use at most 256 MiB of HBM per device.

```python
import jax
import jax.numpy as jnp
from jax import lax

D = 512
HEADS = 8
FF = 2048
BINS = 64
CLASSES = 10
LAYERS = 2
SAMPLES = 512
NF = 16
TASKS = 4


def attention_set(key, keys_reach):
    noise_draw = jax.random.truncated_normal(key, -6.0, 6.0, (LAYERS, 4, D, D), jnp.float32)
    scale_rows = jnp.where(jnp.arange(4) < 3, D ** (-0.5), (keys_reach / (32.0 * D)) ** 0.5)
    return (noise_draw * scale_rows[None, :, None, None]).astype(jnp.bfloat16)


def draw_sample_weights(key, part):
    key = jax.random.fold_in(key, 11)
    return attention_set(key, SAMPLES)


def draw_feature_weights(key, part):
    key = jax.random.fold_in(key, 12)
    return attention_set(key, NF)


def ragged_counts(key, largest):
    first_key, second_key = jax.random.split(key)
    spread_draw = jax.random.randint(first_key, (TASKS,), 0, largest + 1)
    lowest = largest // 8
    counts = lowest + (largest - lowest) * spread_draw * spread_draw // (largest * largest)
    full_task = jax.random.randint(second_key, (), 0, TASKS)
    return jnp.where(jnp.arange(TASKS) == full_task, largest, counts).astype(jnp.int32)


def draw_task_sizes(key, part):
    key = jax.random.fold_in(key, 21)
    return ragged_counts(key, SAMPLES)


def draw_feature_counts(key, part):
    key = jax.random.fold_in(key, 22)
    return ragged_counts(key, NF)


def set_ends(entries, own_key, low, high):
    place = [jax.random.randint(jax.random.fold_in(own_key, axis), (), 0, length) for axis, length in enumerate(entries.shape)]
    longest = entries.shape.index(max(entries.shape))
    neighbour = place[:longest] + [(place[longest] + 1) % entries.shape[longest]] + place[longest + 1:]
    return entries.at[tuple(place)].set(low).at[tuple(neighbour)].set(high)


def block_scale(stream_key, shape, shards, low, high):
    level = 1.0
    for axis_at, parts in shards:
        heights = jax.random.uniform(jax.random.fold_in(jax.random.fold_in(stream_key, 6), axis_at), (parts,), jnp.float32, low / len(shards), high / len(shards))
        level = level * jnp.repeat(jnp.exp(heights), shape[axis_at] // parts).reshape((-1,) + (1,) * (len(shape) - 1 - axis_at))
    return level


def scatter_about(key, dims, deviation, most, cuts=(), kind=jnp.bfloat16):
    drawn = deviation * jax.random.normal(key, dims, jnp.float32)
    if cuts:
        drawn = drawn * block_scale(key, dims, cuts, -0.22, 0.18)
    return jnp.clip(drawn, -most, most).astype(kind)


def setup_inputs(seed: int = 0) -> dict:
    key_of = jax.random.split(jax.random.key(seed), 17)
    return {
        "tokens_in": scatter_about(key_of[0], (TASKS, SAMPLES, NF, D), 1.0, 6.0, ((0, 4), (2, 8))),
        "sample_weights": draw_sample_weights(jax.random.fold_in(key_of[16], 71), 0),
        "feature_weights": draw_feature_weights(jax.random.fold_in(key_of[16], 71), 0),
        "norm_gain": jnp.clip(1.0 + 0.1 * jax.random.normal(key_of[3], (LAYERS, 3, D), jnp.float32), 0.5, 1.5),
        "norm_shift": scatter_about(key_of[4], (LAYERS, 3, D), 0.2, 1.0, (), jnp.float32),
        "up_weight": scatter_about(key_of[5], (LAYERS, D, FF), D ** -0.5, 0.25),
        "up_bias": scatter_about(key_of[6], (LAYERS, FF), 0.2, 1.0, (), jnp.float32),
        "down_weight": scatter_about(key_of[7], (LAYERS, FF, D), FF ** -0.5, 0.125),
        "down_bias": scatter_about(key_of[8], (LAYERS, D), 0.2, 1.0, (), jnp.float32),
        "read_weight": scatter_about(key_of[9], (D, CLASSES), (D * NF // 4) ** -0.5, 0.125),
        "output_grad": scatter_about(key_of[10], (TASKS, SAMPLES, NF, D), 1.0, 6.0, ((0, 4), (2, 8))),
        "task_sizes": draw_task_sizes(jax.random.fold_in(key_of[16], 71), 0),
        "feature_counts": draw_feature_counts(jax.random.fold_in(key_of[16], 71), 0),
        "bin_index": set_ends(jax.random.randint(key_of[13], (TASKS, SAMPLES, NF), 0, BINS), jax.random.fold_in(key_of[13], 1), 0, BINS - 1).astype(jnp.int32),
        "bin_counts": set_ends(jax.random.randint(key_of[14], (TASKS, NF, BINS), 1, 50), jax.random.fold_in(key_of[14], 1), 1, 49).astype(jnp.int32),
        "class_labels": set_ends(jax.random.randint(key_of[15], (TASKS, SAMPLES), 0, CLASSES), jax.random.fold_in(key_of[15], 1), 0, CLASSES - 1).astype(jnp.int32),
    }


highest = lax.Precision.HIGHEST
epsilon = 1e-05
masked_score = -1e+30

@jax.custom_vjp
def low(v):
    return lax.optimization_barrier(v.astype(jnp.bfloat16)).astype(jnp.float32)

@jax.custom_vjp
def low_back(v):
    return v

def low_keep(v):
    return (low(v), None)

def low_pass(kept, grad):
    return (grad,)

def back_keep(v):
    return (v, None)

def back_low(kept, grad):
    return (low(grad),)
low.defvjp(low_keep, low_pass)
low_back.defvjp(back_keep, back_low)

def rounded(values_in):
    return low_back(low(values_in))

def normalize(stream, gain, shift):
    centre = lax.optimization_barrier(jnp.mean(stream, axis=-1, keepdims=True))
    spread = lax.optimization_barrier(jnp.mean(jnp.square(stream - centre), axis=-1, keepdims=True))
    return (stream - centre) * lax.rsqrt(spread + epsilon) * gain + shift

def attend(query_rows, key_rows, value_rows, key_live):
    score_scale = query_rows.shape[-1] ** (-0.5)
    scores = low_back(jnp.einsum('lhe,mhe->hlm', query_rows, key_rows, precision=highest))
    scores = jnp.where(key_live[None, None, :], score_scale * scores, masked_score)
    attention = jax.nn.softmax(scores, axis=-1)
    return jnp.einsum('hlm,mhe->lhe', low(attention), value_rows, precision=highest)

def column_attend(packed):
    return attend(packed[0], packed[1], packed[2], packed[3])

def sample_attend(packed):
    return jax.vmap(attend, in_axes=(0, 0, 0, None))(packed[0], packed[1], packed[2], packed[3])

def one_layer(stream, layer_weights, sample_live, feature_live):
    sample_set, feature_set, gain_rows, shift_rows, up_set, up_biases, down_set, down_biases = layer_weights
    task_count, samples, features, model_width = stream.shape
    head_size = model_width // HEADS
    hidden = rounded(normalize(stream, gain_rows[0], shift_rows[0]))
    projected = [rounded(jnp.dot(hidden, sample_set[member], precision=highest)) for member in range(3)]
    columns = [member_rows.reshape(task_count, samples, features, HEADS, head_size).transpose(0, 2, 1, 3, 4).reshape(task_count * features, samples, HEADS, head_size) for member_rows in projected]
    column_live = jnp.repeat(sample_live, features, axis=0)
    context = lax.map(jax.checkpoint(column_attend), (columns[0], columns[1], columns[2], column_live))
    context = context.reshape(task_count, features, samples, model_width).transpose(0, 2, 1, 3)
    stream = stream + low_back(jnp.dot(rounded(context), sample_set[3], precision=highest))
    hidden = rounded(normalize(stream, gain_rows[1], shift_rows[1]))
    projected = [rounded(jnp.dot(hidden, feature_set[member], precision=highest)).reshape(task_count, samples, features, HEADS, head_size) for member in range(3)]
    context = lax.map(jax.checkpoint(sample_attend), (projected[0], projected[1], projected[2], feature_live))
    context = rounded(context.reshape(task_count, samples, features, model_width))
    stream = stream + rounded(jnp.dot(context, feature_set[3], precision=highest))
    hidden = rounded(normalize(stream, gain_rows[2], shift_rows[2]))
    expanded = low_back(jnp.dot(hidden, up_set, precision=highest) + up_biases)
    active = rounded(jax.nn.gelu(expanded))
    return stream + low_back(jnp.dot(active, down_set, precision=highest) + down_biases)

def reference(tokens_in, sample_weights, feature_weights, norm_gain, norm_shift, up_weight, up_bias, down_weight, down_bias, read_weight, output_grad, task_sizes, feature_counts, bin_index, bin_counts, class_labels):
    samples = tokens_in.shape[1]
    features = tokens_in.shape[2]
    sample_live = jnp.arange(samples, dtype=jnp.int32)[None, :] < task_sizes[:, None]
    feature_live = jnp.arange(features, dtype=jnp.int32)[None, :] < feature_counts[:, None]
    sample_mask = sample_live.astype(jnp.float32)
    feature_mask = feature_live.astype(jnp.float32)
    onehot_bins = (bin_index[..., None] == jnp.arange(BINS, dtype=jnp.int32)).astype(jnp.float32)
    chosen = onehot_bins * sample_mask[:, :, None, None]
    counted = jnp.maximum(lax.optimization_barrier(jnp.sum(chosen, axis=1)), 1.0)
    bin_weight = bin_counts.astype(jnp.float32)
    weight_total = lax.optimization_barrier(jnp.sum(bin_weight, axis=-1, keepdims=True))
    used_bins = onehot_bins * feature_mask[:, None, :, None]
    label_rows = (class_labels[..., None] == jnp.arange(CLASSES, dtype=jnp.int32)).astype(jnp.float32)
    size_floats = task_sizes.astype(jnp.float32)

    def forward(stream, sample_set, feature_set, gain_set, shift_set, up_set, up_biases, down_set, down_biases, reader):
        for layer_number in range(LAYERS):
            layer_weights = (sample_set[layer_number], feature_set[layer_number], gain_set[layer_number], shift_set[layer_number], up_set[layer_number], up_biases[layer_number], down_set[layer_number], down_biases[layer_number])
            stream = one_layer(stream, layer_weights, sample_live, feature_live)
        projected = low_back(jnp.dot(low(stream), reader, precision=highest))
        bin_sums = jnp.einsum('tsfb,tsfc->tfbc', chosen, projected, precision=highest)
        bin_means = bin_sums / counted[..., None]
        centre = lax.optimization_barrier(jnp.sum(bin_weight[..., None] * bin_means, axis=2, keepdims=True)) / weight_total[..., None]
        shapes = bin_means - centre
        logits = jnp.einsum('tsfb,tfbc->tsc', used_bins, shapes, precision=highest)
        log_total = jax.nn.logsumexp(logits, axis=-1)
        picked = lax.optimization_barrier(jnp.sum(logits * label_rows, axis=-1))
        loss = lax.optimization_barrier(jnp.sum(sample_mask * (log_total - picked), axis=1)) / size_floats
        return ((stream, loss), shapes)
    floats = [argument.astype(jnp.float32) for argument in (tokens_in, sample_weights, feature_weights, norm_gain, norm_shift, up_weight, up_bias, down_weight, down_bias, read_weight)]
    outputs, pullback, centered_shapes = jax.vjp(forward, floats[0], floats[1], floats[2], floats[3], floats[4], floats[5], floats[6], floats[7], floats[8], floats[9], has_aux=True)
    tokens_out, task_loss = outputs
    grads = pullback((output_grad.astype(jnp.float32), jnp.ones_like(task_loss)))
    return (tokens_out, centered_shapes, grads[0], task_loss, grads[1], grads[2], grads[3], grads[4], grads[5], grads[6], grads[7], grads[8], grads[9])
```

```python
import functools

import jax
import jax.numpy as jnp
from jax import lax
from jax.experimental import pallas as pl
from jax.experimental.pallas import tpu as pltpu
from jax.sharding import PartitionSpec as P

HEADS = 8
BINS = 64
CLASSES = 10
LAYERS = 2
LANES = 128
CODE_LANE = 32
ROWS = 256

epsilon = 1e-05
masked_score = -1e30
highest = lax.Precision.HIGHEST
bf16 = jnp.bfloat16
f32 = jnp.float32

NN = (((1,), (0,)), ((), ()))
NT = (((1,), (1,)), ((), ()))
TN = (((0,), (0,)), ((), ()))


def mm(left, right, dims=NN):
    return lax.dot_general(left, right, dims, preferred_element_type=f32)


def lane_row():
    return lax.broadcasted_iota(jnp.int32, (1, LANES), 1)


def half_row(half):
    lanes = lane_row()
    picked = lanes < 64 if half == 0 else lanes >= 64
    return picked.astype(f32).astype(bf16)


def piece_row(pair, half):
    offset = lane_row() - 64 * half - 3 * pair
    return jnp.where((offset >= 0) & (offset < 3), -1.0, 0.0).astype(bf16)


def split_pieces(values, order):
    first = values.astype(bf16).astype(f32)
    rest = values - first
    second = rest.astype(bf16).astype(f32)
    third = rest - second
    return jnp.where(order == 0, first, jnp.where(order == 1, second, third))


def layer_norm(rows, gain, shift):
    centred = rows - jnp.mean(rows, axis=-1, keepdims=True)
    inverse = lax.rsqrt(jnp.mean(centred * centred, axis=-1, keepdims=True) + epsilon)
    normed = centred * inverse
    return normed, inverse, normed * gain + shift


def layer_norm_back(grad_rows, rows, gain):
    centred = rows - jnp.mean(rows, axis=-1, keepdims=True)
    inverse = lax.rsqrt(jnp.mean(centred * centred, axis=-1, keepdims=True) + epsilon)
    normed = centred * inverse
    scaled = grad_rows * gain
    inner = (
        scaled
        - jnp.mean(scaled, axis=-1, keepdims=True)
        - normed * jnp.mean(scaled * normed, axis=-1, keepdims=True)
    )
    gain_part = jnp.sum(grad_rows * normed, axis=0, keepdims=True)
    shift_part = jnp.sum(grad_rows, axis=0, keepdims=True)
    return inverse * inner, gain_part, shift_part


def chunk(index, size):
    return pl.ds(pl.multiple_of(index * size, size), size)


def attend_pair(query, key, value, query_code, key_code, pair, extras):
    query_wide = jnp.concatenate([query, query_code], axis=1)
    total = None
    peaks = []
    for half in range(2):
        mask = half_row(half)
        key_wide = jnp.concatenate([key * mask, key_code], axis=1)
        scores = mm(query_wide, key_wide, NT)
        peak = jnp.max(scores, axis=-1, keepdims=True)
        weights = jnp.exp(scores - peak).astype(bf16)
        ones = jnp.broadcast_to(mask, value.shape)
        part = mm(weights, jnp.concatenate([value * mask, ones], axis=1))
        total = part if total is None else total + part
        peaks.append(peak)
    lanes = lane_row()
    row_total = total[:, LANES:]
    context = total[:, :LANES] / row_total
    log_total = jnp.where(lanes < 64, peaks[0], peaks[1]) + jnp.log(row_total)
    order = lanes % 64 - 3 * pair
    extras = jnp.where((order >= 0) & (order < 3), split_pieces(log_total, order), extras)
    return context.astype(bf16), extras


def attend_pair_back(query, key, value, context_grad, query_extra, grad_extra, key_code, pair):
    query_wide = jnp.concatenate([query, query_extra], axis=1)
    grad_wide = jnp.concatenate([context_grad, grad_extra], axis=1)
    query_grad = key_grad = value_grad = None
    for half in range(2):
        mask = half_row(half)
        pieces = piece_row(pair, half)
        key_half = key * mask
        key_wide = jnp.concatenate([key_half, key_code + pieces], axis=1)
        value_wide = jnp.concatenate(
            [value * mask, jnp.broadcast_to(pieces, value.shape)], axis=1
        )
        attention = jnp.exp(mm(key_wide, query_wide, NT))
        score_grad = (attention * mm(value_wide, grad_wide, NT)).astype(bf16)
        value_part = mm(attention.astype(bf16), context_grad * mask)
        key_part = mm(score_grad, query * mask)
        query_part = mm(score_grad, key_half, TN)
        if half == 0:
            query_grad, key_grad, value_grad = query_part, key_part, value_part
        else:
            query_grad, key_grad, value_grad = (
                query_grad + query_part,
                key_grad + key_part,
                value_grad + value_part,
            )
    return query_grad, key_grad, value_grad


def delta_extra(context, context_grad):
    width = context.shape[1]
    products = context.astype(f32) * context_grad.astype(f32)
    high = products.astype(bf16)
    low = (products - high.astype(f32)).astype(bf16)
    head = lax.broadcasted_iota(jnp.int32, (width, LANES), 0) // (width // HEADS)
    offset = lax.broadcasted_iota(jnp.int32, (width, LANES), 1) - 64 * (head % 2) - 3 * (head // 2)
    spread = jnp.where((offset >= 0) & (offset < 3), 1.0, 0.0).astype(bf16)
    sums = mm(high, spread) + mm(low, spread)
    return split_pieces(sums, lane_row() % 64 % 3).astype(bf16)


def sample_forward(x_ref, gain_ref, shift_ref, w_ref, qcode_ref, kcode_ref, x1_ref, h2_ref, qkv_ref, ctx_ref, ext_ref):
    features, samples, width = x_ref.shape
    steps = samples // ROWS

    def project(unit, carry):
        f, rows = unit // steps, chunk(unit % steps, ROWS)
        _, _, hidden = layer_norm(x_ref[f, rows, :], gain_ref[0:1], shift_ref[0:1])
        hidden = hidden.astype(bf16)
        for member in range(3):
            out = mm(hidden, w_ref[member]).astype(bf16)
            if member == 0:
                out = out * jnp.asarray(0.125, bf16)
            qkv_ref[member, f, rows, :] = out
        return carry

    lax.fori_loop(0, features * steps, project, 0)

    def attend(unit, carry):
        f, rows = unit // steps, chunk(unit % steps, ROWS)
        code = qcode_ref[...]

        def pair_step(pair, extras):
            lanes = chunk(pair, LANES)
            context, extras = attend_pair(
                qkv_ref[0, f, rows, lanes],
                qkv_ref[1, f, :, lanes],
                qkv_ref[2, f, :, lanes],
                code,
                kcode_ref[...],
                pair,
                extras,
            )
            ctx_ref[f, rows, lanes] = context
            return extras

        extras = lax.fori_loop(0, width // LANES, pair_step, code.astype(f32))
        ext_ref[f, rows, :] = extras.astype(bf16)
        x1 = x_ref[f, rows, :] + mm(ctx_ref[f, rows, :], w_ref[3])
        x1_ref[f, rows, :] = x1
        _, _, hidden = layer_norm(x1, gain_ref[1:2], shift_ref[1:2])
        h2_ref[f, rows, :] = hidden.astype(bf16)
        return carry

    lax.fori_loop(0, features * steps, attend, 0)


def load_group(ref, group, size):
    features, _, width = ref.shape
    block = ref[:, chunk(group, size), :]
    if size % 16:
        return block.astype(f32).reshape(features * size, width).astype(bf16)
    return block.reshape(features * size, width)


def store_group(ref, group, size, rows):
    features, _, width = ref.shape
    if size % 16:
        block = rows.astype(f32).reshape(features, size, width).astype(bf16)
    else:
        block = rows.reshape(features, size, width)
    ref[:, chunk(group, size), :] = block


def feature_forward(size, h_ref, w_ref, qcode_ref, kcode_ref, a_ref, qkv_ref, ctx_ref, ext_ref):
    _, samples, width = h_ref.shape

    def step(group, carry):
        hidden = load_group(h_ref, group, size)
        for member in range(3):
            out = mm(hidden, w_ref[member]).astype(bf16)
            if member == 0:
                out = out * jnp.asarray(0.125, bf16)
            qkv_ref[group, member] = out
        code = qcode_ref[...]

        def pair_step(pair, extras):
            lanes = chunk(pair, LANES)
            context, extras = attend_pair(
                qkv_ref[group, 0, :, lanes],
                qkv_ref[group, 1, :, lanes],
                qkv_ref[group, 2, :, lanes],
                code,
                kcode_ref[...],
                pair,
                extras,
            )
            ctx_ref[group, :, lanes] = context
            return extras

        extras = lax.fori_loop(0, width // LANES, pair_step, code.astype(f32))
        ext_ref[group] = extras.astype(bf16)
        store_group(a_ref, group, size, mm(ctx_ref[group], w_ref[3]).astype(bf16))
        return carry

    lax.fori_loop(0, samples // size, step, 0)


def gelu_parts(values):
    cubic = values * values * values
    inside = 0.7978845608028654 * (values + 0.044715 * cubic)
    bent = jnp.tanh(inside)
    return bent


def dense_forward(x_ref, a_ref, gain_ref, shift_ref, up_ref, upb_ref, down_ref, downb_ref, out_ref, u_ref):
    rows_total, width = x_ref.shape
    hidden_width = up_ref.shape[1]

    def step(unit, carry):
        rows = chunk(unit, ROWS)
        x2 = x_ref[rows, :] + a_ref[rows, :].astype(f32)
        _, _, hidden = layer_norm(x2, gain_ref[2:3], shift_ref[2:3])
        hidden = hidden.astype(bf16)
        total = x2 + downb_ref[...]
        for part in range(hidden_width // 512):
            cols = slice(part * 512, part * 512 + 512)
            expanded = mm(hidden, up_ref[:, cols]) + upb_ref[:, cols]
            u_ref[rows, cols] = expanded.astype(bf16)
            active = (0.5 * expanded * (1.0 + gelu_parts(expanded))).astype(bf16)
            total = total + mm(active, down_ref[cols, :])
        out_ref[rows, :] = total
        return carry

    lax.fori_loop(0, rows_total // ROWS, step, 0)


def dense_backward(g_ref, x1_ref, a_ref, u_ref, gain_ref, shift_ref, up_ref, down_ref, out_ref, send_ref, dup_ref, ddown_ref, dupb_ref, ddownb_ref, dgs_ref, active_ref, ugrad_ref, hidden_ref, rowgrad_ref):
    rows_total, width = g_ref.shape
    hidden_width = up_ref.shape[1]
    dupb_ref[...] = jnp.zeros_like(dupb_ref)
    ddownb_ref[...] = jnp.zeros_like(ddownb_ref)
    dgs_ref[...] = jnp.zeros_like(dgs_ref)

    def step(unit, carry):
        rows = chunk(unit, ROWS)
        grad = g_ref[rows, :]
        low = grad.astype(bf16)
        rowgrad_ref[rows, :] = low
        ddownb_ref[...] += jnp.sum(low.astype(f32), axis=0, keepdims=True)
        hidden_grad = None
        for part in range(hidden_width // 512):
            cols = slice(part * 512, part * 512 + 512)
            active_grad = mm(low, down_ref[cols, :], NT).astype(bf16).astype(f32)
            u = u_ref[rows, cols].astype(f32)
            bent = gelu_parts(u)
            slope = 0.5 * (1.0 + bent) + u * (1.0 - bent * bent) * (
                0.3989422804014327 + 0.05351611220146811 * u * u
            )
            active_ref[rows, cols] = (0.5 * u * (1.0 + bent)).astype(bf16)
            ugrad = (active_grad * slope).astype(bf16)
            ugrad_ref[rows, cols] = ugrad
            dupb_ref[:, cols] += jnp.sum(ugrad.astype(f32), axis=0, keepdims=True)
            part_grad = mm(ugrad, up_ref[:, cols], NT)
            hidden_grad = part_grad if hidden_grad is None else hidden_grad + part_grad
        x2 = x1_ref[rows, :] + a_ref[rows, :].astype(f32)
        _, _, hidden = layer_norm(x2, gain_ref[2:3], shift_ref[2:3])
        hidden_ref[rows, :] = hidden.astype(bf16)
        norm_grad, gain_part, shift_part = layer_norm_back(
            hidden_grad.astype(bf16).astype(f32), x2, gain_ref[2:3]
        )
        dgs_ref[0:1] += gain_part
        dgs_ref[1:2] += shift_part
        grad = grad + norm_grad
        out_ref[rows, :] = grad
        send_ref[rows, :] = grad.astype(bf16)
        return carry

    lax.fori_loop(0, rows_total // ROWS, step, 0)

    def weights(part, carry):
        cols = chunk(part, 512)
        dup_ref[cols, :] = mm(ugrad_ref[:, cols], hidden_ref[...], TN).astype(bf16)
        ddown_ref[cols, :] = mm(active_ref[:, cols], rowgrad_ref[...], TN).astype(bf16)
        return carry

    lax.fori_loop(0, hidden_width // 512, weights, 0)


def feature_backward(size, da_ref, h_ref, w_ref, kcode_ref, qkv_ref, ctx_ref, ext_ref, dh_ref, dw_ref, dqkv_ref, hidden_ref, dao_ref, dc_ref):
    _, samples, width = h_ref.shape
    groups = samples // size

    def step(group, carry):
        hidden_ref[group] = load_group(h_ref, group, size)
        dao = load_group(da_ref, group, size)
        dao_ref[group] = dao
        context_grad = mm(dao, w_ref[3], NT).astype(bf16)
        dc_ref[...] = context_grad
        grad_extra = delta_extra(ctx_ref[group], context_grad)

        def pair_step(pair, inner):
            lanes = chunk(pair, LANES)
            query_grad, key_grad, value_grad = attend_pair_back(
                qkv_ref[group, 0, :, lanes],
                qkv_ref[group, 1, :, lanes],
                qkv_ref[group, 2, :, lanes],
                dc_ref[:, lanes],
                ext_ref[group],
                grad_extra,
                kcode_ref[...],
                pair,
            )
            dqkv_ref[0, group, :, lanes] = (query_grad * 0.125).astype(bf16)
            dqkv_ref[1, group, :, lanes] = key_grad.astype(bf16)
            dqkv_ref[2, group, :, lanes] = value_grad.astype(bf16)
            return inner

        lax.fori_loop(0, width // LANES, pair_step, 0)
        total = mm(dqkv_ref[0, group], w_ref[0], NT)
        total = total + mm(dqkv_ref[1, group], w_ref[1], NT)
        total = total + mm(dqkv_ref[2, group], w_ref[2], NT)
        store_group(dh_ref, group, size, total.astype(bf16))
        return carry

    lax.fori_loop(0, groups, step, 0)

    def weights(member, carry):
        total = None
        for group in range(groups):
            part = mm(hidden_ref[group], dqkv_ref[member, group], TN)
            total = part if total is None else total + part
        dw_ref[member] = total.astype(bf16)
        return carry

    lax.fori_loop(0, 3, weights, 0)
    total = None
    for group in range(groups):
        part = mm(ctx_ref[group], dao_ref[group], TN)
        total = part if total is None else total + part
    dw_ref[3] = total.astype(bf16)


def sample_backward(g_ref, dh_ref, x1_ref, x_ref, gain_ref, shift_ref, w_ref, kcode_ref, qkv_ref, ctx_ref, ext_ref, out_ref, dw_ref, dgs_ref, dqkv_ref, hidden_ref, low_ref, dc_ref, gext_ref, kacc_ref, vacc_ref):
    features, samples, width = x_ref.shape
    steps = samples // ROWS
    dgs_ref[...] = jnp.zeros_like(dgs_ref)

    def enter(unit, carry):
        f, rows = unit // steps, chunk(unit % steps, ROWS)
        norm_grad, gain_part, shift_part = layer_norm_back(
            dh_ref[f, rows, :].astype(f32), x1_ref[f, rows, :], gain_ref[1:2]
        )
        dgs_ref[1, 0:1] += gain_part
        dgs_ref[1, 1:2] += shift_part
        grad = g_ref[f, rows, :] + norm_grad
        out_ref[f, rows, :] = grad
        low = grad.astype(bf16)
        low_ref[f, rows, :] = low
        context_grad = mm(low, w_ref[3], NT).astype(bf16)
        dc_ref[f, rows, :] = context_grad
        gext_ref[f, rows, :] = delta_extra(ctx_ref[f, rows, :], context_grad)
        return carry

    lax.fori_loop(0, features * steps, enter, 0)

    def attend(unit, carry):
        f, pair = unit // (width // LANES), unit % (width // LANES)
        lanes = chunk(pair, LANES)

        def query_step(step, inner):
            rows = chunk(step, ROWS)
            query_grad, key_grad, value_grad = attend_pair_back(
                qkv_ref[0, f, rows, lanes],
                qkv_ref[1, f, :, lanes],
                qkv_ref[2, f, :, lanes],
                dc_ref[f, rows, lanes],
                ext_ref[f, rows, :],
                gext_ref[f, rows, :],
                kcode_ref[...],
                pair,
            )
            dqkv_ref[0, f, rows, lanes] = (query_grad * 0.125).astype(bf16)
            first = step == 0
            kacc_ref[...] = jnp.where(first, 0.0, kacc_ref[...]) + key_grad
            vacc_ref[...] = jnp.where(first, 0.0, vacc_ref[...]) + value_grad
            return inner

        lax.fori_loop(0, steps, query_step, 0)
        dqkv_ref[1, f, :, lanes] = kacc_ref[...].astype(bf16)
        dqkv_ref[2, f, :, lanes] = vacc_ref[...].astype(bf16)
        return carry

    kacc_ref[...] = jnp.zeros_like(kacc_ref)
    vacc_ref[...] = jnp.zeros_like(vacc_ref)
    lax.fori_loop(0, features * (width // LANES), attend, 0)

    def leave(unit, carry):
        f, rows = unit // steps, chunk(unit % steps, ROWS)
        total = mm(dqkv_ref[0, f, rows, :], w_ref[0], NT)
        total = total + mm(dqkv_ref[1, f, rows, :], w_ref[1], NT)
        total = total + mm(dqkv_ref[2, f, rows, :], w_ref[2], NT)
        x = x_ref[f, rows, :]
        _, _, hidden = layer_norm(x, gain_ref[0:1], shift_ref[0:1])
        hidden_ref[f, rows, :] = hidden.astype(bf16)
        norm_grad, gain_part, shift_part = layer_norm_back(
            total.astype(bf16).astype(f32), x, gain_ref[0:1]
        )
        dgs_ref[0, 0:1] += gain_part
        dgs_ref[0, 1:2] += shift_part
        out_ref[f, rows, :] += norm_grad
        return carry

    lax.fori_loop(0, features * steps, leave, 0)

    def weights(member, carry):
        total = None
        for f in range(features):
            part = mm(hidden_ref[f], dqkv_ref[member, f], TN)
            total = part if total is None else total + part
        dw_ref[member] = total.astype(bf16)
        return carry

    lax.fori_loop(0, 3, weights, 0)
    total = None
    for f in range(features):
        part = mm(ctx_ref[f], low_ref[f], TN)
        total = part if total is None else total + part
    dw_ref[3] = total.astype(bf16)


def call(body, name, outs, scratch, *operands):
    spec = pl.BlockSpec(memory_space=pltpu.VMEM)
    return pl.pallas_call(
        body,
        name=name,
        out_shape=[jax.ShapeDtypeStruct(shape, kind) for shape, kind in outs],
        in_specs=[spec] * len(operands),
        out_specs=[spec] * len(outs),
        scratch_shapes=[pltpu.VMEM(shape, kind) for shape, kind in scratch],
        compiler_params=pltpu.CompilerParams(vmem_limit_bytes=56 << 20),
    )(*operands)


MESH = pl.DeviceIdType.MESH


def remote(source, target, send_sem, recv_sem, device):
    return pltpu.make_async_remote_copy(
        src_ref=source,
        dst_ref=target,
        send_sem=send_sem,
        recv_sem=recv_sem,
        device_id=device,
        device_id_type=MESH,
    )


def sum_partners(task_devices, feature_devices):
    task, place = lax.axis_index("task"), lax.axis_index("feat")
    chip, core = place // 2, lax.rem(place, 2)
    chips = feature_devices // 2
    pair = [{"feat": place + 1 - 2 * core}]
    tasks = [{"task": lax.rem(task + step, task_devices)} for step in range(1, task_devices)]
    line = [{"feat": 2 * lax.rem(chip + step, chips) + core} for step in range(1, chips)]
    return task, chip, core, pair, tasks, line


def greet(devices):
    barrier = pltpu.get_barrier_semaphore()
    for device in devices:
        pl.semaphore_signal(barrier, inc=1, device_id=device, device_id_type=MESH)


def met(count):
    pl.semaphore_wait(pltpu.get_barrier_semaphore(), count)


def sum_tail(pieces, task_devices, feature_devices, *refs):
    chips = feature_devices // 2
    inputs, small_ref = refs[:pieces], refs[pieces]
    outs, small_out = refs[pieces + 1 : 2 * pieces + 1], refs[2 * pieces + 1]
    own, first, summed, second, third_in, third, sends, recvs, loads, small_got, small_sends, small_recvs = refs[2 * pieces + 2 :]
    task, chip, core, pair, tasks, line = sum_partners(task_devices, feature_devices)
    greet(pair + tasks + line)
    own_loads = [
        pltpu.make_async_copy(inputs[p].at[:, :, core], own.at[p], loads.at[p]) for p in range(pieces)
    ]
    for load in own_loads:
        load.start()
    met(len(pair) + len(tasks) + len(line))

    started = []
    for p in range(pieces):
        copy = remote(inputs[p].at[:, :, 1 - core], first.at[p], sends.at[p, 0], recvs.at[p, 0], pair[0])
        copy.start()
        started.append([copy])
    small_slot = [0]

    def small_exchange(values, devices, index, base):
        copies = []
        for k, device in enumerate(devices):
            copy = remote(values, small_got.at[base + index], small_sends.at[base + k], small_recvs.at[base + k], device)
            copy.start()
            copies.append(copy)
        return copies

    def small_finish(copies, count, base):
        for copy in copies:
            copy.wait()
        total = small_got[base]
        for k in range(1, count):
            total = total + small_got[base + k]
        return total

    small_got[core] = small_ref[...]
    small_copies = small_exchange(small_got.at[core], pair, core, 0)
    for p in range(pieces):
        own_loads[p].wait()
        for copy in started[p]:
            copy.wait()

        def add_core(index, carry, p=p):
            t, z = index // chips, lax.rem(index, chips)
            summed[p, t, z] = (own[p, t, z].astype(f32) + first[p, t, z].astype(f32)).astype(bf16)
            return carry

        lax.fori_loop(0, task_devices * chips, add_core, 0)
        started[p] = []
        for k, device in enumerate(tasks):
            other = lax.rem(task + k + 1, task_devices)
            copy = remote(summed.at[p, other], second.at[p, k], sends.at[p, 1 + k], recvs.at[p, 1 + k], device)
            copy.start()
            started[p].append(copy)
    total = small_finish(small_copies, 2, 0)
    small_got[2 + task] = total
    small_copies = small_exchange(small_got.at[2 + task], tasks, task, 2)
    for p in range(pieces):
        for copy in started[p]:
            copy.wait()

        def add_tasks(z, carry, p=p):
            total = summed[p, task, z].astype(f32)
            for k in range(task_devices - 1):
                total = total + second[p, k, z].astype(f32)
            third_in[p, z] = total.astype(bf16)
            return carry

        lax.fori_loop(0, chips, add_tasks, 0)
        started[p] = []
        for k, device in enumerate(line):
            other = lax.rem(chip + k + 1, chips)
            slot = task_devices + k
            copy = remote(third_in.at[p, other], third.at[p, k], sends.at[p, slot], recvs.at[p, slot], device)
            copy.start()
            started[p].append(copy)
    total = small_finish(small_copies, task_devices, 2)
    base = 2 + task_devices
    small_got[base + chip] = total
    small_copies = small_exchange(small_got.at[base + chip], line, chip, base)
    for p in range(pieces):
        for copy in started[p]:
            copy.wait()
        total = third_in[p, chip].astype(f32)
        for k in range(chips - 1):
            total = total + third[p, k].astype(f32)
        outs[p][...] = total
    small_out[...] = small_finish(small_copies, chips, base)


def sum_everywhere(pieces, small, task_devices, feature_devices):
    chips = feature_devices // 2
    rows, width = pieces[0].shape
    share = rows // (task_devices * feature_devices)
    blocks = [piece.reshape(task_devices, chips, 2, share, width) for piece in pieces]
    count = len(pieces)
    copies = task_devices + chips - 1
    small_copies = 2 + task_devices + chips
    vmem, anywhere = pl.BlockSpec(memory_space=pltpu.VMEM), pl.BlockSpec(memory_space=pl.ANY)
    return pl.pallas_call(
        functools.partial(sum_tail, count, task_devices, feature_devices),
        name="sum_tail",
        out_shape=[jax.ShapeDtypeStruct((share, width), f32)] * count
        + [jax.ShapeDtypeStruct(small.shape, f32)],
        in_specs=[anywhere] * count + [vmem],
        out_specs=[vmem] * (count + 1),
        scratch_shapes=[
            pltpu.VMEM((count, task_devices, chips, share, width), bf16),
            pltpu.VMEM((count, task_devices, chips, share, width), bf16),
            pltpu.VMEM((count, task_devices, chips, share, width), bf16),
            pltpu.VMEM((count, task_devices - 1, chips, share, width), bf16),
            pltpu.VMEM((count, chips, share, width), bf16),
            pltpu.VMEM((count, chips - 1, share, width), bf16),
            pltpu.SemaphoreType.DMA((count, copies)),
            pltpu.SemaphoreType.DMA((count, copies)),
            pltpu.SemaphoreType.DMA((count,)),
            pltpu.VMEM((small_copies,) + small.shape, f32),
            pltpu.SemaphoreType.DMA((small_copies,)),
            pltpu.SemaphoreType.DMA((small_copies,)),
        ],
        compiler_params=pltpu.CompilerParams(
            vmem_limit_bytes=56 << 20, collective_id=0, has_side_effects=True
        ),
    )(*blocks, small)


SIZE = 16


class Place:
    def __init__(self, task_devices, feature_devices):
        self.tasks, self.places = task_devices, feature_devices
        self.chips = feature_devices // 2
        self.task, self.place = lax.axis_index("task"), lax.axis_index("feat")
        self.chip, self.core = self.place // 2, lax.rem(self.place, 2)

    def ring(self, step):
        return lax.rem(self.place + step, self.places)

    def line_partner(self, step):
        return lax.rem(self.chip + step, self.chips)

    def task_partner(self, step):
        return lax.rem(self.task + step, self.tasks)

    def greet(self):
        barrier = pltpu.get_barrier_semaphore()
        for step in range(1, self.places):
            pl.semaphore_signal(barrier, inc=1, device_id={"feat": self.ring(step)}, device_id_type=MESH)
        for step in range(1, self.tasks):
            pl.semaphore_signal(barrier, inc=1, device_id={"task": self.task_partner(step)}, device_id_type=MESH)

    def met(self):
        pl.semaphore_wait(pltpu.get_barrier_semaphore(), self.places - 1 + self.tasks - 1)


class SumStep:
    def __init__(self, step, place, source, own, got, sends, recvs, load):
        self.step = step
        if step == 1:
            self.mine = source.at[:, :, place.core]
            parts = [(source.at[:, :, 1 - place.core], got, {"feat": place.place + 1 - 2 * place.core})]
        elif step == 2:
            self.mine = source.at[place.task]
            parts = [
                (source.at[place.task_partner(k)], got.at[k - 1], {"task": place.task_partner(k)})
                for k in range(1, place.tasks)
            ]
        else:
            self.mine = source.at[place.chip]
            parts = [
                (source.at[place.line_partner(k)], got.at[k - 1], {"feat": 2 * place.line_partner(k) + place.core})
                for k in range(1, place.chips)
            ]
        self.copies = [
            remote(part, target, sends.at[k], recvs.at[k], device) for k, (part, target, device) in enumerate(parts)
        ]
        self.load = pltpu.make_async_copy(self.mine, own, load)
        self.own, self.got = own, got

    def start(self):
        for copy in self.copies:
            copy.start()
        self.load.start()

    def finish(self, out):
        self.load.wait()
        for copy in self.copies:
            copy.wait()
        own, got = self.own, self.got
        if self.step == 1:

            def add_core(index, carry):
                t, z = index // own.shape[1], lax.rem(index, own.shape[1])
                out[t, z] = (own[t, z].astype(f32) + got[t, z].astype(f32)).astype(bf16)
                return carry

            lax.fori_loop(0, own.shape[0] * own.shape[1], add_core, 0)
        elif self.step == 2:

            def add_tasks(z, carry):
                total = own[z].astype(f32)
                for k in range(got.shape[0]):
                    total = total + got[k, z].astype(f32)
                out[z] = total.astype(bf16)
                return carry

            lax.fori_loop(0, own.shape[0], add_tasks, 0)
        else:
            total = own[...].astype(f32)
            for k in range(got.shape[0]):
                total = total + got[k].astype(f32)
            out[...] = total


def sum_shapes(step, tasks, chips, share, width):
    if step == 1:
        return (tasks, chips, share, width), (tasks, chips, share, width), bf16, 1
    if step == 2:
        return (chips, share, width), (tasks - 1, chips, share, width), bf16, tasks - 1
    return (share, width), (chips - 1, share, width), f32, chips - 1


class Box:
    def __init__(self, place, ins, bufs, loads, outs, out_bufs, flush_sem, parts, steps):
        self.place, self.ins, self.bufs, self.loads = place, ins, bufs, loads
        self.outs, self.out_bufs, self.flush_sem, self.parts = outs, out_bufs, flush_sem, parts
        self.steps = steps
        self.waited, self.flushed = set(), []

    def use(self, *indices):
        found = []
        for index in indices:
            if index not in self.waited:
                self.waited.add(index)
                for load in self.loads[index]:
                    load.wait()
            found.append(self.bufs[index])
        return found if len(found) > 1 else found[0]

    def out(self, index):
        return self.out_bufs[index]

    def flush(self, index, part=0, view=None):
        source, target = self.out_bufs[index], self.outs[index]
        if view is not None:
            source, target = view(source, part), view(target, part)
        pltpu.make_async_copy(source, target, self.flush_sem.at[index, part]).start()

    def drain(self, index, view=None, parts=1):
        for part in range(parts):
            source, target = self.out_bufs[index], self.outs[index]
            if view is not None:
                source, target = view(source, part), view(target, part)
            pltpu.make_async_copy(source, target, self.flush_sem.at[index, part]).wait()

    def ready(self):
        self.place.met()
        for step, _, _ in self.steps:
            step.start()

    def finish_sums(self):
        for step, out, flush in self.steps:
            step.finish(out)
            flush.start()

    def end(self):
        for _, _, flush in self.steps:
            flush.wait()


def fused(body, name, place_sizes, ins, outs, scratch, sums, identity):
    tasks, places = place_sizes
    chips = places // 2
    anywhere = pl.BlockSpec(memory_space=pl.ANY)
    buffers = []
    for array, layer in ins:
        if layer != "raw":
            buffers.append(pltpu.VMEM(array.shape if layer is None else array.shape[1:], array.dtype))
    out_buffers = [pltpu.VMEM(shape, kind) for shape, kind, buffered in outs if buffered]
    sum_results, sum_scratch = [], []
    for step, array in sums:
        share, width = array.shape[-2:]
        own, got, kind, copies = sum_shapes(step, tasks, chips, share, width)
        sum_results.append(jax.ShapeDtypeStruct(own, kind))
        sum_scratch += [
            pltpu.VMEM(own, bf16),
            pltpu.VMEM(got, bf16),
            pltpu.VMEM(own, kind),
            pltpu.SemaphoreType.DMA((copies,)),
            pltpu.SemaphoreType.DMA((copies,)),
            pltpu.SemaphoreType.DMA((2,)),
        ]
    everything = buffers + out_buffers + list(scratch) + sum_scratch
    needed = 0
    for item in everything:
        if item.memory_space == pltpu.VMEM:
            count = 1
            for extent in item.shape:
                count *= extent
            needed += count * jnp.dtype(item.dtype).itemsize

    def kernel(*refs):
        rest = list(refs)

        def pop(count):
            taken = rest[:count]
            del rest[:count]
            return taken

        in_refs, sum_refs = pop(len(ins)), pop(len(sums))
        out_refs, sum_outs = pop(len(outs)), pop(len(sums))
        flat_in = pop(len(buffers))
        flat_out = pop(len(out_buffers))
        user = pop(len(scratch))
        sum_bufs = [pop(6) for _ in sums]
        load_sem, flush_sem = pop(2)
        place = Place(tasks, places)
        loads, bufs = [], []
        for index, (array, layer) in enumerate(ins):
            if layer == "raw":
                loads.append([])
                bufs.append(None)
                continue
            bufs.append(flat_in[len([1 for buf in bufs if buf is not None])])
            source = in_refs[index] if layer is None else in_refs[index].at[layer]
            copy = pltpu.make_async_copy(source, bufs[index], load_sem.at[index])
            copy.start()
            loads.append([copy])
        place.greet()
        out_bufs, at = [], 0
        for shape, kind, buffered in outs:
            if buffered:
                out_bufs.append(flat_out[at])
                at += 1
            else:
                out_bufs.append(None)
        steps = []
        for (step, array), source, out, (own, got, result, sends, recvs, local_sem) in zip(sums, sum_refs, sum_outs, sum_bufs):
            action = SumStep(step, place, source, own, got, sends, recvs, local_sem.at[0])
            steps.append((action, result, pltpu.make_async_copy(result, out, local_sem.at[1])))
        box = Box(place, in_refs, bufs, loads, out_refs, out_bufs, flush_sem, None, steps)
        body(box, *user)
        box.end()

    return pl.pallas_call(
        kernel,
        name=name,
        out_shape=[jax.ShapeDtypeStruct(shape, kind) for shape, kind, _ in outs] + sum_results,
        in_specs=[anywhere] * (len(ins) + len(sums)),
        out_specs=[anywhere] * (len(outs) + len(sums)),
        scratch_shapes=everything
        + [pltpu.SemaphoreType.DMA((max(len(ins), 1),)), pltpu.SemaphoreType.DMA((len(outs) + 1, 4))],
        compiler_params=pltpu.CompilerParams(
            vmem_limit_bytes=min(needed + (6 << 20), 60 << 20), collective_id=identity, has_side_effects=True
        ),
    )(*[array for array, _ in ins], *[array for _, array in sums])


def cross(ref, unit):
    block = ref[:, :, chunk(unit, SIZE), :]
    return block.reshape(block.shape[0] * block.shape[1] * SIZE, block.shape[3])


def put_cross(ref, unit, rows):
    features, blocks, _, width = ref.shape
    ref[:, :, chunk(unit, SIZE), :] = rows.reshape(features, blocks, SIZE, width)


def cross_view(ref, unit):
    return ref.at[:, :, chunk(unit, SIZE), :]


def own_rows(ref, f, unit, size, lanes=slice(None)):
    block = ref[f, :, chunk(unit, size), lanes]
    return block.reshape(block.shape[0] * size, block.shape[2])


def block_rows(ref, f, unit, per, lanes=slice(None)):
    block = ref[f, chunk(unit, per), :, lanes]
    return block.reshape(per * block.shape[1], block.shape[2])


def all_rows(ref, f, lanes):
    block = ref[f, :, :, lanes]
    return block.reshape(block.shape[0] * block.shape[1], block.shape[2])


def sample_forward_sends(box, h2_ref, sends, recvs, self_sem):
    x_ref, gain_ref, shift_ref = box.use(0, 1, 2)
    features, blocks, own, width = x_ref.shape
    per = ROWS // own
    steps = blocks // per
    size = ROWS // blocks
    place = box.place
    x1_ref, swapped, qkv_ref, ctx_ref, ext_ref = box.out(0), box.outs[1], box.out(2), box.out(3), box.out(4)
    w_ref = box.use(3)

    def project(unit, carry):
        f, part = unit // steps, lax.rem(unit, steps)
        _, _, hidden = layer_norm(block_rows(x_ref, f, part, per), gain_ref[0:1], shift_ref[0:1])
        hidden = hidden.astype(bf16)
        for member in range(3):
            out = mm(hidden, w_ref[member]).astype(bf16)
            if member == 0:
                out = out * jnp.asarray(0.125, bf16)
            qkv_ref[member, f, chunk(part, per), :, :] = out.reshape(per, own, width)
        return carry

    lax.fori_loop(0, features * steps, project, 0)
    box.flush(2)
    box.ready()
    qcode_ref, kcode_ref = box.use(4, 5)
    units = own // size

    def copies(unit):
        f, part = unit // units, lax.rem(unit, units)
        found = []
        for k in range(1, place.places):
            found.append(
                remote(
                    h2_ref.at[f, place.ring(k), chunk(part, size), :],
                    swapped.at[place.place, f, chunk(part, size), :],
                    sends.at[unit, k - 1],
                    recvs.at[unit, k - 1],
                    {"feat": place.ring(k)},
                )
            )
        keep = pltpu.make_async_copy(
            h2_ref.at[f, place.place, chunk(part, size), :],
            swapped.at[place.place, f, chunk(part, size), :],
            self_sem.at[unit],
        )
        return found, keep

    def attend(unit, carry):
        f, part = unit // units, lax.rem(unit, units)
        code = qcode_ref[...]

        def pair_step(pair, extras):
            lanes = chunk(pair, LANES)
            context, extras = attend_pair(
                own_rows(qkv_ref.at[0], f, part, size, lanes),
                all_rows(qkv_ref.at[1], f, lanes),
                all_rows(qkv_ref.at[2], f, lanes),
                code,
                kcode_ref[...],
                pair,
                extras,
            )
            ctx_ref[f, :, chunk(part, size), lanes] = context.reshape(blocks, size, LANES)
            return extras

        extras = lax.fori_loop(0, width // LANES, pair_step, code.astype(f32))
        ext_ref[f, :, chunk(part, size), :] = extras.astype(bf16).reshape(blocks, size, LANES)
        x1 = own_rows(x_ref, f, part, size) + mm(own_rows(ctx_ref, f, part, size), w_ref[3])
        x1_ref[f, :, chunk(part, size), :] = x1.reshape(blocks, size, width)
        _, _, hidden = layer_norm(x1, gain_ref[1:2], shift_ref[1:2])
        h2_ref[f, :, chunk(part, size), :] = hidden.astype(bf16).reshape(blocks, size, width)
        found, keep = copies(unit)
        for copy in found:
            copy.start()
        keep.start()
        return carry

    lax.fori_loop(0, features * units, attend, 0)
    for index in (0, 3, 4):
        box.flush(index)

    def settle(unit, carry):
        found, keep = copies(unit)
        for copy in found:
            copy.wait()
        keep.wait()
        return carry

    lax.fori_loop(0, features * units, settle, 0)
    for index in (0, 2, 3, 4):
        box.drain(index)


def feature_forward_dense(box, a_ref, back_ref, sends, recvs):
    h_ref, w_ref, qcode_ref, kcode_ref = box.use(0, 1, 2, 3)
    _, own, width = h_ref.shape
    place = box.place
    groups = own // SIZE
    qkv_ref, ctx_ref, ext_ref = box.out(0), box.out(1), box.out(2)
    x2_ref, x3_ref, u_ref = box.out(3), box.out(4), box.out(5)
    features = x2_ref.shape[0]
    box.ready()

    def copies(group):
        return [
            remote(
                a_ref.at[pl.ds(features * place.ring(k), features), chunk(group, SIZE), :],
                back_ref.at[:, place.place, chunk(group, SIZE), :],
                sends.at[group, k - 1],
                recvs.at[group, k - 1],
                {"feat": place.ring(k)},
            )
            for k in range(1, place.places)
        ]

    def step(group, carry):
        hidden = load_group(h_ref, group, SIZE)
        for member in range(3):
            out = mm(hidden, w_ref[member]).astype(bf16)
            if member == 0:
                out = out * jnp.asarray(0.125, bf16)
            qkv_ref[group, member] = out
        code = qcode_ref[...]

        def pair_step(pair, extras):
            lanes = chunk(pair, LANES)
            context, extras = attend_pair(
                qkv_ref[group, 0, :, lanes],
                qkv_ref[group, 1, :, lanes],
                qkv_ref[group, 2, :, lanes],
                code,
                kcode_ref[...],
                pair,
                extras,
            )
            ctx_ref[group, :, lanes] = context
            return extras

        extras = lax.fori_loop(0, width // LANES, pair_step, code.astype(f32))
        ext_ref[group] = extras.astype(bf16)
        store_group(a_ref, group, SIZE, mm(ctx_ref[group], w_ref[3]).astype(bf16))
        for copy in copies(group):
            copy.start()
        back_ref[:, place.place, chunk(group, SIZE), :] = a_ref[
            pl.ds(features * place.place, features), chunk(group, SIZE), :
        ]
        return carry

    lax.fori_loop(0, groups, step, 0)
    for index in range(3):
        box.flush(index)
    x1_ref, gain_ref, shift_ref, up_ref, upb_ref, down_ref, downb_ref = box.use(4, 5, 6, 7, 8, 9, 10)
    hidden_width = up_ref.shape[1]

    def dense(group, carry):
        for copy in copies(group):
            copy.wait_recv()
        x2 = cross(x1_ref, group) + cross(back_ref, group).astype(f32)
        put_cross(x2_ref, group, x2)
        _, _, hidden = layer_norm(x2, gain_ref[2:3], shift_ref[2:3])
        hidden = hidden.astype(bf16)
        total = x2 + downb_ref[...]
        for part in range(hidden_width // 512):
            cols = slice(part * 512, part * 512 + 512)
            expanded = mm(hidden, up_ref[:, cols]) + upb_ref[:, cols]
            u_ref[group, :, cols] = expanded.astype(bf16)
            active = (0.5 * expanded * (1.0 + gelu_parts(expanded))).astype(bf16)
            total = total + mm(active, down_ref[cols, :])
        put_cross(x3_ref, group, total)
        box.flush(3, group, cross_view)
        box.flush(4, group, cross_view)
        box.flush(5, group, lambda ref, part: ref.at[part])
        return carry

    lax.fori_loop(0, groups, dense, 0)

    def settle(group, carry):
        for copy in copies(group):
            copy.wait_send()
        return carry

    lax.fori_loop(0, groups, settle, 0)
    for index in range(3):
        box.drain(index)
    box.drain(3, cross_view, groups)
    box.drain(4, cross_view, groups)
    box.drain(5, lambda ref, part: ref.at[part], groups)


def exact(left, right, dims):
    first = right.astype(bf16)
    rest = right - first.astype(f32)
    second = rest.astype(bf16)
    third = (rest - second.astype(f32)).astype(bf16)
    return mm(left, first, dims) + mm(left, second, dims) + mm(left, third, dims)


def exact_left(left, right, dims):
    first = left.astype(bf16)
    rest = left - first.astype(f32)
    second = rest.astype(bf16)
    third = (rest - second.astype(f32)).astype(bf16)
    return mm(first, right, dims) + mm(second, right, dims) + mm(third, right, dims)


def read_out(box, got_ref, reading_ref, bins_ref, counted_ref, sends, recvs):
    x_ref, read_ref, rows_ref, weight_ref, og_ref = box.use(0, 1, 2, 3, 4)
    features, blocks, own, width = x_ref.shape
    samples = blocks * own
    place = box.place
    shapes_ref, loss_ref, rgrad_ref, g_ref = box.out(0), box.out(1), box.out(2), box.out(3)
    mask, task_size, label = rows_ref[0:1, :], rows_ref[1:2, :], rows_ref[2:3, :]
    bins = weight_ref.shape[1]
    logits = None
    for f in range(features):
        reading = x_ref[f].reshape(samples, width).astype(bf16)
        reading_ref[f] = reading
        projected = mm(reading, read_ref[...])
        bin_row = rows_ref[3 + f : 4 + f, :]
        onehot = (lax.broadcasted_iota(jnp.int32, (bins, samples), 0).astype(f32) == bin_row).astype(f32)
        bins_ref[f] = onehot.astype(bf16)
        chosen = onehot * mask
        counted = jnp.maximum(jnp.sum(chosen, axis=1, keepdims=True), 1.0)
        counted_ref[f] = jnp.broadcast_to(counted, (bins, LANES))
        means = exact(chosen.astype(bf16), projected, NN) / counted
        weight = weight_ref[f]
        centre = jnp.sum(weight * means, axis=0, keepdims=True) / jnp.sum(weight, axis=0, keepdims=True)
        shapes = means - centre
        shapes_ref[f] = shapes
        part = exact_left(shapes, bins_ref[f], TN)[:SIZE] * rows_ref[3 + features + f : 4 + features + f, :]
        logits = part if logits is None else logits + part
    box.flush(0)
    got_ref[place.place] = logits
    box.ready()
    copies = [
        remote(
            got_ref.at[place.place],
            got_ref.at[place.place],
            sends.at[k - 1],
            recvs.at[k - 1],
            {"feat": place.ring(k)},
        )
        for k in range(1, place.places)
    ]
    for copy in copies:
        copy.start()
    for copy in copies:
        copy.wait()
    logits = got_ref[0]
    for k in range(1, place.places):
        logits = logits + got_ref[k]
    class_row = lax.broadcasted_iota(jnp.int32, logits.shape, 0)
    inside = class_row < CLASSES
    peak = jnp.max(jnp.where(inside, logits, masked_score), axis=0, keepdims=True)
    weights = jnp.where(inside, jnp.exp(jnp.where(inside, logits - peak, 0.0)), 0.0)
    weight_sum = jnp.sum(weights, axis=0, keepdims=True)
    log_total = peak + jnp.log(weight_sum)
    own_class = (class_row.astype(f32) == label).astype(f32)
    picked = jnp.sum(logits * own_class, axis=0, keepdims=True)
    losses = mask * (log_total - picked)
    loss_ref[...] = jnp.broadcast_to(
        jnp.sum(losses, axis=1, keepdims=True) / task_size[:, 0:1], loss_ref.shape
    )
    logit_grad = mask * (weights / weight_sum - own_class) / task_size
    pad = jnp.zeros((LANES - SIZE, samples), f32)
    total = None
    for f in range(features):
        live = rows_ref[3 + features + f : 4 + features + f, :]
        grad_rows = jnp.concatenate([logit_grad * live, pad], axis=0)
        shape_grad = exact(bins_ref[f], grad_rows, NT)
        weight = weight_ref[f]
        means_grad = shape_grad - weight / jnp.sum(weight, axis=0, keepdims=True) * jnp.sum(
            shape_grad, axis=0, keepdims=True
        )
        chosen = (bins_ref[f].astype(f32) * mask).astype(bf16)
        proj_grad = exact(chosen, means_grad / counted_ref[f], TN).astype(bf16)
        part = mm(proj_grad, reading_ref[f], TN)[:SIZE]
        total = part if total is None else total + part
        back = mm(proj_grad, read_ref[...], NT).reshape(blocks, own, width)
        g_ref[f] = og_ref[f].astype(f32) + back
    rgrad_ref[...] = total
    for index in (1, 2, 3):
        box.flush(index)
    for index in (0, 1, 2, 3):
        box.drain(index)


def dense_backward_sends(box, send_ref, active_ref, ugrad_ref, hidden_ref, rowgrad_ref, sends, recvs, self_sem):
    g2_ref, small_ref, dup_ref, ddown_ref = box.out(1), box.out(2), box.out(3), box.out(4)
    arriving = box.outs[0]
    small_ref[...] = jnp.zeros_like(small_ref)
    g_ref, down_ref, u_ref, up_ref, x2_ref, gain_ref, shift_ref = box.use(0, 1, 2, 3, 4, 5, 6)
    features, blocks, own, width = g_ref.shape
    hidden_width = up_ref.shape[1]
    place = box.place
    groups = own // SIZE
    parts = hidden_width // 512
    box.ready()

    def copies(group):
        found = [
            remote(
                send_ref.at[:, place.ring(k), chunk(group, SIZE), :],
                arriving.at[place.place, :, chunk(group, SIZE), :],
                sends.at[group, k - 1],
                recvs.at[group, k - 1],
                {"feat": place.ring(k)},
            )
            for k in range(1, place.places)
        ]
        keep = pltpu.make_async_copy(
            send_ref.at[:, place.place, chunk(group, SIZE), :],
            arriving.at[place.place, :, chunk(group, SIZE), :],
            self_sem.at[group],
        )
        return found, keep

    def step(group, carry):
        rows = chunk(group, ROWS)
        grad = cross(g_ref, group)
        low = grad.astype(bf16)
        rowgrad_ref[rows, :] = low
        small_ref[parts : parts + 1] += jnp.sum(low.astype(f32), axis=0, keepdims=True)
        hidden_grad = None
        for part in range(parts):
            cols = slice(part * 512, part * 512 + 512)
            active_grad = mm(low, down_ref[cols, :], NT).astype(bf16).astype(f32)
            u = u_ref[group, :, cols].astype(f32)
            bent = gelu_parts(u)
            slope = 0.5 * (1.0 + bent) + u * (1.0 - bent * bent) * (
                0.3989422804014327 + 0.05351611220146811 * u * u
            )
            active_ref[rows, cols] = (0.5 * u * (1.0 + bent)).astype(bf16)
            ugrad = (active_grad * slope).astype(bf16)
            ugrad_ref[rows, cols] = ugrad
            small_ref[part : part + 1] += jnp.sum(ugrad.astype(f32), axis=0, keepdims=True)
            part_grad = mm(ugrad, up_ref[:, cols], NT)
            hidden_grad = part_grad if hidden_grad is None else hidden_grad + part_grad
        x2 = cross(x2_ref, group)
        _, _, hidden = layer_norm(x2, gain_ref[2:3], shift_ref[2:3])
        hidden_ref[rows, :] = hidden.astype(bf16)
        norm_grad, gain_part, shift_part = layer_norm_back(
            hidden_grad.astype(bf16).astype(f32), x2, gain_ref[2:3]
        )
        small_ref[parts + 1 : parts + 2] += gain_part
        small_ref[parts + 2 : parts + 3] += shift_part
        grad = grad + norm_grad
        put_cross(g2_ref, group, grad)
        put_cross(send_ref, group, grad.astype(bf16))
        found, keep = copies(group)
        for copy in found:
            copy.start()
        keep.start()
        return carry

    lax.fori_loop(0, groups, step, 0)
    box.flush(1)
    box.flush(2)

    def weights(part, carry):
        cols = chunk(part, 512)
        dup_ref[cols, :] = mm(ugrad_ref[:, cols], hidden_ref[...], TN).astype(bf16)
        ddown_ref[cols, :] = mm(active_ref[:, cols], rowgrad_ref[...], TN).astype(bf16)
        return carry

    lax.fori_loop(0, parts, weights, 0)
    box.flush(3)
    box.flush(4)
    box.finish_sums()

    def settle(group, carry):
        found, keep = copies(group)
        for copy in found:
            copy.wait()
        keep.wait()
        return carry

    lax.fori_loop(0, groups, settle, 0)
    for index in (1, 2, 3, 4):
        box.drain(index)


def feature_backward_enter(box, dqkv_ref, hidden_ref, dao_ref, dc_ref, dh_ref, back_ref, sends, recvs):
    dw_ref, g1_ref, small_ref = box.out(0), box.out(1), box.out(2)
    small_ref[...] = jnp.zeros_like(small_ref)
    da_ref, w_ref, kcode_ref, qkv_ref, ctx_ref, ext_ref = box.use(0, 1, 2, 3, 4, 5)
    _, own, width = da_ref.shape
    features = g1_ref.shape[0]
    place = box.place
    groups = own // SIZE
    box.ready()

    def copies(group):
        return [
            remote(
                dh_ref.at[pl.ds(features * place.ring(k), features), chunk(group, SIZE), :],
                back_ref.at[:, place.place, chunk(group, SIZE), :],
                sends.at[group, k - 1],
                recvs.at[group, k - 1],
                {"feat": place.ring(k)},
            )
            for k in range(1, place.places)
        ]

    def step(group, carry):
        dao = load_group(da_ref, group, SIZE)
        dao_ref[group] = dao
        context_grad = mm(dao, w_ref[3], NT).astype(bf16)
        dc_ref[...] = context_grad
        grad_extra = delta_extra(ctx_ref[group], context_grad)

        def pair_step(pair, inner):
            lanes = chunk(pair, LANES)
            query_grad, key_grad, value_grad = attend_pair_back(
                qkv_ref[group, 0, :, lanes],
                qkv_ref[group, 1, :, lanes],
                qkv_ref[group, 2, :, lanes],
                dc_ref[:, lanes],
                ext_ref[group],
                grad_extra,
                kcode_ref[...],
                pair,
            )
            dqkv_ref[0, group, :, lanes] = (query_grad * 0.125).astype(bf16)
            dqkv_ref[1, group, :, lanes] = key_grad.astype(bf16)
            dqkv_ref[2, group, :, lanes] = value_grad.astype(bf16)
            return inner

        lax.fori_loop(0, width // LANES, pair_step, 0)
        total = mm(dqkv_ref[0, group], w_ref[0], NT)
        total = total + mm(dqkv_ref[1, group], w_ref[1], NT)
        total = total + mm(dqkv_ref[2, group], w_ref[2], NT)
        store_group(dh_ref, group, SIZE, total.astype(bf16))
        for copy in copies(group):
            copy.start()
        back_ref[:, place.place, chunk(group, SIZE), :] = dh_ref[
            pl.ds(features * place.place, features), chunk(group, SIZE), :
        ]
        return carry

    lax.fori_loop(0, groups, step, 0)
    h_ref = box.use(6)

    def regroup(group, carry):
        hidden_ref[group] = load_group(h_ref, group, SIZE)
        return carry

    lax.fori_loop(0, groups, regroup, 0)

    def weights(member, carry):
        total = None
        for group in range(groups):
            part = mm(hidden_ref[group], dqkv_ref[member, group], TN)
            total = part if total is None else total + part
        dw_ref[member] = total.astype(bf16)
        return carry

    lax.fori_loop(0, 3, weights, 0)
    total = None
    for group in range(groups):
        part = mm(ctx_ref[group], dao_ref[group], TN)
        total = part if total is None else total + part
    dw_ref[3] = total.astype(bf16)
    box.flush(0)
    box.finish_sums()
    g2_ref, x1_ref, gain_ref = box.use(7, 8, 9)

    def enter(group, carry):
        for copy in copies(group):
            copy.wait_recv()
        norm_grad, gain_part, shift_part = layer_norm_back(
            cross(back_ref, group).astype(f32), cross(x1_ref, group), gain_ref[1:2]
        )
        small_ref[0:1] += gain_part
        small_ref[1:2] += shift_part
        put_cross(g1_ref, group, cross(g2_ref, group) + norm_grad)
        box.flush(1, group, cross_view)
        return carry

    lax.fori_loop(0, groups, enter, 0)
    box.flush(2)

    def settle(group, carry):
        for copy in copies(group):
            copy.wait_send()
        return carry

    lax.fori_loop(0, groups, settle, 0)
    box.drain(0)
    box.drain(1, cross_view, groups)
    box.drain(2)


def sample_backward_sums(box, dqkv_ref, hidden_ref, low_ref, dc_ref, gext_ref, kacc_ref, vacc_ref):
    g0_ref, dw_ref, small_ref = box.out(0), box.out(1), box.out(2)
    small_ref[...] = jnp.zeros_like(small_ref)
    g_ref, w_ref, ctx_ref = box.use(0, 1, 2)
    features, blocks, own, width = g_ref.shape
    per = ROWS // own
    steps = blocks // per
    box.ready()

    def enter(unit, carry):
        f, part = unit // steps, lax.rem(unit, steps)
        low = block_rows(g_ref, f, part, per).astype(bf16)
        low_ref[f, chunk(part, ROWS), :] = low
        context_grad = mm(low, w_ref[3], NT).astype(bf16)
        dc_ref[f, chunk(part, ROWS), :] = context_grad
        gext_ref[f, chunk(part, ROWS), :] = delta_extra(block_rows(ctx_ref, f, part, per), context_grad)
        return carry

    lax.fori_loop(0, features * steps, enter, 0)
    qkv_ref, ext_ref, kcode_ref = box.use(3, 4, 5)

    def attend(unit, carry):
        f, pair = unit // (width // LANES), lax.rem(unit, width // LANES)
        lanes = chunk(pair, LANES)

        def query_step(step, inner):
            rows = chunk(step, ROWS)
            query_grad, key_grad, value_grad = attend_pair_back(
                block_rows(qkv_ref.at[0], f, step, per, lanes),
                all_rows(qkv_ref.at[1], f, lanes),
                all_rows(qkv_ref.at[2], f, lanes),
                dc_ref[f, rows, lanes],
                block_rows(ext_ref, f, step, per),
                gext_ref[f, rows, :],
                kcode_ref[...],
                pair,
            )
            dqkv_ref[0, f, rows, lanes] = (query_grad * 0.125).astype(bf16)
            first = step == 0
            kacc_ref[...] = jnp.where(first, 0.0, kacc_ref[...]) + key_grad
            vacc_ref[...] = jnp.where(first, 0.0, vacc_ref[...]) + value_grad
            return inner

        lax.fori_loop(0, steps, query_step, 0)
        dqkv_ref[1, f, :, lanes] = kacc_ref[...].astype(bf16)
        dqkv_ref[2, f, :, lanes] = vacc_ref[...].astype(bf16)
        return carry

    kacc_ref[...] = jnp.zeros_like(kacc_ref)
    vacc_ref[...] = jnp.zeros_like(vacc_ref)
    lax.fori_loop(0, features * (width // LANES), attend, 0)
    x_ref, gain_ref, shift_ref = box.use(6, 7, 8)

    def leave(unit, carry):
        f, part = unit // steps, lax.rem(unit, steps)
        rows = chunk(part, ROWS)
        total = mm(dqkv_ref[0, f, rows, :], w_ref[0], NT)
        total = total + mm(dqkv_ref[1, f, rows, :], w_ref[1], NT)
        total = total + mm(dqkv_ref[2, f, rows, :], w_ref[2], NT)
        x = block_rows(x_ref, f, part, per)
        _, _, hidden = layer_norm(x, gain_ref[0:1], shift_ref[0:1])
        hidden_ref[f, rows, :] = hidden.astype(bf16)
        norm_grad, gain_part, shift_part = layer_norm_back(
            total.astype(bf16).astype(f32), x, gain_ref[0:1]
        )
        small_ref[0:1] += gain_part
        small_ref[1:2] += shift_part
        g0_ref[f, chunk(part, per), :, :] = (block_rows(g_ref, f, part, per) + norm_grad).reshape(per, own, width)
        return carry

    lax.fori_loop(0, features * steps, leave, 0)
    box.flush(0)
    box.flush(2)

    def weights(member, carry):
        total = None
        for f in range(features):
            part = mm(hidden_ref[f], dqkv_ref[member, f], TN)
            total = part if total is None else total + part
        dw_ref[member] = total.astype(bf16)
        return carry

    lax.fori_loop(0, 3, weights, 0)
    total = None
    for f in range(features):
        part = mm(all_rows(ctx_ref, f, slice(None)), low_ref[f], TN)
        total = part if total is None else total + part
    dw_ref[3] = total.astype(bf16)
    box.flush(1)
    box.finish_sums()
    for index in range(3):
        box.drain(index)


def last_sums(layers, box, *refs):
    refs = list(refs)

    def pop(count):
        taken = refs[:count]
        del refs[:count]
        return taken

    place = box.place
    packed, small_got, small_sends, small_recvs = pop(4)
    bufs = [pop(6) for _ in range(7)]

    def make(index, step, source):
        own, got, _, sends, recvs, local_sem = bufs[index]
        return SumStep(step, place, source, own, got, sends, recvs, local_sem.at[0])

    result = [buf[2] for buf in bufs]
    place.met()
    steps = [make(0, 1, box.ins[0]), None, None, make(3, 2, box.ins[1]), None]
    steps += [make(5, 3, box.ins[2]), make(6, 3, box.ins[3])]
    for index in (0, 3, 5, 6):
        steps[index].start()
    smalls = box.use(*range(8, 8 + 3 * layers + 1))
    rows = 0
    for layer in range(layers):
        dense, feature, sample = smalls[3 * layer : 3 * layer + 3]
        packed[12 * layer : 12 * layer + 8] = dense[...]
        packed[12 * layer + 8 : 12 * layer + 10] = feature[0:2]
        packed[12 * layer + 10 : 12 * layer + 12] = sample[0:2]
    packed[12 * layers : 12 * layers + SIZE] = smalls[-1][...]

    def exchange(base, index, devices):
        copies = [
            remote(small_got.at[base + index], small_got.at[base + index], small_sends.at[base + k], small_recvs.at[base + k], device)
            for k, device in enumerate(devices)
        ]
        for copy in copies:
            copy.start()
        return copies

    def gather(copies, base, count):
        for copy in copies:
            copy.wait()
        total = small_got[base]
        for k in range(1, count):
            total = total + small_got[base + k]
        return total

    small_got[place.core] = packed[...]
    small = exchange(0, place.core, [{"feat": place.place + 1 - 2 * place.core}])
    steps[0].finish(result[0])
    steps[1] = make(1, 2, result[0])
    steps[1].start()
    small_got[2 + place.task] = gather(small, 0, 2)
    small = exchange(2, place.task, [{"task": place.task_partner(k)} for k in range(1, place.tasks)])
    steps[3].finish(result[3])
    steps[4] = make(4, 3, result[3])
    steps[4].start()
    for index in (5, 6):
        steps[index].finish(result[index])
    base = 2 + place.tasks
    small_got[base + place.chip] = gather(small, 2, place.tasks)
    small = exchange(
        base, place.chip, [{"feat": 2 * place.line_partner(k) + place.core} for k in range(1, place.chips)]
    )
    steps[1].finish(result[1])
    steps[2] = make(2, 3, result[1])
    steps[2].start()
    sample_out, feature_out, up_out, down_out, gain_out, shift_out, upb_out, downb_out, read_out_ref = [
        box.out(index) for index in range(9)
    ]
    later = box.use(4, 5, 6, 7)
    feature_out[1], up_out[1], down_out[1], sample_out[1] = (
        later[1][...],
        later[2][...].T,
        later[3][...],
        later[0][...],
    )
    up_out[0], down_out[0] = result[5][...].T, result[6][...]
    for index in (2, 3):
        box.flush(index)
    steps[4].finish(result[4])
    feature_out[0] = result[4][...]
    box.flush(1)
    total = gather(small, base, place.chips)
    packed[...] = total
    for layer in range(layers):
        at = 12 * layer
        parts = upb_out.shape[1] // packed.shape[1]
        for part in range(parts):
            upb_out[layer : layer + 1, part * packed.shape[1] : (part + 1) * packed.shape[1]] = packed[at + part : at + part + 1]
        downb_out[layer : layer + 1] = packed[at + parts : at + parts + 1]
        gain_out[layer, 2:3] = packed[at + 5 : at + 6]
        shift_out[layer, 2:3] = packed[at + 6 : at + 7]
        gain_out[layer, 1:2] = packed[at + 8 : at + 9]
        shift_out[layer, 1:2] = packed[at + 9 : at + 10]
        gain_out[layer, 0:1] = packed[at + 10 : at + 11]
        shift_out[layer, 0:1] = packed[at + 11 : at + 12]
    read_out_ref[...] = packed[12 * layers : 12 * layers + SIZE]
    for index in range(4, 9):
        box.flush(index)
    steps[2].finish(result[2])
    sample_out[0] = result[2][...]
    box.flush(0)
    for index in range(9):
        box.drain(index)


def codes(item, live, size, rows):
    lanes = jnp.arange(LANES)[None, :] - CODE_LANE
    inside = (lanes >= 0) & (lanes < size)
    own = lanes == item[:, None]
    query_code = (own & inside).astype(bf16)
    key_code = jnp.where(inside & ~(own & live[:, None]), masked_score, 0.0).astype(bf16)
    return query_code, key_code


def local_fused(
    tokens_in,
    sample_weights,
    feature_weights,
    norm_gain,
    norm_shift,
    up_weight,
    up_bias,
    down_weight,
    down_bias,
    read_weight,
    output_grad,
    task_sizes,
    feature_counts,
    bin_index,
    bin_counts,
    class_labels,
):
    samples, features, width = tokens_in.shape[1:]
    hidden_width = up_weight.shape[2]
    tasks, places = lax.axis_size("task"), lax.axis_size("feat")
    chips = places // 2
    all_features = features * places
    own = samples // places
    groups = own // SIZE
    units = features * (own * places // ROWS)
    sizes = (tasks, places)
    shape = (features, places, own, width)
    block_shape = (places, features, own, width)
    group_shape = (groups, ROWS, width)
    share = width // places
    dma = pltpu.SemaphoreType.DMA

    sample_live = jnp.arange(samples) < task_sizes[0]
    feature_live = jnp.arange(all_features) < feature_counts[0]
    sample_qcode, sample_kcode = codes(jnp.zeros((samples,), jnp.int32), sample_live, 1, samples)
    sample_qcode = sample_qcode[:ROWS]
    item = jnp.arange(ROWS) % SIZE
    feature_qcode, feature_kcode = codes(item, jnp.repeat(feature_live, SIZE), SIZE, ROWS)
    up_bias = up_bias[:, None]
    down_bias = down_bias[:, None]

    stream = tokens_in[0].astype(f32).transpose(1, 0, 2).reshape(shape)
    stored = []
    for layer in range(LAYERS):
        x1, swapped, qkv, ctx, ext = fused(
            sample_forward_sends,
            "sample_forward",
            sizes,
            [
                (stream, None),
                (norm_gain, layer),
                (norm_shift, layer),
                (sample_weights, layer),
                (sample_qcode, None),
                (sample_kcode, None),
            ],
            [
                (shape, f32, True),
                (block_shape, bf16, False),
                ((3,) + shape, bf16, True),
                (shape, bf16, True),
                (shape[:3] + (LANES,), bf16, True),
            ],
            [pltpu.VMEM(shape, bf16), dma((units, places - 1)), dma((units, places - 1)), dma((units,))],
            [],
            1 + 2 * layer,
        )
        swapped = swapped.reshape(all_features, own, width)
        fqkv, fctx, fext, x2, x3, u = fused(
            feature_forward_dense,
            "feature_forward",
            sizes,
            [
                (swapped, None),
                (feature_weights, layer),
                (feature_qcode, None),
                (feature_kcode, None),
                (x1, None),
                (norm_gain, layer),
                (norm_shift, layer),
                (up_weight, layer),
                (up_bias, layer),
                (down_weight, layer),
                (down_bias, layer),
            ],
            [
                ((groups, 3, ROWS, width), bf16, True),
                (group_shape, bf16, True),
                ((groups, ROWS, LANES), bf16, True),
                (shape, f32, True),
                (shape, f32, True),
                ((groups, ROWS, hidden_width), bf16, True),
            ],
            [
                pltpu.VMEM((all_features, own, width), bf16),
                pltpu.VMEM(shape, bf16),
                dma((groups, places - 1)),
                dma((groups, places - 1)),
            ],
            [],
            2 + 2 * layer,
        )
        stored.append((stream, x1, qkv, ctx, ext, swapped, fqkv, fctx, fext, x2, u))
        stream = x3

    size_float = task_sizes[0].astype(f32)
    local_index = lax.axis_index("feat") * features + jnp.arange(features)
    local_live = (local_index < feature_counts[0]).astype(f32)
    rows = jnp.concatenate(
        [
            sample_live.astype(f32)[None],
            jnp.broadcast_to(size_float, (1, samples)),
            class_labels.astype(f32),
            bin_index[0].T.astype(f32),
            jnp.broadcast_to(local_live[:, None], (features, samples)),
        ]
    )
    weight_rows = jnp.broadcast_to(bin_counts[0].astype(f32)[..., None], (features, BINS, LANES))
    read_wide = jnp.pad(read_weight, ((0, 0), (0, LANES - CLASSES)))
    shapes, loss, read_grad, stream_grad = fused(
        read_out,
        "read_out",
        sizes,
        [
            (stream, None),
            (read_wide, None),
            (rows, None),
            (weight_rows, None),
            (output_grad[0].transpose(1, 0, 2).reshape(shape), None),
        ],
        [
            ((features, BINS, LANES), f32, True),
            ((8, LANES), f32, True),
            ((SIZE, width), f32, True),
            (shape, f32, True),
        ],
        [
            pltpu.VMEM((places, SIZE, samples), f32),
            pltpu.VMEM((features, samples, width), bf16),
            pltpu.VMEM((features, BINS, samples), bf16),
            pltpu.VMEM((features, BINS, LANES), f32),
            dma((places - 1,)),
            dma((places - 1,)),
        ],
        [],
        5,
    )

    def piece(array):
        return array.reshape(tasks, chips, 2, share, width)

    smalls = [None] * LAYERS
    waiting = []
    finished = {}
    for layer in reversed(range(LAYERS)):
        x0, x1, qkv, ctx, ext, swapped, fqkv, fctx, fext, x2, u = stored[layer]
        base = 6 + 3 * layer

        def steps(names):
            picked = [entry for entry in waiting if entry[0] in names]
            return picked, [(entry[1], entry[2]) for entry in picked]

        def advance(picked, results):
            for entry, result in zip(picked, results):
                waiting.remove(entry)
                if entry[1] == 3:
                    finished[entry[0]] = result
                else:
                    waiting.append((entry[0], entry[1] + 1, result))

        every = [entry[0] for entry in waiting]
        picked, sums = steps(every)
        arriving, g2, dense_small, dup, ddown, *results = fused(
            dense_backward_sends,
            "dense_backward",
            sizes,
            [
                (stream_grad, None),
                (down_weight, layer),
                (u, None),
                (up_weight, layer),
                (x2, None),
                (norm_gain, layer),
                (norm_shift, layer),
            ],
            [
                (block_shape, bf16, False),
                (shape, f32, True),
                ((8, width), f32, True),
                ((hidden_width, width), bf16, True),
                ((hidden_width, width), bf16, True),
            ],
            [
                pltpu.VMEM(shape, bf16),
                pltpu.VMEM((groups * ROWS, hidden_width), bf16),
                pltpu.VMEM((groups * ROWS, hidden_width), bf16),
                pltpu.VMEM((groups * ROWS, width), bf16),
                pltpu.VMEM((groups * ROWS, width), bf16),
                dma((groups, places - 1)),
                dma((groups, places - 1)),
                dma((groups,)),
            ],
            sums,
            base,
        )
        advance(picked, results)
        waiting += [(("up", layer), 1, piece(dup)), (("down", layer), 1, piece(ddown))]
        picked, sums = steps([entry[0] for entry in waiting])
        dwf, g1, feature_small, *results = fused(
            feature_backward_enter,
            "feature_backward",
            sizes,
            [
                (arriving.reshape(all_features, own, width), None),
                (feature_weights, layer),
                (feature_kcode, None),
                (fqkv, None),
                (fctx, None),
                (fext, None),
                (swapped, None),
                (g2, None),
                (x1, None),
                (norm_gain, layer),
            ],
            [((4, width, width), bf16, True), (shape, f32, True), ((8, width), f32, True)],
            [
                pltpu.VMEM((3,) + group_shape, bf16),
                pltpu.VMEM(group_shape, bf16),
                pltpu.VMEM(group_shape, bf16),
                pltpu.VMEM((ROWS, width), bf16),
                pltpu.VMEM((all_features, own, width), bf16),
                pltpu.VMEM(shape, bf16),
                dma((groups, places - 1)),
                dma((groups, places - 1)),
            ],
            sums,
            base + 1,
        )
        advance(picked, results)
        waiting += [(("feature", layer), 1, piece(dwf))]
        picked, sums = steps([entry[0] for entry in waiting])
        stream_grad, dws, sample_small, *results = fused(
            sample_backward_sums,
            "sample_backward",
            sizes,
            [
                (g1, None),
                (sample_weights, layer),
                (ctx, None),
                (qkv, None),
                (ext, None),
                (sample_kcode, None),
                (x0, None),
                (norm_gain, layer),
                (norm_shift, layer),
            ],
            [(shape, f32, True), ((4, width, width), bf16, True), ((8, width), f32, True)],
            [
                pltpu.VMEM((3, features, samples, width), bf16),
                pltpu.VMEM((features, samples, width), bf16),
                pltpu.VMEM((features, samples, width), bf16),
                pltpu.VMEM((features, samples, width), bf16),
                pltpu.VMEM((features, samples, LANES), bf16),
                pltpu.VMEM((samples, LANES), f32),
                pltpu.VMEM((samples, LANES), f32),
            ],
            sums,
            base + 2,
        )
        advance(picked, results)
        waiting += [(("sample", layer), 1, piece(dws))]
        smalls[layer] = (dense_small, feature_small, sample_small)

    left = {entry[0]: entry for entry in waiting}
    order = [("sample", 0), ("feature", 0), ("up", 0), ("down", 0)]
    begin = [left[name] for name in order]
    scratch = []
    for step in (1, 2, 3, 2, 3, 3, 3):
        mine, got, kind, count = sum_shapes(step, tasks, chips, share, width)
        scratch += [
            pltpu.VMEM(mine, bf16),
            pltpu.VMEM(got, bf16),
            pltpu.VMEM(mine, kind),
            dma((count,)),
            dma((count,)),
            dma((2,)),
        ]
    packed_rows = 12 * LAYERS + SIZE
    slots = 2 + tasks + chips
    ins = [(entry[2], "raw") for entry in begin]
    ins += [(finished[(name, 1)], None) for name, _ in order]
    ins += [(row, None) for layer in range(LAYERS) for row in smalls[layer]]
    ins.append((read_grad, None))
    matrix_shape = (LAYERS, share, width)
    tail = fused(
        functools.partial(last_sums, LAYERS),
        "sum_tail",
        sizes,
        ins,
        [
            (matrix_shape, f32, True),
            (matrix_shape, f32, True),
            ((LAYERS, width, share), f32, True),
            (matrix_shape, f32, True),
            ((LAYERS, 3, width), f32, True),
            ((LAYERS, 3, width), f32, True),
            ((LAYERS, hidden_width), f32, True),
            ((LAYERS, width), f32, True),
            ((SIZE, width), f32, True),
        ],
        [
            pltpu.VMEM((packed_rows, width), f32),
            pltpu.VMEM((slots, packed_rows, width), f32),
            dma((slots,)),
            dma((slots,)),
        ]
        + scratch,
        [],
        12,
    )
    return (
        stream.reshape(features, samples, width).transpose(1, 0, 2)[None],
        shapes[None, :, :, :CLASSES],
        stream_grad.reshape(features, samples, width).transpose(1, 0, 2)[None],
        loss[0, :1],
        tail[0][:, None],
        tail[1][:, None],
        tail[4],
        tail[5],
        tail[2],
        tail[6],
        tail[3],
        tail[7],
        tail[8][:CLASSES].T,
    )


def local(
    tokens_in,
    sample_weights,
    feature_weights,
    norm_gain,
    norm_shift,
    up_weight,
    up_bias,
    down_weight,
    down_bias,
    read_weight,
    output_grad,
    task_sizes,
    feature_counts,
    bin_index,
    bin_counts,
    class_labels,
):
    samples = tokens_in.shape[1]
    features = tokens_in.shape[2]
    width = tokens_in.shape[3]
    hidden_width = up_weight.shape[2]
    task_devices = lax.axis_size("task")
    feature_devices = lax.axis_size("feat")
    all_features = features * feature_devices
    own_samples = samples // feature_devices
    size = min(16, own_samples)
    groups = own_samples // size
    group_rows = all_features * size
    rows_total = features * samples

    if (
        own_samples % 32 == 0
        and samples % ROWS == 0
        and ROWS % own_samples == 0
        and group_rows == ROWS
        and task_devices == hidden_width // width == 4
    ):
        return local_fused(
            tokens_in,
            sample_weights,
            feature_weights,
            norm_gain,
            norm_shift,
            up_weight,
            up_bias,
            down_weight,
            down_bias,
            read_weight,
            output_grad,
            task_sizes,
            feature_counts,
            bin_index,
            bin_counts,
            class_labels,
        )

    sample_live = jnp.arange(samples) < task_sizes[0]
    feature_live = jnp.arange(all_features) < feature_counts[0]
    sample_mask = sample_live.astype(f32)
    local_index = lax.axis_index("feat") * features + jnp.arange(features)
    local_live = (local_index < feature_counts[0]).astype(f32)
    sample_qcode, sample_kcode = codes(jnp.zeros((samples,), jnp.int32), sample_live, 1, samples)
    sample_qcode = sample_qcode[:ROWS]
    item = jnp.arange(group_rows) % size
    feature_qcode, feature_kcode = codes(item, jnp.repeat(feature_live, size), size, group_rows)

    def exchange_out(rows):
        parts = rows.reshape(features, feature_devices, own_samples, width)
        got = lax.all_to_all(parts, "feat", split_axis=1, concat_axis=0, tiled=True)
        return got.reshape(all_features, own_samples, width)

    def exchange_back(rows):
        parts = rows.reshape(feature_devices, features, own_samples, width)
        got = lax.all_to_all(parts, "feat", split_axis=0, concat_axis=2, tiled=True)
        return got.reshape(features, samples, width)

    stream = tokens_in[0].astype(f32).transpose(1, 0, 2)
    token_shape = (features, samples, width)
    stored = []
    for layer in range(LAYERS):
        gain, shift = norm_gain[layer], norm_shift[layer]
        x1, h2, qkv, ctx, ext = call(
            sample_forward,
            "sample_forward",
            [
                (token_shape, f32),
                (token_shape, bf16),
                ((3,) + token_shape, bf16),
                (token_shape, bf16),
                ((features, samples, LANES), bf16),
            ],
            [],
            stream,
            gain,
            shift,
            sample_weights[layer],
            sample_qcode,
            sample_kcode,
        )
        swapped = exchange_out(h2)
        a, fqkv, fctx, fext = call(
            functools.partial(feature_forward, size),
            "feature_forward",
            [
                ((all_features, own_samples, width), bf16),
                ((groups, 3, group_rows, width), bf16),
                ((groups, group_rows, width), bf16),
                ((groups, group_rows, LANES), bf16),
            ],
            [],
            swapped,
            feature_weights[layer],
            feature_qcode,
            feature_kcode,
        )
        back = exchange_back(a)
        x3, u = call(
            dense_forward,
            "dense_forward",
            [((rows_total, width), f32), ((rows_total, hidden_width), bf16)],
            [],
            x1.reshape(rows_total, width),
            back.reshape(rows_total, width),
            gain,
            shift,
            up_weight[layer],
            up_bias[layer][None],
            down_weight[layer],
            down_bias[layer][None],
        )
        stored.append((stream, x1, qkv, ctx, ext, swapped, fqkv, fctx, fext, back, u))
        stream = x3.reshape(token_shape)

    reading = stream.astype(bf16)
    projected = jnp.einsum("fsd,dc->fsc", reading, read_weight, preferred_element_type=f32)
    onehot_bins = (bin_index[0].T[..., None] == jnp.arange(BINS)).astype(f32)
    chosen = onehot_bins * sample_mask[None, :, None]
    counted = jnp.maximum(jnp.sum(chosen, axis=1), 1.0)
    bin_sums = jnp.einsum("fsb,fsc->fbc", chosen, projected, precision=highest)
    bin_means = bin_sums / counted[..., None]
    bin_weight = bin_counts[0].astype(f32)
    weight_total = jnp.sum(bin_weight, axis=-1, keepdims=True)
    centre = jnp.sum(bin_weight[..., None] * bin_means, axis=1, keepdims=True) / weight_total[..., None]
    shapes = bin_means - centre
    used_bins = onehot_bins * local_live[:, None, None]
    local_logits = jnp.einsum("fsb,fbc->sc", used_bins, shapes, precision=highest)
    logits = lax.psum(local_logits, "feat")
    row_max = jnp.max(logits, axis=-1, keepdims=True)
    log_total = row_max + jnp.log(jnp.sum(jnp.exp(logits - row_max), axis=-1, keepdims=True))
    label_rows = (class_labels[0][:, None] == jnp.arange(CLASSES)).astype(f32)
    picked = jnp.sum(logits * label_rows, axis=-1)
    live_count = task_sizes[0].astype(f32)
    task_loss = jnp.sum(sample_mask * (log_total[:, 0] - picked)) / live_count
    logit_grad = sample_mask[:, None] * (jnp.exp(logits - log_total) - label_rows) / live_count
    shape_grad = jnp.einsum("fsb,sc->fbc", used_bins, logit_grad, precision=highest)
    means_grad = shape_grad - bin_weight[..., None] / weight_total[..., None] * jnp.sum(
        shape_grad, axis=1, keepdims=True
    )
    sum_grad = means_grad / counted[..., None]
    projected_grad = jnp.einsum("fsb,fbc->fsc", chosen, sum_grad, precision=highest).astype(bf16)
    read_grad = jnp.einsum("fsd,fsc->dc", reading, projected_grad, preferred_element_type=f32)
    stream_grad = output_grad[0].astype(f32).transpose(1, 0, 2) + jnp.einsum(
        "fsc,dc->fsd", projected_grad, read_weight, preferred_element_type=f32
    )

    small = [None] * LAYERS
    big = [None] * LAYERS
    for layer in reversed(range(LAYERS)):
        gain, shift = norm_gain[layer], norm_shift[layer]
        x0, x1, qkv, ctx, ext, swapped, fqkv, fctx, fext, back, u = stored[layer]
        flat = (rows_total, width)
        g2, sent, dup, ddown, dupb, ddownb, dgs2 = call(
            dense_backward,
            "dense_backward",
            [
                (flat, f32),
                (flat, bf16),
                ((hidden_width, width), bf16),
                ((hidden_width, width), bf16),
                ((1, hidden_width), f32),
                ((1, width), f32),
                ((2, width), f32),
            ],
            [
                ((rows_total, hidden_width), bf16),
                ((rows_total, hidden_width), bf16),
                (flat, bf16),
                (flat, bf16),
            ],
            stream_grad.reshape(flat),
            x1.reshape(flat),
            back.reshape(flat),
            u,
            gain,
            shift,
            up_weight[layer],
            down_weight[layer],
        )
        arriving = exchange_out(sent.reshape(token_shape))
        group_shape = (groups, group_rows, width)
        dh, dwf = call(
            functools.partial(feature_backward, size),
            "feature_backward",
            [((all_features, own_samples, width), bf16), ((4, width, width), bf16)],
            [
                ((3,) + group_shape, bf16),
                (group_shape, bf16),
                (group_shape, bf16),
                ((group_rows, width), bf16),
            ],
            arriving,
            swapped,
            feature_weights[layer],
            feature_kcode,
            fqkv,
            fctx,
            fext,
        )
        returned = exchange_back(dh)
        g0, dws, dgs01 = call(
            sample_backward,
            "sample_backward",
            [(token_shape, f32), ((4, width, width), bf16), ((2, 2, width), f32)],
            [
                ((3,) + token_shape, bf16),
                (token_shape, bf16),
                (token_shape, bf16),
                (token_shape, bf16),
                ((features, samples, LANES), bf16),
                ((samples, LANES), f32),
                ((samples, LANES), f32),
            ],
            g2.reshape(token_shape),
            returned,
            x1,
            x0,
            gain,
            shift,
            sample_weights[layer],
            sample_kcode,
            qkv,
            ctx,
            ext,
        )
        stream_grad = g0
        small[layer] = (
            jnp.stack([dgs01[0, 0], dgs01[1, 0], dgs2[0]]),
            jnp.stack([dgs01[0, 1], dgs01[1, 1], dgs2[1]]),
            dupb[0],
            ddownb[0],
        )
        big[layer] = [dws.reshape(4 * width, width), dwf.reshape(4 * width, width), dup, ddown]
    shard_shape = (LAYERS, 4 // task_devices, width // feature_devices, width)
    pieces = [big[layer][member] for member in range(4) for layer in range(LAYERS)]
    rows = [row.reshape(-1, width) for layer in range(LAYERS) for row in small[layer]]
    rows.append(read_grad.T)
    lengths = [row.shape[0] for row in rows]
    fill = -sum(lengths) % 8
    small_rows = jnp.concatenate(rows + [jnp.zeros((fill, width), f32)])
    if (width // feature_devices) % 16 == 0:
        *shares, small_sums = sum_everywhere(pieces, small_rows, task_devices, feature_devices)
    else:
        shares = [
            lax.psum_scatter(piece, ("task", "feat"), scatter_dimension=0, tiled=True).astype(f32)
            for piece in pieces
        ]
        small_sums = lax.psum(small_rows, ("task", "feat"))
    matrices = [jnp.stack(shares[member * LAYERS : member * LAYERS + LAYERS]) for member in range(4)]
    split = []
    at = 0
    for length in lengths:
        split.append(small_sums[at : at + length])
        at += length
    summed = [jnp.stack([split[4 * layer + member] for layer in range(LAYERS)]) for member in range(4)]
    summed[2] = summed[2].reshape(LAYERS, hidden_width)
    summed[3] = summed[3].reshape(LAYERS, width)
    summed.append(split[-1].T)
    return (
        stream.transpose(1, 0, 2)[None],
        shapes[None],
        stream_grad.transpose(1, 0, 2)[None],
        task_loss[None],
        matrices[0].reshape(shard_shape),
        matrices[1].reshape(shard_shape),
        summed[0],
        summed[1],
        matrices[2].transpose(0, 2, 1),
        summed[2],
        matrices[3],
        summed[3],
        summed[4],
    )


def solution(mesh):
    in_specs = (
        P("task", None, "feat", None),
        P(),
        P(),
        P(),
        P(),
        P(),
        P(),
        P(),
        P(),
        P(),
        P("task", None, "feat", None),
        P("task"),
        P("task"),
        P("task", None, "feat"),
        P("task", "feat", None),
        P("task", None),
    )
    out_specs = (
        P("task", None, "feat", None),
        P("task", "feat", None, None),
        P("task", None, "feat", None),
        P("task"),
        P(None, "task", "feat", None),
        P(None, "task", "feat", None),
        P(),
        P(),
        P(None, None, ("task", "feat")),
        P(),
        P(None, ("task", "feat"), None),
        P(),
        P(),
    )
    return jax.shard_map(local, mesh=mesh, in_specs=in_specs, out_specs=out_specs, check_vma=False)
```

```python
import functools

import jax
import jax.numpy as jnp
from jax import lax
from jax.experimental import pallas as pl
from jax.experimental.pallas import tpu as pltpu
from jax.sharding import PartitionSpec as P

HEADS = 8
BINS = 64
CLASSES = 10
LAYERS = 2
LANES = 128
CODE_LANE = 32
ROWS = 256

epsilon = 1e-05
masked_score = -1e30
highest = lax.Precision.HIGHEST
bf16 = jnp.bfloat16
f32 = jnp.float32

NN = (((1,), (0,)), ((), ()))
NT = (((1,), (1,)), ((), ()))
TN = (((0,), (0,)), ((), ()))


def mm(left, right, dims=NN):
    return lax.dot_general(left, right, dims, preferred_element_type=f32)


def lane_row():
    return lax.broadcasted_iota(jnp.int32, (1, LANES), 1)


def half_row(half):
    lanes = lane_row()
    picked = lanes < 64 if half == 0 else lanes >= 64
    return picked.astype(f32).astype(bf16)


def piece_row(pair, half):
    offset = lane_row() - 64 * half - 3 * pair
    return jnp.where((offset >= 0) & (offset < 3), -1.0, 0.0).astype(bf16)


def split_pieces(values, order):
    first = values.astype(bf16).astype(f32)
    rest = values - first
    second = rest.astype(bf16).astype(f32)
    third = rest - second
    return jnp.where(order == 0, first, jnp.where(order == 1, second, third))


def layer_norm(rows, gain, shift):
    centred = rows - jnp.mean(rows, axis=-1, keepdims=True)
    inverse = lax.rsqrt(jnp.mean(centred * centred, axis=-1, keepdims=True) + epsilon)
    normed = centred * inverse
    return normed, inverse, normed * gain + shift


def layer_norm_back(grad_rows, rows, gain):
    centred = rows - jnp.mean(rows, axis=-1, keepdims=True)
    inverse = lax.rsqrt(jnp.mean(centred * centred, axis=-1, keepdims=True) + epsilon)
    normed = centred * inverse
    scaled = grad_rows * gain
    inner = (
        scaled
        - jnp.mean(scaled, axis=-1, keepdims=True)
        - normed * jnp.mean(scaled * normed, axis=-1, keepdims=True)
    )
    gain_part = jnp.sum(grad_rows * normed, axis=0, keepdims=True)
    shift_part = jnp.sum(grad_rows, axis=0, keepdims=True)
    return inverse * inner, gain_part, shift_part


def chunk(index, size):
    return pl.ds(pl.multiple_of(index * size, size), size)


def attend_pair(query, key, value, query_code, key_code, pair, extras):
    query_wide = jnp.concatenate([query, query_code], axis=1)
    total = None
    peaks = []
    for half in range(2):
        mask = half_row(half)
        key_wide = jnp.concatenate([key * mask, key_code], axis=1)
        scores = mm(query_wide, key_wide, NT)
        peak = jnp.max(scores, axis=-1, keepdims=True)
        weights = jnp.exp(scores - peak).astype(bf16)
        ones = jnp.broadcast_to(mask, value.shape)
        part = mm(weights, jnp.concatenate([value * mask, ones], axis=1))
        total = part if total is None else total + part
        peaks.append(peak)
    lanes = lane_row()
    row_total = total[:, LANES:]
    context = total[:, :LANES] / row_total
    log_total = jnp.where(lanes < 64, peaks[0], peaks[1]) + jnp.log(row_total)
    order = lanes % 64 - 3 * pair
    extras = jnp.where((order >= 0) & (order < 3), split_pieces(log_total, order), extras)
    return context.astype(bf16), extras


def attend_pair_back(query, key, value, context_grad, query_extra, grad_extra, key_code, pair):
    query_wide = jnp.concatenate([query, query_extra], axis=1)
    grad_wide = jnp.concatenate([context_grad, grad_extra], axis=1)
    query_grad = key_grad = value_grad = None
    for half in range(2):
        mask = half_row(half)
        pieces = piece_row(pair, half)
        key_half = key * mask
        key_wide = jnp.concatenate([key_half, key_code + pieces], axis=1)
        value_wide = jnp.concatenate(
            [value * mask, jnp.broadcast_to(pieces, value.shape)], axis=1
        )
        attention = jnp.exp(mm(key_wide, query_wide, NT))
        score_grad = (attention * mm(value_wide, grad_wide, NT)).astype(bf16)
        value_part = mm(attention.astype(bf16), context_grad * mask)
        key_part = mm(score_grad, query * mask)
        query_part = mm(score_grad, key_half, TN)
        if half == 0:
            query_grad, key_grad, value_grad = query_part, key_part, value_part
        else:
            query_grad, key_grad, value_grad = (
                query_grad + query_part,
                key_grad + key_part,
                value_grad + value_part,
            )
    return query_grad, key_grad, value_grad


def delta_extra(context, context_grad):
    width = context.shape[1]
    products = context.astype(f32) * context_grad.astype(f32)
    high = products.astype(bf16)
    low = (products - high.astype(f32)).astype(bf16)
    head = lax.broadcasted_iota(jnp.int32, (width, LANES), 0) // (width // HEADS)
    offset = lax.broadcasted_iota(jnp.int32, (width, LANES), 1) - 64 * (head % 2) - 3 * (head // 2)
    spread = jnp.where((offset >= 0) & (offset < 3), 1.0, 0.0).astype(bf16)
    sums = mm(high, spread) + mm(low, spread)
    return split_pieces(sums, lane_row() % 64 % 3).astype(bf16)


def sample_forward(x_ref, gain_ref, shift_ref, w_ref, qcode_ref, kcode_ref, x1_ref, h2_ref, qkv_ref, ctx_ref, ext_ref):
    features, samples, width = x_ref.shape
    steps = samples // ROWS

    def project(unit, carry):
        f, rows = unit // steps, chunk(unit % steps, ROWS)
        _, _, hidden = layer_norm(x_ref[f, rows, :], gain_ref[0:1], shift_ref[0:1])
        hidden = hidden.astype(bf16)
        for member in range(3):
            out = mm(hidden, w_ref[member]).astype(bf16)
            if member == 0:
                out = out * jnp.asarray(0.125, bf16)
            qkv_ref[member, f, rows, :] = out
        return carry

    lax.fori_loop(0, features * steps, project, 0)

    def attend(unit, carry):
        f, rows = unit // steps, chunk(unit % steps, ROWS)
        code = qcode_ref[...]

        def pair_step(pair, extras):
            lanes = chunk(pair, LANES)
            context, extras = attend_pair(
                qkv_ref[0, f, rows, lanes],
                qkv_ref[1, f, :, lanes],
                qkv_ref[2, f, :, lanes],
                code,
                kcode_ref[...],
                pair,
                extras,
            )
            ctx_ref[f, rows, lanes] = context
            return extras

        extras = lax.fori_loop(0, width // LANES, pair_step, code.astype(f32))
        ext_ref[f, rows, :] = extras.astype(bf16)
        x1 = x_ref[f, rows, :] + mm(ctx_ref[f, rows, :], w_ref[3])
        x1_ref[f, rows, :] = x1
        _, _, hidden = layer_norm(x1, gain_ref[1:2], shift_ref[1:2])
        h2_ref[f, rows, :] = hidden.astype(bf16)
        return carry

    lax.fori_loop(0, features * steps, attend, 0)


def load_group(ref, group, size):
    features, _, width = ref.shape
    block = ref[:, chunk(group, size), :]
    if size % 16:
        return block.astype(f32).reshape(features * size, width).astype(bf16)
    return block.reshape(features * size, width)


def store_group(ref, group, size, rows):
    features, _, width = ref.shape
    if size % 16:
        block = rows.astype(f32).reshape(features, size, width).astype(bf16)
    else:
        block = rows.reshape(features, size, width)
    ref[:, chunk(group, size), :] = block


def feature_forward(size, h_ref, w_ref, qcode_ref, kcode_ref, a_ref, qkv_ref, ctx_ref, ext_ref):
    _, samples, width = h_ref.shape

    def step(group, carry):
        hidden = load_group(h_ref, group, size)
        for member in range(3):
            out = mm(hidden, w_ref[member]).astype(bf16)
            if member == 0:
                out = out * jnp.asarray(0.125, bf16)
            qkv_ref[group, member] = out
        code = qcode_ref[...]

        def pair_step(pair, extras):
            lanes = chunk(pair, LANES)
            context, extras = attend_pair(
                qkv_ref[group, 0, :, lanes],
                qkv_ref[group, 1, :, lanes],
                qkv_ref[group, 2, :, lanes],
                code,
                kcode_ref[...],
                pair,
                extras,
            )
            ctx_ref[group, :, lanes] = context
            return extras

        extras = lax.fori_loop(0, width // LANES, pair_step, code.astype(f32))
        ext_ref[group] = extras.astype(bf16)
        store_group(a_ref, group, size, mm(ctx_ref[group], w_ref[3]).astype(bf16))
        return carry

    lax.fori_loop(0, samples // size, step, 0)


def gelu_parts(values):
    cubic = values * values * values
    inside = 0.7978845608028654 * (values + 0.044715 * cubic)
    bent = jnp.tanh(inside)
    return bent


def dense_forward(x_ref, a_ref, gain_ref, shift_ref, up_ref, upb_ref, down_ref, downb_ref, out_ref, u_ref):
    rows_total, width = x_ref.shape
    hidden_width = up_ref.shape[1]

    def step(unit, carry):
        rows = chunk(unit, ROWS)
        x2 = x_ref[rows, :] + a_ref[rows, :].astype(f32)
        _, _, hidden = layer_norm(x2, gain_ref[2:3], shift_ref[2:3])
        hidden = hidden.astype(bf16)
        total = x2 + downb_ref[...]
        for part in range(hidden_width // 512):
            cols = slice(part * 512, part * 512 + 512)
            expanded = mm(hidden, up_ref[:, cols]) + upb_ref[:, cols]
            u_ref[rows, cols] = expanded.astype(bf16)
            active = (0.5 * expanded * (1.0 + gelu_parts(expanded))).astype(bf16)
            total = total + mm(active, down_ref[cols, :])
        out_ref[rows, :] = total
        return carry

    lax.fori_loop(0, rows_total // ROWS, step, 0)


def dense_backward(g_ref, x1_ref, a_ref, u_ref, gain_ref, shift_ref, up_ref, down_ref, out_ref, send_ref, dup_ref, ddown_ref, dupb_ref, ddownb_ref, dgs_ref, active_ref, ugrad_ref, hidden_ref, rowgrad_ref):
    rows_total, width = g_ref.shape
    hidden_width = up_ref.shape[1]
    dupb_ref[...] = jnp.zeros_like(dupb_ref)
    ddownb_ref[...] = jnp.zeros_like(ddownb_ref)
    dgs_ref[...] = jnp.zeros_like(dgs_ref)

    def step(unit, carry):
        rows = chunk(unit, ROWS)
        grad = g_ref[rows, :]
        low = grad.astype(bf16)
        rowgrad_ref[rows, :] = low
        ddownb_ref[...] += jnp.sum(low.astype(f32), axis=0, keepdims=True)
        hidden_grad = None
        for part in range(hidden_width // 512):
            cols = slice(part * 512, part * 512 + 512)
            active_grad = mm(low, down_ref[cols, :], NT).astype(bf16).astype(f32)
            u = u_ref[rows, cols].astype(f32)
            bent = gelu_parts(u)
            slope = 0.5 * (1.0 + bent) + u * (1.0 - bent * bent) * (
                0.3989422804014327 + 0.05351611220146811 * u * u
            )
            active_ref[rows, cols] = (0.5 * u * (1.0 + bent)).astype(bf16)
            ugrad = (active_grad * slope).astype(bf16)
            ugrad_ref[rows, cols] = ugrad
            dupb_ref[:, cols] += jnp.sum(ugrad.astype(f32), axis=0, keepdims=True)
            part_grad = mm(ugrad, up_ref[:, cols], NT)
            hidden_grad = part_grad if hidden_grad is None else hidden_grad + part_grad
        x2 = x1_ref[rows, :] + a_ref[rows, :].astype(f32)
        _, _, hidden = layer_norm(x2, gain_ref[2:3], shift_ref[2:3])
        hidden_ref[rows, :] = hidden.astype(bf16)
        norm_grad, gain_part, shift_part = layer_norm_back(
            hidden_grad.astype(bf16).astype(f32), x2, gain_ref[2:3]
        )
        dgs_ref[0:1] += gain_part
        dgs_ref[1:2] += shift_part
        grad = grad + norm_grad
        out_ref[rows, :] = grad
        send_ref[rows, :] = grad.astype(bf16)
        return carry

    lax.fori_loop(0, rows_total // ROWS, step, 0)

    def weights(part, carry):
        cols = chunk(part, 512)
        dup_ref[cols, :] = mm(ugrad_ref[:, cols], hidden_ref[...], TN).astype(bf16)
        ddown_ref[cols, :] = mm(active_ref[:, cols], rowgrad_ref[...], TN).astype(bf16)
        return carry

    lax.fori_loop(0, hidden_width // 512, weights, 0)


def feature_backward(size, da_ref, h_ref, w_ref, kcode_ref, qkv_ref, ctx_ref, ext_ref, dh_ref, dw_ref, dqkv_ref, hidden_ref, dao_ref, dc_ref):
    _, samples, width = h_ref.shape
    groups = samples // size

    def step(group, carry):
        hidden_ref[group] = load_group(h_ref, group, size)
        dao = load_group(da_ref, group, size)
        dao_ref[group] = dao
        context_grad = mm(dao, w_ref[3], NT).astype(bf16)
        dc_ref[...] = context_grad
        grad_extra = delta_extra(ctx_ref[group], context_grad)

        def pair_step(pair, inner):
            lanes = chunk(pair, LANES)
            query_grad, key_grad, value_grad = attend_pair_back(
                qkv_ref[group, 0, :, lanes],
                qkv_ref[group, 1, :, lanes],
                qkv_ref[group, 2, :, lanes],
                dc_ref[:, lanes],
                ext_ref[group],
                grad_extra,
                kcode_ref[...],
                pair,
            )
            dqkv_ref[0, group, :, lanes] = (query_grad * 0.125).astype(bf16)
            dqkv_ref[1, group, :, lanes] = key_grad.astype(bf16)
            dqkv_ref[2, group, :, lanes] = value_grad.astype(bf16)
            return inner

        lax.fori_loop(0, width // LANES, pair_step, 0)
        total = mm(dqkv_ref[0, group], w_ref[0], NT)
        total = total + mm(dqkv_ref[1, group], w_ref[1], NT)
        total = total + mm(dqkv_ref[2, group], w_ref[2], NT)
        store_group(dh_ref, group, size, total.astype(bf16))
        return carry

    lax.fori_loop(0, groups, step, 0)

    def weights(member, carry):
        total = None
        for group in range(groups):
            part = mm(hidden_ref[group], dqkv_ref[member, group], TN)
            total = part if total is None else total + part
        dw_ref[member] = total.astype(bf16)
        return carry

    lax.fori_loop(0, 3, weights, 0)
    total = None
    for group in range(groups):
        part = mm(ctx_ref[group], dao_ref[group], TN)
        total = part if total is None else total + part
    dw_ref[3] = total.astype(bf16)


def sample_backward(g_ref, dh_ref, x1_ref, x_ref, gain_ref, shift_ref, w_ref, kcode_ref, qkv_ref, ctx_ref, ext_ref, out_ref, dw_ref, dgs_ref, dqkv_ref, hidden_ref, low_ref, dc_ref, gext_ref, kacc_ref, vacc_ref):
    features, samples, width = x_ref.shape
    steps = samples // ROWS
    dgs_ref[...] = jnp.zeros_like(dgs_ref)

    def enter(unit, carry):
        f, rows = unit // steps, chunk(unit % steps, ROWS)
        norm_grad, gain_part, shift_part = layer_norm_back(
            dh_ref[f, rows, :].astype(f32), x1_ref[f, rows, :], gain_ref[1:2]
        )
        dgs_ref[1, 0:1] += gain_part
        dgs_ref[1, 1:2] += shift_part
        grad = g_ref[f, rows, :] + norm_grad
        out_ref[f, rows, :] = grad
        low = grad.astype(bf16)
        low_ref[f, rows, :] = low
        context_grad = mm(low, w_ref[3], NT).astype(bf16)
        dc_ref[f, rows, :] = context_grad
        gext_ref[f, rows, :] = delta_extra(ctx_ref[f, rows, :], context_grad)
        return carry

    lax.fori_loop(0, features * steps, enter, 0)

    def attend(unit, carry):
        f, pair = unit // (width // LANES), unit % (width // LANES)
        lanes = chunk(pair, LANES)

        def query_step(step, inner):
            rows = chunk(step, ROWS)
            query_grad, key_grad, value_grad = attend_pair_back(
                qkv_ref[0, f, rows, lanes],
                qkv_ref[1, f, :, lanes],
                qkv_ref[2, f, :, lanes],
                dc_ref[f, rows, lanes],
                ext_ref[f, rows, :],
                gext_ref[f, rows, :],
                kcode_ref[...],
                pair,
            )
            dqkv_ref[0, f, rows, lanes] = (query_grad * 0.125).astype(bf16)
            first = step == 0
            kacc_ref[...] = jnp.where(first, 0.0, kacc_ref[...]) + key_grad
            vacc_ref[...] = jnp.where(first, 0.0, vacc_ref[...]) + value_grad
            return inner

        lax.fori_loop(0, steps, query_step, 0)
        dqkv_ref[1, f, :, lanes] = kacc_ref[...].astype(bf16)
        dqkv_ref[2, f, :, lanes] = vacc_ref[...].astype(bf16)
        return carry

    kacc_ref[...] = jnp.zeros_like(kacc_ref)
    vacc_ref[...] = jnp.zeros_like(vacc_ref)
    lax.fori_loop(0, features * (width // LANES), attend, 0)

    def leave(unit, carry):
        f, rows = unit // steps, chunk(unit % steps, ROWS)
        total = mm(dqkv_ref[0, f, rows, :], w_ref[0], NT)
        total = total + mm(dqkv_ref[1, f, rows, :], w_ref[1], NT)
        total = total + mm(dqkv_ref[2, f, rows, :], w_ref[2], NT)
        x = x_ref[f, rows, :]
        _, _, hidden = layer_norm(x, gain_ref[0:1], shift_ref[0:1])
        hidden_ref[f, rows, :] = hidden.astype(bf16)
        norm_grad, gain_part, shift_part = layer_norm_back(
            total.astype(bf16).astype(f32), x, gain_ref[0:1]
        )
        dgs_ref[0, 0:1] += gain_part
        dgs_ref[0, 1:2] += shift_part
        out_ref[f, rows, :] += norm_grad
        return carry

    lax.fori_loop(0, features * steps, leave, 0)

    def weights(member, carry):
        total = None
        for f in range(features):
            part = mm(hidden_ref[f], dqkv_ref[member, f], TN)
            total = part if total is None else total + part
        dw_ref[member] = total.astype(bf16)
        return carry

    lax.fori_loop(0, 3, weights, 0)
    total = None
    for f in range(features):
        part = mm(ctx_ref[f], low_ref[f], TN)
        total = part if total is None else total + part
    dw_ref[3] = total.astype(bf16)


def call(body, name, outs, scratch, *operands):
    spec = pl.BlockSpec(memory_space=pltpu.VMEM)
    return pl.pallas_call(
        body,
        name=name,
        out_shape=[jax.ShapeDtypeStruct(shape, kind) for shape, kind in outs],
        in_specs=[spec] * len(operands),
        out_specs=[spec] * len(outs),
        scratch_shapes=[pltpu.VMEM(shape, kind) for shape, kind in scratch],
        compiler_params=pltpu.CompilerParams(vmem_limit_bytes=56 << 20),
    )(*operands)


MESH = pl.DeviceIdType.MESH


def remote(source, target, send_sem, recv_sem, device):
    return pltpu.make_async_remote_copy(
        src_ref=source,
        dst_ref=target,
        send_sem=send_sem,
        recv_sem=recv_sem,
        device_id=device,
        device_id_type=MESH,
    )


def sum_partners(task_devices, feature_devices):
    task, place = lax.axis_index("task"), lax.axis_index("feat")
    chip, core = place // 2, lax.rem(place, 2)
    chips = feature_devices // 2
    pair = [{"feat": place + 1 - 2 * core}]
    tasks = [{"task": lax.rem(task + step, task_devices)} for step in range(1, task_devices)]
    line = [{"feat": 2 * lax.rem(chip + step, chips) + core} for step in range(1, chips)]
    return task, chip, core, pair, tasks, line


def greet(devices):
    barrier = pltpu.get_barrier_semaphore()
    for device in devices:
        pl.semaphore_signal(barrier, inc=1, device_id=device, device_id_type=MESH)


def met(count):
    pl.semaphore_wait(pltpu.get_barrier_semaphore(), count)


def sum_tail(pieces, task_devices, feature_devices, *refs):
    chips = feature_devices // 2
    inputs, small_ref = refs[:pieces], refs[pieces]
    outs, small_out = refs[pieces + 1 : 2 * pieces + 1], refs[2 * pieces + 1]
    own, first, summed, second, third_in, third, sends, recvs, loads, small_got, small_sends, small_recvs = refs[2 * pieces + 2 :]
    task, chip, core, pair, tasks, line = sum_partners(task_devices, feature_devices)
    greet(pair + tasks + line)
    own_loads = [
        pltpu.make_async_copy(inputs[p].at[:, :, core], own.at[p], loads.at[p]) for p in range(pieces)
    ]
    for load in own_loads:
        load.start()
    met(len(pair) + len(tasks) + len(line))

    started = []
    for p in range(pieces):
        copy = remote(inputs[p].at[:, :, 1 - core], first.at[p], sends.at[p, 0], recvs.at[p, 0], pair[0])
        copy.start()
        started.append([copy])
    small_slot = [0]

    def small_exchange(values, devices, index, base):
        copies = []
        for k, device in enumerate(devices):
            copy = remote(values, small_got.at[base + index], small_sends.at[base + k], small_recvs.at[base + k], device)
            copy.start()
            copies.append(copy)
        return copies

    def small_finish(copies, count, base):
        for copy in copies:
            copy.wait()
        total = small_got[base]
        for k in range(1, count):
            total = total + small_got[base + k]
        return total

    small_got[core] = small_ref[...]
    small_copies = small_exchange(small_got.at[core], pair, core, 0)
    for p in range(pieces):
        own_loads[p].wait()
        for copy in started[p]:
            copy.wait()

        def add_core(index, carry, p=p):
            t, z = index // chips, lax.rem(index, chips)
            summed[p, t, z] = (own[p, t, z].astype(f32) + first[p, t, z].astype(f32)).astype(bf16)
            return carry

        lax.fori_loop(0, task_devices * chips, add_core, 0)
        started[p] = []
        for k, device in enumerate(tasks):
            other = lax.rem(task + k + 1, task_devices)
            copy = remote(summed.at[p, other], second.at[p, k], sends.at[p, 1 + k], recvs.at[p, 1 + k], device)
            copy.start()
            started[p].append(copy)
    total = small_finish(small_copies, 2, 0)
    small_got[2 + task] = total
    small_copies = small_exchange(small_got.at[2 + task], tasks, task, 2)
    for p in range(pieces):
        for copy in started[p]:
            copy.wait()

        def add_tasks(z, carry, p=p):
            total = summed[p, task, z].astype(f32)
            for k in range(task_devices - 1):
                total = total + second[p, k, z].astype(f32)
            third_in[p, z] = total.astype(bf16)
            return carry

        lax.fori_loop(0, chips, add_tasks, 0)
        started[p] = []
        for k, device in enumerate(line):
            other = lax.rem(chip + k + 1, chips)
            slot = task_devices + k
            copy = remote(third_in.at[p, other], third.at[p, k], sends.at[p, slot], recvs.at[p, slot], device)
            copy.start()
            started[p].append(copy)
    total = small_finish(small_copies, task_devices, 2)
    base = 2 + task_devices
    small_got[base + chip] = total
    small_copies = small_exchange(small_got.at[base + chip], line, chip, base)
    for p in range(pieces):
        for copy in started[p]:
            copy.wait()
        total = third_in[p, chip].astype(f32)
        for k in range(chips - 1):
            total = total + third[p, k].astype(f32)
        outs[p][...] = total
    small_out[...] = small_finish(small_copies, chips, base)


def sum_everywhere(pieces, small, task_devices, feature_devices):
    chips = feature_devices // 2
    rows, width = pieces[0].shape
    share = rows // (task_devices * feature_devices)
    blocks = [piece.reshape(task_devices, chips, 2, share, width) for piece in pieces]
    count = len(pieces)
    copies = task_devices + chips - 1
    small_copies = 2 + task_devices + chips
    vmem, anywhere = pl.BlockSpec(memory_space=pltpu.VMEM), pl.BlockSpec(memory_space=pl.ANY)
    return pl.pallas_call(
        functools.partial(sum_tail, count, task_devices, feature_devices),
        name="sum_tail",
        out_shape=[jax.ShapeDtypeStruct((share, width), f32)] * count
        + [jax.ShapeDtypeStruct(small.shape, f32)],
        in_specs=[anywhere] * count + [vmem],
        out_specs=[vmem] * (count + 1),
        scratch_shapes=[
            pltpu.VMEM((count, task_devices, chips, share, width), bf16),
            pltpu.VMEM((count, task_devices, chips, share, width), bf16),
            pltpu.VMEM((count, task_devices, chips, share, width), bf16),
            pltpu.VMEM((count, task_devices - 1, chips, share, width), bf16),
            pltpu.VMEM((count, chips, share, width), bf16),
            pltpu.VMEM((count, chips - 1, share, width), bf16),
            pltpu.SemaphoreType.DMA((count, copies)),
            pltpu.SemaphoreType.DMA((count, copies)),
            pltpu.SemaphoreType.DMA((count,)),
            pltpu.VMEM((small_copies,) + small.shape, f32),
            pltpu.SemaphoreType.DMA((small_copies,)),
            pltpu.SemaphoreType.DMA((small_copies,)),
        ],
        compiler_params=pltpu.CompilerParams(
            vmem_limit_bytes=56 << 20, collective_id=0, has_side_effects=True
        ),
    )(*blocks, small)


SIZE = 16


class Place:
    def __init__(self, task_devices, feature_devices):
        self.tasks, self.places = task_devices, feature_devices
        self.chips = feature_devices // 2
        self.task, self.place = lax.axis_index("task"), lax.axis_index("feat")
        self.chip, self.core = self.place // 2, lax.rem(self.place, 2)

    def ring(self, step):
        return lax.rem(self.place + step, self.places)

    def line_partner(self, step):
        return lax.rem(self.chip + step, self.chips)

    def task_partner(self, step):
        return lax.rem(self.task + step, self.tasks)

    def greet(self):
        barrier = pltpu.get_barrier_semaphore()
        for step in range(1, self.places):
            pl.semaphore_signal(barrier, inc=1, device_id={"feat": self.ring(step)}, device_id_type=MESH)
        for step in range(1, self.tasks):
            pl.semaphore_signal(barrier, inc=1, device_id={"task": self.task_partner(step)}, device_id_type=MESH)

    def met(self):
        pl.semaphore_wait(pltpu.get_barrier_semaphore(), self.places - 1 + self.tasks - 1)


class SumStep:
    def __init__(self, step, place, source, own, got, sends, recvs, load):
        self.step = step
        if step == 1:
            self.mine = source.at[:, :, place.core]
            parts = [(source.at[:, :, 1 - place.core], got, {"feat": place.place + 1 - 2 * place.core})]
        elif step == 2:
            self.mine = source.at[place.task]
            parts = [
                (source.at[place.task_partner(k)], got.at[k - 1], {"task": place.task_partner(k)})
                for k in range(1, place.tasks)
            ]
        else:
            self.mine = source.at[place.chip]
            parts = [
                (source.at[place.line_partner(k)], got.at[k - 1], {"feat": 2 * place.line_partner(k) + place.core})
                for k in range(1, place.chips)
            ]
        self.copies = [
            remote(part, target, sends.at[k], recvs.at[k], device) for k, (part, target, device) in enumerate(parts)
        ]
        self.load = pltpu.make_async_copy(self.mine, own, load)
        self.own, self.got = own, got

    def start(self):
        for copy in self.copies:
            copy.start()
        self.load.start()

    def finish(self, out):
        self.load.wait()
        for copy in self.copies:
            copy.wait()
        own, got = self.own, self.got
        if self.step == 1:

            def add_core(index, carry):
                t, z = index // own.shape[1], lax.rem(index, own.shape[1])
                out[t, z] = (own[t, z].astype(f32) + got[t, z].astype(f32)).astype(bf16)
                return carry

            lax.fori_loop(0, own.shape[0] * own.shape[1], add_core, 0)
        elif self.step == 2:

            def add_tasks(z, carry):
                total = own[z].astype(f32)
                for k in range(got.shape[0]):
                    total = total + got[k, z].astype(f32)
                out[z] = total.astype(bf16)
                return carry

            lax.fori_loop(0, own.shape[0], add_tasks, 0)
        else:
            total = own[...].astype(f32)
            for k in range(got.shape[0]):
                total = total + got[k].astype(f32)
            out[...] = total


def sum_shapes(step, tasks, chips, share, width):
    if step == 1:
        return (tasks, chips, share, width), (tasks, chips, share, width), bf16, 1
    if step == 2:
        return (chips, share, width), (tasks - 1, chips, share, width), bf16, tasks - 1
    return (share, width), (chips - 1, share, width), f32, chips - 1


class Chain:
    def __init__(self, place, steps, points, bufs, out):
        self.place, self.steps, self.points, self.bufs, self.out = place, steps, points, bufs, out
        self.at, self.running = 0, False
        self.actions = [None] + [self.make(at, bufs[at - 1][2]) for at in range(1, len(steps))]

    def make(self, at, source):
        own, got, _, sends, recvs, local_sem = self.bufs[at]
        return SumStep(self.steps[at], self.place, source, own, got, sends, recvs, local_sem.at[0])

    def begin(self, source):
        self.actions[0] = self.make(0, source)
        self.actions[0].start()
        self.running = True

    def reached(self, point):
        if not self.running or self.points[self.at] != point:
            return
        self.actions[self.at].finish(self.bufs[self.at][2])
        self.at += 1
        if self.at < len(self.steps):
            self.actions[self.at].start()
            return
        self.running = False
        if self.out is not None:
            self.flush().start()

    def flush(self):
        return pltpu.make_async_copy(self.bufs[-1][2], self.out, self.bufs[-1][5].at[1])


class Box:
    def __init__(self, place, bufs, loads, outs, out_bufs, flush_sem, chains, sources):
        self.place, self.bufs, self.loads = place, bufs, loads
        self.outs, self.out_bufs, self.flush_sem = outs, out_bufs, flush_sem
        self.chains, self.sources = chains, sources
        self.waited, self.flushed = set(), []

    def use(self, *indices):
        found = []
        for index in indices:
            if index not in self.waited:
                self.waited.add(index)
                if self.loads[index] is not None:
                    self.loads[index].wait()
            found.append(self.bufs[index])
        return found if len(found) > 1 else found[0]

    def out(self, *indices):
        found = [self.out_bufs[index] for index in indices]
        return found if len(found) > 1 else found[0]

    def copy_out(self, index, part, view):
        source, target = self.out_bufs[index], self.outs[index]
        if view is not None:
            source, target = view(source, part), view(target, part)
        return pltpu.make_async_copy(source, target, self.flush_sem.at[index, part])

    def flush(self, *indices):
        for index in indices:
            self.copy_out(index, 0, None).start()
            self.flushed.append((index, 0, None))

    def flush_part(self, index, part, view):
        self.copy_out(index, part, view).start()
        if (index, 0, view) not in self.flushed:
            self.flushed += [(index, at, view) for at in range(4)]

    def ready(self):
        self.place.met()
        for chain, source in zip(self.chains, self.sources):
            if source is not None:
                chain.begin(source)

    def point(self, name):
        for chain in self.chains:
            chain.reached(name)

    def end(self):
        for index, part, view in self.flushed:
            self.copy_out(index, part, view).wait()
        for chain in self.chains:
            if chain.out is not None:
                chain.flush().wait()


def fused(body, name, place_sizes, ins, outs, scratch, sums, share_shape, identity):
    tasks, places = place_sizes
    chips = places // 2
    share, width = share_shape
    anywhere = pl.BlockSpec(memory_space=pltpu.HBM)
    scalar = pl.BlockSpec(memory_space=pltpu.SMEM)
    buffers = []
    for array, layer in ins:
        if layer != "scalar":
            buffers.append(pltpu.VMEM(array.shape if layer is None else array.shape[1:], array.dtype))
    out_buffers = [pltpu.VMEM(shape, kind) for shape, kind in outs]
    sum_results, sum_scratch, sum_arrays = [], [], []
    for steps, _, array, goes_out in sums:
        for step in steps:
            own, got, kind, copies = sum_shapes(step, tasks, chips, share, width)
            sum_scratch += [
                pltpu.VMEM(own, bf16),
                pltpu.VMEM(got, bf16),
                pltpu.VMEM(own, kind),
                pltpu.SemaphoreType.DMA((copies,)),
                pltpu.SemaphoreType.DMA((copies,)),
                pltpu.SemaphoreType.DMA((2,)),
            ]
        if goes_out:
            sum_results.append(jax.ShapeDtypeStruct(own, kind))
        if array is not None:
            sum_arrays.append(array)
    everything = buffers + out_buffers + list(scratch) + sum_scratch
    needed = 0
    for item in everything:
        if item.memory_space == pltpu.VMEM:
            count = 1
            for extent in item.shape:
                count *= extent
            needed += count * jnp.dtype(item.dtype).itemsize

    def kernel(*refs):
        rest = list(refs)

        def pop(count):
            taken = rest[:count]
            del rest[:count]
            return taken

        in_refs, sum_refs = pop(len(ins)), pop(len(sum_arrays))
        out_refs, sum_outs = pop(len(outs)), pop(len(sum_results))
        flat_in = pop(len(buffers))
        out_bufs = pop(len(out_buffers))
        user = pop(len(scratch))
        chain_bufs = [[pop(6) for _ in steps] for steps, _, _, _ in sums]
        load_sem, flush_sem = pop(2)
        place = Place(tasks, places)
        loads, bufs = [], []
        for index, (array, layer) in enumerate(ins):
            if layer == "scalar":
                loads.append(None)
                bufs.append(in_refs[index])
                continue
            source = in_refs[index] if layer is None else in_refs[index].at[layer]
            bufs.append(flat_in.pop(0))
            copy = pltpu.make_async_copy(source, bufs[-1], load_sem.at[index])
            copy.start()
            loads.append(copy)
        place.greet()
        chains, sources = [], []
        for (steps, points, array, goes_out), chain_buf in zip(sums, chain_bufs):
            chains.append(Chain(place, steps, points, chain_buf, sum_outs.pop(0) if goes_out else None))
            sources.append(sum_refs.pop(0) if array is not None else None)
        box = Box(place, bufs, loads, out_refs, out_bufs, flush_sem, chains, sources)
        body(box, *user)
        box.end()

    return pl.pallas_call(
        kernel,
        name=name,
        out_shape=[jax.ShapeDtypeStruct(shape, kind) for shape, kind in outs] + sum_results,
        in_specs=[scalar if layer == "scalar" else anywhere for _, layer in ins] + [anywhere] * len(sum_arrays),
        out_specs=[anywhere] * (len(outs) + len(sum_results)),
        scratch_shapes=everything
        + [pltpu.SemaphoreType.DMA((len(ins),)), pltpu.SemaphoreType.DMA((len(outs), 4))],
        compiler_params=pltpu.CompilerParams(
            vmem_limit_bytes=63 << 20, collective_id=identity, has_side_effects=True
        ),
    )(*[array for array, _ in ins], *sum_arrays)


def cross(ref, unit):
    block = ref[:, :, chunk(unit, SIZE), :]
    return block.reshape(block.shape[0] * block.shape[1] * SIZE, block.shape[3])


def put_cross(ref, unit, rows):
    first, second, _, width = ref.shape
    ref[:, :, chunk(unit, SIZE), :] = rows.reshape(first, second, SIZE, width)


def cross_view(ref, unit):
    return ref.at[:, :, chunk(unit, SIZE), :]


def first_view(ref, unit):
    return ref.at[unit]


def own_rows(ref, f, unit, size, lanes=slice(None)):
    block = ref[f, :, chunk(unit, size), lanes]
    return block.reshape(block.shape[0] * size, block.shape[2])


def block_rows(ref, f, unit, per, lanes=slice(None)):
    block = ref[f, chunk(unit, per), :, lanes]
    return block.reshape(per * block.shape[1], block.shape[2])


def all_rows(ref, f, lanes=slice(None)):
    block = ref[f, :, :, lanes]
    return block.reshape(block.shape[0] * block.shape[1], block.shape[2])


def pair_lanes(pair):
    return slice(pair * LANES, pair * LANES + LANES)


def fill_sample_codes(size, query_ref, key_ref):
    lanes = lax.broadcasted_iota(jnp.int32, query_ref.shape, 1)
    query_ref[...] = jnp.where(lanes == CODE_LANE, 1.0, 0.0).astype(bf16)
    lanes = lax.broadcasted_iota(jnp.int32, key_ref.shape, 1)
    rows = lax.broadcasted_iota(jnp.int32, key_ref.shape, 0)
    key_ref[...] = jnp.where((lanes == CODE_LANE) & (rows >= size), masked_score, 0.0).astype(bf16)


def fill_feature_codes(count, query_ref, key_ref):
    lanes = lax.broadcasted_iota(jnp.int32, key_ref.shape, 1) - CODE_LANE
    rows = lax.broadcasted_iota(jnp.int32, key_ref.shape, 0)
    own = lanes == (rows & (SIZE - 1))
    inside = (lanes >= 0) & (lanes < SIZE)
    if query_ref is not None:
        query_ref[...] = jnp.where(own, 1.0, 0.0).astype(bf16)
    live = rows < count * SIZE
    key_ref[...] = jnp.where(inside & ~(own & live), masked_score, 0.0).astype(bf16)


def forward_layer(layer, box, sq_ref, sk_ref, fq_ref, fk_ref, h2_ref, swapped_ref, a_ref, back_ref, active_ref, sends, recvs, self_sem, back_sends, back_recvs):
    place = box.place
    x1_ref, qkv_ref, ctx_ref, ext_ref = box.out(0, 1, 2, 3)
    hidden_ref, fqkv_ref, fctx_ref, fext_ref, x2_ref, x3_ref, u_ref = box.out(4, 5, 6, 7, 8, 9, 10)
    size_ref, count_ref = box.use(0, 1)
    fill_sample_codes(size_ref[0], sq_ref, sk_ref)
    fill_feature_codes(count_ref[0], fq_ref, fk_ref)
    x_ref, gain_ref, shift_ref, w_ref = box.use(2, 3, 4, 5)
    features, blocks, own, width = x_ref.shape
    per = ROWS // own
    steps = blocks // per
    size = ROWS // blocks
    units = own // size
    pairs = width // LANES

    def gain(index):
        return gain_ref[index, layer : layer + 1, :], shift_ref[index, layer : layer + 1, :]

    def project(unit, carry):
        f, part = unit // steps, lax.rem(unit, steps)
        _, _, hidden = layer_norm(block_rows(x_ref, f, part, per), *gain(0))
        hidden = hidden.astype(bf16)
        for member in range(3):
            out = mm(hidden, w_ref[member]).astype(bf16)
            if member == 0:
                out = out * jnp.asarray(0.125, bf16)
            qkv_ref[member, f, chunk(part, per), :, :] = out.reshape(per, own, width)
        return carry

    lax.fori_loop(0, features * steps, project, 0)
    box.flush(1)
    box.ready()

    def copies(unit):
        part, f = unit // features, lax.rem(unit, features)
        found = [
            remote(
                h2_ref.at[f, place.ring(k), chunk(part, size), :],
                swapped_ref.at[place.place, f, chunk(part, size), :],
                sends.at[unit, k - 1],
                recvs.at[unit, k - 1],
                {"feat": place.ring(k)},
            )
            for k in range(1, place.places)
        ]
        keep = pltpu.make_async_copy(
            h2_ref.at[f, place.place, chunk(part, size), :],
            swapped_ref.at[place.place, f, chunk(part, size), :],
            self_sem.at[unit],
        )
        return found, keep

    def attend(unit, carry):
        part, f = unit // features, lax.rem(unit, features)
        code = sq_ref[...]
        extras = code.astype(f32)
        for pair in range(pairs):
            lanes = pair_lanes(pair)
            context, extras = attend_pair(
                own_rows(qkv_ref.at[0], f, part, size, lanes),
                all_rows(qkv_ref.at[1], f, lanes),
                all_rows(qkv_ref.at[2], f, lanes),
                code,
                sk_ref[...],
                pair,
                extras,
            )
            ctx_ref[f, :, chunk(part, size), lanes] = context.reshape(blocks, size, LANES)
        ext_ref[f, :, chunk(part, size), :] = extras.astype(bf16).reshape(blocks, size, LANES)
        x1 = own_rows(x_ref, f, part, size) + mm(own_rows(ctx_ref, f, part, size), w_ref[3])
        x1_ref[f, :, chunk(part, size), :] = x1.reshape(blocks, size, width)
        _, _, hidden = layer_norm(x1, *gain(1))
        h2_ref[f, :, chunk(part, size), :] = hidden.astype(bf16).reshape(blocks, size, width)
        found, keep = copies(unit)
        for copy in found:
            copy.start()
        keep.start()
        return carry

    lax.fori_loop(0, features * units, attend, 0)
    box.flush(0, 2, 3)
    fw_ref = box.use(6)
    groups = own // SIZE
    shared = size // SIZE

    def back_copies(group):
        return [
            remote(
                a_ref.at[place.ring(k), :, chunk(group, SIZE), :],
                back_ref.at[:, place.place, chunk(group, SIZE), :],
                back_sends.at[group, k - 1],
                back_recvs.at[group, k - 1],
                {"feat": place.ring(k)},
            )
            for k in range(1, place.places)
        ]

    def feature(group, carry):
        @pl.when(lax.rem(group, shared) == 0)
        def _():
            for f in range(features):
                found, keep = copies((group // shared) * features + f)
                for copy in found:
                    copy.wait_recv()
                keep.wait()

        hidden = cross(swapped_ref, group)
        hidden_ref[group] = hidden
        for member in range(3):
            out = mm(hidden, fw_ref[member]).astype(bf16)
            if member == 0:
                out = out * jnp.asarray(0.125, bf16)
            fqkv_ref[group, member] = out
        code = fq_ref[...]
        extras = code.astype(f32)
        for pair in range(pairs):
            lanes = pair_lanes(pair)
            context, extras = attend_pair(
                fqkv_ref[group, 0, :, lanes],
                fqkv_ref[group, 1, :, lanes],
                fqkv_ref[group, 2, :, lanes],
                code,
                fk_ref[...],
                pair,
                extras,
            )
            fctx_ref[group, :, lanes] = context
        fext_ref[group] = extras.astype(bf16)
        put_cross(a_ref, group, mm(fctx_ref[group], fw_ref[3]).astype(bf16))
        for copy in back_copies(group):
            copy.start()
        back_ref[:, place.place, chunk(group, SIZE), :] = a_ref[place.place, :, chunk(group, SIZE), :]
        return carry

    lax.fori_loop(0, groups, feature, 0)
    box.flush(4, 5, 6, 7)
    up_ref, upb_ref, down_ref, downb_ref = box.use(7, 8, 9, 10)
    hidden_width = up_ref.shape[1]

    def dense(group, carry):
        for copy in back_copies(group):
            copy.wait_recv()
        x2 = cross(x1_ref, group) + cross(back_ref, group).astype(f32)
        put_cross(x2_ref, group, x2)
        _, _, hidden = layer_norm(x2, *gain(2))
        hidden = hidden.astype(bf16)
        for part in range(hidden_width // 512):
            cols = slice(part * 512, part * 512 + 512)
            expanded = mm(hidden, up_ref[:, cols]) + upb_ref[layer : layer + 1, cols]
            u_ref[group, :, cols] = expanded.astype(bf16)
            active_ref[:, cols] = (0.5 * expanded * (1.0 + gelu_parts(expanded))).astype(bf16)
        total = x2 + downb_ref[layer : layer + 1, :] + mm(active_ref[...], down_ref[...])
        put_cross(x3_ref, group, total)
        box.flush_part(8, group, cross_view)
        box.flush_part(9, group, cross_view)
        box.flush_part(10, group, first_view)
        return carry

    lax.fori_loop(0, groups, dense, 0)

    def settle(unit, carry):
        for copy in copies(unit)[0]:
            copy.wait_send()
        return carry

    lax.fori_loop(0, features * units, settle, 0)

    def settle_back(group, carry):
        for copy in back_copies(group):
            copy.wait_send()
        return carry

    lax.fori_loop(0, groups, settle_back, 0)


def pieces_of(values):
    first = values.astype(bf16)
    rest = values - first.astype(f32)
    second = rest.astype(bf16)
    return first, second, (rest - second.astype(f32)).astype(bf16)


def exact(left, right, dims):
    first, second, third = pieces_of(right)
    return mm(left, first, dims) + mm(left, second, dims) + mm(left, third, dims)


def exact_left(left, right, dims):
    first, second, third = pieces_of(left)
    return mm(first, right, dims) + mm(second, right, dims) + mm(third, right, dims)


def read_out(box, got_ref, reading_ref, bins_ref, counted_ref, read_ref, weight_ref, sends, recvs):
    place = box.place
    shapes_ref, loss_ref, rgrad_ref, g_ref = box.out(0, 1, 2, 3)
    size_ref, count_ref = box.use(0, 1)
    read_ref[...] = jnp.zeros_like(read_ref)
    label_ref, index_ref, population_ref, narrow_ref, x_ref = box.use(2, 3, 4, 5, 6)
    read_ref[0 : narrow_ref.shape[0], :] = narrow_ref[...]
    features, blocks, own, width = x_ref.shape
    samples = blocks * own
    bins = population_ref.shape[1]
    size, count = size_ref[0], count_ref[0]
    mask = (lax.broadcasted_iota(jnp.int32, (1, samples), 1) < size).astype(f32)
    task_size = jnp.zeros((1, samples), f32) + size.astype(f32)
    level = lax.broadcasted_iota(jnp.int32, (bins, bins), 0)
    diagonal = (level == lax.broadcasted_iota(jnp.int32, (bins, bins), 1)).astype(f32)
    live = [
        jnp.where(place.place * features + f < count, 1.0, 0.0) for f in range(features)
    ]
    logits = None
    for f in range(features):
        reading = x_ref[f].reshape(samples, width).astype(bf16)
        reading_ref[f] = reading
        projected = mm(reading, read_ref[...], NT)
        onehot = (lax.broadcasted_iota(jnp.int32, (bins, samples), 0) == index_ref[f : f + 1, :]).astype(f32)
        bins_ref[f] = onehot.astype(bf16)
        chosen = onehot * mask
        counted = jnp.maximum(jnp.sum(chosen, axis=1, keepdims=True), 1.0)
        counted_ref[f] = jnp.broadcast_to(counted, (bins, LANES))
        means = exact(chosen.astype(bf16), projected, NN) / counted
        weight = jnp.sum(diagonal * population_ref[f : f + 1, :].astype(f32), axis=1, keepdims=True)
        weight_ref[f] = jnp.broadcast_to(weight, (bins, LANES))
        weight = weight_ref[f]
        centre = jnp.sum(weight * means, axis=0, keepdims=True) / jnp.sum(weight, axis=0, keepdims=True)
        shapes = means - centre
        shapes_ref[f] = shapes
        part = exact_left(shapes, bins_ref[f], TN)[:SIZE] * live[f]
        logits = part if logits is None else logits + part
    box.flush(0)
    got_ref[place.place] = logits
    box.ready()
    copies = [
        remote(
            got_ref.at[place.place],
            got_ref.at[place.place],
            sends.at[k - 1],
            recvs.at[k - 1],
            {"feat": place.ring(k)},
        )
        for k in range(1, place.places)
    ]
    for copy in copies:
        copy.start()
    og_ref = box.use(7)
    for copy in copies:
        copy.wait()
    logits = got_ref[0]
    for k in range(1, place.places):
        logits = logits + got_ref[k]
    class_row = lax.broadcasted_iota(jnp.int32, logits.shape, 0)
    inside = class_row < CLASSES
    peak = jnp.max(jnp.where(inside, logits, masked_score), axis=0, keepdims=True)
    weights = jnp.where(inside, jnp.exp(jnp.where(inside, logits - peak, 0.0)), 0.0)
    weight_sum = jnp.sum(weights, axis=0, keepdims=True)
    log_total = peak + jnp.log(weight_sum)
    own_class = (class_row == label_ref[...]).astype(f32)
    picked = jnp.sum(logits * own_class, axis=0, keepdims=True)
    losses = mask * (log_total - picked)
    loss_ref[...] = jnp.broadcast_to(
        jnp.sum(losses, axis=1, keepdims=True) / task_size[:, 0:1], loss_ref.shape
    )
    logit_grad = mask * (weights / weight_sum - own_class) / task_size
    pad = jnp.zeros((LANES - SIZE, samples), f32)
    total = None
    for f in range(features):
        grad_rows = jnp.concatenate([logit_grad * live[f], pad], axis=0)
        shape_grad = exact(bins_ref[f], grad_rows, NT)
        weight = weight_ref[f]
        means_grad = shape_grad - weight / jnp.sum(weight, axis=0, keepdims=True) * jnp.sum(
            shape_grad, axis=0, keepdims=True
        )
        chosen = (bins_ref[f].astype(f32) * mask).astype(bf16)
        proj_grad = exact(chosen, means_grad / counted_ref[f], TN).astype(bf16)
        part = mm(proj_grad, reading_ref[f], TN)[:SIZE]
        total = part if total is None else total + part
        back = mm(proj_grad, read_ref[...]).reshape(blocks, own, width)
        g_ref[f] = og_ref[f].astype(f32) + back
    rgrad_ref[...] = total
    box.flush(1, 2, 3)


def dense_feature_backward(layer, box, fk_ref, send_ref, active_ref, ugrad_ref, hidden3_ref, rowgrad_ref, dup_ref, ddown_ref, arriving_ref, dqkv_ref, dao_ref, dc_ref, dh_ref, back_ref, dwf_ref, sends, recvs, self_sem, back_sends, back_recvs):
    place = box.place
    g1_ref, small_ref = box.out(0, 1)
    small_ref[...] = jnp.zeros_like(small_ref)
    fill_feature_codes(box.use(0)[0], None, fk_ref)
    g_ref, down_ref, u_ref, up_ref, x2_ref, gain_ref, shift_ref = box.use(1, 2, 3, 4, 5, 6, 7)
    features, blocks, own, width = g_ref.shape
    hidden_width = up_ref.shape[1]
    groups = own // SIZE
    parts = hidden_width // 512
    pairs = width // LANES
    box.ready()

    def copies(group):
        found = [
            remote(
                send_ref.at[:, place.ring(k), chunk(group, SIZE), :],
                arriving_ref.at[place.place, :, chunk(group, SIZE), :],
                sends.at[group, k - 1],
                recvs.at[group, k - 1],
                {"feat": place.ring(k)},
            )
            for k in range(1, place.places)
        ]
        keep = pltpu.make_async_copy(
            send_ref.at[:, place.place, chunk(group, SIZE), :],
            arriving_ref.at[place.place, :, chunk(group, SIZE), :],
            self_sem.at[group],
        )
        return found, keep

    def dense(group, carry):
        rows = chunk(group, ROWS)
        grad = cross(g_ref, group)
        low = grad.astype(bf16)
        rowgrad_ref[rows, :] = low
        small_ref[parts : parts + 1] += jnp.sum(low.astype(f32), axis=0, keepdims=True)
        for part in range(parts):
            cols = slice(part * 512, part * 512 + 512)
            active_grad = mm(low, down_ref[cols, :], NT).astype(bf16).astype(f32)
            u = u_ref[group, :, cols].astype(f32)
            bent = gelu_parts(u)
            slope = 0.5 * (1.0 + bent) + u * (1.0 - bent * bent) * (
                0.3989422804014327 + 0.05351611220146811 * u * u
            )
            active_ref[rows, cols] = (0.5 * u * (1.0 + bent)).astype(bf16)
            ugrad = (active_grad * slope).astype(bf16)
            ugrad_ref[rows, cols] = ugrad
            small_ref[part : part + 1] += jnp.sum(ugrad.astype(f32), axis=0, keepdims=True)
        hidden_grad = mm(ugrad_ref[rows, :], up_ref[...], NT)
        x2 = cross(x2_ref, group)
        gain, shift = gain_ref[2, layer : layer + 1, :], shift_ref[2, layer : layer + 1, :]
        _, _, hidden = layer_norm(x2, gain, shift)
        hidden3_ref[rows, :] = hidden.astype(bf16)
        norm_grad, gain_part, shift_part = layer_norm_back(hidden_grad.astype(bf16).astype(f32), x2, gain)
        small_ref[parts + 1 : parts + 2] += gain_part
        small_ref[parts + 2 : parts + 3] += shift_part
        grad = grad + norm_grad
        put_cross(g1_ref, group, grad)
        put_cross(send_ref, group, grad.astype(bf16))
        found, keep = copies(group)
        for copy in found:
            copy.start()
        keep.start()
        return carry

    lax.fori_loop(0, groups, dense, 0)

    def dense_weights(part, carry):
        cols = chunk(part, 512)
        block = dup_ref.shape[1:]
        dup_ref[part] = mm(ugrad_ref[:, cols], hidden3_ref[...], TN).astype(bf16).reshape(block)
        ddown_ref[part] = mm(active_ref[:, cols], rowgrad_ref[...], TN).astype(bf16).reshape(block)
        return carry

    lax.fori_loop(0, parts, dense_weights, 0)
    box.chains[0].begin(dup_ref)
    box.chains[1].begin(ddown_ref)
    w_ref, qkv_ref, ctx_ref, ext_ref = box.use(8, 9, 10, 11)

    def back_copies(group):
        return [
            remote(
                dh_ref.at[place.ring(k), :, chunk(group, SIZE), :],
                back_ref.at[:, place.place, chunk(group, SIZE), :],
                back_sends.at[group, k - 1],
                back_recvs.at[group, k - 1],
                {"feat": place.ring(k)},
            )
            for k in range(1, place.places)
        ]

    def feature(group, carry):
        found, keep = copies(group)
        for copy in found:
            copy.wait_recv()
        keep.wait()
        dao = cross(arriving_ref, group)
        dao_ref[group] = dao
        context_grad = mm(dao, w_ref[3], NT).astype(bf16)
        dc_ref[...] = context_grad
        grad_extra = delta_extra(ctx_ref[group], context_grad)
        for pair in range(pairs):
            lanes = pair_lanes(pair)
            query_grad, key_grad, value_grad = attend_pair_back(
                qkv_ref[group, 0, :, lanes],
                qkv_ref[group, 1, :, lanes],
                qkv_ref[group, 2, :, lanes],
                dc_ref[:, lanes],
                ext_ref[group],
                grad_extra,
                fk_ref[...],
                pair,
            )
            dqkv_ref[0, group, :, lanes] = (query_grad * 0.125).astype(bf16)
            dqkv_ref[1, group, :, lanes] = key_grad.astype(bf16)
            dqkv_ref[2, group, :, lanes] = value_grad.astype(bf16)
        total = mm(dqkv_ref[0, group], w_ref[0], NT)
        total = total + mm(dqkv_ref[1, group], w_ref[1], NT)
        total = total + mm(dqkv_ref[2, group], w_ref[2], NT)
        put_cross(dh_ref, group, total.astype(bf16))
        for copy in back_copies(group):
            copy.start()
        back_ref[:, place.place, chunk(group, SIZE), :] = dh_ref[place.place, :, chunk(group, SIZE), :]

        @pl.when(group == 0)
        def _():
            box.point("group")

        return carry

    lax.fori_loop(0, groups, feature, 0)
    hidden_ref = box.use(12)

    def weights(member, carry):
        total = None
        for group in range(groups):
            part = mm(hidden_ref[group], dqkv_ref[member, group], TN)
            total = part if total is None else total + part
        dwf_ref[member] = total.astype(bf16).reshape(dwf_ref.shape[1:])
        return carry

    lax.fori_loop(0, 3, weights, 0)
    total = None
    for group in range(groups):
        part = mm(ctx_ref[group], dao_ref[group], TN)
        total = part if total is None else total + part
    dwf_ref[3] = total.astype(bf16).reshape(dwf_ref.shape[1:])
    box.chains[2].begin(dwf_ref)
    x1_ref = box.use(13)

    def enter(group, carry):
        for copy in back_copies(group):
            copy.wait_recv()
        norm_grad, gain_part, shift_part = layer_norm_back(
            cross(back_ref, group).astype(f32), cross(x1_ref, group), gain_ref[1, layer : layer + 1, :]
        )
        small_ref[parts + 3 : parts + 4] += gain_part
        small_ref[parts + 4 : parts + 5] += shift_part
        put_cross(g1_ref, group, cross(g1_ref, group) + norm_grad)
        box.flush_part(0, group, cross_view)

        @pl.when(group == 0)
        def _():
            box.point("enter")

        return carry

    lax.fori_loop(0, groups, enter, 0)
    box.flush(1)
    box.point("end")

    def settle(group, carry):
        for copy in copies(group)[0]:
            copy.wait_send()
        for copy in back_copies(group):
            copy.wait_send()
        return carry

    lax.fori_loop(0, groups, settle, 0)


def sample_backward_sums(layer, last, box, sk_ref, sq_ref, dqkv_ref, hidden_ref, low_ref, dc_ref, gext_ref, kacc_ref, vacc_ref, dw_ref, *tail):
    place = box.place
    g0_ref, small_ref = box.out(0, 1)
    small_ref[...] = jnp.zeros_like(small_ref)
    fill_sample_codes(box.use(0)[0], sq_ref, sk_ref)
    g_ref, w_ref, ctx_ref = box.use(1, 2, 3)
    features, blocks, own, width = g_ref.shape
    per = ROWS // own
    steps = blocks // per
    pairs = width // LANES
    box.ready()

    def enter(unit, carry):
        f, part = unit // steps, lax.rem(unit, steps)
        low = block_rows(g_ref, f, part, per).astype(bf16)
        low_ref[f, chunk(part, ROWS), :] = low
        context_grad = mm(low, w_ref[3], NT).astype(bf16)
        dc_ref[f, chunk(part, ROWS), :] = context_grad
        gext_ref[f, chunk(part, ROWS), :] = delta_extra(block_rows(ctx_ref, f, part, per), context_grad)
        return carry

    lax.fori_loop(0, features * steps, enter, 0)
    box.point("enter")
    qkv_ref, ext_ref = box.use(4, 5)

    def attend(unit, carry):
        f, step = unit // steps, lax.rem(unit, steps)
        rows = chunk(step, ROWS)
        first = step == 0
        for pair in range(pairs):
            lanes = pair_lanes(pair)
            query_grad, key_grad, value_grad = attend_pair_back(
                block_rows(qkv_ref.at[0], f, step, per, lanes),
                all_rows(qkv_ref.at[1], f, lanes),
                all_rows(qkv_ref.at[2], f, lanes),
                dc_ref[f, rows, lanes],
                block_rows(ext_ref, f, step, per),
                gext_ref[f, rows, :],
                sk_ref[...],
                pair,
            )
            dqkv_ref[0, f, rows, lanes] = (query_grad * 0.125).astype(bf16)
            kacc_ref[:, lanes] = jnp.where(first, 0.0, kacc_ref[:, lanes]) + key_grad
            vacc_ref[:, lanes] = jnp.where(first, 0.0, vacc_ref[:, lanes]) + value_grad
        dqkv_ref[1, f] = kacc_ref[...].astype(bf16)
        dqkv_ref[2, f] = vacc_ref[...].astype(bf16)
        return carry

    kacc_ref[...] = jnp.zeros_like(kacc_ref)
    vacc_ref[...] = jnp.zeros_like(vacc_ref)
    lax.fori_loop(0, features * steps, attend, 0)
    box.point("attend")
    x_ref, gain_ref, shift_ref = box.use(6, 7, 8)
    gain, shift = gain_ref[0, layer : layer + 1, :], shift_ref[0, layer : layer + 1, :]

    def again(unit, carry):
        f, part = unit // steps, lax.rem(unit, steps)
        _, _, hidden = layer_norm(block_rows(x_ref, f, part, per), gain, shift)
        hidden_ref[f, chunk(part, ROWS), :] = hidden.astype(bf16)
        return carry

    lax.fori_loop(0, features * steps, again, 0)

    def weights(member, carry):
        total = None
        for f in range(features):
            part = mm(hidden_ref[f], dqkv_ref[member, f], TN)
            total = part if total is None else total + part
        dw_ref[member] = total.astype(bf16).reshape(dw_ref.shape[1:])
        return carry

    lax.fori_loop(0, 3, weights, 0)
    total = None
    for f in range(features):
        part = mm(all_rows(ctx_ref, f), low_ref[f], TN)
        total = part if total is None else total + part
    dw_ref[3] = total.astype(bf16).reshape(dw_ref.shape[1:])
    box.chains[0].begin(dw_ref)

    def leave(unit, carry):
        f, part = unit // steps, lax.rem(unit, steps)
        rows = chunk(part, ROWS)
        total = mm(dqkv_ref[0, f, rows, :], w_ref[0], NT)
        total = total + mm(dqkv_ref[1, f, rows, :], w_ref[1], NT)
        total = total + mm(dqkv_ref[2, f, rows, :], w_ref[2], NT)
        norm_grad, gain_part, shift_part = layer_norm_back(
            total.astype(bf16).astype(f32), block_rows(x_ref, f, part, per), gain
        )
        small_ref[0:1] += gain_part
        small_ref[1:2] += shift_part
        g0_ref[f, chunk(part, per), :, :] = (block_rows(g_ref, f, part, per) + norm_grad).reshape(per, own, width)

        @pl.when(unit == 1)
        def _():
            box.point("leave")

        return carry

    lax.fori_loop(0, features * steps, leave, 0)
    box.flush(0)
    if last:
        last_sums(box, small_ref, *tail)
    else:
        box.flush(1)
        box.point("end")


def last_sums(box, sample_small, packed, small_got, small_sends, small_recvs):
    place = box.place
    dense_small, layer_small, last_dense, read_grad = box.use(9, 10, 11, 12)
    chains = box.chains
    rows = 11
    packed[0:9] = last_dense[0:9]
    packed[9:11] = sample_small[0:2]
    packed[rows : rows + 9] = dense_small[0:9]
    packed[rows + 9 : rows + 11] = layer_small[0:2]
    packed[2 * rows : 2 * rows + SIZE] = read_grad[...]

    def exchange(base, index, devices):
        copies = [
            remote(small_got.at[base + index], small_got.at[base + index], small_sends.at[base + k], small_recvs.at[base + k], device)
            for k, device in enumerate(devices)
        ]
        for copy in copies:
            copy.start()
        return copies

    def gather(copies, base, count):
        for copy in copies:
            copy.wait()
        total = small_got[base]
        for k in range(1, count):
            total = total + small_got[base + k]
        return total

    small_got[place.core] = packed[...]
    small = exchange(0, place.core, [{"feat": place.place + 1 - 2 * place.core}])
    sample_out, feature_out, up_out, down_out, gain_out, shift_out, upb_out, downb_out, read_out_ref = box.out(
        2, 3, 4, 5, 6, 7, 8, 9, 10
    )
    sample_later, feature_later, up_later, down_later = None, *box.use(13, 14, 15)
    small_got[2 + place.task] = gather(small, 0, 2)
    small = exchange(2, place.task, [{"task": place.task_partner(k)} for k in range(1, place.tasks)])
    box.point("early")
    up_out[0], up_out[1] = chains[2].bufs[-1][2][...].T, up_later[...].T
    down_out[0], down_out[1] = chains[3].bufs[-1][2][...], down_later[...]
    feature_out[1] = feature_later[...]
    sample_out[1] = chains[4].bufs[-1][2][...]
    box.flush(4, 5)
    base = 2 + place.tasks
    small_got[base + place.chip] = gather(small, 2, place.tasks)
    small = exchange(
        base, place.chip, [{"feat": 2 * place.line_partner(k) + place.core} for k in range(1, place.chips)]
    )
    box.point("late")
    feature_out[0] = chains[1].bufs[-1][2][...]
    box.flush(3)
    packed[...] = gather(small, base, place.chips)
    width = packed.shape[1]
    parts = upb_out.shape[1] // width
    for layer in range(2):
        at = rows * layer
        for part in range(parts):
            upb_out[layer : layer + 1, part * width : (part + 1) * width] = packed[at + part : at + part + 1]
        downb_out[layer : layer + 1] = packed[at + parts : at + parts + 1]
        for member, row in ((2, parts + 1), (1, parts + 3), (0, parts + 5)):
            gain_out[member, layer : layer + 1] = packed[at + row : at + row + 1]
            shift_out[member, layer : layer + 1] = packed[at + row + 1 : at + row + 2]
    read_out_ref[...] = packed[2 * rows : 2 * rows + SIZE]
    box.flush(6, 7, 8, 9, 10)
    box.point("end")
    sample_out[0] = chains[0].bufs[-1][2][...]
    box.flush(2)


def codes(item, live, size, rows):
    lanes = jnp.arange(LANES)[None, :] - CODE_LANE
    inside = (lanes >= 0) & (lanes < size)
    own = lanes == item[:, None]
    query_code = (own & inside).astype(bf16)
    key_code = jnp.where(inside & ~(own & live[:, None]), masked_score, 0.0).astype(bf16)
    return query_code, key_code


def local_fused(
    tokens_in,
    sample_weights,
    feature_weights,
    norm_gain,
    norm_shift,
    up_weight,
    up_bias,
    down_weight,
    down_bias,
    read_weight,
    output_grad,
    task_sizes,
    feature_counts,
    bin_index,
    bin_counts,
    class_labels,
):
    samples, features, width = tokens_in.shape[1:]
    hidden_width = up_weight.shape[2]
    tasks, places = lax.axis_size("task"), lax.axis_size("feat")
    chips = places // 2
    own = samples // places
    groups = own // SIZE
    units = features * (own * places // ROWS)
    sizes = (tasks, places)
    shape = (features, places, own, width)
    block_shape = (places, features, own, width)
    group_shape = (groups, ROWS, width)
    share = width // places
    share_shape = (share, width)
    piece_shape = (tasks, chips, 2, share, width)
    rows_total = groups * ROWS
    vmem = pltpu.VMEM

    def dma(*counts):
        return pltpu.SemaphoreType.DMA(counts)

    gains = norm_gain.transpose(1, 0, 2)
    shifts = norm_shift.transpose(1, 0, 2)
    stream = tokens_in[0].astype(f32).transpose(1, 0, 2).reshape(shape)
    stored = []
    for layer in range(LAYERS):
        x1, qkv, ctx, ext, hidden, fqkv, fctx, fext, x2, x3, u = fused(
            functools.partial(forward_layer, layer),
            "forward_layer",
            sizes,
            [
                (task_sizes, "scalar"),
                (feature_counts, "scalar"),
                (stream, None),
                (gains, None),
                (shifts, None),
                (sample_weights, layer),
                (feature_weights, layer),
                (up_weight, layer),
                (up_bias, None),
                (down_weight, layer),
                (down_bias, None),
            ],
            [
                (shape, f32),
                ((3,) + shape, bf16),
                (shape, bf16),
                (shape[:3] + (LANES,), bf16),
                (group_shape, bf16),
                ((groups, 3, ROWS, width), bf16),
                (group_shape, bf16),
                ((groups, ROWS, LANES), bf16),
                (shape, f32),
                (shape, f32),
                ((groups, ROWS, hidden_width), bf16),
            ],
            [
                vmem((ROWS, LANES), bf16),
                vmem((samples, LANES), bf16),
                vmem((ROWS, LANES), bf16),
                vmem((ROWS, LANES), bf16),
                vmem(shape, bf16),
                vmem(block_shape, bf16),
                vmem(block_shape, bf16),
                vmem(shape, bf16),
                vmem((ROWS, hidden_width), bf16),
                dma(units, places - 1),
                dma(units, places - 1),
                dma(units),
                dma(groups, places - 1),
                dma(groups, places - 1),
            ],
            [],
            share_shape,
            1 + layer,
        )
        stored.append((stream, x1, qkv, ctx, ext, hidden, fqkv, fctx, fext, x2, u))
        stream = x3

    shapes, loss, read_grad, stream_grad = fused(
        read_out,
        "read_out",
        sizes,
        [
            (task_sizes, "scalar"),
            (feature_counts, "scalar"),
            (class_labels, None),
            (bin_index[0].T, None),
            (bin_counts[0], None),
            (read_weight.T, None),
            (stream, None),
            (output_grad[0].transpose(1, 0, 2).reshape(shape), None),
        ],
        [((features, BINS, LANES), f32), ((8, LANES), f32), ((SIZE, width), f32), (shape, f32)],
        [
            vmem((places, SIZE, samples), f32),
            vmem((features, samples, width), bf16),
            vmem((features, BINS, samples), bf16),
            vmem((features, BINS, LANES), f32),
            vmem((LANES, width), bf16),
            vmem((features, BINS, LANES), f32),
            dma(places - 1),
            dma(places - 1),
        ],
        [],
        share_shape,
        3,
    )

    later = {}
    smalls = {}
    for layer in reversed(range(LAYERS)):
        x0, x1, qkv, ctx, ext, hidden, fqkv, fctx, fext, x2, u = stored[layer]
        last = layer == 0
        sums = [
            ((1, 2), ("group", "end"), None, True),
            ((1, 2), ("group", "end"), None, True),
            ((1,), ("enter",), None, True),
        ]
        if last:
            sums.append(((2,), ("end",), later["sample"], True))
        g1, dense_small, up_sum, down_sum, feature_sum, *more = fused(
            functools.partial(dense_feature_backward, layer),
            "dense_feature_backward",
            sizes,
            [
                (feature_counts, "scalar"),
                (stream_grad, None),
                (down_weight, layer),
                (u, None),
                (up_weight, layer),
                (x2, None),
                (gains, None),
                (shifts, None),
                (feature_weights, layer),
                (fqkv, None),
                (fctx, None),
                (fext, None),
                (hidden, None),
                (x1, None),
            ],
            [(shape, f32), ((16, width), f32)],
            [
                vmem((ROWS, LANES), bf16),
                vmem(shape, bf16),
                vmem((rows_total, hidden_width), bf16),
                vmem((rows_total, hidden_width), bf16),
                vmem((rows_total, width), bf16),
                vmem((rows_total, width), bf16),
                vmem(piece_shape, bf16),
                vmem(piece_shape, bf16),
                vmem(block_shape, bf16),
                vmem((3,) + group_shape, bf16),
                vmem(group_shape, bf16),
                vmem((ROWS, width), bf16),
                vmem(block_shape, bf16),
                vmem(shape, bf16),
                vmem(piece_shape, bf16),
                dma(groups, places - 1),
                dma(groups, places - 1),
                dma(groups),
                dma(groups, places - 1),
                dma(groups, places - 1),
            ],
            sums,
            share_shape,
            4 + layer,
        )
        if last:
            later["sample"] = more[0]
        ins = [
            (task_sizes, "scalar"),
            (g1, None),
            (sample_weights, layer),
            (ctx, None),
            (qkv, None),
            (ext, None),
            (x0, None),
            (gains, None),
            (shifts, None),
        ]
        outs = [(shape, f32), ((8, width), f32)]
        scratch = [
            vmem((samples, LANES), bf16),
            vmem((ROWS, LANES), bf16),
            vmem((3, features, samples, width), bf16),
            vmem((features, samples, width), bf16),
            vmem((features, samples, width), bf16),
            vmem((features, samples, width), bf16),
            vmem((features, samples, LANES), bf16),
            vmem((samples, width), f32),
            vmem((samples, width), f32),
            vmem(piece_shape, bf16),
        ]
        if last:
            matrix_shape = (LAYERS, share, width)
            small_shape = (2 * 11 + SIZE + 2, width)
            slots = 2 + tasks + chips
            sums = [
                ((1, 2, 3), ("leave", "late", "end"), None, False),
                ((2, 3), ("attend", "late"), feature_sum, False),
                ((3,), ("early",), up_sum, False),
                ((3,), ("early",), down_sum, False),
                ((3,), ("early",), later["sample"], False),
            ]
            ins += [(smalls["dense"], None), (smalls["sample"], None), (dense_small, None), (read_grad, None)]
            ins += [(later[name], None) for name in ("feature", "up", "down")]
            outs += [
                (matrix_shape, f32),
                (matrix_shape, f32),
                ((LAYERS, width, share), f32),
                (matrix_shape, f32),
                ((3, LAYERS, width), f32),
                ((3, LAYERS, width), f32),
                ((LAYERS, hidden_width), f32),
                ((LAYERS, width), f32),
                ((SIZE, width), f32),
            ]
            scratch += [vmem(small_shape, f32), vmem((slots,) + small_shape, f32), dma(slots), dma(slots)]
        else:
            sums = [
                ((1,), ("end",), None, True),
                ((2, 3), ("attend", "end"), feature_sum, True),
                ((3,), ("attend",), up_sum, True),
                ((3,), ("attend",), down_sum, True),
            ]
        stream_grad, sample_small, *more = fused(
            functools.partial(sample_backward_sums, layer, last),
            "sample_backward",
            sizes,
            ins,
            outs,
            scratch,
            sums,
            share_shape,
            6 + layer,
        )
        if not last:
            later = dict(zip(("sample", "feature", "up", "down"), more))
            smalls = {"dense": dense_small, "sample": sample_small}

    sample_grad, feature_grad, up_grad, down_grad, gain_grad, shift_grad, upb_grad, downb_grad, reader_grad = more
    return (
        stream.reshape(features, samples, width).transpose(1, 0, 2)[None],
        shapes[None, :, :, :CLASSES],
        stream_grad.reshape(features, samples, width).transpose(1, 0, 2)[None],
        loss[0, :1],
        sample_grad[:, None],
        feature_grad[:, None],
        gain_grad.transpose(1, 0, 2),
        shift_grad.transpose(1, 0, 2),
        up_grad,
        upb_grad,
        down_grad,
        downb_grad,
        reader_grad[:CLASSES].T,
    )


def local(
    tokens_in,
    sample_weights,
    feature_weights,
    norm_gain,
    norm_shift,
    up_weight,
    up_bias,
    down_weight,
    down_bias,
    read_weight,
    output_grad,
    task_sizes,
    feature_counts,
    bin_index,
    bin_counts,
    class_labels,
):
    samples = tokens_in.shape[1]
    features = tokens_in.shape[2]
    width = tokens_in.shape[3]
    hidden_width = up_weight.shape[2]
    task_devices = lax.axis_size("task")
    feature_devices = lax.axis_size("feat")
    all_features = features * feature_devices
    own_samples = samples // feature_devices
    size = min(16, own_samples)
    groups = own_samples // size
    group_rows = all_features * size
    rows_total = features * samples

    if (
        own_samples % 32 == 0
        and samples % ROWS == 0
        and ROWS % own_samples == 0
        and group_rows == ROWS
        and own_samples == 4 * SIZE
        and task_devices == hidden_width // width == 4
    ):
        return local_fused(
            tokens_in,
            sample_weights,
            feature_weights,
            norm_gain,
            norm_shift,
            up_weight,
            up_bias,
            down_weight,
            down_bias,
            read_weight,
            output_grad,
            task_sizes,
            feature_counts,
            bin_index,
            bin_counts,
            class_labels,
        )

    sample_live = jnp.arange(samples) < task_sizes[0]
    feature_live = jnp.arange(all_features) < feature_counts[0]
    sample_mask = sample_live.astype(f32)
    local_index = lax.axis_index("feat") * features + jnp.arange(features)
    local_live = (local_index < feature_counts[0]).astype(f32)
    sample_qcode, sample_kcode = codes(jnp.zeros((samples,), jnp.int32), sample_live, 1, samples)
    sample_qcode = sample_qcode[:ROWS]
    item = jnp.arange(group_rows) % size
    feature_qcode, feature_kcode = codes(item, jnp.repeat(feature_live, size), size, group_rows)

    def exchange_out(rows):
        parts = rows.reshape(features, feature_devices, own_samples, width)
        got = lax.all_to_all(parts, "feat", split_axis=1, concat_axis=0, tiled=True)
        return got.reshape(all_features, own_samples, width)

    def exchange_back(rows):
        parts = rows.reshape(feature_devices, features, own_samples, width)
        got = lax.all_to_all(parts, "feat", split_axis=0, concat_axis=2, tiled=True)
        return got.reshape(features, samples, width)

    stream = tokens_in[0].astype(f32).transpose(1, 0, 2)
    token_shape = (features, samples, width)
    stored = []
    for layer in range(LAYERS):
        gain, shift = norm_gain[layer], norm_shift[layer]
        x1, h2, qkv, ctx, ext = call(
            sample_forward,
            "sample_forward",
            [
                (token_shape, f32),
                (token_shape, bf16),
                ((3,) + token_shape, bf16),
                (token_shape, bf16),
                ((features, samples, LANES), bf16),
            ],
            [],
            stream,
            gain,
            shift,
            sample_weights[layer],
            sample_qcode,
            sample_kcode,
        )
        swapped = exchange_out(h2)
        a, fqkv, fctx, fext = call(
            functools.partial(feature_forward, size),
            "feature_forward",
            [
                ((all_features, own_samples, width), bf16),
                ((groups, 3, group_rows, width), bf16),
                ((groups, group_rows, width), bf16),
                ((groups, group_rows, LANES), bf16),
            ],
            [],
            swapped,
            feature_weights[layer],
            feature_qcode,
            feature_kcode,
        )
        back = exchange_back(a)
        x3, u = call(
            dense_forward,
            "dense_forward",
            [((rows_total, width), f32), ((rows_total, hidden_width), bf16)],
            [],
            x1.reshape(rows_total, width),
            back.reshape(rows_total, width),
            gain,
            shift,
            up_weight[layer],
            up_bias[layer][None],
            down_weight[layer],
            down_bias[layer][None],
        )
        stored.append((stream, x1, qkv, ctx, ext, swapped, fqkv, fctx, fext, back, u))
        stream = x3.reshape(token_shape)

    reading = stream.astype(bf16)
    projected = jnp.einsum("fsd,dc->fsc", reading, read_weight, preferred_element_type=f32)
    onehot_bins = (bin_index[0].T[..., None] == jnp.arange(BINS)).astype(f32)
    chosen = onehot_bins * sample_mask[None, :, None]
    counted = jnp.maximum(jnp.sum(chosen, axis=1), 1.0)
    bin_sums = jnp.einsum("fsb,fsc->fbc", chosen, projected, precision=highest)
    bin_means = bin_sums / counted[..., None]
    bin_weight = bin_counts[0].astype(f32)
    weight_total = jnp.sum(bin_weight, axis=-1, keepdims=True)
    centre = jnp.sum(bin_weight[..., None] * bin_means, axis=1, keepdims=True) / weight_total[..., None]
    shapes = bin_means - centre
    used_bins = onehot_bins * local_live[:, None, None]
    local_logits = jnp.einsum("fsb,fbc->sc", used_bins, shapes, precision=highest)
    logits = lax.psum(local_logits, "feat")
    row_max = jnp.max(logits, axis=-1, keepdims=True)
    log_total = row_max + jnp.log(jnp.sum(jnp.exp(logits - row_max), axis=-1, keepdims=True))
    label_rows = (class_labels[0][:, None] == jnp.arange(CLASSES)).astype(f32)
    picked = jnp.sum(logits * label_rows, axis=-1)
    live_count = task_sizes[0].astype(f32)
    task_loss = jnp.sum(sample_mask * (log_total[:, 0] - picked)) / live_count
    logit_grad = sample_mask[:, None] * (jnp.exp(logits - log_total) - label_rows) / live_count
    shape_grad = jnp.einsum("fsb,sc->fbc", used_bins, logit_grad, precision=highest)
    means_grad = shape_grad - bin_weight[..., None] / weight_total[..., None] * jnp.sum(
        shape_grad, axis=1, keepdims=True
    )
    sum_grad = means_grad / counted[..., None]
    projected_grad = jnp.einsum("fsb,fbc->fsc", chosen, sum_grad, precision=highest).astype(bf16)
    read_grad = jnp.einsum("fsd,fsc->dc", reading, projected_grad, preferred_element_type=f32)
    stream_grad = output_grad[0].astype(f32).transpose(1, 0, 2) + jnp.einsum(
        "fsc,dc->fsd", projected_grad, read_weight, preferred_element_type=f32
    )

    small = [None] * LAYERS
    big = [None] * LAYERS
    for layer in reversed(range(LAYERS)):
        gain, shift = norm_gain[layer], norm_shift[layer]
        x0, x1, qkv, ctx, ext, swapped, fqkv, fctx, fext, back, u = stored[layer]
        flat = (rows_total, width)
        g2, sent, dup, ddown, dupb, ddownb, dgs2 = call(
            dense_backward,
            "dense_backward",
            [
                (flat, f32),
                (flat, bf16),
                ((hidden_width, width), bf16),
                ((hidden_width, width), bf16),
                ((1, hidden_width), f32),
                ((1, width), f32),
                ((2, width), f32),
            ],
            [
                ((rows_total, hidden_width), bf16),
                ((rows_total, hidden_width), bf16),
                (flat, bf16),
                (flat, bf16),
            ],
            stream_grad.reshape(flat),
            x1.reshape(flat),
            back.reshape(flat),
            u,
            gain,
            shift,
            up_weight[layer],
            down_weight[layer],
        )
        arriving = exchange_out(sent.reshape(token_shape))
        group_shape = (groups, group_rows, width)
        dh, dwf = call(
            functools.partial(feature_backward, size),
            "feature_backward",
            [((all_features, own_samples, width), bf16), ((4, width, width), bf16)],
            [
                ((3,) + group_shape, bf16),
                (group_shape, bf16),
                (group_shape, bf16),
                ((group_rows, width), bf16),
            ],
            arriving,
            swapped,
            feature_weights[layer],
            feature_kcode,
            fqkv,
            fctx,
            fext,
        )
        returned = exchange_back(dh)
        g0, dws, dgs01 = call(
            sample_backward,
            "sample_backward",
            [(token_shape, f32), ((4, width, width), bf16), ((2, 2, width), f32)],
            [
                ((3,) + token_shape, bf16),
                (token_shape, bf16),
                (token_shape, bf16),
                (token_shape, bf16),
                ((features, samples, LANES), bf16),
                ((samples, LANES), f32),
                ((samples, LANES), f32),
            ],
            g2.reshape(token_shape),
            returned,
            x1,
            x0,
            gain,
            shift,
            sample_weights[layer],
            sample_kcode,
            qkv,
            ctx,
            ext,
        )
        stream_grad = g0
        small[layer] = (
            jnp.stack([dgs01[0, 0], dgs01[1, 0], dgs2[0]]),
            jnp.stack([dgs01[0, 1], dgs01[1, 1], dgs2[1]]),
            dupb[0],
            ddownb[0],
        )
        big[layer] = [dws.reshape(4 * width, width), dwf.reshape(4 * width, width), dup, ddown]
    shard_shape = (LAYERS, 4 // task_devices, width // feature_devices, width)
    pieces = [big[layer][member] for member in range(4) for layer in range(LAYERS)]
    rows = [row.reshape(-1, width) for layer in range(LAYERS) for row in small[layer]]
    rows.append(read_grad.T)
    lengths = [row.shape[0] for row in rows]
    fill = -sum(lengths) % 8
    small_rows = jnp.concatenate(rows + [jnp.zeros((fill, width), f32)])
    if (width // feature_devices) % 16 == 0:
        *shares, small_sums = sum_everywhere(pieces, small_rows, task_devices, feature_devices)
    else:
        shares = [
            lax.psum_scatter(piece, ("task", "feat"), scatter_dimension=0, tiled=True).astype(f32)
            for piece in pieces
        ]
        small_sums = lax.psum(small_rows, ("task", "feat"))
    matrices = [jnp.stack(shares[member * LAYERS : member * LAYERS + LAYERS]) for member in range(4)]
    split = []
    at = 0
    for length in lengths:
        split.append(small_sums[at : at + length])
        at += length
    summed = [jnp.stack([split[4 * layer + member] for layer in range(LAYERS)]) for member in range(4)]
    summed[2] = summed[2].reshape(LAYERS, hidden_width)
    summed[3] = summed[3].reshape(LAYERS, width)
    summed.append(split[-1].T)
    return (
        stream.transpose(1, 0, 2)[None],
        shapes[None],
        stream_grad.transpose(1, 0, 2)[None],
        task_loss[None],
        matrices[0].reshape(shard_shape),
        matrices[1].reshape(shard_shape),
        summed[0],
        summed[1],
        matrices[2].transpose(0, 2, 1),
        summed[2],
        matrices[3],
        summed[3],
        summed[4],
    )


def solution(mesh):
    in_specs = (
        P("task", None, "feat", None),
        P(),
        P(),
        P(),
        P(),
        P(),
        P(),
        P(),
        P(),
        P(),
        P("task", None, "feat", None),
        P("task"),
        P("task"),
        P("task", None, "feat"),
        P("task", "feat", None),
        P("task", None),
    )
    out_specs = (
        P("task", None, "feat", None),
        P("task", "feat", None, None),
        P("task", None, "feat", None),
        P("task"),
        P(None, "task", "feat", None),
        P(None, "task", "feat", None),
        P(),
        P(),
        P(None, None, ("task", "feat")),
        P(),
        P(None, ("task", "feat"), None),
        P(),
        P(),
    )
    return jax.shard_map(local, mesh=mesh, in_specs=in_specs, out_specs=out_specs, check_vma=False)
```

```python
import functools

import jax
import jax.numpy as jnp
from jax import lax
from jax.experimental import pallas as pl
from jax.experimental.pallas import tpu as pltpu
from jax.sharding import PartitionSpec as P

HEADS = 8
BINS = 64
CLASSES = 10
LAYERS = 2
LANES = 128
CODE_LANE = 32
ROWS = 256

epsilon = 1e-05
masked_score = -1e30
highest = lax.Precision.HIGHEST
bf16 = jnp.bfloat16
f32 = jnp.float32

NN = (((1,), (0,)), ((), ()))
NT = (((1,), (1,)), ((), ()))
TN = (((0,), (0,)), ((), ()))


def mm(left, right, dims=NN):
    return lax.dot_general(left, right, dims, preferred_element_type=f32)


def lane_row():
    return lax.broadcasted_iota(jnp.int32, (1, LANES), 1)


def half_row(half):
    lanes = lane_row()
    picked = lanes < 64 if half == 0 else lanes >= 64
    return picked.astype(f32).astype(bf16)


def piece_row(pair, half):
    offset = lane_row() - 64 * half - 3 * pair
    return jnp.where((offset >= 0) & (offset < 3), -1.0, 0.0).astype(bf16)


def split_pieces(values, order):
    first = values.astype(bf16).astype(f32)
    rest = values - first
    second = rest.astype(bf16).astype(f32)
    third = rest - second
    return jnp.where(order == 0, first, jnp.where(order == 1, second, third))


def layer_norm(rows, gain, shift):
    centred = rows - jnp.mean(rows, axis=-1, keepdims=True)
    inverse = lax.rsqrt(jnp.mean(centred * centred, axis=-1, keepdims=True) + epsilon)
    normed = centred * inverse
    return normed, inverse, normed * gain + shift


def layer_norm_back(grad_rows, rows, gain):
    centred = rows - jnp.mean(rows, axis=-1, keepdims=True)
    inverse = lax.rsqrt(jnp.mean(centred * centred, axis=-1, keepdims=True) + epsilon)
    normed = centred * inverse
    scaled = grad_rows * gain
    inner = (
        scaled
        - jnp.mean(scaled, axis=-1, keepdims=True)
        - normed * jnp.mean(scaled * normed, axis=-1, keepdims=True)
    )
    gain_part = jnp.sum(grad_rows * normed, axis=0, keepdims=True)
    shift_part = jnp.sum(grad_rows, axis=0, keepdims=True)
    return inverse * inner, gain_part, shift_part


def chunk(index, size):
    return pl.ds(pl.multiple_of(index * size, size), size)


def attend_pair(query, key, value, query_code, key_code, pair, extras):
    query_wide = jnp.concatenate([query, query_code], axis=1)
    total = None
    peaks = []
    for half in range(2):
        mask = half_row(half)
        key_wide = jnp.concatenate([key * mask, key_code], axis=1)
        scores = mm(query_wide, key_wide, NT)
        peak = jnp.max(scores, axis=-1, keepdims=True)
        weights = jnp.exp(scores - peak).astype(bf16)
        ones = jnp.broadcast_to(mask, value.shape)
        part = mm(weights, jnp.concatenate([value * mask, ones], axis=1))
        total = part if total is None else total + part
        peaks.append(peak)
    lanes = lane_row()
    row_total = total[:, LANES:]
    context = total[:, :LANES] / row_total
    log_total = jnp.where(lanes < 64, peaks[0], peaks[1]) + jnp.log(row_total)
    order = lanes % 64 - 3 * pair
    extras = jnp.where((order >= 0) & (order < 3), split_pieces(log_total, order), extras)
    return context.astype(bf16), extras


def attend_pair_back(query, key, value, context_grad, query_extra, grad_extra, key_code, pair):
    query_wide = jnp.concatenate([query, query_extra], axis=1)
    grad_wide = jnp.concatenate([context_grad, grad_extra], axis=1)
    query_grad = key_grad = value_grad = None
    for half in range(2):
        mask = half_row(half)
        pieces = piece_row(pair, half)
        key_half = key * mask
        key_wide = jnp.concatenate([key_half, key_code + pieces], axis=1)
        value_wide = jnp.concatenate(
            [value * mask, jnp.broadcast_to(pieces, value.shape)], axis=1
        )
        attention = jnp.exp(mm(key_wide, query_wide, NT))
        score_grad = (attention * mm(value_wide, grad_wide, NT)).astype(bf16)
        value_part = mm(attention.astype(bf16), context_grad * mask)
        key_part = mm(score_grad, query * mask)
        query_part = mm(score_grad, key_half, TN)
        if half == 0:
            query_grad, key_grad, value_grad = query_part, key_part, value_part
        else:
            query_grad, key_grad, value_grad = (
                query_grad + query_part,
                key_grad + key_part,
                value_grad + value_part,
            )
    return query_grad, key_grad, value_grad


def delta_extra(context, context_grad):
    width = context.shape[1]
    products = context.astype(f32) * context_grad.astype(f32)
    high = products.astype(bf16)
    low = (products - high.astype(f32)).astype(bf16)
    head = lax.broadcasted_iota(jnp.int32, (width, LANES), 0) // (width // HEADS)
    offset = lax.broadcasted_iota(jnp.int32, (width, LANES), 1) - 64 * (head % 2) - 3 * (head // 2)
    spread = jnp.where((offset >= 0) & (offset < 3), 1.0, 0.0).astype(bf16)
    sums = mm(high, spread) + mm(low, spread)
    return split_pieces(sums, lane_row() % 64 % 3).astype(bf16)


def sample_forward(x_ref, gain_ref, shift_ref, w_ref, qcode_ref, kcode_ref, x1_ref, h2_ref, qkv_ref, ctx_ref, ext_ref):
    features, samples, width = x_ref.shape
    steps = samples // ROWS

    def project(unit, carry):
        f, rows = unit // steps, chunk(unit % steps, ROWS)
        _, _, hidden = layer_norm(x_ref[f, rows, :], gain_ref[0:1], shift_ref[0:1])
        hidden = hidden.astype(bf16)
        for member in range(3):
            out = mm(hidden, w_ref[member]).astype(bf16)
            if member == 0:
                out = out * jnp.asarray(0.125, bf16)
            qkv_ref[member, f, rows, :] = out
        return carry

    lax.fori_loop(0, features * steps, project, 0)

    def attend(unit, carry):
        f, rows = unit // steps, chunk(unit % steps, ROWS)
        code = qcode_ref[...]

        def pair_step(pair, extras):
            lanes = chunk(pair, LANES)
            context, extras = attend_pair(
                qkv_ref[0, f, rows, lanes],
                qkv_ref[1, f, :, lanes],
                qkv_ref[2, f, :, lanes],
                code,
                kcode_ref[...],
                pair,
                extras,
            )
            ctx_ref[f, rows, lanes] = context
            return extras

        extras = lax.fori_loop(0, width // LANES, pair_step, code.astype(f32))
        ext_ref[f, rows, :] = extras.astype(bf16)
        x1 = x_ref[f, rows, :] + mm(ctx_ref[f, rows, :], w_ref[3])
        x1_ref[f, rows, :] = x1
        _, _, hidden = layer_norm(x1, gain_ref[1:2], shift_ref[1:2])
        h2_ref[f, rows, :] = hidden.astype(bf16)
        return carry

    lax.fori_loop(0, features * steps, attend, 0)


def load_group(ref, group, size):
    features, _, width = ref.shape
    block = ref[:, chunk(group, size), :]
    if size % 16:
        return block.astype(f32).reshape(features * size, width).astype(bf16)
    return block.reshape(features * size, width)


def store_group(ref, group, size, rows):
    features, _, width = ref.shape
    if size % 16:
        block = rows.astype(f32).reshape(features, size, width).astype(bf16)
    else:
        block = rows.reshape(features, size, width)
    ref[:, chunk(group, size), :] = block


def feature_forward(size, h_ref, w_ref, qcode_ref, kcode_ref, a_ref, qkv_ref, ctx_ref, ext_ref):
    _, samples, width = h_ref.shape

    def step(group, carry):
        hidden = load_group(h_ref, group, size)
        for member in range(3):
            out = mm(hidden, w_ref[member]).astype(bf16)
            if member == 0:
                out = out * jnp.asarray(0.125, bf16)
            qkv_ref[group, member] = out
        code = qcode_ref[...]

        def pair_step(pair, extras):
            lanes = chunk(pair, LANES)
            context, extras = attend_pair(
                qkv_ref[group, 0, :, lanes],
                qkv_ref[group, 1, :, lanes],
                qkv_ref[group, 2, :, lanes],
                code,
                kcode_ref[...],
                pair,
                extras,
            )
            ctx_ref[group, :, lanes] = context
            return extras

        extras = lax.fori_loop(0, width // LANES, pair_step, code.astype(f32))
        ext_ref[group] = extras.astype(bf16)
        store_group(a_ref, group, size, mm(ctx_ref[group], w_ref[3]).astype(bf16))
        return carry

    lax.fori_loop(0, samples // size, step, 0)


def gelu_parts(values):
    cubic = values * values * values
    inside = 0.7978845608028654 * (values + 0.044715 * cubic)
    bent = jnp.tanh(inside)
    return bent


def dense_forward(x_ref, a_ref, gain_ref, shift_ref, up_ref, upb_ref, down_ref, downb_ref, out_ref, u_ref):
    rows_total, width = x_ref.shape
    hidden_width = up_ref.shape[1]

    def step(unit, carry):
        rows = chunk(unit, ROWS)
        x2 = x_ref[rows, :] + a_ref[rows, :].astype(f32)
        _, _, hidden = layer_norm(x2, gain_ref[2:3], shift_ref[2:3])
        hidden = hidden.astype(bf16)
        total = x2 + downb_ref[...]
        for part in range(hidden_width // 512):
            cols = slice(part * 512, part * 512 + 512)
            expanded = mm(hidden, up_ref[:, cols]) + upb_ref[:, cols]
            u_ref[rows, cols] = expanded.astype(bf16)
            active = (0.5 * expanded * (1.0 + gelu_parts(expanded))).astype(bf16)
            total = total + mm(active, down_ref[cols, :])
        out_ref[rows, :] = total
        return carry

    lax.fori_loop(0, rows_total // ROWS, step, 0)


def dense_backward(g_ref, x1_ref, a_ref, u_ref, gain_ref, shift_ref, up_ref, down_ref, out_ref, send_ref, dup_ref, ddown_ref, dupb_ref, ddownb_ref, dgs_ref, active_ref, ugrad_ref, hidden_ref, rowgrad_ref):
    rows_total, width = g_ref.shape
    hidden_width = up_ref.shape[1]
    dupb_ref[...] = jnp.zeros_like(dupb_ref)
    ddownb_ref[...] = jnp.zeros_like(ddownb_ref)
    dgs_ref[...] = jnp.zeros_like(dgs_ref)

    def step(unit, carry):
        rows = chunk(unit, ROWS)
        grad = g_ref[rows, :]
        low = grad.astype(bf16)
        rowgrad_ref[rows, :] = low
        ddownb_ref[...] += jnp.sum(low.astype(f32), axis=0, keepdims=True)
        hidden_grad = None
        for part in range(hidden_width // 512):
            cols = slice(part * 512, part * 512 + 512)
            active_grad = mm(low, down_ref[cols, :], NT).astype(bf16).astype(f32)
            u = u_ref[rows, cols].astype(f32)
            bent = gelu_parts(u)
            slope = 0.5 * (1.0 + bent) + u * (1.0 - bent * bent) * (
                0.3989422804014327 + 0.05351611220146811 * u * u
            )
            active_ref[rows, cols] = (0.5 * u * (1.0 + bent)).astype(bf16)
            ugrad = (active_grad * slope).astype(bf16)
            ugrad_ref[rows, cols] = ugrad
            dupb_ref[:, cols] += jnp.sum(ugrad.astype(f32), axis=0, keepdims=True)
            part_grad = mm(ugrad, up_ref[:, cols], NT)
            hidden_grad = part_grad if hidden_grad is None else hidden_grad + part_grad
        x2 = x1_ref[rows, :] + a_ref[rows, :].astype(f32)
        _, _, hidden = layer_norm(x2, gain_ref[2:3], shift_ref[2:3])
        hidden_ref[rows, :] = hidden.astype(bf16)
        norm_grad, gain_part, shift_part = layer_norm_back(
            hidden_grad.astype(bf16).astype(f32), x2, gain_ref[2:3]
        )
        dgs_ref[0:1] += gain_part
        dgs_ref[1:2] += shift_part
        grad = grad + norm_grad
        out_ref[rows, :] = grad
        send_ref[rows, :] = grad.astype(bf16)
        return carry

    lax.fori_loop(0, rows_total // ROWS, step, 0)

    def weights(part, carry):
        cols = chunk(part, 512)
        dup_ref[cols, :] = mm(ugrad_ref[:, cols], hidden_ref[...], TN).astype(bf16)
        ddown_ref[cols, :] = mm(active_ref[:, cols], rowgrad_ref[...], TN).astype(bf16)
        return carry

    lax.fori_loop(0, hidden_width // 512, weights, 0)


def feature_backward(size, da_ref, h_ref, w_ref, kcode_ref, qkv_ref, ctx_ref, ext_ref, dh_ref, dw_ref, dqkv_ref, hidden_ref, dao_ref, dc_ref):
    _, samples, width = h_ref.shape
    groups = samples // size

    def step(group, carry):
        hidden_ref[group] = load_group(h_ref, group, size)
        dao = load_group(da_ref, group, size)
        dao_ref[group] = dao
        context_grad = mm(dao, w_ref[3], NT).astype(bf16)
        dc_ref[...] = context_grad
        grad_extra = delta_extra(ctx_ref[group], context_grad)

        def pair_step(pair, inner):
            lanes = chunk(pair, LANES)
            query_grad, key_grad, value_grad = attend_pair_back(
                qkv_ref[group, 0, :, lanes],
                qkv_ref[group, 1, :, lanes],
                qkv_ref[group, 2, :, lanes],
                dc_ref[:, lanes],
                ext_ref[group],
                grad_extra,
                kcode_ref[...],
                pair,
            )
            dqkv_ref[0, group, :, lanes] = (query_grad * 0.125).astype(bf16)
            dqkv_ref[1, group, :, lanes] = key_grad.astype(bf16)
            dqkv_ref[2, group, :, lanes] = value_grad.astype(bf16)
            return inner

        lax.fori_loop(0, width // LANES, pair_step, 0)
        total = mm(dqkv_ref[0, group], w_ref[0], NT)
        total = total + mm(dqkv_ref[1, group], w_ref[1], NT)
        total = total + mm(dqkv_ref[2, group], w_ref[2], NT)
        store_group(dh_ref, group, size, total.astype(bf16))
        return carry

    lax.fori_loop(0, groups, step, 0)

    def weights(member, carry):
        total = None
        for group in range(groups):
            part = mm(hidden_ref[group], dqkv_ref[member, group], TN)
            total = part if total is None else total + part
        dw_ref[member] = total.astype(bf16)
        return carry

    lax.fori_loop(0, 3, weights, 0)
    total = None
    for group in range(groups):
        part = mm(ctx_ref[group], dao_ref[group], TN)
        total = part if total is None else total + part
    dw_ref[3] = total.astype(bf16)


def sample_backward(g_ref, dh_ref, x1_ref, x_ref, gain_ref, shift_ref, w_ref, kcode_ref, qkv_ref, ctx_ref, ext_ref, out_ref, dw_ref, dgs_ref, dqkv_ref, hidden_ref, low_ref, dc_ref, gext_ref, kacc_ref, vacc_ref):
    features, samples, width = x_ref.shape
    steps = samples // ROWS
    dgs_ref[...] = jnp.zeros_like(dgs_ref)

    def enter(unit, carry):
        f, rows = unit // steps, chunk(unit % steps, ROWS)
        norm_grad, gain_part, shift_part = layer_norm_back(
            dh_ref[f, rows, :].astype(f32), x1_ref[f, rows, :], gain_ref[1:2]
        )
        dgs_ref[1, 0:1] += gain_part
        dgs_ref[1, 1:2] += shift_part
        grad = g_ref[f, rows, :] + norm_grad
        out_ref[f, rows, :] = grad
        low = grad.astype(bf16)
        low_ref[f, rows, :] = low
        context_grad = mm(low, w_ref[3], NT).astype(bf16)
        dc_ref[f, rows, :] = context_grad
        gext_ref[f, rows, :] = delta_extra(ctx_ref[f, rows, :], context_grad)
        return carry

    lax.fori_loop(0, features * steps, enter, 0)

    def attend(unit, carry):
        f, pair = unit // (width // LANES), unit % (width // LANES)
        lanes = chunk(pair, LANES)

        def query_step(step, inner):
            rows = chunk(step, ROWS)
            query_grad, key_grad, value_grad = attend_pair_back(
                qkv_ref[0, f, rows, lanes],
                qkv_ref[1, f, :, lanes],
                qkv_ref[2, f, :, lanes],
                dc_ref[f, rows, lanes],
                ext_ref[f, rows, :],
                gext_ref[f, rows, :],
                kcode_ref[...],
                pair,
            )
            dqkv_ref[0, f, rows, lanes] = (query_grad * 0.125).astype(bf16)
            first = step == 0
            kacc_ref[...] = jnp.where(first, 0.0, kacc_ref[...]) + key_grad
            vacc_ref[...] = jnp.where(first, 0.0, vacc_ref[...]) + value_grad
            return inner

        lax.fori_loop(0, steps, query_step, 0)
        dqkv_ref[1, f, :, lanes] = kacc_ref[...].astype(bf16)
        dqkv_ref[2, f, :, lanes] = vacc_ref[...].astype(bf16)
        return carry

    kacc_ref[...] = jnp.zeros_like(kacc_ref)
    vacc_ref[...] = jnp.zeros_like(vacc_ref)
    lax.fori_loop(0, features * (width // LANES), attend, 0)

    def leave(unit, carry):
        f, rows = unit // steps, chunk(unit % steps, ROWS)
        total = mm(dqkv_ref[0, f, rows, :], w_ref[0], NT)
        total = total + mm(dqkv_ref[1, f, rows, :], w_ref[1], NT)
        total = total + mm(dqkv_ref[2, f, rows, :], w_ref[2], NT)
        x = x_ref[f, rows, :]
        _, _, hidden = layer_norm(x, gain_ref[0:1], shift_ref[0:1])
        hidden_ref[f, rows, :] = hidden.astype(bf16)
        norm_grad, gain_part, shift_part = layer_norm_back(
            total.astype(bf16).astype(f32), x, gain_ref[0:1]
        )
        dgs_ref[0, 0:1] += gain_part
        dgs_ref[0, 1:2] += shift_part
        out_ref[f, rows, :] += norm_grad
        return carry

    lax.fori_loop(0, features * steps, leave, 0)

    def weights(member, carry):
        total = None
        for f in range(features):
            part = mm(hidden_ref[f], dqkv_ref[member, f], TN)
            total = part if total is None else total + part
        dw_ref[member] = total.astype(bf16)
        return carry

    lax.fori_loop(0, 3, weights, 0)
    total = None
    for f in range(features):
        part = mm(ctx_ref[f], low_ref[f], TN)
        total = part if total is None else total + part
    dw_ref[3] = total.astype(bf16)


def call(body, name, outs, scratch, *operands):
    spec = pl.BlockSpec(memory_space=pltpu.VMEM)
    return pl.pallas_call(
        body,
        name=name,
        out_shape=[jax.ShapeDtypeStruct(shape, kind) for shape, kind in outs],
        in_specs=[spec] * len(operands),
        out_specs=[spec] * len(outs),
        scratch_shapes=[pltpu.VMEM(shape, kind) for shape, kind in scratch],
        compiler_params=pltpu.CompilerParams(vmem_limit_bytes=56 << 20),
    )(*operands)


MESH = pl.DeviceIdType.MESH


def remote(source, target, send_sem, recv_sem, device):
    return pltpu.make_async_remote_copy(
        src_ref=source,
        dst_ref=target,
        send_sem=send_sem,
        recv_sem=recv_sem,
        device_id=device,
        device_id_type=MESH,
    )


def sum_partners(task_devices, feature_devices):
    task, place = lax.axis_index("task"), lax.axis_index("feat")
    chip, core = place // 2, lax.rem(place, 2)
    chips = feature_devices // 2
    pair = [{"feat": place + 1 - 2 * core}]
    tasks = [{"task": lax.rem(task + step, task_devices)} for step in range(1, task_devices)]
    line = [{"feat": 2 * lax.rem(chip + step, chips) + core} for step in range(1, chips)]
    return task, chip, core, pair, tasks, line


def greet(devices):
    barrier = pltpu.get_barrier_semaphore()
    for device in devices:
        pl.semaphore_signal(barrier, inc=1, device_id=device, device_id_type=MESH)


def met(count):
    pl.semaphore_wait(pltpu.get_barrier_semaphore(), count)


def sum_tail(pieces, task_devices, feature_devices, *refs):
    chips = feature_devices // 2
    inputs, small_ref = refs[:pieces], refs[pieces]
    outs, small_out = refs[pieces + 1 : 2 * pieces + 1], refs[2 * pieces + 1]
    own, first, summed, second, third_in, third, sends, recvs, loads, small_got, small_sends, small_recvs = refs[2 * pieces + 2 :]
    task, chip, core, pair, tasks, line = sum_partners(task_devices, feature_devices)
    greet(pair + tasks + line)
    own_loads = [
        pltpu.make_async_copy(inputs[p].at[:, :, core], own.at[p], loads.at[p]) for p in range(pieces)
    ]
    for load in own_loads:
        load.start()
    met(len(pair) + len(tasks) + len(line))

    started = []
    for p in range(pieces):
        copy = remote(inputs[p].at[:, :, 1 - core], first.at[p], sends.at[p, 0], recvs.at[p, 0], pair[0])
        copy.start()
        started.append([copy])
    small_slot = [0]

    def small_exchange(values, devices, index, base):
        copies = []
        for k, device in enumerate(devices):
            copy = remote(values, small_got.at[base + index], small_sends.at[base + k], small_recvs.at[base + k], device)
            copy.start()
            copies.append(copy)
        return copies

    def small_finish(copies, count, base):
        for copy in copies:
            copy.wait()
        total = small_got[base]
        for k in range(1, count):
            total = total + small_got[base + k]
        return total

    small_got[core] = small_ref[...]
    small_copies = small_exchange(small_got.at[core], pair, core, 0)
    for p in range(pieces):
        own_loads[p].wait()
        for copy in started[p]:
            copy.wait()

        def add_core(index, carry, p=p):
            t, z = index // chips, lax.rem(index, chips)
            summed[p, t, z] = (own[p, t, z].astype(f32) + first[p, t, z].astype(f32)).astype(bf16)
            return carry

        lax.fori_loop(0, task_devices * chips, add_core, 0)
        started[p] = []
        for k, device in enumerate(tasks):
            other = lax.rem(task + k + 1, task_devices)
            copy = remote(summed.at[p, other], second.at[p, k], sends.at[p, 1 + k], recvs.at[p, 1 + k], device)
            copy.start()
            started[p].append(copy)
    total = small_finish(small_copies, 2, 0)
    small_got[2 + task] = total
    small_copies = small_exchange(small_got.at[2 + task], tasks, task, 2)
    for p in range(pieces):
        for copy in started[p]:
            copy.wait()

        def add_tasks(z, carry, p=p):
            total = summed[p, task, z].astype(f32)
            for k in range(task_devices - 1):
                total = total + second[p, k, z].astype(f32)
            third_in[p, z] = total.astype(bf16)
            return carry

        lax.fori_loop(0, chips, add_tasks, 0)
        started[p] = []
        for k, device in enumerate(line):
            other = lax.rem(chip + k + 1, chips)
            slot = task_devices + k
            copy = remote(third_in.at[p, other], third.at[p, k], sends.at[p, slot], recvs.at[p, slot], device)
            copy.start()
            started[p].append(copy)
    total = small_finish(small_copies, task_devices, 2)
    base = 2 + task_devices
    small_got[base + chip] = total
    small_copies = small_exchange(small_got.at[base + chip], line, chip, base)
    for p in range(pieces):
        for copy in started[p]:
            copy.wait()
        total = third_in[p, chip].astype(f32)
        for k in range(chips - 1):
            total = total + third[p, k].astype(f32)
        outs[p][...] = total
    small_out[...] = small_finish(small_copies, chips, base)


def sum_everywhere(pieces, small, task_devices, feature_devices):
    chips = feature_devices // 2
    rows, width = pieces[0].shape
    share = rows // (task_devices * feature_devices)
    blocks = [piece.reshape(task_devices, chips, 2, share, width) for piece in pieces]
    count = len(pieces)
    copies = task_devices + chips - 1
    small_copies = 2 + task_devices + chips
    vmem, anywhere = pl.BlockSpec(memory_space=pltpu.VMEM), pl.BlockSpec(memory_space=pl.ANY)
    return pl.pallas_call(
        functools.partial(sum_tail, count, task_devices, feature_devices),
        name="sum_tail",
        out_shape=[jax.ShapeDtypeStruct((share, width), f32)] * count
        + [jax.ShapeDtypeStruct(small.shape, f32)],
        in_specs=[anywhere] * count + [vmem],
        out_specs=[vmem] * (count + 1),
        scratch_shapes=[
            pltpu.VMEM((count, task_devices, chips, share, width), bf16),
            pltpu.VMEM((count, task_devices, chips, share, width), bf16),
            pltpu.VMEM((count, task_devices, chips, share, width), bf16),
            pltpu.VMEM((count, task_devices - 1, chips, share, width), bf16),
            pltpu.VMEM((count, chips, share, width), bf16),
            pltpu.VMEM((count, chips - 1, share, width), bf16),
            pltpu.SemaphoreType.DMA((count, copies)),
            pltpu.SemaphoreType.DMA((count, copies)),
            pltpu.SemaphoreType.DMA((count,)),
            pltpu.VMEM((small_copies,) + small.shape, f32),
            pltpu.SemaphoreType.DMA((small_copies,)),
            pltpu.SemaphoreType.DMA((small_copies,)),
        ],
        compiler_params=pltpu.CompilerParams(
            vmem_limit_bytes=56 << 20, collective_id=0, has_side_effects=True
        ),
    )(*blocks, small)


SIZE = 16


class Place:
    def __init__(self, task_devices, feature_devices):
        self.tasks, self.places = task_devices, feature_devices
        self.chips = feature_devices // 2
        self.task, self.place = lax.axis_index("task"), lax.axis_index("feat")
        self.chip, self.core = self.place // 2, lax.rem(self.place, 2)
        self.far, self.near = self.chip // 2, lax.rem(self.chip, 2)
        self.y, self.x = self.task // 2, lax.rem(self.task, 2)
        self.x_task = {"task": self.task + 1 - 2 * self.x}
        self.y_task = {"task": self.task + 2 - 4 * self.y}
        self.other_core = {"feat": self.place + 1 - 2 * self.core}
        self.near_chip = {"feat": self.place + 2 - 4 * self.near}
        self.far_chip = {"feat": self.place + 4 - 8 * self.far}

    def ring(self, step):
        return lax.rem(self.place + step, self.places)

    def task_partner(self, step):
        return lax.rem(self.task + step, self.tasks)

    def greet(self):
        barrier = pltpu.get_barrier_semaphore()
        for step in range(1, self.places):
            pl.semaphore_signal(barrier, inc=1, device_id={"feat": self.ring(step)}, device_id_type=MESH)
        for step in range(1, self.tasks):
            pl.semaphore_signal(barrier, inc=1, device_id={"task": self.task_partner(step)}, device_id_type=MESH)

    def met(self):
        pl.semaphore_wait(pltpu.get_barrier_semaphore(), self.places - 1 + self.tasks - 1)


class SumStep:
    def __init__(self, step, place, source, own, got, sends, recvs, load):
        self.step = step
        y, x, far, near, core = place.y, place.x, place.far, place.near, place.core
        if step == 1:
            self.mine = [source.at[:, :, :, :, core]]
            parts = [(source.at[:, :, :, :, 1 - core], got, place.other_core)]
        elif step == 2:
            self.mine = [source.at[y, x]]
            parts = []
            for k in range(1, place.tasks):
                other = place.task_partner(k)
                parts.append((source.at[other // 2, lax.rem(other, 2)], got.at[k - 1], {"task": other}))
        elif step == 6:
            self.mine = [source.at[:, x, 0], source.at[y, :, 1]]
            parts = [
                (source.at[:, 1 - x, 0], got.at[0], place.x_task),
                (source.at[1 - y, :, 1], got.at[1], place.y_task),
            ]
        elif step == 7:
            self.mine = [source.at[0, y], source.at[1, x]]
            parts = [
                (source.at[0, 1 - y], got.at[0], place.y_task),
                (source.at[1, 1 - x], got.at[1], place.x_task),
            ]
        elif step == 3:
            self.mine = [source.at[:, near]]
            parts = [(source.at[:, 1 - near], got, place.near_chip)]
        elif step == 4:
            self.mine = [source.at[far]]
            parts = [(source.at[1 - far], got, place.far_chip)]
        else:
            self.mine = [source.at[far, near]]
            parts = []
            for k in range(1, place.chips):
                other = lax.rem(place.chip + k, place.chips)
                parts.append(
                    (source.at[other // 2, lax.rem(other, 2)], got.at[k - 1], {"feat": 2 * other + core})
                )
        self.copies = [
            remote(part, target, sends.at[k], recvs.at[k], device) for k, (part, target, device) in enumerate(parts)
        ]
        self.loads = []
        if own is not None:
            kept = [own] if len(self.mine) == 1 else [own.at[half] for half in range(2)]
            self.loads = [
                pltpu.make_async_copy(part, target, load.at[half])
                for half, (part, target) in enumerate(zip(self.mine, kept))
            ]
            self.mine = kept
        self.got = got

    def start(self):
        for copy in self.copies:
            copy.start()
        for load in self.loads:
            load.start()

    def finish(self, out):
        for load in self.loads:
            load.wait()
        for copy in self.copies:
            copy.wait()
        own, got = self.mine[0], self.got
        if self.step == 1:

            def add_core(index, carry):
                y, x, far = index // 4, lax.rem(index // 2, 2), lax.rem(index, 2)
                out[y, x, far] = (own[y, x, far].astype(f32) + got[y, x, far].astype(f32)).astype(bf16)
                return carry

            lax.fori_loop(0, 8, add_core, 0)
        elif self.step in (2, 5):
            total = own[...].astype(f32)
            for k in range(got.shape[0]):
                total = total + got[k].astype(f32)
            out[...] = total.astype(out.dtype)
        elif self.step in (6, 7):
            for half in range(2):
                out[half] = (self.mine[half][...].astype(f32) + got[half].astype(f32)).astype(bf16)
        else:
            out[...] = (own[...].astype(f32) + got[...].astype(f32)).astype(out.dtype)


def sum_shapes(step, tasks, share, width):
    block = (share, width)
    if step == 1:
        whole = (2, 2, 2, 2) + block
        return whole, whole, whole, bf16, 1
    if step == 2:
        return (2, 2) + block, (tasks - 1, 2, 2) + block, (2, 2) + block, bf16, tasks - 1
    if step == 6:
        return None, (2, 2, 2) + block, (2, 2, 2) + block, bf16, 2
    if step == 7:
        return (2, 2) + block, (2, 2) + block, (2, 2) + block, bf16, 2
    if step == 3:
        return (2,) + block, (2,) + block, (2,) + block, bf16, 1
    if step == 4:
        return block, block, block, f32, 1
    return block, (3,) + block, block, f32, 3


class Chain:
    def __init__(self, place, steps, points, bufs, source, out):
        self.place, self.steps, self.points, self.bufs, self.out = place, steps, points, bufs, out
        self.at, self.running = 0, False
        self.first = None
        if len(points) > len(steps):
            self.first, self.points = points[0], points[1:]
        self.actions = [None if source is None else self.make(0, source)]
        self.actions += [self.make(at, bufs[at - 1][2]) for at in range(1, len(steps))]

    def make(self, at, source):
        own, got, _, sends, recvs, local_sem = self.bufs[at]
        return SumStep(self.steps[at], self.place, source, own, got, sends, recvs, local_sem)

    def begin(self, source=None):
        if source is not None:
            self.actions[0] = self.make(0, source)
        self.actions[0].start()
        self.running = True

    def reached(self, point):
        if self.first is not None and point == self.first:
            self.begin()
            return
        if not self.running or self.points[self.at] != point:
            return
        self.actions[self.at].finish(self.bufs[self.at][2])
        self.at += 1
        if self.at < len(self.steps):
            self.actions[self.at].start()
            return
        self.running = False
        if self.out is not None:
            self.flush().start()

    def flush(self):
        return pltpu.make_async_copy(self.bufs[-1][2], self.out, self.bufs[-1][5].at[2])


class Box:
    def __init__(self, place, bufs, loads, outs, out_bufs, flush_sem, chains):
        self.place, self.bufs, self.loads = place, bufs, loads
        self.outs, self.out_bufs, self.flush_sem = outs, out_bufs, flush_sem
        self.chains = chains
        self.waited, self.flushed = set(), []

    def start(self, *indices):
        for index in indices:
            for copy in self.loads[index]:
                copy.start()

    def use(self, *indices):
        found = []
        for index in indices:
            if index not in self.waited:
                self.waited.add(index)
                for copy in self.loads[index]:
                    copy.wait()
            found.append(self.bufs[index])
        return found if len(found) > 1 else found[0]

    def part(self, index, part):
        self.waited.add(index)
        self.loads[index].one(part).wait()

    def out(self, *indices):
        found = [self.out_bufs[index] for index in indices]
        return found if len(found) > 1 else found[0]

    def copy_out(self, index, part, view):
        source, target = self.out_bufs[index], self.outs[index]
        if view is not None:
            source, target = view(source, part), view(target, part)
        return pltpu.make_async_copy(source, target, self.flush_sem.at[index, part])

    def flush(self, *indices):
        for index in indices:
            self.copy_out(index, 0, None).start()
            self.flushed.append((index, 0, None))

    def flush_part(self, index, part, view):
        self.copy_out(index, part, view).start()
        if (index, 0, view) not in self.flushed:
            self.flushed += [(index, at, view) for at in range(4)]

    def ready(self):
        self.place.met()
        for chain in self.chains:
            if chain.actions[0] is not None and chain.first is None:
                chain.begin()

    def point(self, name):
        for chain in self.chains:
            chain.reached(name)

    def end(self):
        for index, part, view in self.flushed:
            self.copy_out(index, part, view).wait()
        for chain in self.chains:
            if chain.out is not None:
                chain.flush().wait()


class Parts:
    def __init__(self, source, target, view, count, sem):
        self.source, self.target, self.view, self.count, self.sem = source, target, view, count, sem

    def one(self, part):
        if self.view is None:
            return pltpu.make_async_copy(self.source, self.target, self.sem.at[0])
        return pltpu.make_async_copy(self.view(self.source, part), self.view(self.target, part), self.sem.at[part])

    def __iter__(self):
        return iter([self.one(part) for part in range(self.count)])


def fused(body, name, place_sizes, ins, outs, scratch, sums, share_shape, identity):
    tasks, places = place_sizes
    anywhere = pl.BlockSpec(memory_space=pltpu.HBM)
    scalar = pl.BlockSpec(memory_space=pltpu.SMEM)
    buffers = []
    ins = [tuple(item) + (None, 1) if len(item) == 2 else item for item in ins]
    for array, layer, _, _ in ins:
        if layer not in ("scalar", "raw"):
            depth = 0 if layer is None else len(layer) if isinstance(layer, tuple) else 1
            buffers.append(pltpu.VMEM(array.shape[depth:], array.dtype))
    out_buffers = [pltpu.VMEM(shape, kind) for shape, kind in outs]
    sum_results, sum_scratch, sum_arrays = [], [], []
    chain_layout = []
    for steps, _, array, goes_out in sums:
        share, width = share_shape if array is None else array.shape[-2:]
        for at, step in enumerate(steps):
            own, got, result, kind, copies = sum_shapes(step, tasks, share, width)
            loaded = at == 0 and array is not None
            chain_layout.append(loaded)
            sum_scratch += [pltpu.VMEM(own, bf16)] if loaded else []
            sum_scratch += [
                pltpu.VMEM(got, bf16),
                pltpu.VMEM(result, kind),
                pltpu.SemaphoreType.DMA((copies,)),
                pltpu.SemaphoreType.DMA((copies,)),
                pltpu.SemaphoreType.DMA((3,)),
            ]
        if goes_out:
            sum_results.append(jax.ShapeDtypeStruct(result, kind))
        if array is not None:
            sum_arrays.append(array)
    flat_scratch = []
    for item in scratch:
        flat_scratch += list(item) if isinstance(item, tuple) else [item]
    everything = buffers + out_buffers + flat_scratch + sum_scratch
    def kernel(*refs):
        rest = list(refs)

        def pop(count):
            taken = rest[:count]
            del rest[:count]
            return taken

        in_refs, sum_refs = pop(len(ins)), pop(len(sum_arrays))
        out_refs, sum_outs = pop(len(outs)), pop(len(sum_results))
        flat_in = pop(len(buffers))
        out_bufs = pop(len(out_buffers))
        user = [tuple(pop(len(item))) if isinstance(item, tuple) else pop(1)[0] for item in scratch]
        layout = list(chain_layout)
        chain_bufs = [
            [pop(6) if layout.pop(0) else [None] + pop(5) for _ in steps] for steps, _, _, _ in sums
        ]
        load_sem, flush_sem = pop(2)
        place = Place(tasks, places)
        loads, bufs = [], []
        for index, (array, layer, view, count) in enumerate(ins):
            if layer in ("scalar", "raw"):
                loads.append([])
                bufs.append(in_refs[index])
                continue
            bufs.append(flat_in.pop(0))
            source = in_refs[index]
            if layer is not None:
                source = source.at[layer]
            loads.append(Parts(source, bufs[-1], view, count, load_sem.at[index]))
        place.greet()
        chains = []
        for (steps, points, array, goes_out), chain_buf in zip(sums, chain_bufs):
            source = None if array is None else sum_refs.pop(0)
            chains.append(Chain(place, steps, points, chain_buf, source, sum_outs.pop(0) if goes_out else None))
        box = Box(place, bufs, loads, out_refs, out_bufs, flush_sem, chains)
        body(box, *user)
        box.end()

    return pl.pallas_call(
        kernel,
        name=name,
        out_shape=[jax.ShapeDtypeStruct(shape, kind) for shape, kind in outs] + sum_results,
        in_specs=[scalar if layer == "scalar" else anywhere for _, layer, _, _ in ins] + [anywhere] * len(sum_arrays),
        out_specs=[anywhere] * (len(outs) + len(sum_results)),
        scratch_shapes=everything
        + [pltpu.SemaphoreType.DMA((len(ins), 8)), pltpu.SemaphoreType.DMA((len(outs), 4))],
        compiler_params=pltpu.CompilerParams(
            vmem_limit_bytes=63 << 20, collective_id=identity, has_side_effects=True
        ),
    )(*[item[0] for item in ins], *sum_arrays)


def cross(ref, unit):
    block = ref[:, :, chunk(unit, SIZE), :]
    return block.reshape(block.shape[0] * block.shape[1] * SIZE, block.shape[3])


def put_cross(ref, unit, rows):
    first, second, _, width = ref.shape
    ref[:, :, chunk(unit, SIZE), :] = rows.reshape(first, second, SIZE, width)


def cross_view(ref, unit):
    return ref.at[:, :, chunk(unit, SIZE), :]


def first_view(ref, unit):
    return ref.at[unit]


def last_view(ref, unit):
    return ref.at[(slice(None),) * (len(ref.shape) - 1) + (chunk(unit, LANES),)]


def own_rows(ref, f, unit, size, lanes=slice(None)):
    block = ref[f, :, chunk(unit, size), lanes]
    return block.reshape(block.shape[0] * size, block.shape[2])


def block_rows(ref, f, unit, per, lanes=slice(None)):
    block = ref[f, chunk(unit, per), :, lanes]
    return block.reshape(per * block.shape[1], block.shape[2])


def all_rows(ref, f, lanes=slice(None)):
    block = ref[f, :, :, lanes]
    return block.reshape(block.shape[0] * block.shape[1], block.shape[2])


def pair_lanes(pair):
    return slice(pair * LANES, pair * LANES + LANES)


def fill_sample_codes(size, query_ref, key_ref):
    if query_ref is not None:
        lanes = lax.broadcasted_iota(jnp.int32, query_ref.shape, 1)
        query_ref[...] = jnp.where(lanes == CODE_LANE, 1.0, 0.0).astype(bf16)
    lanes = lax.broadcasted_iota(jnp.int32, key_ref.shape, 1)
    rows = lax.broadcasted_iota(jnp.int32, key_ref.shape, 0)
    key_ref[...] = jnp.where((lanes == CODE_LANE) & (rows >= size), masked_score, 0.0).astype(bf16)


def fill_feature_codes(count, query_ref, key_ref):
    lanes = lax.broadcasted_iota(jnp.int32, key_ref.shape, 1) - CODE_LANE
    rows = lax.broadcasted_iota(jnp.int32, key_ref.shape, 0)
    own = lanes == (rows & (SIZE - 1))
    inside = (lanes >= 0) & (lanes < SIZE)
    if query_ref is not None:
        query_ref[...] = jnp.where(own, 1.0, 0.0).astype(bf16)
    live = rows < count * SIZE
    key_ref[...] = jnp.where(inside & ~(own & live), masked_score, 0.0).astype(bf16)


def forward_layer(layer, box, sq_ref, sk_ref, fq_ref, fk_ref, h2_ref, swapped_ref, a_ref, back_ref, active_ref, sends, recvs, self_sem, back_sends, back_recvs):
    place = box.place
    x1_ref, qkv_ref, ctx_ref, ext_ref = box.out(0, 1, 2, 3)
    hidden_ref, fqkv_ref, fctx_ref, fext_ref, x2_ref, x3_ref, u_ref, h1_ref = box.out(4, 5, 6, 7, 8, 9, 10, 11)
    box.start(3, 4, 2, 5)
    size_ref, count_ref = box.use(0, 1)
    fill_sample_codes(size_ref[0], sq_ref, sk_ref)
    fill_feature_codes(count_ref[0], fq_ref, fk_ref)
    gain_ref, shift_ref, w_ref = box.use(3, 4, 5)
    x_ref = box.bufs[2]
    box.start(6, 7, 8, 9, 10)
    features, blocks, own, width = x_ref.shape
    per = ROWS // own
    steps = blocks // per
    size = ROWS // blocks
    units = own // size
    pairs = width // LANES

    def gain(index):
        return gain_ref[index, layer : layer + 1, :], shift_ref[index, layer : layer + 1, :]

    def project(f):
        box.part(2, f)

        def rows(part, carry):
            _, _, hidden = layer_norm(block_rows(x_ref, f, part, per), *gain(0))
            hidden = hidden.astype(bf16)
            h1_ref[f, chunk(part, per), :, :] = hidden.reshape(per, own, width)
            for member in range(3):
                out = mm(hidden, w_ref[member]).astype(bf16)
                if member == 0:
                    out = out * jnp.asarray(0.125, bf16)
                qkv_ref[member, f, chunk(part, per), :, :] = out.reshape(per, own, width)
            return carry

        lax.fori_loop(0, steps, rows, 0)

    def copies(unit):
        part, f = unit // features, lax.rem(unit, features)
        found = [
            remote(
                h2_ref.at[f, place.ring(k), chunk(part, size), :],
                swapped_ref.at[place.place, f, chunk(part, size), :],
                sends.at[unit, k - 1],
                recvs.at[unit, k - 1],
                {"feat": place.ring(k)},
            )
            for k in range(1, place.places)
        ]
        keep = pltpu.make_async_copy(
            h2_ref.at[f, place.place, chunk(part, size), :],
            swapped_ref.at[place.place, f, chunk(part, size), :],
            self_sem.at[unit],
        )
        return found, keep

    def attend(unit, carry):
        part, f = unit // features, lax.rem(unit, features)

        @pl.when(unit < features)
        def _():
            project(unit)

        code = sq_ref[...]
        extras = code.astype(f32)
        for pair in range(pairs):
            lanes = pair_lanes(pair)
            context, extras = attend_pair(
                own_rows(qkv_ref.at[0], f, part, size, lanes),
                all_rows(qkv_ref.at[1], f, lanes),
                all_rows(qkv_ref.at[2], f, lanes),
                code,
                sk_ref[...],
                pair,
                extras,
            )
            ctx_ref[f, :, chunk(part, size), lanes] = context.reshape(blocks, size, LANES)
        ext_ref[f, :, chunk(part, size), :] = extras.astype(bf16).reshape(blocks, size, LANES)
        x1 = own_rows(x_ref, f, part, size) + mm(own_rows(ctx_ref, f, part, size), w_ref[3])
        x1_ref[f, :, chunk(part, size), :] = x1.reshape(blocks, size, width)
        _, _, hidden = layer_norm(x1, *gain(1))
        h2_ref[f, :, chunk(part, size), :] = hidden.astype(bf16).reshape(blocks, size, width)

        @pl.when(unit == 0)
        def _():
            box.ready()

        found, keep = copies(unit)
        for copy in found:
            copy.start()
        keep.start()
        return carry

    lax.fori_loop(0, features * units, attend, 0)
    box.flush(0, 1, 2, 3, 11)
    fw_ref = box.use(6)
    groups = own // SIZE
    shared = size // SIZE

    def back_copies(group):
        return [
            remote(
                a_ref.at[place.ring(k), :, chunk(group, SIZE), :],
                back_ref.at[:, place.place, chunk(group, SIZE), :],
                back_sends.at[group, k - 1],
                back_recvs.at[group, k - 1],
                {"feat": place.ring(k)},
            )
            for k in range(1, place.places)
        ]

    def feature(group, carry):
        @pl.when(lax.rem(group, shared) == 0)
        def _():
            for f in range(features):
                found, keep = copies((group // shared) * features + f)
                for copy in found:
                    copy.wait_recv()
                keep.wait()

        hidden = cross(swapped_ref, group)
        hidden_ref[group] = hidden
        for member in range(3):
            out = mm(hidden, fw_ref[member]).astype(bf16)
            if member == 0:
                out = out * jnp.asarray(0.125, bf16)
            fqkv_ref[group, member] = out
        code = fq_ref[...]
        extras = code.astype(f32)
        for pair in range(pairs):
            lanes = pair_lanes(pair)
            context, extras = attend_pair(
                fqkv_ref[group, 0, :, lanes],
                fqkv_ref[group, 1, :, lanes],
                fqkv_ref[group, 2, :, lanes],
                code,
                fk_ref[...],
                pair,
                extras,
            )
            fctx_ref[group, :, lanes] = context
        fext_ref[group] = extras.astype(bf16)
        put_cross(a_ref, group, mm(fctx_ref[group], fw_ref[3]).astype(bf16))
        for copy in back_copies(group):
            copy.start()
        back_ref[:, place.place, chunk(group, SIZE), :] = a_ref[place.place, :, chunk(group, SIZE), :]
        return carry

    lax.fori_loop(0, groups, feature, 0)
    box.flush(4, 5, 6, 7)
    up_ref, upb_ref, down_ref, downb_ref = box.use(7, 8, 9, 10)
    hidden_width = up_ref.shape[1]

    def dense(group, carry):
        for copy in back_copies(group):
            copy.wait_recv()
        x2 = cross(x1_ref, group) + cross(back_ref, group).astype(f32)
        put_cross(x2_ref, group, x2)
        _, _, hidden = layer_norm(x2, *gain(2))
        hidden = hidden.astype(bf16)
        for part in range(hidden_width // 512):
            cols = slice(part * 512, part * 512 + 512)
            expanded = mm(hidden, up_ref[:, cols]) + upb_ref[layer : layer + 1, cols]
            u_ref[group, :, cols] = expanded.astype(bf16)
            active_ref[:, cols] = (0.5 * expanded * (1.0 + gelu_parts(expanded))).astype(bf16)
        total = x2 + downb_ref[layer : layer + 1, :] + mm(active_ref[...], down_ref[...])
        put_cross(x3_ref, group, total)
        box.flush_part(8, group, cross_view)
        box.flush_part(9, group, cross_view)
        box.flush_part(10, group, first_view)
        return carry

    lax.fori_loop(0, groups, dense, 0)

    def settle(unit, carry):
        for copy in copies(unit)[0]:
            copy.wait_send()
        return carry

    lax.fori_loop(0, features * units, settle, 0)

    def settle_back(group, carry):
        for copy in back_copies(group):
            copy.wait_send()
        return carry

    lax.fori_loop(0, groups, settle_back, 0)


def pieces_of(values):
    first = values.astype(bf16)
    rest = values - first.astype(f32)
    second = rest.astype(bf16)
    return first, second, (rest - second.astype(f32)).astype(bf16)


def exact(left, right, dims):
    first, second, third = pieces_of(right)
    return mm(left, first, dims) + mm(left, second, dims) + mm(left, third, dims)


def exact_left(left, right, dims):
    first, second, third = pieces_of(left)
    return mm(first, right, dims) + mm(second, right, dims) + mm(third, right, dims)


def read_out(box, raw_ref, got_ref, reading_ref, bins_ref, counted_ref, read_ref, weight_ref, sends, recvs):
    place = box.place
    shapes_ref, loss_ref, rgrad_ref, g_ref = box.out(0, 1, 2, 3)
    size_ref, count_ref = box.use(0, 1)
    box.start(2, 3, 4, 5, 6, 7)
    read_ref[...] = jnp.zeros_like(read_ref)
    label_ref, index_ref, population_ref, narrow_ref, x_ref = box.use(2, 3, 4, 5, 6)
    read_ref[0 : narrow_ref.shape[0], :] = narrow_ref[...]
    features, blocks, own, width = x_ref.shape
    samples = blocks * own
    bins = population_ref.shape[1]
    size, count = size_ref[0], count_ref[0]
    mask = (lax.broadcasted_iota(jnp.int32, (1, samples), 1) < size).astype(f32)
    task_size = jnp.zeros((1, samples), f32) + size.astype(f32)
    level = lax.broadcasted_iota(jnp.int32, (bins, bins), 0)
    diagonal = (level == lax.broadcasted_iota(jnp.int32, (bins, bins), 1)).astype(f32)
    live = [
        jnp.where(place.place * features + f < count, 1.0, 0.0) for f in range(features)
    ]
    logits = None
    for f in range(features):
        reading = x_ref[f].reshape(samples, width).astype(bf16)
        reading_ref[f] = reading
        projected = mm(reading, read_ref[...], NT)
        onehot = (lax.broadcasted_iota(jnp.int32, (bins, samples), 0) == index_ref[f : f + 1, :]).astype(f32)
        bins_ref[f] = onehot.astype(bf16)
        chosen = onehot * mask
        counted = jnp.maximum(jnp.sum(chosen, axis=1, keepdims=True), 1.0)
        counted_ref[f] = jnp.broadcast_to(counted, (bins, LANES))
        means = exact(chosen.astype(bf16), projected, NN) / counted
        weight = jnp.sum(diagonal * population_ref[f : f + 1, :].astype(f32), axis=1, keepdims=True)
        weight_ref[f] = jnp.broadcast_to(weight, (bins, LANES))
        weight = weight_ref[f]
        centre = jnp.sum(weight * means, axis=0, keepdims=True) / jnp.sum(weight, axis=0, keepdims=True)
        shapes = means - centre
        shapes_ref[f] = shapes
        part = exact_left(shapes, bins_ref[f], TN)[:SIZE] * live[f]
        logits = part if logits is None else logits + part
    box.flush(0)
    spans = range(samples // LANES)
    got_ref[place.place] = jnp.concatenate([logits[0:CLASSES, pair_lanes(span)] for span in spans], axis=0)
    box.ready()
    copies = [
        remote(
            got_ref.at[place.place],
            got_ref.at[place.place],
            sends.at[k - 1],
            recvs.at[k - 1],
            {"feat": place.ring(k)},
        )
        for k in range(1, place.places)
    ]
    for copy in copies:
        copy.start()
    og_ref = box.use(7)
    raw_ref[...] = og_ref[...].astype(f32)
    period = features * (width // LANES)
    for f in range(features):
        for block in range(width // LANES):
            rows = raw_ref[pl.ds(block * features + f, samples, stride=period), :]
            g_ref[f, :, :, pair_lanes(block)] = rows.reshape(blocks, own, LANES)
    for copy in copies:
        copy.wait()
    total = got_ref[0]
    for k in range(1, place.places):
        total = total + got_ref[k]
    rows_left = jnp.zeros((SIZE - CLASSES, LANES), f32)
    logits = jnp.concatenate(
        [
            jnp.concatenate([total[span * CLASSES : span * CLASSES + CLASSES], rows_left], axis=0)
            for span in spans
        ],
        axis=1,
    )
    class_row = lax.broadcasted_iota(jnp.int32, logits.shape, 0)
    inside = class_row < CLASSES
    peak = jnp.max(jnp.where(inside, logits, masked_score), axis=0, keepdims=True)
    weights = jnp.where(inside, jnp.exp(jnp.where(inside, logits - peak, 0.0)), 0.0)
    weight_sum = jnp.sum(weights, axis=0, keepdims=True)
    log_total = peak + jnp.log(weight_sum)
    own_class = (class_row == label_ref[...]).astype(f32)
    picked = jnp.sum(logits * own_class, axis=0, keepdims=True)
    losses = mask * (log_total - picked)
    loss_ref[...] = jnp.broadcast_to(
        jnp.sum(losses, axis=1, keepdims=True) / task_size[:, 0:1], loss_ref.shape
    )
    logit_grad = mask * (weights / weight_sum - own_class) / task_size
    pad = jnp.zeros((LANES - SIZE, samples), f32)
    total = None
    for f in range(features):
        grad_rows = jnp.concatenate([logit_grad * live[f], pad], axis=0)
        shape_grad = exact(bins_ref[f], grad_rows, NT)
        weight = weight_ref[f]
        means_grad = shape_grad - weight / jnp.sum(weight, axis=0, keepdims=True) * jnp.sum(
            shape_grad, axis=0, keepdims=True
        )
        chosen = (bins_ref[f].astype(f32) * mask).astype(bf16)
        proj_grad = exact(chosen, means_grad / counted_ref[f], TN).astype(bf16)
        part = mm(proj_grad, reading_ref[f], TN)[:SIZE]
        total = part if total is None else total + part
        back = mm(proj_grad, read_ref[...]).reshape(blocks, own, width)
        g_ref[f] = g_ref[f] + back
    rgrad_ref[...] = total
    box.flush(1, 2, 3)


def dense_feature_backward(layer, box, fk_ref, send_ref, active_ref, ugrad_ref, hidden3_ref, rowgrad_ref, dup_ref, ddown_ref, arriving_ref, dc_ref, dh_ref, back_ref, dwf_ref, sends, recvs, self_sem, back_sends, back_recvs):
    place = box.place
    g1_ref, small_ref, sdc_ref, sext_ref, slow_ref = box.out(0, 1, 2, 3, 4)
    box.start(6, 7, 1, 2, 3, 4, 5)
    small_ref[...] = jnp.zeros_like(small_ref)
    fill_feature_codes(box.use(0)[0], None, fk_ref)
    gain_ref, shift_ref, down_ref, up_ref = box.use(6, 7, 2, 4)
    g_ref, u_ref, x2_ref = box.bufs[1], box.bufs[3], box.bufs[5]
    box.start(8, 9, 10, 11, 12, 13, 14, 15)
    features, blocks, own, width = g_ref.shape
    hidden_width = up_ref.shape[1]
    groups = own // SIZE
    parts = hidden_width // 512
    pairs = width // LANES

    def copies(group):
        found = [
            remote(
                send_ref.at[:, place.ring(k), chunk(group, SIZE), :],
                arriving_ref.at[place.place, :, chunk(group, SIZE), :],
                sends.at[group, k - 1],
                recvs.at[group, k - 1],
                {"feat": place.ring(k)},
            )
            for k in range(1, place.places)
        ]
        keep = pltpu.make_async_copy(
            send_ref.at[:, place.place, chunk(group, SIZE), :],
            arriving_ref.at[place.place, :, chunk(group, SIZE), :],
            self_sem.at[group],
        )
        return found, keep

    def dense(group, carry):
        rows = chunk(group, ROWS)
        box.part(1, group)
        box.part(3, group)
        box.part(5, group)
        grad = cross(g_ref, group)
        low = grad.astype(bf16)
        rowgrad_ref[rows, :] = low
        small_ref[parts : parts + 1] += jnp.sum(low.astype(f32), axis=0, keepdims=True)
        for part in range(parts):
            cols = slice(part * 512, part * 512 + 512)
            active_grad = mm(low, down_ref[cols, :], NT).astype(bf16).astype(f32)
            u = u_ref[group, :, cols].astype(f32)
            bent = gelu_parts(u)
            slope = 0.5 * (1.0 + bent) + u * (1.0 - bent * bent) * (
                0.3989422804014327 + 0.05351611220146811 * u * u
            )
            active_ref[rows, cols] = (0.5 * u * (1.0 + bent)).astype(bf16)
            ugrad = (active_grad * slope).astype(bf16)
            ugrad_ref[rows, cols] = ugrad
            small_ref[part : part + 1] += jnp.sum(ugrad.astype(f32), axis=0, keepdims=True)
        hidden_grad = mm(ugrad_ref[rows, :], up_ref[...], NT)
        x2 = cross(x2_ref, group)
        gain, shift = gain_ref[2, layer : layer + 1, :], shift_ref[2, layer : layer + 1, :]
        _, _, hidden = layer_norm(x2, gain, shift)
        hidden3_ref[rows, :] = hidden.astype(bf16)
        norm_grad, gain_part, shift_part = layer_norm_back(hidden_grad.astype(bf16).astype(f32), x2, gain)
        small_ref[parts + 1 : parts + 2] += gain_part
        small_ref[parts + 2 : parts + 3] += shift_part
        grad = grad + norm_grad
        put_cross(g1_ref, group, grad)
        put_cross(send_ref, group, grad.astype(bf16))

        @pl.when(group == 0)
        def _():
            box.ready()

        found, keep = copies(group)
        for copy in found:
            copy.start()
        keep.start()
        return carry

    lax.fori_loop(0, groups, dense, 0)

    def up_weights(part, carry):
        cols = chunk(part, 512)
        out = mm(ugrad_ref[:, cols], hidden3_ref[...], TN)
        dup_ref[part // 2, lax.rem(part, 2)] = out.astype(bf16).reshape(dup_ref.shape[2:])
        return carry

    def down_weights(part, carry):
        cols = chunk(part, 512)
        out = mm(active_ref[:, cols], rowgrad_ref[...], TN)
        ddown_ref[part // 2, lax.rem(part, 2)] = out.astype(bf16).reshape(ddown_ref.shape[2:])
        return carry

    lax.fori_loop(0, parts, up_weights, 0)
    box.chains[0].begin(dup_ref)
    lax.fori_loop(0, parts, down_weights, 0)
    box.point("dense")
    box.chains[1].begin(ddown_ref)
    grads_ref = active_ref
    w_ref, qkv_ref, ctx_ref, ext_ref = box.use(8, 9, 10, 11)

    def back_copies(group):
        return [
            remote(
                dh_ref.at[place.ring(k), :, chunk(group, SIZE), :],
                back_ref.at[:, place.place, chunk(group, SIZE), :],
                back_sends.at[group, k - 1],
                back_recvs.at[group, k - 1],
                {"feat": place.ring(k)},
            )
            for k in range(1, place.places)
        ]

    def feature(group, carry):
        found, keep = copies(group)
        for copy in found:
            copy.wait_recv()
        keep.wait()
        rows = chunk(group, ROWS)
        dao = cross(arriving_ref, group)
        grads_ref[rows, 3 * width : 4 * width] = dao
        context_grad = mm(dao, w_ref[3], NT).astype(bf16)
        dc_ref[...] = context_grad
        grad_extra = delta_extra(ctx_ref[group], context_grad)
        for pair in range(pairs):
            lanes = pair_lanes(pair)
            query_grad, key_grad, value_grad = attend_pair_back(
                qkv_ref[group, 0, :, lanes],
                qkv_ref[group, 1, :, lanes],
                qkv_ref[group, 2, :, lanes],
                dc_ref[:, lanes],
                ext_ref[group],
                grad_extra,
                fk_ref[...],
                pair,
            )
            for member, grad in enumerate((query_grad * 0.125, key_grad, value_grad)):
                at = member * width + pair * LANES
                grads_ref[rows, at : at + LANES] = grad.astype(bf16)
        total = mm(grads_ref[rows, 0:width], w_ref[0], NT)
        total = total + mm(grads_ref[rows, width : 2 * width], w_ref[1], NT)
        total = total + mm(grads_ref[rows, 2 * width : 3 * width], w_ref[2], NT)
        put_cross(dh_ref, group, total.astype(bf16))
        for copy in back_copies(group):
            copy.start()
        back_ref[:, place.place, chunk(group, SIZE), :] = dh_ref[place.place, :, chunk(group, SIZE), :]

        for at in range(groups):

            @pl.when(group == at)
            def _(at=at):
                box.point(at)

        return carry

    lax.fori_loop(0, groups, feature, 0)
    hidden_ref = box.use(12)

    def weights(member, carry):
        hidden = hidden_ref[...].reshape(groups * ROWS, width)
        out = mm(hidden, grads_ref[:, chunk(member, width)], TN)
        dwf_ref[member // 2, lax.rem(member, 2)] = out.astype(bf16).reshape(dwf_ref.shape[2:])
        return carry

    lax.fori_loop(0, 3, weights, 0)
    context = ctx_ref[...].reshape(groups * ROWS, width)
    out = mm(context, grads_ref[:, 3 * width : 4 * width], TN)
    dwf_ref[1, 1] = out.astype(bf16).reshape(dwf_ref.shape[2:])
    box.chains[2].begin(dwf_ref)
    box.point("weights")
    x1_ref, wo_ref, sctx_ref = box.use(13, 14, 15)

    def enter(group, carry):
        for copy in back_copies(group):
            copy.wait_recv()
        norm_grad, gain_part, shift_part = layer_norm_back(
            cross(back_ref, group).astype(f32), cross(x1_ref, group), gain_ref[1, layer : layer + 1, :]
        )
        small_ref[parts + 3 : parts + 4] += gain_part
        small_ref[parts + 4 : parts + 5] += shift_part
        grad = cross(g1_ref, group) + norm_grad
        put_cross(g1_ref, group, grad)
        low = grad.astype(bf16)
        put_cross(slow_ref, group, low)
        context_grad = mm(low, wo_ref[...], NT).astype(bf16)
        put_cross(sdc_ref, group, context_grad)
        put_cross(sext_ref, group, delta_extra(cross(sctx_ref, group), context_grad))
        box.flush_part(0, group, cross_view)
        box.flush_part(2, group, cross_view)
        box.flush_part(3, group, cross_view)
        box.flush_part(4, group, cross_view)

        for at in range(groups):

            @pl.when(group == at)
            def _(at=at):
                box.point(10 + at)

        return carry

    lax.fori_loop(0, groups, enter, 0)
    box.flush(1)
    box.point("end")

    def settle(group, carry):
        for copy in copies(group)[0]:
            copy.wait_send()
        for copy in back_copies(group):
            copy.wait_send()
        return carry

    lax.fori_loop(0, groups, settle, 0)


def sample_backward_last(layer, last, box, sk_ref, dqkv_ref, *tail):
    place = box.place
    g0_ref, small_ref = box.out(0, 1)
    box.start(1, 2, 3, 4)
    small_ref[...] = jnp.zeros_like(small_ref)
    fill_sample_codes(box.use(0)[0], None, sk_ref)
    qkv_ref, dc_ref = box.bufs[1], box.bufs[2]
    features, blocks, own, width = dc_ref.shape
    samples = blocks * own
    per = ROWS // own
    steps = blocks // per
    pairs = width // LANES
    total_rows = features * samples
    if last:
        dw_ref, bufs_1, bufs_2, bufs_3, *small_bufs = tail
        share_ref = box.out(3)
    else:
        dw_ref, *small_bufs = tail
    exchange = SmallSums(place, last, *small_bufs)
    box.start(9, 10, 11)
    ext_ref, gext_ref = box.use(3, 4)
    box.ready()
    box.start(5, 6, 7, 8)
    box.start(12, 13)

    def step_of(step, pair):
        got_ref, _, sends, recvs = (bufs_1, bufs_2, bufs_3)[step - 1]
        source = dw_ref.at[pair] if step == 1 else (bufs_1, bufs_2)[step - 2][1].at[pair]
        return SumStep(5 if step == 3 else step, place, source, None, got_ref.at[pair], sends.at[pair], recvs.at[pair], None)

    def pass_on(step, pair):
        step_of(step, pair).finish((bufs_1, bufs_2, bufs_3)[step - 1][1].at[pair])
        if step < 3:
            step_of(step + 1, pair).start()

    def attend(pair, carry):
        lanes = chunk(pair, LANES)
        box.part(1, pair)
        box.part(2, pair)
        for f in range(features):
            key_total = value_total = None
            for step in range(steps):
                rows = slice(f * samples + step * ROWS, f * samples + step * ROWS + ROWS)
                query_grad, key_grad, value_grad = attend_pair_back(
                    block_rows(qkv_ref.at[0], f, step, per, lanes),
                    all_rows(qkv_ref.at[1], f, lanes),
                    all_rows(qkv_ref.at[2], f, lanes),
                    block_rows(dc_ref, f, step, per, lanes),
                    block_rows(ext_ref, f, step, per),
                    block_rows(gext_ref, f, step, per),
                    sk_ref[...],
                    pair,
                )
                dqkv_ref[0, rows, lanes] = (query_grad * 0.125).astype(bf16)
                key_total = key_grad if key_total is None else key_total + key_grad
                value_total = value_grad if value_total is None else value_total + value_grad
            rows = slice(f * samples, f * samples + samples)
            dqkv_ref[1, rows, lanes] = key_total.astype(bf16)
            dqkv_ref[2, rows, lanes] = value_total.astype(bf16)

        for at in range(1, pairs):

            @pl.when(pair == at)
            def _(at=at):
                box.point(at)

        @pl.when(pair == 0)
        def _():
            dense_rows, other_rows = box.use(12, 13)
            if last:
                exchange.start([(0, 9, dense_rows, 9), (9, 11, other_rows, 2)])
            else:
                exchange.start([(0, 9, dense_rows, 9), (9, 9 + SIZE, other_rows, SIZE)])

        for stage in range(1, 4):

            @pl.when(pair == stage)
            def _(stage=stage):
                exchange.move(stage)

        if not last:
            return carry

        @pl.when(pair == 0)
        def _():
            box.use(9, 10, 11)

        hidden = box.bufs[9][...].reshape(total_rows, width)
        context = box.bufs[10][...].reshape(total_rows, width)
        low_ref = box.bufs[11]
        block = dw_ref.shape[3:]
        for member in range(3):
            out = mm(dqkv_ref[member, :, lanes], hidden, TN).T
            dw_ref[pair, member // 2, member % 2] = out.astype(bf16).reshape(block)
        low = low_ref[:, :, :, lanes].reshape(total_rows, LANES)
        dw_ref[pair, 1, 1] = mm(low, context, TN).T.astype(bf16).reshape(block)
        step_of(1, pair).start()

        @pl.when(pair >= 1)
        def _():
            pass_on(1, pair - 1)

        @pl.when(pair >= 2)
        def _():
            pass_on(2, pair - 2)

        return carry

    lax.fori_loop(0, pairs, attend, 0)
    box.point("attend")
    if not last:
        hidden_ref, context_ref, low_ref = box.use(9, 10, 11)

        def weights(member, carry):
            hidden = hidden_ref[...].reshape(total_rows, width)
            out = mm(hidden, dqkv_ref[member], TN)
            dw_ref[member // 2, lax.rem(member, 2)] = out.astype(bf16).reshape(dw_ref.shape[2:])
            return carry

        lax.fori_loop(0, 3, weights, 0)
        context = context_ref[...].reshape(total_rows, width)
        out = mm(context, low_ref[...].reshape(total_rows, width), TN)
        dw_ref[1, 1] = out.astype(bf16).reshape(dw_ref.shape[2:])
        box.chains[-1].begin(dw_ref)
    w_ref, x_ref, gain_ref, g_ref = box.use(5, 6, 7, 8)
    gain = gain_ref[0, layer : layer + 1, :]

    def leave(unit, carry):
        f, part = unit // steps, lax.rem(unit, steps)
        rows = chunk(unit, ROWS)
        total = mm(dqkv_ref[0, rows, :], w_ref[0], NT)
        total = total + mm(dqkv_ref[1, rows, :], w_ref[1], NT)
        total = total + mm(dqkv_ref[2, rows, :], w_ref[2], NT)
        norm_grad, gain_part, shift_part = layer_norm_back(
            total.astype(bf16).astype(f32), block_rows(x_ref, f, part, per), gain
        )
        small_ref[0:1] += gain_part
        small_ref[1:2] += shift_part
        g0_ref[f, chunk(part, per), :, :] = (block_rows(g_ref, f, part, per) + norm_grad).reshape(per, own, width)
        if last:

            @pl.when(unit == 1)
            def _():
                pass_on(1, pairs - 1)

            @pl.when(unit == 2)
            def _():
                pass_on(2, pairs - 2)

        @pl.when(unit == 2)
        def _():
            box.point("leave")
            box.out(2)[...] = exchange.sum(3)
            box.flush(2)

        return carry

    lax.fori_loop(0, features * steps, leave, 0)
    box.flush(0, 1)
    if last:
        exchange.start_late(small_ref)
        pass_on(2, pairs - 1)
        exchange.move(5)
    box.point("end")
    if last:
        for pair in range(pairs):
            pass_on(3, pair)
            share_ref[:, pair_lanes(pair)] = bufs_3[1][pair]
        box.flush(3)
        box.out(4)[...] = exchange.sum(5)
        box.flush(4)


class SmallSums:
    def __init__(self, place, last, packed, early, late, sends, recvs):
        self.packed, self.early, self.late = packed, early, late
        tasks = [{"task": place.task_partner(k)} for k in range(1, place.tasks)]
        ring = [{"feat": place.ring(k)} for k in range(1, place.places)]
        plan = [
            (early, 0, 2, place.core, [place.other_core]),
            (early, 2, place.tasks, place.task, tasks),
            (early, 2 + place.tasks, 2, place.near, [place.near_chip]),
            (early, 4 + place.tasks, 2, place.far, [place.far_chip]),
            (late, 0, place.places, place.place, ring),
            (late, place.places, place.tasks, place.task, tasks),
        ]
        plan = plan if last else plan[:4]
        self.plan, self.copies, at = plan, [], 0
        for buffer, first, count, mine, devices in plan:
            slot = buffer.at[first + mine]
            self.copies.append(
                [remote(slot, slot, sends.at[at + k], recvs.at[at + k], device) for k, device in enumerate(devices)]
            )
            at += len(devices)

    def send(self, stage, rows):
        buffer, first, _, mine, _ = self.plan[stage]
        buffer[first + mine] = rows
        for copy in self.copies[stage]:
            copy.start()

    def start(self, parts):
        self.packed[...] = jnp.zeros_like(self.packed)
        for begin, end, source, count in parts:
            self.packed[begin:end] = source[0:count]
        self.send(0, self.packed[...])

    def start_late(self, rows_ref):
        blocks = [rows_ref[row : row + 1, pair_lanes(block)] for row in range(2) for block in range(4)]
        self.send(4, jnp.concatenate(blocks, axis=0))

    def sum(self, stage):
        buffer, first, count, _, _ = self.plan[stage]
        for copy in self.copies[stage]:
            copy.wait()
        total = buffer[first]
        for k in range(1, count):
            total = total + buffer[first + k]
        return total

    def move(self, stage):
        self.send(stage, self.sum(stage - 1))


def write_out(dense_rows, x_ref, g_ref, *refs):
    refs = list(refs)
    shares, packed_rows, late, bins, loss, outs = refs[:8], refs[8:10], refs[10], refs[11], refs[12], refs[13:26]
    raw_x, raw_g, x_buf, g_buf, load_sem, out_sem = refs[26:]
    outs[12][0] = loss[0, 0]
    for f in range(bins.shape[0]):
        outs[11][:, f, :] = bins[f].T[0:CLASSES]
    features, blocks, own, width = x_ref.shape
    period = features * (width // LANES)
    per = blocks // 4
    rows_part = per * own

    def load(part, which):
        source, target = ((x_ref, x_buf), (g_ref, g_buf))[which]
        view = (slice(None), pl.ds(part * per, per))
        return pltpu.make_async_copy(source.at[view], target.at[view], load_sem.at[which, part])

    def store(part, which):
        source, target = ((raw_x, outs[0]), (raw_g, outs[1]))[which]
        view = pl.ds(part * rows_part * period, rows_part * period)
        return pltpu.make_async_copy(source.at[view], target.at[view], out_sem.at[which, part])

    for part in range(4):
        load(part, 0).start()
        load(part, 1).start()
    for member in range(4):
        outs[2 + member][0] = shares[2 * member][...]
        outs[2 + member][1] = shares[2 * member + 1][...]
    parts = dense_rows - 5
    for layer in range(2):
        packed, at = packed_rows[layer], 0
        for part in range(parts):
            outs[8][layer : layer + 1, part * width : (part + 1) * width] = packed[at + part : at + part + 1]
        outs[9][layer : layer + 1] = packed[at + parts : at + parts + 1]
        for member, row in ((2, parts + 1), (1, parts + 3)):
            outs[6][member, layer : layer + 1] = packed[at + row : at + row + 1]
            outs[7][member, layer : layer + 1] = packed[at + row + 1 : at + row + 2]
    at = dense_rows
    for block in range(4):
        lanes = pair_lanes(block)
        outs[6][0, 0:1, lanes], outs[7][0, 0:1, lanes] = late[block : block + 1], late[4 + block : 5 + block]
    outs[6][0, 1:2], outs[7][0, 1:2] = packed_rows[0][at : at + 1], packed_rows[0][at + 1 : at + 2]
    outs[10][...] = packed_rows[1][at : at + CLASSES]

    for part in range(4):
        for which, buf, raw in ((0, x_buf, raw_x), (1, g_buf, raw_g)):
            load(part, which).wait()
            for f in range(features):
                for block in range(width // LANES):
                    rows = buf[f, part * per : (part + 1) * per, :, pair_lanes(block)].reshape(rows_part, LANES)
                    start = part * rows_part * period + block * features + f
                    raw[pl.ds(start, rows_part, stride=period), :] = rows
            store(part, which).start()
    for part in range(4):
        store(part, 0).wait()
        store(part, 1).wait()


def codes(item, live, size, rows):
    lanes = jnp.arange(LANES)[None, :] - CODE_LANE
    inside = (lanes >= 0) & (lanes < size)
    own = lanes == item[:, None]
    query_code = (own & inside).astype(bf16)
    key_code = jnp.where(inside & ~(own & live[:, None]), masked_score, 0.0).astype(bf16)
    return query_code, key_code


def local_fused(
    tokens_in,
    sample_weights,
    feature_weights,
    norm_gain,
    norm_shift,
    up_weight,
    up_bias,
    down_weight,
    down_bias,
    read_weight,
    output_grad,
    task_sizes,
    feature_counts,
    bin_index,
    bin_counts,
    class_labels,
):
    samples, features, width = tokens_in.shape[1:]
    hidden_width = up_weight.shape[2]
    tasks, places = lax.axis_size("task"), lax.axis_size("feat")
    own = samples // places
    groups = own // SIZE
    units = features * (own * places // ROWS)
    sizes = (tasks, places)
    shape = (features, places, own, width)
    block_shape = (places, features, own, width)
    group_shape = (groups, ROWS, width)
    share = width // places
    share_shape = (share, width)
    piece_shape = (2, 2, 2, 2, 2, share, width)
    rows_total = groups * ROWS
    vmem = pltpu.VMEM

    def dma(*counts):
        return pltpu.SemaphoreType.DMA(counts)

    def raw_rows(tokens):
        parts = tokens.reshape(samples, features, width // LANES, LANES)
        return parts.transpose(0, 2, 1, 3).reshape(samples * features * (width // LANES), LANES)

    def from_raw(rows):
        parts = rows.reshape(samples, width // LANES, features, LANES)
        return parts.transpose(0, 2, 1, 3).reshape(1, samples, features, width)

    gains = norm_gain.transpose(1, 0, 2)
    shifts = norm_shift.transpose(1, 0, 2)
    stream = tokens_in[0].astype(f32).transpose(1, 0, 2).reshape(shape)
    stored = []
    for layer in range(LAYERS):
        x1, qkv, ctx, ext, hidden, fqkv, fctx, fext, x2, x3, u, h1 = fused(
            functools.partial(forward_layer, layer),
            "forward_layer",
            sizes,
            [
                (task_sizes, "scalar"),
                (feature_counts, "scalar"),
                (stream, None, first_view, features),
                (gains, None),
                (shifts, None),
                (sample_weights, layer),
                (feature_weights, layer),
                (up_weight, layer),
                (up_bias, None),
                (down_weight, layer),
                (down_bias, None),
            ],
            [
                (shape, f32),
                ((3,) + shape, bf16),
                (shape, bf16),
                (shape[:3] + (LANES,), bf16),
                (group_shape, bf16),
                ((groups, 3, ROWS, width), bf16),
                (group_shape, bf16),
                ((groups, ROWS, LANES), bf16),
                (shape, f32),
                (shape, f32),
                ((groups, ROWS, hidden_width), bf16),
                (shape, bf16),
            ],
            [
                vmem((ROWS, LANES), bf16),
                vmem((samples, LANES), bf16),
                vmem((ROWS, LANES), bf16),
                vmem((ROWS, LANES), bf16),
                vmem(shape, bf16),
                vmem(block_shape, bf16),
                vmem(block_shape, bf16),
                vmem(shape, bf16),
                vmem((ROWS, hidden_width), bf16),
                dma(units, places - 1),
                dma(units, places - 1),
                dma(units),
                dma(groups, places - 1),
                dma(groups, places - 1),
            ],
            [],
            share_shape,
            1 + layer,
        )
        stored.append((stream, x1, qkv, ctx, ext, hidden, fqkv, fctx, fext, x2, u, h1))
        stream = x3

    shapes, loss, read_grad, stream_grad = fused(
        read_out,
        "read_out",
        sizes,
        [
            (task_sizes, "scalar"),
            (feature_counts, "scalar"),
            (class_labels, None),
            (bin_index[0].T, None),
            (bin_counts[0], None),
            (read_weight.T, None),
            (stream, None),
            (raw_rows(output_grad), None),
        ],
        [((features, BINS, LANES), f32), ((8, LANES), f32), ((SIZE, width), f32), (shape, f32)],
        [
            vmem((samples * features * (width // LANES), LANES), f32),
            vmem((places, CLASSES * (samples // LANES), LANES), f32),
            vmem((features, samples, width), bf16),
            vmem((features, BINS, samples), bf16),
            vmem((features, BINS, LANES), f32),
            vmem((LANES, width), bf16),
            vmem((features, BINS, LANES), f32),
            dma(places - 1),
            dma(places - 1),
        ],
        [],
        share_shape,
        3,
    )

    finished = {}
    dense_rows = hidden_width // width + 5
    pairs = width // LANES
    flat = (rows_total, width)
    for layer in reversed(range(LAYERS)):
        x0, x1, qkv, ctx, ext, hidden, fqkv, fctx, fext, x2, u, h1 = stored[layer]
        last = layer == 0
        ins = [
            (feature_counts, "scalar"),
            (stream_grad, None, cross_view, groups),
            (down_weight, layer),
            (u, None, first_view, groups),
            (up_weight, layer),
            (x2, None, cross_view, groups),
            (gains, None),
            (shifts, None),
            (feature_weights, layer),
            (fqkv, None),
            (fctx, None),
            (fext, None),
            (hidden, None),
            (x1, None),
            (sample_weights, (layer, 3)),
            (ctx, None),
        ]
        sums = [
            ((1, 6, 7, 3), ("dense", 1, 3, 12), None, True),
            ((1, 6, 7, 3), (0, 2, "weights", 12), None, True),
            ((1, 6), (10, 12), None, True),
        ]
        if last:
            sums += [((2, 3), (0, 11), sample_sum, True), ((3,), (0, 11), finished[1][0], True)]
        g1, dense_small, sdc, sext, slow, up_sum, down_sum, feature_sum, *later_sum = fused(
            functools.partial(dense_feature_backward, layer),
            "dense_feature_backward",
            sizes,
            ins,
            [
                (shape, f32),
                ((16, width), f32),
                (shape, bf16),
                (shape[:3] + (LANES,), bf16),
                (shape, bf16),
            ],
            [
                vmem((ROWS, LANES), bf16),
                vmem(shape, bf16),
                vmem((rows_total, hidden_width), bf16),
                vmem((rows_total, hidden_width), bf16),
                vmem(flat, bf16),
                vmem(flat, bf16),
                vmem(piece_shape, bf16),
                vmem(piece_shape, bf16),
                vmem(block_shape, bf16),
                vmem((ROWS, width), bf16),
                vmem(block_shape, bf16),
                vmem(shape, bf16),
                vmem(piece_shape, bf16),
                dma(groups, places - 1),
                dma(groups, places - 1),
                dma(groups),
                dma(groups, places - 1),
                dma(groups, places - 1),
            ],
            sums,
            share_shape,
            4 + layer,
        )
        ins = [
            (task_sizes, "scalar"),
            (qkv, None, last_view, pairs),
            (sdc, None, last_view, pairs),
            (ext, None),
            (sext, None),
            (sample_weights, layer),
            (x0, None),
            (gains, None),
            (g1, None),
        ]
        other_small = sample_small if last else read_grad
        ins += [(array, None) for array in (h1, ctx, slow, dense_small, other_small)]
        early_rows = -(-(dense_rows + (2 if last else SIZE)) // 8) * 8
        slots = 6 + tasks
        copies = 1 + (tasks - 1) + 1 + 1 + (places - 1) + (tasks - 1)
        small_scratch = [
            vmem((early_rows, width), f32),
            vmem((slots, early_rows, width), f32),
            vmem((places + tasks, 8, LANES), f32),
            dma(copies),
            dma(copies),
        ]
        outs = [(shape, f32), ((8, width), f32), ((early_rows, width), f32)]
        scratch = [vmem((samples, LANES), bf16), vmem((3,) + flat, bf16)]
        if last:
            outs += [(share_shape, f32), ((8, LANES), f32)]
            scratch.append(vmem((pairs, 2, 2, 2, 2, 2, share, LANES), bf16))
            for step in (1, 2, 5):
                _, got, mine, kind, count = sum_shapes(step, tasks, share, LANES)
                scratch += [
                    (
                        vmem((pairs,) + got, bf16),
                        vmem((pairs,) + mine, kind),
                        dma(pairs, count),
                        dma(pairs, count),
                    )
                ]
            scratch += small_scratch
            sums = [
                ((7, 3, 4), (2, "attend", "end"), feature_sum, True),
                ((4,), ("attend",), up_sum, True),
                ((4,), ("attend",), down_sum, True),
                ((4,), ("attend",), later_sum[0], True),
                ((4,), ("attend",), later_sum[1], True),
            ]
        else:
            scratch += [vmem(piece_shape, bf16), *small_scratch]
            sums = [
                ((7,), (3,), feature_sum, True),
                ((4,), ("attend",), up_sum, True),
                ((4,), ("attend",), down_sum, True),
                ((1,), ("leave",), None, True),
            ]
        stream_grad, sample_small, *more = fused(
            functools.partial(sample_backward_last, layer, last),
            "sample_backward",
            sizes,
            ins,
            outs,
            scratch,
            sums,
            share_shape,
            6 + layer,
        )
        if last:
            packed, share_sum, late, *first = more
            finished[0] = (share_sum, *first[:3])
            finished[1] = (first[3], first[4], *finished[1][1:])
        else:
            later_packed, *finished[1], sample_sum = more

    whole, parked = pl.BlockSpec(memory_space=pltpu.VMEM), pl.BlockSpec(memory_space=pltpu.HBM)
    scalar = pl.BlockSpec(memory_space=pltpu.SMEM)
    matrix = jax.ShapeDtypeStruct((LAYERS, share, width), f32)
    norm = jax.ShapeDtypeStruct((3, LAYERS, width), f32)
    raw_shape = (samples * features * (width // LANES), LANES)
    raw = jax.ShapeDtypeStruct(raw_shape, f32)
    shares = [finished[layer][member] for member in range(4) for layer in range(LAYERS)]
    results = pl.pallas_call(
        functools.partial(write_out, dense_rows),
        name="write_out",
        out_shape=[
            raw,
            raw,
            matrix,
            matrix,
            matrix,
            matrix,
            norm,
            norm,
            jax.ShapeDtypeStruct((LAYERS, hidden_width), f32),
            jax.ShapeDtypeStruct((LAYERS, width), f32),
            jax.ShapeDtypeStruct((CLASSES, width), f32),
            jax.ShapeDtypeStruct((CLASSES, features, BINS), f32),
            jax.ShapeDtypeStruct((1,), f32),
        ],
        in_specs=[parked] * 2 + [whole] * 12 + [scalar],
        out_specs=[parked] * 2 + [whole] * 10 + [scalar],
        scratch_shapes=[
            vmem(raw_shape, f32),
            vmem(raw_shape, f32),
            vmem(shape, f32),
            vmem(shape, f32),
            dma(2, 4),
            dma(2, 4),
        ],
        compiler_params=pltpu.CompilerParams(vmem_limit_bytes=63 << 20),
    )(stream, stream_grad, *shares, packed, later_packed, late, shapes, loss)
    return (
        from_raw(results[0]),
        results[11].transpose(1, 2, 0)[None],
        from_raw(results[1]),
        results[12],
        results[2][:, None],
        results[3][:, None],
        results[6].transpose(1, 0, 2),
        results[7].transpose(1, 0, 2),
        results[4].transpose(0, 2, 1),
        results[8],
        results[5],
        results[9],
        results[10].T,
    )


def local(
    tokens_in,
    sample_weights,
    feature_weights,
    norm_gain,
    norm_shift,
    up_weight,
    up_bias,
    down_weight,
    down_bias,
    read_weight,
    output_grad,
    task_sizes,
    feature_counts,
    bin_index,
    bin_counts,
    class_labels,
):
    samples = tokens_in.shape[1]
    features = tokens_in.shape[2]
    width = tokens_in.shape[3]
    hidden_width = up_weight.shape[2]
    task_devices = lax.axis_size("task")
    feature_devices = lax.axis_size("feat")
    all_features = features * feature_devices
    own_samples = samples // feature_devices
    size = min(16, own_samples)
    groups = own_samples // size
    group_rows = all_features * size
    rows_total = features * samples

    if (
        own_samples % 32 == 0
        and samples % ROWS == 0
        and ROWS % own_samples == 0
        and group_rows == ROWS
        and own_samples == 4 * SIZE
        and task_devices == hidden_width // width == 4
        and feature_devices == 8
    ):
        return local_fused(
            tokens_in,
            sample_weights,
            feature_weights,
            norm_gain,
            norm_shift,
            up_weight,
            up_bias,
            down_weight,
            down_bias,
            read_weight,
            output_grad,
            task_sizes,
            feature_counts,
            bin_index,
            bin_counts,
            class_labels,
        )

    sample_live = jnp.arange(samples) < task_sizes[0]
    feature_live = jnp.arange(all_features) < feature_counts[0]
    sample_mask = sample_live.astype(f32)
    local_index = lax.axis_index("feat") * features + jnp.arange(features)
    local_live = (local_index < feature_counts[0]).astype(f32)
    sample_qcode, sample_kcode = codes(jnp.zeros((samples,), jnp.int32), sample_live, 1, samples)
    sample_qcode = sample_qcode[:ROWS]
    item = jnp.arange(group_rows) % size
    feature_qcode, feature_kcode = codes(item, jnp.repeat(feature_live, size), size, group_rows)

    def exchange_out(rows):
        parts = rows.reshape(features, feature_devices, own_samples, width)
        got = lax.all_to_all(parts, "feat", split_axis=1, concat_axis=0, tiled=True)
        return got.reshape(all_features, own_samples, width)

    def exchange_back(rows):
        parts = rows.reshape(feature_devices, features, own_samples, width)
        got = lax.all_to_all(parts, "feat", split_axis=0, concat_axis=2, tiled=True)
        return got.reshape(features, samples, width)

    stream = tokens_in[0].astype(f32).transpose(1, 0, 2)
    token_shape = (features, samples, width)
    stored = []
    for layer in range(LAYERS):
        gain, shift = norm_gain[layer], norm_shift[layer]
        x1, h2, qkv, ctx, ext = call(
            sample_forward,
            "sample_forward",
            [
                (token_shape, f32),
                (token_shape, bf16),
                ((3,) + token_shape, bf16),
                (token_shape, bf16),
                ((features, samples, LANES), bf16),
            ],
            [],
            stream,
            gain,
            shift,
            sample_weights[layer],
            sample_qcode,
            sample_kcode,
        )
        swapped = exchange_out(h2)
        a, fqkv, fctx, fext = call(
            functools.partial(feature_forward, size),
            "feature_forward",
            [
                ((all_features, own_samples, width), bf16),
                ((groups, 3, group_rows, width), bf16),
                ((groups, group_rows, width), bf16),
                ((groups, group_rows, LANES), bf16),
            ],
            [],
            swapped,
            feature_weights[layer],
            feature_qcode,
            feature_kcode,
        )
        back = exchange_back(a)
        x3, u = call(
            dense_forward,
            "dense_forward",
            [((rows_total, width), f32), ((rows_total, hidden_width), bf16)],
            [],
            x1.reshape(rows_total, width),
            back.reshape(rows_total, width),
            gain,
            shift,
            up_weight[layer],
            up_bias[layer][None],
            down_weight[layer],
            down_bias[layer][None],
        )
        stored.append((stream, x1, qkv, ctx, ext, swapped, fqkv, fctx, fext, back, u))
        stream = x3.reshape(token_shape)

    reading = stream.astype(bf16)
    projected = jnp.einsum("fsd,dc->fsc", reading, read_weight, preferred_element_type=f32)
    onehot_bins = (bin_index[0].T[..., None] == jnp.arange(BINS)).astype(f32)
    chosen = onehot_bins * sample_mask[None, :, None]
    counted = jnp.maximum(jnp.sum(chosen, axis=1), 1.0)
    bin_sums = jnp.einsum("fsb,fsc->fbc", chosen, projected, precision=highest)
    bin_means = bin_sums / counted[..., None]
    bin_weight = bin_counts[0].astype(f32)
    weight_total = jnp.sum(bin_weight, axis=-1, keepdims=True)
    centre = jnp.sum(bin_weight[..., None] * bin_means, axis=1, keepdims=True) / weight_total[..., None]
    shapes = bin_means - centre
    used_bins = onehot_bins * local_live[:, None, None]
    local_logits = jnp.einsum("fsb,fbc->sc", used_bins, shapes, precision=highest)
    logits = lax.psum(local_logits, "feat")
    row_max = jnp.max(logits, axis=-1, keepdims=True)
    log_total = row_max + jnp.log(jnp.sum(jnp.exp(logits - row_max), axis=-1, keepdims=True))
    label_rows = (class_labels[0][:, None] == jnp.arange(CLASSES)).astype(f32)
    picked = jnp.sum(logits * label_rows, axis=-1)
    live_count = task_sizes[0].astype(f32)
    task_loss = jnp.sum(sample_mask * (log_total[:, 0] - picked)) / live_count
    logit_grad = sample_mask[:, None] * (jnp.exp(logits - log_total) - label_rows) / live_count
    shape_grad = jnp.einsum("fsb,sc->fbc", used_bins, logit_grad, precision=highest)
    means_grad = shape_grad - bin_weight[..., None] / weight_total[..., None] * jnp.sum(
        shape_grad, axis=1, keepdims=True
    )
    sum_grad = means_grad / counted[..., None]
    projected_grad = jnp.einsum("fsb,fbc->fsc", chosen, sum_grad, precision=highest).astype(bf16)
    read_grad = jnp.einsum("fsd,fsc->dc", reading, projected_grad, preferred_element_type=f32)
    stream_grad = output_grad[0].astype(f32).transpose(1, 0, 2) + jnp.einsum(
        "fsc,dc->fsd", projected_grad, read_weight, preferred_element_type=f32
    )

    small = [None] * LAYERS
    big = [None] * LAYERS
    for layer in reversed(range(LAYERS)):
        gain, shift = norm_gain[layer], norm_shift[layer]
        x0, x1, qkv, ctx, ext, swapped, fqkv, fctx, fext, back, u = stored[layer]
        flat = (rows_total, width)
        g2, sent, dup, ddown, dupb, ddownb, dgs2 = call(
            dense_backward,
            "dense_backward",
            [
                (flat, f32),
                (flat, bf16),
                ((hidden_width, width), bf16),
                ((hidden_width, width), bf16),
                ((1, hidden_width), f32),
                ((1, width), f32),
                ((2, width), f32),
            ],
            [
                ((rows_total, hidden_width), bf16),
                ((rows_total, hidden_width), bf16),
                (flat, bf16),
                (flat, bf16),
            ],
            stream_grad.reshape(flat),
            x1.reshape(flat),
            back.reshape(flat),
            u,
            gain,
            shift,
            up_weight[layer],
            down_weight[layer],
        )
        arriving = exchange_out(sent.reshape(token_shape))
        group_shape = (groups, group_rows, width)
        dh, dwf = call(
            functools.partial(feature_backward, size),
            "feature_backward",
            [((all_features, own_samples, width), bf16), ((4, width, width), bf16)],
            [
                ((3,) + group_shape, bf16),
                (group_shape, bf16),
                (group_shape, bf16),
                ((group_rows, width), bf16),
            ],
            arriving,
            swapped,
            feature_weights[layer],
            feature_kcode,
            fqkv,
            fctx,
            fext,
        )
        returned = exchange_back(dh)
        g0, dws, dgs01 = call(
            sample_backward,
            "sample_backward",
            [(token_shape, f32), ((4, width, width), bf16), ((2, 2, width), f32)],
            [
                ((3,) + token_shape, bf16),
                (token_shape, bf16),
                (token_shape, bf16),
                (token_shape, bf16),
                ((features, samples, LANES), bf16),
                ((samples, LANES), f32),
                ((samples, LANES), f32),
            ],
            g2.reshape(token_shape),
            returned,
            x1,
            x0,
            gain,
            shift,
            sample_weights[layer],
            sample_kcode,
            qkv,
            ctx,
            ext,
        )
        stream_grad = g0
        small[layer] = (
            jnp.stack([dgs01[0, 0], dgs01[1, 0], dgs2[0]]),
            jnp.stack([dgs01[0, 1], dgs01[1, 1], dgs2[1]]),
            dupb[0],
            ddownb[0],
        )
        big[layer] = [dws.reshape(4 * width, width), dwf.reshape(4 * width, width), dup, ddown]
    shard_shape = (LAYERS, 4 // task_devices, width // feature_devices, width)
    pieces = [big[layer][member] for member in range(4) for layer in range(LAYERS)]
    rows = [row.reshape(-1, width) for layer in range(LAYERS) for row in small[layer]]
    rows.append(read_grad.T)
    lengths = [row.shape[0] for row in rows]
    fill = -sum(lengths) % 8
    small_rows = jnp.concatenate(rows + [jnp.zeros((fill, width), f32)])
    if (width // feature_devices) % 16 == 0:
        *shares, small_sums = sum_everywhere(pieces, small_rows, task_devices, feature_devices)
    else:
        shares = [
            lax.psum_scatter(piece, ("task", "feat"), scatter_dimension=0, tiled=True).astype(f32)
            for piece in pieces
        ]
        small_sums = lax.psum(small_rows, ("task", "feat"))
    matrices = [jnp.stack(shares[member * LAYERS : member * LAYERS + LAYERS]) for member in range(4)]
    split = []
    at = 0
    for length in lengths:
        split.append(small_sums[at : at + length])
        at += length
    summed = [jnp.stack([split[4 * layer + member] for layer in range(LAYERS)]) for member in range(4)]
    summed[2] = summed[2].reshape(LAYERS, hidden_width)
    summed[3] = summed[3].reshape(LAYERS, width)
    summed.append(split[-1].T)
    return (
        stream.transpose(1, 0, 2)[None],
        shapes[None],
        stream_grad.transpose(1, 0, 2)[None],
        task_loss[None],
        matrices[0].reshape(shard_shape),
        matrices[1].reshape(shard_shape),
        summed[0],
        summed[1],
        matrices[2].transpose(0, 2, 1),
        summed[2],
        matrices[3],
        summed[3],
        summed[4],
    )


def solution(mesh):
    in_specs = (
        P("task", None, "feat", None),
        P(),
        P(),
        P(),
        P(),
        P(),
        P(),
        P(),
        P(),
        P(),
        P("task", None, "feat", None),
        P("task"),
        P("task"),
        P("task", None, "feat"),
        P("task", "feat", None),
        P("task", None),
    )
    out_specs = (
        P("task", None, "feat", None),
        P("task", "feat", None, None),
        P("task", None, "feat", None),
        P("task"),
        P(None, "task", "feat", None),
        P(None, "task", "feat", None),
        P(),
        P(),
        P(None, None, ("task", "feat")),
        P(),
        P(None, ("task", "feat"), None),
        P(),
        P(),
    )
    return jax.shard_map(local, mesh=mesh, in_specs=in_specs, out_specs=out_specs, check_vma=False)
```

```python
import functools

import jax
import jax.numpy as jnp
from jax import lax
from jax.experimental import pallas as pl
from jax.experimental.pallas import tpu as pltpu
from jax.sharding import PartitionSpec as P

HEADS = 8
BINS = 64
CLASSES = 10
LAYERS = 2
LANES = 128
CODE_LANE = 32
ROWS = 256

epsilon = 1e-05
masked_score = -1e30
highest = lax.Precision.HIGHEST
bf16 = jnp.bfloat16
f32 = jnp.float32

NN = (((1,), (0,)), ((), ()))
NT = (((1,), (1,)), ((), ()))
TN = (((0,), (0,)), ((), ()))


def mm(left, right, dims=NN):
    return lax.dot_general(left, right, dims, preferred_element_type=f32)


def lane_row():
    return lax.broadcasted_iota(jnp.int32, (1, LANES), 1)


def half_row(half):
    lanes = lane_row()
    picked = lanes < 64 if half == 0 else lanes >= 64
    return picked.astype(f32).astype(bf16)


def piece_row(pair, half):
    offset = lane_row() - 64 * half - 3 * pair
    return jnp.where((offset >= 0) & (offset < 3), -1.0, 0.0).astype(bf16)


def split_pieces(values, order):
    first = values.astype(bf16).astype(f32)
    rest = values - first
    second = rest.astype(bf16).astype(f32)
    third = rest - second
    return jnp.where(order == 0, first, jnp.where(order == 1, second, third))


def layer_norm(rows, gain, shift):
    centred = rows - jnp.mean(rows, axis=-1, keepdims=True)
    inverse = lax.rsqrt(jnp.mean(centred * centred, axis=-1, keepdims=True) + epsilon)
    normed = centred * inverse
    return normed, inverse, normed * gain + shift


def layer_norm_back(grad_rows, rows, gain):
    centred = rows - jnp.mean(rows, axis=-1, keepdims=True)
    inverse = lax.rsqrt(jnp.mean(centred * centred, axis=-1, keepdims=True) + epsilon)
    normed = centred * inverse
    scaled = grad_rows * gain
    inner = (
        scaled
        - jnp.mean(scaled, axis=-1, keepdims=True)
        - normed * jnp.mean(scaled * normed, axis=-1, keepdims=True)
    )
    gain_part = jnp.sum(grad_rows * normed, axis=0, keepdims=True)
    shift_part = jnp.sum(grad_rows, axis=0, keepdims=True)
    return inverse * inner, gain_part, shift_part


def chunk(index, size):
    return pl.ds(pl.multiple_of(index * size, size), size)


def attend_pair(query, key, value, query_code, key_code, pair, extras):
    query_wide = jnp.concatenate([query, query_code], axis=1)
    total = None
    peaks = []
    for half in range(2):
        mask = half_row(half)
        key_wide = jnp.concatenate([key * mask, key_code], axis=1)
        scores = mm(query_wide, key_wide, NT)
        peak = jnp.max(scores, axis=-1, keepdims=True)
        weights = jnp.exp(scores - peak).astype(bf16)
        ones = jnp.broadcast_to(mask, value.shape)
        part = mm(weights, jnp.concatenate([value * mask, ones], axis=1))
        total = part if total is None else total + part
        peaks.append(peak)
    lanes = lane_row()
    row_total = total[:, LANES:]
    context = total[:, :LANES] / row_total
    log_total = jnp.where(lanes < 64, peaks[0], peaks[1]) + jnp.log(row_total)
    order = lanes % 64 - 3 * pair
    extras = jnp.where((order >= 0) & (order < 3), split_pieces(log_total, order), extras)
    return context.astype(bf16), extras


def attend_pair_back(query, key, value, context_grad, query_extra, grad_extra, key_code, pair):
    query_wide = jnp.concatenate([query, query_extra], axis=1)
    grad_wide = jnp.concatenate([context_grad, grad_extra], axis=1)
    query_grad = key_grad = value_grad = None
    for half in range(2):
        mask = half_row(half)
        pieces = piece_row(pair, half)
        key_half = key * mask
        key_wide = jnp.concatenate([key_half, key_code + pieces], axis=1)
        value_wide = jnp.concatenate(
            [value * mask, jnp.broadcast_to(pieces, value.shape)], axis=1
        )
        attention = jnp.exp(mm(key_wide, query_wide, NT))
        score_grad = (attention * mm(value_wide, grad_wide, NT)).astype(bf16)
        value_part = mm(attention.astype(bf16), context_grad * mask)
        key_part = mm(score_grad, query * mask)
        query_part = mm(score_grad, key_half, TN)
        if half == 0:
            query_grad, key_grad, value_grad = query_part, key_part, value_part
        else:
            query_grad, key_grad, value_grad = (
                query_grad + query_part,
                key_grad + key_part,
                value_grad + value_part,
            )
    return query_grad, key_grad, value_grad


def delta_extra(context, context_grad):
    width = context.shape[1]
    products = context.astype(f32) * context_grad.astype(f32)
    high = products.astype(bf16)
    low = (products - high.astype(f32)).astype(bf16)
    head = lax.broadcasted_iota(jnp.int32, (width, LANES), 0) // (width // HEADS)
    offset = lax.broadcasted_iota(jnp.int32, (width, LANES), 1) - 64 * (head % 2) - 3 * (head // 2)
    spread = jnp.where((offset >= 0) & (offset < 3), 1.0, 0.0).astype(bf16)
    sums = mm(high, spread) + mm(low, spread)
    return split_pieces(sums, lane_row() % 64 % 3).astype(bf16)


def sample_forward(x_ref, gain_ref, shift_ref, w_ref, qcode_ref, kcode_ref, x1_ref, h2_ref, qkv_ref, ctx_ref, ext_ref):
    features, samples, width = x_ref.shape
    steps = samples // ROWS

    def project(unit, carry):
        f, rows = unit // steps, chunk(unit % steps, ROWS)
        _, _, hidden = layer_norm(x_ref[f, rows, :], gain_ref[0:1], shift_ref[0:1])
        hidden = hidden.astype(bf16)
        for member in range(3):
            out = mm(hidden, w_ref[member]).astype(bf16)
            if member == 0:
                out = out * jnp.asarray(0.125, bf16)
            qkv_ref[member, f, rows, :] = out
        return carry

    lax.fori_loop(0, features * steps, project, 0)

    def attend(unit, carry):
        f, rows = unit // steps, chunk(unit % steps, ROWS)
        code = qcode_ref[...]

        def pair_step(pair, extras):
            lanes = chunk(pair, LANES)
            context, extras = attend_pair(
                qkv_ref[0, f, rows, lanes],
                qkv_ref[1, f, :, lanes],
                qkv_ref[2, f, :, lanes],
                code,
                kcode_ref[...],
                pair,
                extras,
            )
            ctx_ref[f, rows, lanes] = context
            return extras

        extras = lax.fori_loop(0, width // LANES, pair_step, code.astype(f32))
        ext_ref[f, rows, :] = extras.astype(bf16)
        x1 = x_ref[f, rows, :] + mm(ctx_ref[f, rows, :], w_ref[3])
        x1_ref[f, rows, :] = x1
        _, _, hidden = layer_norm(x1, gain_ref[1:2], shift_ref[1:2])
        h2_ref[f, rows, :] = hidden.astype(bf16)
        return carry

    lax.fori_loop(0, features * steps, attend, 0)


def load_group(ref, group, size):
    features, _, width = ref.shape
    block = ref[:, chunk(group, size), :]
    if size % 16:
        return block.astype(f32).reshape(features * size, width).astype(bf16)
    return block.reshape(features * size, width)


def store_group(ref, group, size, rows):
    features, _, width = ref.shape
    if size % 16:
        block = rows.astype(f32).reshape(features, size, width).astype(bf16)
    else:
        block = rows.reshape(features, size, width)
    ref[:, chunk(group, size), :] = block


def feature_forward(size, h_ref, w_ref, qcode_ref, kcode_ref, a_ref, qkv_ref, ctx_ref, ext_ref):
    _, samples, width = h_ref.shape

    def step(group, carry):
        hidden = load_group(h_ref, group, size)
        for member in range(3):
            out = mm(hidden, w_ref[member]).astype(bf16)
            if member == 0:
                out = out * jnp.asarray(0.125, bf16)
            qkv_ref[group, member] = out
        code = qcode_ref[...]

        def pair_step(pair, extras):
            lanes = chunk(pair, LANES)
            context, extras = attend_pair(
                qkv_ref[group, 0, :, lanes],
                qkv_ref[group, 1, :, lanes],
                qkv_ref[group, 2, :, lanes],
                code,
                kcode_ref[...],
                pair,
                extras,
            )
            ctx_ref[group, :, lanes] = context
            return extras

        extras = lax.fori_loop(0, width // LANES, pair_step, code.astype(f32))
        ext_ref[group] = extras.astype(bf16)
        store_group(a_ref, group, size, mm(ctx_ref[group], w_ref[3]).astype(bf16))
        return carry

    lax.fori_loop(0, samples // size, step, 0)


def gelu_parts(values):
    cubic = values * values * values
    inside = 0.7978845608028654 * (values + 0.044715 * cubic)
    bent = jnp.tanh(inside)
    return bent


def dense_forward(x_ref, a_ref, gain_ref, shift_ref, up_ref, upb_ref, down_ref, downb_ref, out_ref, u_ref):
    rows_total, width = x_ref.shape
    hidden_width = up_ref.shape[1]

    def step(unit, carry):
        rows = chunk(unit, ROWS)
        x2 = x_ref[rows, :] + a_ref[rows, :].astype(f32)
        _, _, hidden = layer_norm(x2, gain_ref[2:3], shift_ref[2:3])
        hidden = hidden.astype(bf16)
        total = x2 + downb_ref[...]
        for part in range(hidden_width // 512):
            cols = slice(part * 512, part * 512 + 512)
            expanded = mm(hidden, up_ref[:, cols]) + upb_ref[:, cols]
            u_ref[rows, cols] = expanded.astype(bf16)
            active = (0.5 * expanded * (1.0 + gelu_parts(expanded))).astype(bf16)
            total = total + mm(active, down_ref[cols, :])
        out_ref[rows, :] = total
        return carry

    lax.fori_loop(0, rows_total // ROWS, step, 0)


def dense_backward(g_ref, x1_ref, a_ref, u_ref, gain_ref, shift_ref, up_ref, down_ref, out_ref, send_ref, dup_ref, ddown_ref, dupb_ref, ddownb_ref, dgs_ref, active_ref, ugrad_ref, hidden_ref, rowgrad_ref):
    rows_total, width = g_ref.shape
    hidden_width = up_ref.shape[1]
    dupb_ref[...] = jnp.zeros_like(dupb_ref)
    ddownb_ref[...] = jnp.zeros_like(ddownb_ref)
    dgs_ref[...] = jnp.zeros_like(dgs_ref)

    def step(unit, carry):
        rows = chunk(unit, ROWS)
        grad = g_ref[rows, :]
        low = grad.astype(bf16)
        rowgrad_ref[rows, :] = low
        ddownb_ref[...] += jnp.sum(low.astype(f32), axis=0, keepdims=True)
        hidden_grad = None
        for part in range(hidden_width // 512):
            cols = slice(part * 512, part * 512 + 512)
            active_grad = mm(low, down_ref[cols, :], NT).astype(bf16).astype(f32)
            u = u_ref[rows, cols].astype(f32)
            bent = gelu_parts(u)
            slope = 0.5 * (1.0 + bent) + u * (1.0 - bent * bent) * (
                0.3989422804014327 + 0.05351611220146811 * u * u
            )
            active_ref[rows, cols] = (0.5 * u * (1.0 + bent)).astype(bf16)
            ugrad = (active_grad * slope).astype(bf16)
            ugrad_ref[rows, cols] = ugrad
            dupb_ref[:, cols] += jnp.sum(ugrad.astype(f32), axis=0, keepdims=True)
            part_grad = mm(ugrad, up_ref[:, cols], NT)
            hidden_grad = part_grad if hidden_grad is None else hidden_grad + part_grad
        x2 = x1_ref[rows, :] + a_ref[rows, :].astype(f32)
        _, _, hidden = layer_norm(x2, gain_ref[2:3], shift_ref[2:3])
        hidden_ref[rows, :] = hidden.astype(bf16)
        norm_grad, gain_part, shift_part = layer_norm_back(
            hidden_grad.astype(bf16).astype(f32), x2, gain_ref[2:3]
        )
        dgs_ref[0:1] += gain_part
        dgs_ref[1:2] += shift_part
        grad = grad + norm_grad
        out_ref[rows, :] = grad
        send_ref[rows, :] = grad.astype(bf16)
        return carry

    lax.fori_loop(0, rows_total // ROWS, step, 0)

    def weights(part, carry):
        cols = chunk(part, 512)
        dup_ref[cols, :] = mm(ugrad_ref[:, cols], hidden_ref[...], TN).astype(bf16)
        ddown_ref[cols, :] = mm(active_ref[:, cols], rowgrad_ref[...], TN).astype(bf16)
        return carry

    lax.fori_loop(0, hidden_width // 512, weights, 0)


def feature_backward(size, da_ref, h_ref, w_ref, kcode_ref, qkv_ref, ctx_ref, ext_ref, dh_ref, dw_ref, dqkv_ref, hidden_ref, dao_ref, dc_ref):
    _, samples, width = h_ref.shape
    groups = samples // size

    def step(group, carry):
        hidden_ref[group] = load_group(h_ref, group, size)
        dao = load_group(da_ref, group, size)
        dao_ref[group] = dao
        context_grad = mm(dao, w_ref[3], NT).astype(bf16)
        dc_ref[...] = context_grad
        grad_extra = delta_extra(ctx_ref[group], context_grad)

        def pair_step(pair, inner):
            lanes = chunk(pair, LANES)
            query_grad, key_grad, value_grad = attend_pair_back(
                qkv_ref[group, 0, :, lanes],
                qkv_ref[group, 1, :, lanes],
                qkv_ref[group, 2, :, lanes],
                dc_ref[:, lanes],
                ext_ref[group],
                grad_extra,
                kcode_ref[...],
                pair,
            )
            dqkv_ref[0, group, :, lanes] = (query_grad * 0.125).astype(bf16)
            dqkv_ref[1, group, :, lanes] = key_grad.astype(bf16)
            dqkv_ref[2, group, :, lanes] = value_grad.astype(bf16)
            return inner

        lax.fori_loop(0, width // LANES, pair_step, 0)
        total = mm(dqkv_ref[0, group], w_ref[0], NT)
        total = total + mm(dqkv_ref[1, group], w_ref[1], NT)
        total = total + mm(dqkv_ref[2, group], w_ref[2], NT)
        store_group(dh_ref, group, size, total.astype(bf16))
        return carry

    lax.fori_loop(0, groups, step, 0)

    def weights(member, carry):
        total = None
        for group in range(groups):
            part = mm(hidden_ref[group], dqkv_ref[member, group], TN)
            total = part if total is None else total + part
        dw_ref[member] = total.astype(bf16)
        return carry

    lax.fori_loop(0, 3, weights, 0)
    total = None
    for group in range(groups):
        part = mm(ctx_ref[group], dao_ref[group], TN)
        total = part if total is None else total + part
    dw_ref[3] = total.astype(bf16)


def sample_backward(g_ref, dh_ref, x1_ref, x_ref, gain_ref, shift_ref, w_ref, kcode_ref, qkv_ref, ctx_ref, ext_ref, out_ref, dw_ref, dgs_ref, dqkv_ref, hidden_ref, low_ref, dc_ref, gext_ref, kacc_ref, vacc_ref):
    features, samples, width = x_ref.shape
    steps = samples // ROWS
    dgs_ref[...] = jnp.zeros_like(dgs_ref)

    def enter(unit, carry):
        f, rows = unit // steps, chunk(unit % steps, ROWS)
        norm_grad, gain_part, shift_part = layer_norm_back(
            dh_ref[f, rows, :].astype(f32), x1_ref[f, rows, :], gain_ref[1:2]
        )
        dgs_ref[1, 0:1] += gain_part
        dgs_ref[1, 1:2] += shift_part
        grad = g_ref[f, rows, :] + norm_grad
        out_ref[f, rows, :] = grad
        low = grad.astype(bf16)
        low_ref[f, rows, :] = low
        context_grad = mm(low, w_ref[3], NT).astype(bf16)
        dc_ref[f, rows, :] = context_grad
        gext_ref[f, rows, :] = delta_extra(ctx_ref[f, rows, :], context_grad)
        return carry

    lax.fori_loop(0, features * steps, enter, 0)

    def attend(unit, carry):
        f, pair = unit // (width // LANES), unit % (width // LANES)
        lanes = chunk(pair, LANES)

        def query_step(step, inner):
            rows = chunk(step, ROWS)
            query_grad, key_grad, value_grad = attend_pair_back(
                qkv_ref[0, f, rows, lanes],
                qkv_ref[1, f, :, lanes],
                qkv_ref[2, f, :, lanes],
                dc_ref[f, rows, lanes],
                ext_ref[f, rows, :],
                gext_ref[f, rows, :],
                kcode_ref[...],
                pair,
            )
            dqkv_ref[0, f, rows, lanes] = (query_grad * 0.125).astype(bf16)
            first = step == 0
            kacc_ref[...] = jnp.where(first, 0.0, kacc_ref[...]) + key_grad
            vacc_ref[...] = jnp.where(first, 0.0, vacc_ref[...]) + value_grad
            return inner

        lax.fori_loop(0, steps, query_step, 0)
        dqkv_ref[1, f, :, lanes] = kacc_ref[...].astype(bf16)
        dqkv_ref[2, f, :, lanes] = vacc_ref[...].astype(bf16)
        return carry

    kacc_ref[...] = jnp.zeros_like(kacc_ref)
    vacc_ref[...] = jnp.zeros_like(vacc_ref)
    lax.fori_loop(0, features * (width // LANES), attend, 0)

    def leave(unit, carry):
        f, rows = unit // steps, chunk(unit % steps, ROWS)
        total = mm(dqkv_ref[0, f, rows, :], w_ref[0], NT)
        total = total + mm(dqkv_ref[1, f, rows, :], w_ref[1], NT)
        total = total + mm(dqkv_ref[2, f, rows, :], w_ref[2], NT)
        x = x_ref[f, rows, :]
        _, _, hidden = layer_norm(x, gain_ref[0:1], shift_ref[0:1])
        hidden_ref[f, rows, :] = hidden.astype(bf16)
        norm_grad, gain_part, shift_part = layer_norm_back(
            total.astype(bf16).astype(f32), x, gain_ref[0:1]
        )
        dgs_ref[0, 0:1] += gain_part
        dgs_ref[0, 1:2] += shift_part
        out_ref[f, rows, :] += norm_grad
        return carry

    lax.fori_loop(0, features * steps, leave, 0)

    def weights(member, carry):
        total = None
        for f in range(features):
            part = mm(hidden_ref[f], dqkv_ref[member, f], TN)
            total = part if total is None else total + part
        dw_ref[member] = total.astype(bf16)
        return carry

    lax.fori_loop(0, 3, weights, 0)
    total = None
    for f in range(features):
        part = mm(ctx_ref[f], low_ref[f], TN)
        total = part if total is None else total + part
    dw_ref[3] = total.astype(bf16)


def call(body, name, outs, scratch, *operands):
    spec = pl.BlockSpec(memory_space=pltpu.VMEM)
    return pl.pallas_call(
        body,
        name=name,
        out_shape=[jax.ShapeDtypeStruct(shape, kind) for shape, kind in outs],
        in_specs=[spec] * len(operands),
        out_specs=[spec] * len(outs),
        scratch_shapes=[pltpu.VMEM(shape, kind) for shape, kind in scratch],
        compiler_params=pltpu.CompilerParams(vmem_limit_bytes=56 << 20),
    )(*operands)


MESH = pl.DeviceIdType.MESH


def remote(source, target, send_sem, recv_sem, device):
    return pltpu.make_async_remote_copy(
        src_ref=source,
        dst_ref=target,
        send_sem=send_sem,
        recv_sem=recv_sem,
        device_id=device,
        device_id_type=MESH,
    )


def sum_partners(task_devices, feature_devices):
    task, place = lax.axis_index("task"), lax.axis_index("feat")
    chip, core = place // 2, lax.rem(place, 2)
    chips = feature_devices // 2
    pair = [{"feat": place + 1 - 2 * core}]
    tasks = [{"task": lax.rem(task + step, task_devices)} for step in range(1, task_devices)]
    line = [{"feat": 2 * lax.rem(chip + step, chips) + core} for step in range(1, chips)]
    return task, chip, core, pair, tasks, line


def greet(devices):
    barrier = pltpu.get_barrier_semaphore()
    for device in devices:
        pl.semaphore_signal(barrier, inc=1, device_id=device, device_id_type=MESH)


def met(count):
    pl.semaphore_wait(pltpu.get_barrier_semaphore(), count)


def sum_tail(pieces, task_devices, feature_devices, *refs):
    chips = feature_devices // 2
    inputs, small_ref = refs[:pieces], refs[pieces]
    outs, small_out = refs[pieces + 1 : 2 * pieces + 1], refs[2 * pieces + 1]
    own, first, summed, second, third_in, third, sends, recvs, loads, small_got, small_sends, small_recvs = refs[2 * pieces + 2 :]
    task, chip, core, pair, tasks, line = sum_partners(task_devices, feature_devices)
    greet(pair + tasks + line)
    own_loads = [
        pltpu.make_async_copy(inputs[p].at[:, :, core], own.at[p], loads.at[p]) for p in range(pieces)
    ]
    for load in own_loads:
        load.start()
    met(len(pair) + len(tasks) + len(line))

    started = []
    for p in range(pieces):
        copy = remote(inputs[p].at[:, :, 1 - core], first.at[p], sends.at[p, 0], recvs.at[p, 0], pair[0])
        copy.start()
        started.append([copy])
    small_slot = [0]

    def small_exchange(values, devices, index, base):
        copies = []
        for k, device in enumerate(devices):
            copy = remote(values, small_got.at[base + index], small_sends.at[base + k], small_recvs.at[base + k], device)
            copy.start()
            copies.append(copy)
        return copies

    def small_finish(copies, count, base):
        for copy in copies:
            copy.wait()
        total = small_got[base]
        for k in range(1, count):
            total = total + small_got[base + k]
        return total

    small_got[core] = small_ref[...]
    small_copies = small_exchange(small_got.at[core], pair, core, 0)
    for p in range(pieces):
        own_loads[p].wait()
        for copy in started[p]:
            copy.wait()

        def add_core(index, carry, p=p):
            t, z = index // chips, lax.rem(index, chips)
            summed[p, t, z] = (own[p, t, z].astype(f32) + first[p, t, z].astype(f32)).astype(bf16)
            return carry

        lax.fori_loop(0, task_devices * chips, add_core, 0)
        started[p] = []
        for k, device in enumerate(tasks):
            other = lax.rem(task + k + 1, task_devices)
            copy = remote(summed.at[p, other], second.at[p, k], sends.at[p, 1 + k], recvs.at[p, 1 + k], device)
            copy.start()
            started[p].append(copy)
    total = small_finish(small_copies, 2, 0)
    small_got[2 + task] = total
    small_copies = small_exchange(small_got.at[2 + task], tasks, task, 2)
    for p in range(pieces):
        for copy in started[p]:
            copy.wait()

        def add_tasks(z, carry, p=p):
            total = summed[p, task, z].astype(f32)
            for k in range(task_devices - 1):
                total = total + second[p, k, z].astype(f32)
            third_in[p, z] = total.astype(bf16)
            return carry

        lax.fori_loop(0, chips, add_tasks, 0)
        started[p] = []
        for k, device in enumerate(line):
            other = lax.rem(chip + k + 1, chips)
            slot = task_devices + k
            copy = remote(third_in.at[p, other], third.at[p, k], sends.at[p, slot], recvs.at[p, slot], device)
            copy.start()
            started[p].append(copy)
    total = small_finish(small_copies, task_devices, 2)
    base = 2 + task_devices
    small_got[base + chip] = total
    small_copies = small_exchange(small_got.at[base + chip], line, chip, base)
    for p in range(pieces):
        for copy in started[p]:
            copy.wait()
        total = third_in[p, chip].astype(f32)
        for k in range(chips - 1):
            total = total + third[p, k].astype(f32)
        outs[p][...] = total
    small_out[...] = small_finish(small_copies, chips, base)


def sum_everywhere(pieces, small, task_devices, feature_devices):
    chips = feature_devices // 2
    rows, width = pieces[0].shape
    share = rows // (task_devices * feature_devices)
    blocks = [piece.reshape(task_devices, chips, 2, share, width) for piece in pieces]
    count = len(pieces)
    copies = task_devices + chips - 1
    small_copies = 2 + task_devices + chips
    vmem, anywhere = pl.BlockSpec(memory_space=pltpu.VMEM), pl.BlockSpec(memory_space=pl.ANY)
    return pl.pallas_call(
        functools.partial(sum_tail, count, task_devices, feature_devices),
        name="sum_tail",
        out_shape=[jax.ShapeDtypeStruct((share, width), f32)] * count
        + [jax.ShapeDtypeStruct(small.shape, f32)],
        in_specs=[anywhere] * count + [vmem],
        out_specs=[vmem] * (count + 1),
        scratch_shapes=[
            pltpu.VMEM((count, task_devices, chips, share, width), bf16),
            pltpu.VMEM((count, task_devices, chips, share, width), bf16),
            pltpu.VMEM((count, task_devices, chips, share, width), bf16),
            pltpu.VMEM((count, task_devices - 1, chips, share, width), bf16),
            pltpu.VMEM((count, chips, share, width), bf16),
            pltpu.VMEM((count, chips - 1, share, width), bf16),
            pltpu.SemaphoreType.DMA((count, copies)),
            pltpu.SemaphoreType.DMA((count, copies)),
            pltpu.SemaphoreType.DMA((count,)),
            pltpu.VMEM((small_copies,) + small.shape, f32),
            pltpu.SemaphoreType.DMA((small_copies,)),
            pltpu.SemaphoreType.DMA((small_copies,)),
        ],
        compiler_params=pltpu.CompilerParams(
            vmem_limit_bytes=56 << 20, collective_id=0, has_side_effects=True
        ),
    )(*blocks, small)


SIZE = 16


class Place:
    def __init__(self, task_devices, feature_devices):
        self.tasks, self.places = task_devices, feature_devices
        self.chips = feature_devices // 2
        self.task, self.place = lax.axis_index("task"), lax.axis_index("feat")
        self.chip, self.core = self.place // 2, lax.rem(self.place, 2)
        self.far, self.near = self.chip // 2, lax.rem(self.chip, 2)
        self.y, self.x = self.task // 2, lax.rem(self.task, 2)
        self.x_task = {"task": self.task + 1 - 2 * self.x}
        self.y_task = {"task": self.task + 2 - 4 * self.y}
        self.other_core = {"feat": self.place + 1 - 2 * self.core}
        self.near_chip = {"feat": self.place + 2 - 4 * self.near}
        self.far_chip = {"feat": self.place + 4 - 8 * self.far}

    def ring(self, step):
        return lax.rem(self.place + step, self.places)

    def task_partner(self, step):
        return lax.rem(self.task + step, self.tasks)

    def greet(self):
        barrier = pltpu.get_barrier_semaphore()
        for step in range(1, self.places):
            pl.semaphore_signal(barrier, inc=1, device_id={"feat": self.ring(step)}, device_id_type=MESH)
        for step in range(1, self.tasks):
            pl.semaphore_signal(barrier, inc=1, device_id={"task": self.task_partner(step)}, device_id_type=MESH)

    def met(self):
        pl.semaphore_wait(pltpu.get_barrier_semaphore(), self.places - 1 + self.tasks - 1)


class SumStep:
    def __init__(self, step, place, source, own, got, sends, recvs, load):
        self.step = step
        y, x, far, near, core = place.y, place.x, place.far, place.near, place.core
        if step == 1:
            self.mine = [source.at[:, :, :, :, core]]
            parts = [(source.at[:, :, :, :, 1 - core], got, place.other_core)]
        elif step == 2:
            self.mine = [source.at[y, x]]
            parts = []
            for k in range(1, place.tasks):
                other = place.task_partner(k)
                parts.append((source.at[other // 2, lax.rem(other, 2)], got.at[k - 1], {"task": other}))
        elif step == 6:
            self.mine = [source.at[:, x, 0], source.at[y, :, 1]]
            parts = [
                (source.at[:, 1 - x, 0], got.at[0], place.x_task),
                (source.at[1 - y, :, 1], got.at[1], place.y_task),
            ]
        elif step == 7:
            self.mine = [source.at[0, y], source.at[1, x]]
            parts = [
                (source.at[0, 1 - y], got.at[0], place.y_task),
                (source.at[1, 1 - x], got.at[1], place.x_task),
            ]
        elif step == 3:
            self.mine = [source.at[:, near]]
            parts = [(source.at[:, 1 - near], got, place.near_chip)]
        elif step == 4:
            self.mine = [source.at[far]]
            parts = [(source.at[1 - far], got, place.far_chip)]
        else:
            self.mine = [source.at[far, near]]
            parts = []
            for k in range(1, place.chips):
                other = lax.rem(place.chip + k, place.chips)
                parts.append(
                    (source.at[other // 2, lax.rem(other, 2)], got.at[k - 1], {"feat": 2 * other + core})
                )
        self.copies = [
            remote(part, target, sends.at[k], recvs.at[k], device) for k, (part, target, device) in enumerate(parts)
        ]
        self.loads = []
        if own is not None:
            kept = [own] if len(self.mine) == 1 else [own.at[half] for half in range(2)]
            self.loads = [
                pltpu.make_async_copy(part, target, load.at[half])
                for half, (part, target) in enumerate(zip(self.mine, kept))
            ]
            self.mine = kept
        self.got = got

    def start(self):
        for copy in self.copies:
            copy.start()
        for load in self.loads:
            load.start()

    def finish(self, out):
        for load in self.loads:
            load.wait()
        for copy in self.copies:
            copy.wait()
        own, got = self.mine[0], self.got
        if self.step == 1:

            def add_core(index, carry):
                y, x, far = index // 4, lax.rem(index // 2, 2), lax.rem(index, 2)
                out[y, x, far] = own[y, x, far] + got[y, x, far]
                return carry

            lax.fori_loop(0, 8, add_core, 0)
        elif self.step in (2, 5):
            total = own[...].astype(f32)
            for k in range(got.shape[0]):
                total = total + got[k].astype(f32)
            out[...] = total.astype(out.dtype)
        elif self.step in (6, 7):
            for half in range(2):
                out[half] = self.mine[half][...] + got[half]
        elif self.step == 3:
            out[...] = own[...] + got[...]
        else:
            out[...] = own[...].astype(f32) + got[...].astype(f32)


def sum_shapes(step, tasks, share, width):
    block = (share, width)
    if step == 1:
        whole = (2, 2, 2, 2) + block
        return whole, whole, whole, bf16, 1
    if step == 2:
        return (2, 2) + block, (tasks - 1, 2, 2) + block, (2, 2) + block, bf16, tasks - 1
    if step == 6:
        return None, (2, 2, 2) + block, (2, 2, 2) + block, bf16, 2
    if step == 7:
        return (2, 2) + block, (2, 2) + block, (2, 2) + block, bf16, 2
    if step == 3:
        return (2,) + block, (2,) + block, (2,) + block, bf16, 1
    if step == 4:
        return block, block, block, f32, 1
    return block, (3,) + block, block, f32, 3


class Chain:
    def __init__(self, place, steps, points, bufs, source, out):
        self.place, self.steps, self.points, self.bufs, self.out = place, steps, points, bufs, out
        self.at, self.running = 0, False
        self.first = None
        if len(points) > len(steps):
            self.first, self.points = points[0], points[1:]
        self.actions = [None if source is None else self.make(0, source)]
        self.actions += [self.make(at, bufs[at - 1][2]) for at in range(1, len(steps))]

    def make(self, at, source):
        own, got, _, sends, recvs, local_sem = self.bufs[at]
        return SumStep(self.steps[at], self.place, source, own, got, sends, recvs, local_sem)

    def begin(self, source=None):
        if source is not None:
            self.actions[0] = self.make(0, source)
        self.actions[0].start()
        self.running = True

    def reached(self, point):
        if self.first is not None and point == self.first:
            self.begin()
            return
        if not self.running or self.points[self.at] != point:
            return
        self.actions[self.at].finish(self.bufs[self.at][2])
        self.at += 1
        if self.at < len(self.steps):
            self.actions[self.at].start()
            return
        self.running = False
        if self.out is not None:
            self.flush().start()

    def flush(self):
        return pltpu.make_async_copy(self.bufs[-1][2], self.out, self.bufs[-1][5].at[2])


class Box:
    def __init__(self, place, bufs, loads, outs, out_bufs, flush_sem, chains):
        self.place, self.bufs, self.loads = place, bufs, loads
        self.outs, self.out_bufs, self.flush_sem = outs, out_bufs, flush_sem
        self.chains = chains
        self.waited, self.flushed = set(), []

    def start(self, *indices):
        for index in indices:
            if isinstance(index, tuple):
                for part in index[1:]:
                    self.loads[index[0]].one(part).start()
                continue
            for copy in self.loads[index]:
                copy.start()

    def use(self, *indices):
        found = []
        for index in indices:
            if index not in self.waited:
                self.waited.add(index)
                for copy in self.loads[index]:
                    copy.wait()
            found.append(self.bufs[index])
        return found if len(found) > 1 else found[0]

    def part(self, index, part):
        self.waited.add(index)
        self.loads[index].one(part).wait()

    def out(self, *indices):
        found = [self.out_bufs[index] for index in indices]
        return found if len(found) > 1 else found[0]

    def copy_out(self, index, part, view):
        source, target = self.out_bufs[index], self.outs[index]
        if view is not None:
            source, target = view(source, part), view(target, part)
        return pltpu.make_async_copy(source, target, self.flush_sem.at[index, part])

    def flush(self, *indices):
        for index in indices:
            self.copy_out(index, 0, None).start()
            self.flushed.append((index, 0, None))

    def flush_part(self, index, part, view):
        self.copy_out(index, part, view).start()
        if (index, 0, view) not in self.flushed:
            self.flushed += [(index, at, view) for at in range(4)]

    def ready(self):
        self.place.met()
        for chain in self.chains:
            if chain.actions[0] is not None and chain.first is None:
                chain.begin()

    def point(self, name):
        for chain in self.chains:
            chain.reached(name)

    def end(self):
        for index, part, view in self.flushed:
            self.copy_out(index, part, view).wait()
        for chain in self.chains:
            if chain.out is not None:
                chain.flush().wait()


class Parts:
    def __init__(self, source, target, view, count, sem):
        self.source, self.target, self.view, self.count, self.sem = source, target, view, count, sem

    def one(self, part):
        if self.view is None:
            return pltpu.make_async_copy(self.source, self.target, self.sem.at[0])
        return pltpu.make_async_copy(self.view(self.source, part), self.view(self.target, part), self.sem.at[part])

    def __iter__(self):
        return iter([self.one(part) for part in range(self.count)])


def fused(body, name, place_sizes, ins, outs, scratch, sums, share_shape, identity):
    tasks, places = place_sizes
    anywhere = pl.BlockSpec(memory_space=pltpu.HBM)
    scalar = pl.BlockSpec(memory_space=pltpu.SMEM)
    buffers = []
    ins = [tuple(item) + (None, 1) if len(item) == 2 else item for item in ins]
    for array, layer, _, _ in ins:
        if layer not in ("scalar", "raw"):
            depth = 0 if layer is None else len(layer) if isinstance(layer, tuple) else 1
            buffers.append(pltpu.VMEM(array.shape[depth:], array.dtype))
    out_buffers = [pltpu.VMEM(shape, kind) for shape, kind in outs]
    sum_results, sum_scratch, sum_arrays = [], [], []
    chain_layout = []
    for steps, _, array, goes_out in sums:
        share, width = share_shape if array is None else array.shape[-2:]
        for at, step in enumerate(steps):
            own, got, result, kind, copies = sum_shapes(step, tasks, share, width)
            loaded = at == 0 and array is not None
            chain_layout.append(loaded)
            sum_scratch += [pltpu.VMEM(own, bf16)] if loaded else []
            sum_scratch += [
                pltpu.VMEM(got, bf16),
                pltpu.VMEM(result, kind),
                pltpu.SemaphoreType.DMA((copies,)),
                pltpu.SemaphoreType.DMA((copies,)),
                pltpu.SemaphoreType.DMA((3,)),
            ]
        if goes_out:
            sum_results.append(jax.ShapeDtypeStruct(result, kind))
        if array is not None:
            sum_arrays.append(array)
    flat_scratch = []
    for item in scratch:
        flat_scratch += list(item) if isinstance(item, tuple) else [item]
    everything = buffers + out_buffers + flat_scratch + sum_scratch
    def kernel(*refs):
        rest = list(refs)

        def pop(count):
            taken = rest[:count]
            del rest[:count]
            return taken

        in_refs, sum_refs = pop(len(ins)), pop(len(sum_arrays))
        out_refs, sum_outs = pop(len(outs)), pop(len(sum_results))
        flat_in = pop(len(buffers))
        out_bufs = pop(len(out_buffers))
        user = [tuple(pop(len(item))) if isinstance(item, tuple) else pop(1)[0] for item in scratch]
        layout = list(chain_layout)
        chain_bufs = [
            [pop(6) if layout.pop(0) else [None] + pop(5) for _ in steps] for steps, _, _, _ in sums
        ]
        load_sem, flush_sem = pop(2)
        place = Place(tasks, places)
        loads, bufs = [], []
        for index, (array, layer, view, count) in enumerate(ins):
            if layer in ("scalar", "raw"):
                loads.append([])
                bufs.append(in_refs[index])
                continue
            bufs.append(flat_in.pop(0))
            source = in_refs[index]
            if layer is not None:
                source = source.at[layer]
            loads.append(Parts(source, bufs[-1], view, count, load_sem.at[index]))
        place.greet()
        chains = []
        for (steps, points, array, goes_out), chain_buf in zip(sums, chain_bufs):
            source = None if array is None else sum_refs.pop(0)
            chains.append(Chain(place, steps, points, chain_buf, source, sum_outs.pop(0) if goes_out else None))
        box = Box(place, bufs, loads, out_refs, out_bufs, flush_sem, chains)
        body(box, *user)
        box.end()

    return pl.pallas_call(
        kernel,
        name=name,
        out_shape=[jax.ShapeDtypeStruct(shape, kind) for shape, kind in outs] + sum_results,
        in_specs=[scalar if layer == "scalar" else anywhere for _, layer, _, _ in ins] + [anywhere] * len(sum_arrays),
        out_specs=[anywhere] * (len(outs) + len(sum_results)),
        scratch_shapes=everything
        + [pltpu.SemaphoreType.DMA((len(ins), 8)), pltpu.SemaphoreType.DMA((len(outs), 4))],
        compiler_params=pltpu.CompilerParams(
            vmem_limit_bytes=63 << 20, collective_id=identity, has_side_effects=True
        ),
    )(*[item[0] for item in ins], *sum_arrays)


def cross(ref, unit):
    block = ref[:, :, chunk(unit, SIZE), :]
    return block.reshape(block.shape[0] * block.shape[1] * SIZE, block.shape[3])


def put_cross(ref, unit, rows):
    first, second, _, width = ref.shape
    ref[:, :, chunk(unit, SIZE), :] = rows.reshape(first, second, SIZE, width)


def cross_view(ref, unit):
    return ref.at[:, :, chunk(unit, SIZE), :]


def first_view(ref, unit):
    return ref.at[unit]


def last_view(ref, unit):
    return ref.at[(slice(None),) * (len(ref.shape) - 1) + (chunk(unit, LANES),)]


def own_rows(ref, f, unit, size, lanes=slice(None)):
    block = ref[f, :, chunk(unit, size), lanes]
    return block.reshape(block.shape[0] * size, block.shape[2])


def block_rows(ref, f, unit, per, lanes=slice(None)):
    block = ref[f, chunk(unit, per), :, lanes]
    return block.reshape(per * block.shape[1], block.shape[2])


def all_rows(ref, f, lanes=slice(None)):
    block = ref[f, :, :, lanes]
    return block.reshape(block.shape[0] * block.shape[1], block.shape[2])


def pair_lanes(pair):
    return slice(pair * LANES, pair * LANES + LANES)


def fill_sample_codes(size, query_ref, key_ref):
    if query_ref is not None:
        lanes = lax.broadcasted_iota(jnp.int32, query_ref.shape, 1)
        query_ref[...] = jnp.where(lanes == CODE_LANE, 1.0, 0.0).astype(bf16)
    lanes = lax.broadcasted_iota(jnp.int32, key_ref.shape, 1)
    rows = lax.broadcasted_iota(jnp.int32, key_ref.shape, 0)
    key_ref[...] = jnp.where((lanes == CODE_LANE) & (rows >= size), masked_score, 0.0).astype(bf16)


def fill_feature_codes(count, query_ref, key_ref):
    lanes = lax.broadcasted_iota(jnp.int32, key_ref.shape, 1) - CODE_LANE
    rows = lax.broadcasted_iota(jnp.int32, key_ref.shape, 0)
    own = lanes == (rows & (SIZE - 1))
    inside = (lanes >= 0) & (lanes < SIZE)
    if query_ref is not None:
        query_ref[...] = jnp.where(own, 1.0, 0.0).astype(bf16)
    live = rows < count * SIZE
    key_ref[...] = jnp.where(inside & ~(own & live), masked_score, 0.0).astype(bf16)


def forward_layer(layer, last, box, sq_ref, sk_ref, fq_ref, fk_ref, h2_ref, swapped_ref, a_ref, back_ref, sends, recvs, self_sem, back_sends, back_recvs, *raw):
    place = box.place
    x1_ref, qkv_ref, ctx_ref, ext_ref = box.out(0, 1, 2, 3)
    hidden_ref, fqkv_ref, fctx_ref, fext_ref, x2_ref, x3_ref, u_ref, h1_ref = box.out(4, 5, 6, 7, 8, 9, 10, 11)
    active_ref, h3_ref = box.out(12, 13)
    box.start(3, 4, (2, 0), 5)
    size_ref, count_ref = box.use(0, 1)
    fill_sample_codes(size_ref[0], sq_ref, sk_ref)
    fill_feature_codes(count_ref[0], fq_ref, fk_ref)
    gain_ref, shift_ref, w_ref = box.use(3, 4, 5)
    x_ref = box.bufs[2]
    features, blocks, own, width = x_ref.shape
    box.start((2, *range(1, features)))
    per = ROWS // own
    steps = blocks // per
    size = ROWS // blocks
    units = own // size
    pairs = width // LANES

    def gain(index):
        return gain_ref[index, layer : layer + 1, :], shift_ref[index, layer : layer + 1, :]

    def project(f):
        box.part(2, f)

        def rows(part, carry):
            _, _, hidden = layer_norm(block_rows(x_ref, f, part, per), *gain(0))
            hidden = hidden.astype(bf16)
            h1_ref[f, chunk(part, per), :, :] = hidden.reshape(per, own, width)
            for member in range(3):
                out = mm(hidden, w_ref[member]).astype(bf16)
                if member == 0:
                    out = out * jnp.asarray(0.125, bf16)
                qkv_ref[member, f, chunk(part, per), :, :] = out.reshape(per, own, width)
            return carry

        lax.fori_loop(0, steps, rows, 0)

    def copies(unit):
        part, f = unit // features, lax.rem(unit, features)
        found = [
            remote(
                h2_ref.at[f, place.ring(k), chunk(part, size), :],
                swapped_ref.at[place.place, f, chunk(part, size), :],
                sends.at[unit, k - 1],
                recvs.at[unit, k - 1],
                {"feat": place.ring(k)},
            )
            for k in range(1, place.places)
        ]
        keep = pltpu.make_async_copy(
            h2_ref.at[f, place.place, chunk(part, size), :],
            swapped_ref.at[place.place, f, chunk(part, size), :],
            self_sem.at[unit],
        )
        return found, keep

    def attend(unit, carry):
        part, f = unit // features, lax.rem(unit, features)

        @pl.when(unit < features)
        def _():
            project(unit)

        code = sq_ref[...]
        extras = code.astype(f32)
        for pair in range(pairs):
            lanes = pair_lanes(pair)
            context, extras = attend_pair(
                own_rows(qkv_ref.at[0], f, part, size, lanes),
                all_rows(qkv_ref.at[1], f, lanes),
                all_rows(qkv_ref.at[2], f, lanes),
                code,
                sk_ref[...],
                pair,
                extras,
            )
            ctx_ref[f, :, chunk(part, size), lanes] = context.reshape(blocks, size, LANES)
        ext_ref[f, :, chunk(part, size), :] = extras.astype(bf16).reshape(blocks, size, LANES)
        x1 = own_rows(x_ref, f, part, size) + mm(own_rows(ctx_ref, f, part, size), w_ref[3])
        x1_ref[f, :, chunk(part, size), :] = x1.reshape(blocks, size, width)
        _, _, hidden = layer_norm(x1, *gain(1))
        h2_ref[f, :, chunk(part, size), :] = hidden.astype(bf16).reshape(blocks, size, width)

        @pl.when(unit == 0)
        def _():
            box.ready()
            box.start(6, 7, 8, 9, 10)
            if last:
                box.start(11)

        found, keep = copies(unit)
        for copy in found:
            copy.start()
        keep.start()
        return carry

    lax.fori_loop(0, features * units, attend, 0)
    box.flush(0, 1, 2, 3, 11)
    fw_ref = box.use(6)
    groups = own // SIZE
    shared = size // SIZE

    def back_copies(group):
        return [
            remote(
                a_ref.at[place.ring(k), :, chunk(group, SIZE), :],
                back_ref.at[:, place.place, chunk(group, SIZE), :],
                back_sends.at[group, k - 1],
                back_recvs.at[group, k - 1],
                {"feat": place.ring(k)},
            )
            for k in range(1, place.places)
        ]

    def feature(group, carry):
        @pl.when(lax.rem(group, shared) == 0)
        def _():
            for f in range(features):
                found, keep = copies((group // shared) * features + f)
                for copy in found:
                    copy.wait_recv()
                keep.wait()

        hidden = cross(swapped_ref, group)
        hidden_ref[group] = hidden
        for member in range(3):
            out = mm(hidden, fw_ref[member]).astype(bf16)
            if member == 0:
                out = out * jnp.asarray(0.125, bf16)
            fqkv_ref[group, member] = out
        code = fq_ref[...]
        extras = code.astype(f32)
        for pair in range(pairs):
            lanes = pair_lanes(pair)
            context, extras = attend_pair(
                fqkv_ref[group, 0, :, lanes],
                fqkv_ref[group, 1, :, lanes],
                fqkv_ref[group, 2, :, lanes],
                code,
                fk_ref[...],
                pair,
                extras,
            )
            fctx_ref[group, :, lanes] = context
        fext_ref[group] = extras.astype(bf16)
        put_cross(a_ref, group, mm(fctx_ref[group], fw_ref[3]).astype(bf16))
        for copy in back_copies(group):
            copy.start()
        back_ref[:, place.place, chunk(group, SIZE), :] = a_ref[place.place, :, chunk(group, SIZE), :]
        return carry

    lax.fori_loop(0, groups, feature, 0)
    box.flush(4, 5, 6, 7)
    if last:
        raw_ref, og_ref = raw[0], box.out(14)
        raw_ref[...] = box.use(11)[...].astype(f32)
        period = features * pairs
        for f in range(features):
            for block in range(pairs):
                rows = raw_ref[pl.ds(block * features + f, blocks * own, stride=period), :]
                og_ref[f, :, :, pair_lanes(block)] = rows.reshape(blocks, own, LANES)
        box.flush(14)
    up_ref, upb_ref, down_ref, downb_ref = box.use(7, 8, 9, 10)
    hidden_width = up_ref.shape[1]

    def dense(group, carry):
        for copy in back_copies(group):
            copy.wait_recv()
        x2 = cross(x1_ref, group) + cross(back_ref, group).astype(f32)
        put_cross(x2_ref, group, x2)
        _, _, hidden = layer_norm(x2, *gain(2))
        hidden = hidden.astype(bf16)
        h3_ref[group] = hidden
        for part in range(hidden_width // 512):
            cols = slice(part * 512, part * 512 + 512)
            u = mm(hidden, up_ref[:, cols]) + upb_ref[layer : layer + 1, cols]
            bent = gelu_parts(u)
            both = 0.5 * (1.0 + bent)
            active_ref[group, :, cols] = (u * both).astype(bf16)
            slope = both + u * (1.0 - bent * bent) * (0.3989422804014327 + 0.05351611220146811 * u * u)
            u_ref[group, :, cols] = slope.astype(bf16)
        total = x2 + downb_ref[layer : layer + 1, :] + mm(active_ref[group], down_ref[...])
        put_cross(x3_ref, group, total)
        box.flush_part(8, group, cross_view)
        box.flush_part(9, group, cross_view)
        box.flush_part(10, group, first_view)
        box.flush_part(12, group, first_view)
        box.flush_part(13, group, first_view)
        return carry

    lax.fori_loop(0, groups, dense, 0)

    def settle(unit, carry):
        for copy in copies(unit)[0]:
            copy.wait_send()
        return carry

    lax.fori_loop(0, features * units, settle, 0)

    def settle_back(group, carry):
        for copy in back_copies(group):
            copy.wait_send()
        return carry

    lax.fori_loop(0, groups, settle_back, 0)


def pieces_of(values):
    first = values.astype(bf16)
    rest = values - first.astype(f32)
    second = rest.astype(bf16)
    return first, second, (rest - second.astype(f32)).astype(bf16)


def exact(left, right, dims):
    first, second, third = pieces_of(right)
    return mm(left, first, dims) + mm(left, second, dims) + mm(left, third, dims)


def exact_left(left, right, dims):
    first, second, third = pieces_of(left)
    return mm(first, right, dims) + mm(second, right, dims) + mm(third, right, dims)


def read_out(box, ins, later, outs, x_ref, x_load, g_ref, reading_ref, got_ref, bins_ref, counted_ref, read_ref, weight_ref, sends, recvs):
    place = box.place
    shapes_ref, loss_ref, rgrad_ref = box.out(*outs)
    read_ref[...] = jnp.zeros_like(read_ref)
    size_ref, count_ref, label_ref, index_ref, population_ref, narrow_ref = box.use(*ins)
    x_load.wait()
    box.start(*later)
    read_ref[0 : narrow_ref.shape[0], :] = narrow_ref[...]
    features, blocks, own, width = x_ref.shape
    samples = blocks * own
    bins = population_ref.shape[1]
    size, count = size_ref[0], count_ref[0]
    mask = (lax.broadcasted_iota(jnp.int32, (1, samples), 1) < size).astype(f32)
    task_size = jnp.zeros((1, samples), f32) + size.astype(f32)
    level = lax.broadcasted_iota(jnp.int32, (bins, bins), 0)
    diagonal = (level == lax.broadcasted_iota(jnp.int32, (bins, bins), 1)).astype(f32)
    live = [
        jnp.where(place.place * features + f < count, 1.0, 0.0) for f in range(features)
    ]
    logits = None
    for f in range(features):
        reading = x_ref[f].reshape(samples, width).astype(bf16)
        reading_ref[f] = reading.reshape(blocks, own, width)
        projected = mm(reading, read_ref[...], NT)
        onehot = (lax.broadcasted_iota(jnp.int32, (bins, samples), 0) == index_ref[f : f + 1, :]).astype(f32)
        bins_ref[f] = onehot.astype(bf16)
        chosen = onehot * mask
        counted = jnp.maximum(jnp.sum(chosen, axis=1, keepdims=True), 1.0)
        counted_ref[f] = jnp.broadcast_to(counted, (bins, LANES))
        means = exact(chosen.astype(bf16), projected, NN) / counted
        weight = jnp.sum(diagonal * population_ref[f : f + 1, :].astype(f32), axis=1, keepdims=True)
        weight_ref[f] = jnp.broadcast_to(weight, (bins, LANES))
        weight = weight_ref[f]
        centre = jnp.sum(weight * means, axis=0, keepdims=True) / jnp.sum(weight, axis=0, keepdims=True)
        shapes = means - centre
        shapes_ref[f] = shapes
        part = exact_left(shapes, bins_ref[f], TN)[:SIZE] * live[f]
        logits = part if logits is None else logits + part
    spans = range(samples // LANES)
    got_ref[place.place] = jnp.concatenate([logits[0:CLASSES, pair_lanes(span)] for span in spans], axis=0)
    box.ready()
    copies = [
        remote(
            got_ref.at[place.place],
            got_ref.at[place.place],
            sends.at[k - 1],
            recvs.at[k - 1],
            {"feat": place.ring(k)},
        )
        for k in range(1, place.places)
    ]
    for copy in copies:
        copy.start()
    for copy in copies:
        copy.wait()
    total = got_ref[0]
    for k in range(1, place.places):
        total = total + got_ref[k]
    rows_left = jnp.zeros((SIZE - CLASSES, LANES), f32)
    logits = jnp.concatenate(
        [
            jnp.concatenate([total[span * CLASSES : span * CLASSES + CLASSES], rows_left], axis=0)
            for span in spans
        ],
        axis=1,
    )
    class_row = lax.broadcasted_iota(jnp.int32, logits.shape, 0)
    inside = class_row < CLASSES
    peak = jnp.max(jnp.where(inside, logits, masked_score), axis=0, keepdims=True)
    weights = jnp.where(inside, jnp.exp(jnp.where(inside, logits - peak, 0.0)), 0.0)
    weight_sum = jnp.sum(weights, axis=0, keepdims=True)
    log_total = peak + jnp.log(weight_sum)
    own_class = (class_row == label_ref[...]).astype(f32)
    picked = jnp.sum(logits * own_class, axis=0, keepdims=True)
    losses = mask * (log_total - picked)
    loss_ref[...] = jnp.broadcast_to(
        jnp.sum(losses, axis=1, keepdims=True) / task_size[:, 0:1], loss_ref.shape
    )
    logit_grad = mask * (weights / weight_sum - own_class) / task_size
    pad = jnp.zeros((LANES - SIZE, samples), f32)
    total = None
    for f in range(features):
        grad_rows = jnp.concatenate([logit_grad * live[f], pad], axis=0)
        shape_grad = exact(bins_ref[f], grad_rows, NT)
        weight = weight_ref[f]
        means_grad = shape_grad - weight / jnp.sum(weight, axis=0, keepdims=True) * jnp.sum(
            shape_grad, axis=0, keepdims=True
        )
        chosen = (bins_ref[f].astype(f32) * mask).astype(bf16)
        proj_grad = exact(chosen, means_grad / counted_ref[f], TN).astype(bf16)
        part = mm(proj_grad, all_rows(reading_ref, f), TN)[:SIZE]
        total = part if total is None else total + part
        if f == 0:
            box.use(1)
        back = mm(proj_grad, read_ref[...]).reshape(blocks, own, width)
        g_ref[f] = g_ref[f] + back
    rgrad_ref[...] = total
    box.flush(*outs)


def dense_feature_backward(layer, box, fk_ref, send_ref, ugrad_ref, rowgrad_ref, dup_ref, ddown_ref, arriving_ref, dc_ref, dh_ref, back_ref, dwf_ref, sends, recvs, self_sem, back_sends, back_recvs, *head):
    place = box.place
    g1_ref, small_ref, sdc_ref, sext_ref, slow_ref = box.out(0, 1, 2, 3, 4)
    if head:
        x_load = pltpu.make_async_copy(box.bufs[18], g1_ref, head[-1])
        box.start(19, 20, 21, 22)
        x_load.start()
    else:
        box.start(6, 7, (1, 0), 2, (3, 0), 4, (5, 0))
    small_ref[...] = jnp.zeros_like(small_ref)
    fill_feature_codes(box.use(0)[0], None, fk_ref)
    if not head:
        box.use(6, 7, 2, 4)
    gain_ref, shift_ref, down_ref, up_ref = box.bufs[6], box.bufs[7], box.bufs[2], box.bufs[4]
    g_ref, slope_ref, x2_ref = box.bufs[1], box.bufs[3], box.bufs[5]
    active_ref, hidden3_ref = box.bufs[16], box.bufs[17]
    if not head:
        box.start((1, 1, 2, 3), (3, 1, 2, 3), (5, 1, 2, 3))
    else:
        later = (1, 6, 7, 2, 3, 4, 5, 17, 16, 8, 9, 10, 11, 12, 13, 14, 15)
        read_out(box, (23, 0, 19, 20, 21, 22), later, (5, 6, 7), g1_ref, x_load, g_ref, send_ref, *head[:-1])
        box.use(6, 7, 2, 4)
    features, blocks, own, width = g_ref.shape
    hidden_width = up_ref.shape[1]
    groups = own // SIZE
    parts = hidden_width // 512
    pairs = width // LANES

    def copies(group):
        found = [
            remote(
                send_ref.at[:, place.ring(k), chunk(group, SIZE), :],
                arriving_ref.at[place.place, :, chunk(group, SIZE), :],
                sends.at[group, k - 1],
                recvs.at[group, k - 1],
                {"feat": place.ring(k)},
            )
            for k in range(1, place.places)
        ]
        keep = pltpu.make_async_copy(
            send_ref.at[:, place.place, chunk(group, SIZE), :],
            arriving_ref.at[place.place, :, chunk(group, SIZE), :],
            self_sem.at[group],
        )
        return found, keep

    def dense(group, carry):
        rows = chunk(group, ROWS)
        if not head:
            box.part(1, group)
        box.part(3, group)
        box.part(5, group)
        grad = cross(g_ref, group)
        low = grad.astype(bf16)
        rowgrad_ref[rows, :] = low
        small_ref[parts : parts + 1] += jnp.sum(low.astype(f32), axis=0, keepdims=True)
        for part in range(parts):
            cols = slice(part * 512, part * 512 + 512)
            active_grad = mm(low, down_ref[cols, :], NT).astype(bf16).astype(f32)
            ugrad = (active_grad * slope_ref[group, :, cols].astype(f32)).astype(bf16)
            ugrad_ref[rows, cols] = ugrad
            small_ref[part : part + 1] += jnp.sum(ugrad.astype(f32), axis=0, keepdims=True)
        hidden_grad = mm(ugrad_ref[rows, :], up_ref[...], NT)
        x2 = cross(x2_ref, group)
        gain = gain_ref[2, layer : layer + 1, :]
        norm_grad, gain_part, shift_part = layer_norm_back(hidden_grad.astype(bf16).astype(f32), x2, gain)
        small_ref[parts + 1 : parts + 2] += gain_part
        small_ref[parts + 2 : parts + 3] += shift_part
        grad = grad + norm_grad
        put_cross(g1_ref, group, grad)
        put_cross(send_ref, group, grad.astype(bf16))
        if not head:

            @pl.when(group == 0)
            def _():
                box.ready()
                box.start(17, 16, 8, 9, 10, 11, 12, 13, 14, 15)

        found, keep = copies(group)
        for copy in found:
            copy.start()
        keep.start()
        return carry

    lax.fori_loop(0, groups, dense, 0)

    def up_weights(part, carry):
        cols = chunk(part, 512)
        out = mm(ugrad_ref[:, cols], hidden3_ref[...], TN)
        dup_ref[part // 2, lax.rem(part, 2)] = out.astype(bf16).reshape(dup_ref.shape[2:])
        return carry

    def down_weights(part, carry):
        cols = chunk(part, 512)
        out = mm(active_ref[:, cols], rowgrad_ref[...], TN)
        ddown_ref[part // 2, lax.rem(part, 2)] = out.astype(bf16).reshape(ddown_ref.shape[2:])
        return carry

    box.use(16, 17)
    lax.fori_loop(0, parts, up_weights, 0)
    box.chains[0].begin(dup_ref)
    lax.fori_loop(0, parts, down_weights, 0)
    box.point("dense")
    box.chains[1].begin(ddown_ref)
    grads_ref = active_ref
    w_ref, qkv_ref, ctx_ref, ext_ref = box.use(8, 9, 10, 11)

    def back_copies(group):
        return [
            remote(
                dh_ref.at[place.ring(k), :, chunk(group, SIZE), :],
                back_ref.at[:, place.place, chunk(group, SIZE), :],
                back_sends.at[group, k - 1],
                back_recvs.at[group, k - 1],
                {"feat": place.ring(k)},
            )
            for k in range(1, place.places)
        ]

    def feature(group, carry):
        found, keep = copies(group)
        for copy in found:
            copy.wait_recv()
        keep.wait()
        rows = chunk(group, ROWS)
        dao = cross(arriving_ref, group)
        grads_ref[rows, 3 * width : 4 * width] = dao
        context_grad = mm(dao, w_ref[3], NT).astype(bf16)
        dc_ref[...] = context_grad
        grad_extra = delta_extra(ctx_ref[group], context_grad)
        for pair in range(pairs):
            lanes = pair_lanes(pair)
            query_grad, key_grad, value_grad = attend_pair_back(
                qkv_ref[group, 0, :, lanes],
                qkv_ref[group, 1, :, lanes],
                qkv_ref[group, 2, :, lanes],
                dc_ref[:, lanes],
                ext_ref[group],
                grad_extra,
                fk_ref[...],
                pair,
            )
            for member, grad in enumerate((query_grad * 0.125, key_grad, value_grad)):
                at = member * width + pair * LANES
                grads_ref[rows, at : at + LANES] = grad.astype(bf16)
        total = mm(grads_ref[rows, 0:width], w_ref[0], NT)
        total = total + mm(grads_ref[rows, width : 2 * width], w_ref[1], NT)
        total = total + mm(grads_ref[rows, 2 * width : 3 * width], w_ref[2], NT)
        put_cross(dh_ref, group, total.astype(bf16))
        for copy in back_copies(group):
            copy.start()
        back_ref[:, place.place, chunk(group, SIZE), :] = dh_ref[place.place, :, chunk(group, SIZE), :]

        for at in range(groups):

            @pl.when(group == at)
            def _(at=at):
                box.point(at)

        return carry

    lax.fori_loop(0, groups, feature, 0)
    hidden_ref = box.use(12)

    def weights(member, carry):
        hidden = hidden_ref[...].reshape(groups * ROWS, width)
        out = mm(hidden, grads_ref[:, chunk(member, width)], TN)
        dwf_ref[member // 2, lax.rem(member, 2)] = out.astype(bf16).reshape(dwf_ref.shape[2:])
        return carry

    lax.fori_loop(0, 3, weights, 0)
    context = ctx_ref[...].reshape(groups * ROWS, width)
    out = mm(context, grads_ref[:, 3 * width : 4 * width], TN)
    dwf_ref[1, 1] = out.astype(bf16).reshape(dwf_ref.shape[2:])
    box.chains[2].begin(dwf_ref)
    box.point("weights")
    x1_ref, wo_ref, sctx_ref = box.use(13, 14, 15)

    def enter(group, carry):
        for copy in back_copies(group):
            copy.wait_recv()
        norm_grad, gain_part, shift_part = layer_norm_back(
            cross(back_ref, group).astype(f32), cross(x1_ref, group), gain_ref[1, layer : layer + 1, :]
        )
        small_ref[parts + 3 : parts + 4] += gain_part
        small_ref[parts + 4 : parts + 5] += shift_part
        grad = cross(g1_ref, group) + norm_grad
        put_cross(g1_ref, group, grad)
        low = grad.astype(bf16)
        put_cross(slow_ref, group, low)
        context_grad = mm(low, wo_ref[...], NT).astype(bf16)
        put_cross(sdc_ref, group, context_grad)
        put_cross(sext_ref, group, delta_extra(cross(sctx_ref, group), context_grad))
        box.flush_part(0, group, cross_view)
        box.flush_part(2, group, cross_view)
        box.flush_part(3, group, cross_view)
        box.flush_part(4, group, cross_view)

        for at in range(groups):

            @pl.when(group == at)
            def _(at=at):
                box.point(10 + at)

        return carry

    lax.fori_loop(0, groups, enter, 0)
    box.flush(1)
    box.point("end")

    def settle(group, carry):
        for copy in copies(group)[0]:
            copy.wait_send()
        for copy in back_copies(group):
            copy.wait_send()
        return carry

    lax.fori_loop(0, groups, settle, 0)


def sample_backward_last(layer, last, box, sk_ref, dqkv_ref, *tail):
    place = box.place
    g0_ref, small_ref = box.out(0, 1)
    box.start((1, 0), (2, 0), 3, 4)
    small_ref[...] = jnp.zeros_like(small_ref)
    fill_sample_codes(box.use(0)[0], None, sk_ref)
    qkv_ref, dc_ref = box.bufs[1], box.bufs[2]
    features, blocks, own, width = dc_ref.shape
    samples = blocks * own
    per = ROWS // own
    steps = blocks // per
    pairs = width // LANES
    total_rows = features * samples
    if last:
        dw_ref, bufs_1, bufs_2, bufs_3, *small_bufs = tail
        share_ref = box.out(3)
    else:
        dw_ref, *small_bufs = tail
    exchange = SmallSums(place, last, *small_bufs)
    ext_ref, gext_ref = box.use(3, 4)
    box.ready()
    box.start((1, 1, 2, 3), (2, 1, 2, 3), 9, 10, 11, 12, 13)

    def step_of(step, pair):
        got_ref, _, sends, recvs = (bufs_1, bufs_2, bufs_3)[step - 1]
        source = dw_ref.at[pair] if step == 1 else (bufs_1, bufs_2)[step - 2][1].at[pair]
        return SumStep(5 if step == 3 else step, place, source, None, got_ref.at[pair], sends.at[pair], recvs.at[pair], None)

    def pass_on(step, pair):
        step_of(step, pair).finish((bufs_1, bufs_2, bufs_3)[step - 1][1].at[pair])
        if step < 3:
            step_of(step + 1, pair).start()

    def attend(pair, carry):
        lanes = chunk(pair, LANES)
        box.part(1, pair)
        box.part(2, pair)
        for f in range(features):
            key_total = value_total = None
            for step in range(steps):
                rows = slice(f * samples + step * ROWS, f * samples + step * ROWS + ROWS)
                query_grad, key_grad, value_grad = attend_pair_back(
                    block_rows(qkv_ref.at[0], f, step, per, lanes),
                    all_rows(qkv_ref.at[1], f, lanes),
                    all_rows(qkv_ref.at[2], f, lanes),
                    block_rows(dc_ref, f, step, per, lanes),
                    block_rows(ext_ref, f, step, per),
                    block_rows(gext_ref, f, step, per),
                    sk_ref[...],
                    pair,
                )
                dqkv_ref[0, rows, lanes] = (query_grad * 0.125).astype(bf16)
                key_total = key_grad if key_total is None else key_total + key_grad
                value_total = value_grad if value_total is None else value_total + value_grad
            rows = slice(f * samples, f * samples + samples)
            dqkv_ref[1, rows, lanes] = key_total.astype(bf16)
            dqkv_ref[2, rows, lanes] = value_total.astype(bf16)

        for at in range(1, pairs):

            @pl.when(pair == at)
            def _(at=at):
                box.point(at)

        @pl.when(pair == 0)
        def _():
            box.start(5, 6, 7, 8)
            dense_rows, other_rows = box.use(12, 13)
            if last:
                exchange.start([(0, 9, dense_rows, 9), (9, 11, other_rows, 2)])
            else:
                exchange.start([(0, 9, dense_rows, 9), (9, 9 + SIZE, other_rows, SIZE)])

        for stage in range(1, 4):

            @pl.when(pair == stage)
            def _(stage=stage):
                exchange.move(stage)

        if not last:
            return carry

        @pl.when(pair == 0)
        def _():
            box.use(9, 10, 11)

        hidden = box.bufs[9][...].reshape(total_rows, width)
        context = box.bufs[10][...].reshape(total_rows, width)
        low_ref = box.bufs[11]
        block = dw_ref.shape[3:]
        for member in range(3):
            out = mm(dqkv_ref[member, :, lanes], hidden, TN).T
            dw_ref[pair, member // 2, member % 2] = out.astype(bf16).reshape(block)
        low = low_ref[:, :, :, lanes].reshape(total_rows, LANES)
        dw_ref[pair, 1, 1] = mm(low, context, TN).T.astype(bf16).reshape(block)
        step_of(1, pair).start()

        @pl.when(pair >= 1)
        def _():
            pass_on(1, pair - 1)

        @pl.when(pair >= 2)
        def _():
            pass_on(2, pair - 2)

        return carry

    lax.fori_loop(0, pairs, attend, 0)
    box.point("attend")
    if not last:
        hidden_ref, context_ref, low_ref = box.use(9, 10, 11)

        def weights(member, carry):
            hidden = hidden_ref[...].reshape(total_rows, width)
            out = mm(hidden, dqkv_ref[member], TN)
            dw_ref[member // 2, lax.rem(member, 2)] = out.astype(bf16).reshape(dw_ref.shape[2:])
            return carry

        lax.fori_loop(0, 3, weights, 0)
        context = context_ref[...].reshape(total_rows, width)
        out = mm(context, low_ref[...].reshape(total_rows, width), TN)
        dw_ref[1, 1] = out.astype(bf16).reshape(dw_ref.shape[2:])
        box.chains[-1].begin(dw_ref)
    w_ref, x_ref, gain_ref, g_ref = box.use(5, 6, 7, 8)
    gain = gain_ref[0, layer : layer + 1, :]

    def leave(unit, carry):
        f, part = unit // steps, lax.rem(unit, steps)
        rows = chunk(unit, ROWS)
        total = mm(dqkv_ref[0, rows, :], w_ref[0], NT)
        total = total + mm(dqkv_ref[1, rows, :], w_ref[1], NT)
        total = total + mm(dqkv_ref[2, rows, :], w_ref[2], NT)
        norm_grad, gain_part, shift_part = layer_norm_back(
            total.astype(bf16).astype(f32), block_rows(x_ref, f, part, per), gain
        )
        small_ref[0:1] += gain_part
        small_ref[1:2] += shift_part
        g0_ref[f, chunk(part, per), :, :] = (block_rows(g_ref, f, part, per) + norm_grad).reshape(per, own, width)
        if last:

            @pl.when(unit == 1)
            def _():
                pass_on(1, pairs - 1)

            @pl.when(unit == 2)
            def _():
                pass_on(2, pairs - 2)

        @pl.when(unit == 2)
        def _():
            box.point("leave")
            box.out(2)[...] = exchange.sum(3)
            box.flush(2)

        return carry

    lax.fori_loop(0, features * steps, leave, 0)
    box.flush(0, 1)
    if last:
        exchange.start_late(small_ref)
        pass_on(2, pairs - 1)
        exchange.move(5)
    box.point("end")
    if last:
        for pair in range(pairs):
            pass_on(3, pair)
            share_ref[:, pair_lanes(pair)] = bufs_3[1][pair]
        box.flush(3)
        box.out(4)[...] = exchange.sum(5)
        box.flush(4)


class SmallSums:
    def __init__(self, place, last, packed, early, late, sends, recvs):
        self.packed, self.early, self.late = packed, early, late
        tasks = [{"task": place.task_partner(k)} for k in range(1, place.tasks)]
        ring = [{"feat": place.ring(k)} for k in range(1, place.places)]
        plan = [
            (early, 0, 2, place.core, [place.other_core]),
            (early, 2, place.tasks, place.task, tasks),
            (early, 2 + place.tasks, 2, place.near, [place.near_chip]),
            (early, 4 + place.tasks, 2, place.far, [place.far_chip]),
            (late, 0, place.places, place.place, ring),
            (late, place.places, place.tasks, place.task, tasks),
        ]
        plan = plan if last else plan[:4]
        self.plan, self.copies, at = plan, [], 0
        for buffer, first, count, mine, devices in plan:
            slot = buffer.at[first + mine]
            self.copies.append(
                [remote(slot, slot, sends.at[at + k], recvs.at[at + k], device) for k, device in enumerate(devices)]
            )
            at += len(devices)

    def send(self, stage, rows):
        buffer, first, _, mine, _ = self.plan[stage]
        buffer[first + mine] = rows
        for copy in self.copies[stage]:
            copy.start()

    def start(self, parts):
        self.packed[...] = jnp.zeros_like(self.packed)
        for begin, end, source, count in parts:
            self.packed[begin:end] = source[0:count]
        self.send(0, self.packed[...])

    def start_late(self, rows_ref):
        blocks = [rows_ref[row : row + 1, pair_lanes(block)] for row in range(2) for block in range(4)]
        self.send(4, jnp.concatenate(blocks, axis=0))

    def sum(self, stage):
        buffer, first, count, _, _ = self.plan[stage]
        for copy in self.copies[stage]:
            copy.wait()
        total = buffer[first]
        for k in range(1, count):
            total = total + buffer[first + k]
        return total

    def move(self, stage):
        self.send(stage, self.sum(stage - 1))


def write_out(dense_rows, x_ref, g_ref, *refs):
    refs = list(refs)
    shares, packed_rows, late, bins, loss, outs = refs[:8], refs[8:10], refs[10], refs[11], refs[12], refs[13:26]
    raw_x, raw_g, x_buf, g_buf, load_sem, out_sem = refs[26:]
    outs[12][0] = loss[0, 0]
    for f in range(bins.shape[0]):
        outs[11][:, f, :] = bins[f].T[0:CLASSES]
    features, blocks, own, width = x_ref.shape
    period = features * (width // LANES)
    per = blocks // 4
    rows_part = per * own

    def load(part, which):
        source, target = ((x_ref, x_buf), (g_ref, g_buf))[which]
        view = (slice(None), pl.ds(part * per, per))
        return pltpu.make_async_copy(source.at[view], target.at[view], load_sem.at[which, part])

    def store(part, which):
        source, target = ((raw_x, outs[0]), (raw_g, outs[1]))[which]
        view = pl.ds(part * rows_part * period, rows_part * period)
        return pltpu.make_async_copy(source.at[view], target.at[view], out_sem.at[which, part])

    for part in range(4):
        load(part, 0).start()
        load(part, 1).start()
    for member in range(4):
        outs[2 + member][0] = shares[2 * member][...]
        outs[2 + member][1] = shares[2 * member + 1][...]
    parts = dense_rows - 5
    for layer in range(2):
        packed, at = packed_rows[layer], 0
        for part in range(parts):
            outs[8][layer : layer + 1, part * width : (part + 1) * width] = packed[at + part : at + part + 1]
        outs[9][layer : layer + 1] = packed[at + parts : at + parts + 1]
        for member, row in ((2, parts + 1), (1, parts + 3)):
            outs[6][member, layer : layer + 1] = packed[at + row : at + row + 1]
            outs[7][member, layer : layer + 1] = packed[at + row + 1 : at + row + 2]
    at = dense_rows
    for block in range(4):
        lanes = pair_lanes(block)
        outs[6][0, 0:1, lanes], outs[7][0, 0:1, lanes] = late[block : block + 1], late[4 + block : 5 + block]
    outs[6][0, 1:2], outs[7][0, 1:2] = packed_rows[0][at : at + 1], packed_rows[0][at + 1 : at + 2]
    outs[10][...] = packed_rows[1][at : at + CLASSES]

    for part in range(4):
        for which, buf, raw in ((0, x_buf, raw_x), (1, g_buf, raw_g)):
            load(part, which).wait()
            for f in range(features):
                for block in range(width // LANES):
                    rows = buf[f, part * per : (part + 1) * per, :, pair_lanes(block)].reshape(rows_part, LANES)
                    start = part * rows_part * period + block * features + f
                    raw[pl.ds(start, rows_part, stride=period), :] = rows
            store(part, which).start()
    for part in range(4):
        store(part, 0).wait()
        store(part, 1).wait()


def codes(item, live, size, rows):
    lanes = jnp.arange(LANES)[None, :] - CODE_LANE
    inside = (lanes >= 0) & (lanes < size)
    own = lanes == item[:, None]
    query_code = (own & inside).astype(bf16)
    key_code = jnp.where(inside & ~(own & live[:, None]), masked_score, 0.0).astype(bf16)
    return query_code, key_code


def local_fused(
    tokens_in,
    sample_weights,
    feature_weights,
    norm_gain,
    norm_shift,
    up_weight,
    up_bias,
    down_weight,
    down_bias,
    read_weight,
    output_grad,
    task_sizes,
    feature_counts,
    bin_index,
    bin_counts,
    class_labels,
):
    samples, features, width = tokens_in.shape[1:]
    hidden_width = up_weight.shape[2]
    tasks, places = lax.axis_size("task"), lax.axis_size("feat")
    own = samples // places
    groups = own // SIZE
    units = features * (own * places // ROWS)
    sizes = (tasks, places)
    shape = (features, places, own, width)
    block_shape = (places, features, own, width)
    group_shape = (groups, ROWS, width)
    share = width // places
    share_shape = (share, width)
    piece_shape = (2, 2, 2, 2, 2, share, width)
    rows_total = groups * ROWS
    vmem = pltpu.VMEM

    def dma(*counts):
        return pltpu.SemaphoreType.DMA(counts)

    def raw_rows(tokens):
        parts = tokens.reshape(samples, features, width // LANES, LANES)
        return parts.transpose(0, 2, 1, 3).reshape(samples * features * (width // LANES), LANES)

    def from_raw(rows):
        parts = rows.reshape(samples, width // LANES, features, LANES)
        return parts.transpose(0, 2, 1, 3).reshape(1, samples, features, width)

    gains = norm_gain.transpose(1, 0, 2)
    shifts = norm_shift.transpose(1, 0, 2)
    stream = tokens_in[0].astype(f32).transpose(1, 0, 2).reshape(shape)
    stored = []
    for layer in range(LAYERS):
        final = layer == LAYERS - 1
        x1, qkv, ctx, ext, hidden, fqkv, fctx, fext, x2, x3, u, h1, act, h3, *out_grad = fused(
            functools.partial(forward_layer, layer, final),
            "forward_layer",
            sizes,
            [
                (task_sizes, "scalar"),
                (feature_counts, "scalar"),
                (stream, None, first_view, features),
                (gains, None),
                (shifts, None),
                (sample_weights, layer),
                (feature_weights, layer),
                (up_weight, layer),
                (up_bias, None),
                (down_weight, layer),
                (down_bias, None),
            ]
            + ([(raw_rows(output_grad), None)] if final else []),
            [
                (shape, f32),
                ((3,) + shape, bf16),
                (shape, bf16),
                (shape[:3] + (LANES,), bf16),
                (group_shape, bf16),
                ((groups, 3, ROWS, width), bf16),
                (group_shape, bf16),
                ((groups, ROWS, LANES), bf16),
                (shape, f32),
                (shape, f32),
                ((groups, ROWS, hidden_width), bf16),
                (shape, bf16),
                ((groups, ROWS, hidden_width), bf16),
                (group_shape, bf16),
            ]
            + ([(shape, f32)] if final else []),
            [
                vmem((ROWS, LANES), bf16),
                vmem((samples, LANES), bf16),
                vmem((ROWS, LANES), bf16),
                vmem((ROWS, LANES), bf16),
                vmem(shape, bf16),
                vmem(block_shape, bf16),
                vmem(block_shape, bf16),
                vmem(shape, bf16),
                dma(units, places - 1),
                dma(units, places - 1),
                dma(units),
                dma(groups, places - 1),
                dma(groups, places - 1),
            ]
            + ([vmem((samples * features * (width // LANES), LANES), f32)] if final else []),
            [],
            share_shape,
            1 + layer,
        )
        stored.append((stream, x1, qkv, ctx, ext, hidden, fqkv, fctx, fext, x2, u, h1, act, h3))
        stream = x3

    stream_grad = out_grad[0]
    finished = {}
    dense_rows = hidden_width // width + 5
    pairs = width // LANES
    flat = (rows_total, width)
    for layer in reversed(range(LAYERS)):
        x0, x1, qkv, ctx, ext, hidden, fqkv, fctx, fext, x2, u, h1, act, h3 = stored[layer]
        last = layer == 0
        ins = [
            (feature_counts, "scalar"),
            (stream_grad, None, cross_view, groups),
            (down_weight, layer),
            (u, None, first_view, groups),
            (up_weight, layer),
            (x2, None, cross_view, groups),
            (gains, None),
            (shifts, None),
            (feature_weights, layer),
            (fqkv, None),
            (fctx, None),
            (fext, None),
            (hidden, None),
            (x1, None),
            (sample_weights, (layer, 3)),
            (ctx, None),
            (act.reshape(rows_total, hidden_width), None),
            (h3.reshape(flat), None),
        ]
        head = []
        if not last:
            ins += [
                (stream, "raw"),
                (class_labels, None),
                (bin_index[0].T, None),
                (bin_counts[0], None),
                (read_weight.T, None),
                (task_sizes, "scalar"),
            ]
            ins[1] = (stream_grad, None)
            head = [
                vmem((places, CLASSES * (samples // LANES), LANES), f32),
                vmem((features, BINS, samples), bf16),
                vmem((features, BINS, LANES), f32),
                vmem((LANES, width), bf16),
                vmem((features, BINS, LANES), f32),
                dma(places - 1),
                dma(places - 1),
                pltpu.SemaphoreType.DMA,
            ]
        sums = [
            ((1, 6, 7, 3), ("dense", 1, 3, 12), None, True),
            ((1, 6, 7, 3), (0, 2, "weights", 12), None, True),
            ((1, 6), (10, 12), None, True),
        ]
        if last:
            sums += [((2, 3), (0, 11), sample_sum, True), ((3,), (0, 11), finished[1][0], True)]
        g1, dense_small, sdc, sext, slow, *results = fused(
            functools.partial(dense_feature_backward, layer),
            "dense_feature_backward",
            sizes,
            ins,
            [
                (shape, f32),
                ((16, width), f32),
                (shape, bf16),
                (shape[:3] + (LANES,), bf16),
                (shape, bf16),
            ]
            + ([] if last else [((features, BINS, LANES), f32), ((8, LANES), f32), ((SIZE, width), f32)]),
            [
                vmem((ROWS, LANES), bf16),
                vmem(shape, bf16),
                vmem((rows_total, hidden_width), bf16),
                vmem(flat, bf16),
                vmem(piece_shape, bf16),
                vmem(piece_shape, bf16),
                vmem(block_shape, bf16),
                vmem((ROWS, width), bf16),
                vmem(block_shape, bf16),
                vmem(shape, bf16),
                vmem(piece_shape, bf16),
                dma(groups, places - 1),
                dma(groups, places - 1),
                dma(groups),
                dma(groups, places - 1),
                dma(groups, places - 1),
            ]
            + head,
            sums,
            share_shape,
            4 + layer,
        )
        if not last:
            shapes, loss, read_grad, *results = results
        up_sum, down_sum, feature_sum, *later_sum = results
        ins = [
            (task_sizes, "scalar"),
            (qkv, None, last_view, pairs),
            (sdc, None, last_view, pairs),
            (ext, None),
            (sext, None),
            (sample_weights, layer),
            (x0, None),
            (gains, None),
            (g1, None),
        ]
        other_small = sample_small if last else read_grad
        ins += [(array, None) for array in (h1, ctx, slow, dense_small, other_small)]
        early_rows = -(-(dense_rows + (2 if last else SIZE)) // 8) * 8
        slots = 6 + tasks
        copies = 1 + (tasks - 1) + 1 + 1 + (places - 1) + (tasks - 1)
        small_scratch = [
            vmem((early_rows, width), f32),
            vmem((slots, early_rows, width), f32),
            vmem((places + tasks, 8, LANES), f32),
            dma(copies),
            dma(copies),
        ]
        outs = [(shape, f32), ((8, width), f32), ((early_rows, width), f32)]
        scratch = [vmem((samples, LANES), bf16), vmem((3,) + flat, bf16)]
        if last:
            outs += [(share_shape, f32), ((8, LANES), f32)]
            scratch.append(vmem((pairs, 2, 2, 2, 2, 2, share, LANES), bf16))
            for step in (1, 2, 5):
                _, got, mine, kind, count = sum_shapes(step, tasks, share, LANES)
                scratch += [
                    (
                        vmem((pairs,) + got, bf16),
                        vmem((pairs,) + mine, kind),
                        dma(pairs, count),
                        dma(pairs, count),
                    )
                ]
            scratch += small_scratch
            sums = [
                ((7, 3, 4), (2, "attend", "end"), feature_sum, True),
                ((4,), ("attend",), up_sum, True),
                ((4,), ("attend",), down_sum, True),
                ((4,), ("attend",), later_sum[0], True),
                ((4,), ("attend",), later_sum[1], True),
            ]
        else:
            scratch += [vmem(piece_shape, bf16), *small_scratch]
            sums = [
                ((7,), (3,), feature_sum, True),
                ((4,), ("attend",), up_sum, True),
                ((4,), ("attend",), down_sum, True),
                ((1,), ("leave",), None, True),
            ]
        stream_grad, sample_small, *more = fused(
            functools.partial(sample_backward_last, layer, last),
            "sample_backward",
            sizes,
            ins,
            outs,
            scratch,
            sums,
            share_shape,
            6 + layer,
        )
        if last:
            packed, share_sum, late, *first = more
            finished[0] = (share_sum, *first[:3])
            finished[1] = (first[3], first[4], *finished[1][1:])
        else:
            later_packed, *finished[1], sample_sum = more

    whole, parked = pl.BlockSpec(memory_space=pltpu.VMEM), pl.BlockSpec(memory_space=pltpu.HBM)
    scalar = pl.BlockSpec(memory_space=pltpu.SMEM)
    matrix = jax.ShapeDtypeStruct((LAYERS, share, width), f32)
    norm = jax.ShapeDtypeStruct((3, LAYERS, width), f32)
    raw_shape = (samples * features * (width // LANES), LANES)
    raw = jax.ShapeDtypeStruct(raw_shape, f32)
    shares = [finished[layer][member] for member in range(4) for layer in range(LAYERS)]
    results = pl.pallas_call(
        functools.partial(write_out, dense_rows),
        name="write_out",
        out_shape=[
            raw,
            raw,
            matrix,
            matrix,
            matrix,
            matrix,
            norm,
            norm,
            jax.ShapeDtypeStruct((LAYERS, hidden_width), f32),
            jax.ShapeDtypeStruct((LAYERS, width), f32),
            jax.ShapeDtypeStruct((CLASSES, width), f32),
            jax.ShapeDtypeStruct((CLASSES, features, BINS), f32),
            jax.ShapeDtypeStruct((1,), f32),
        ],
        in_specs=[parked] * 2 + [whole] * 12 + [scalar],
        out_specs=[parked] * 2 + [whole] * 10 + [scalar],
        scratch_shapes=[
            vmem(raw_shape, f32),
            vmem(raw_shape, f32),
            vmem(shape, f32),
            vmem(shape, f32),
            dma(2, 4),
            dma(2, 4),
        ],
        compiler_params=pltpu.CompilerParams(vmem_limit_bytes=63 << 20),
    )(stream, stream_grad, *shares, packed, later_packed, late, shapes, loss)
    return (
        from_raw(results[0]),
        results[11].transpose(1, 2, 0)[None],
        from_raw(results[1]),
        results[12],
        results[2][:, None],
        results[3][:, None],
        results[6].transpose(1, 0, 2),
        results[7].transpose(1, 0, 2),
        results[4].transpose(0, 2, 1),
        results[8],
        results[5],
        results[9],
        results[10].T,
    )


def local(
    tokens_in,
    sample_weights,
    feature_weights,
    norm_gain,
    norm_shift,
    up_weight,
    up_bias,
    down_weight,
    down_bias,
    read_weight,
    output_grad,
    task_sizes,
    feature_counts,
    bin_index,
    bin_counts,
    class_labels,
):
    samples = tokens_in.shape[1]
    features = tokens_in.shape[2]
    width = tokens_in.shape[3]
    hidden_width = up_weight.shape[2]
    task_devices = lax.axis_size("task")
    feature_devices = lax.axis_size("feat")
    all_features = features * feature_devices
    own_samples = samples // feature_devices
    size = min(16, own_samples)
    groups = own_samples // size
    group_rows = all_features * size
    rows_total = features * samples

    if (
        own_samples % 32 == 0
        and samples % ROWS == 0
        and ROWS % own_samples == 0
        and group_rows == ROWS
        and own_samples == 4 * SIZE
        and task_devices == hidden_width // width == 4
        and feature_devices == 8
    ):
        return local_fused(
            tokens_in,
            sample_weights,
            feature_weights,
            norm_gain,
            norm_shift,
            up_weight,
            up_bias,
            down_weight,
            down_bias,
            read_weight,
            output_grad,
            task_sizes,
            feature_counts,
            bin_index,
            bin_counts,
            class_labels,
        )

    sample_live = jnp.arange(samples) < task_sizes[0]
    feature_live = jnp.arange(all_features) < feature_counts[0]
    sample_mask = sample_live.astype(f32)
    local_index = lax.axis_index("feat") * features + jnp.arange(features)
    local_live = (local_index < feature_counts[0]).astype(f32)
    sample_qcode, sample_kcode = codes(jnp.zeros((samples,), jnp.int32), sample_live, 1, samples)
    sample_qcode = sample_qcode[:ROWS]
    item = jnp.arange(group_rows) % size
    feature_qcode, feature_kcode = codes(item, jnp.repeat(feature_live, size), size, group_rows)

    def exchange_out(rows):
        parts = rows.reshape(features, feature_devices, own_samples, width)
        got = lax.all_to_all(parts, "feat", split_axis=1, concat_axis=0, tiled=True)
        return got.reshape(all_features, own_samples, width)

    def exchange_back(rows):
        parts = rows.reshape(feature_devices, features, own_samples, width)
        got = lax.all_to_all(parts, "feat", split_axis=0, concat_axis=2, tiled=True)
        return got.reshape(features, samples, width)

    stream = tokens_in[0].astype(f32).transpose(1, 0, 2)
    token_shape = (features, samples, width)
    stored = []
    for layer in range(LAYERS):
        gain, shift = norm_gain[layer], norm_shift[layer]
        x1, h2, qkv, ctx, ext = call(
            sample_forward,
            "sample_forward",
            [
                (token_shape, f32),
                (token_shape, bf16),
                ((3,) + token_shape, bf16),
                (token_shape, bf16),
                ((features, samples, LANES), bf16),
            ],
            [],
            stream,
            gain,
            shift,
            sample_weights[layer],
            sample_qcode,
            sample_kcode,
        )
        swapped = exchange_out(h2)
        a, fqkv, fctx, fext = call(
            functools.partial(feature_forward, size),
            "feature_forward",
            [
                ((all_features, own_samples, width), bf16),
                ((groups, 3, group_rows, width), bf16),
                ((groups, group_rows, width), bf16),
                ((groups, group_rows, LANES), bf16),
            ],
            [],
            swapped,
            feature_weights[layer],
            feature_qcode,
            feature_kcode,
        )
        back = exchange_back(a)
        x3, u = call(
            dense_forward,
            "dense_forward",
            [((rows_total, width), f32), ((rows_total, hidden_width), bf16)],
            [],
            x1.reshape(rows_total, width),
            back.reshape(rows_total, width),
            gain,
            shift,
            up_weight[layer],
            up_bias[layer][None],
            down_weight[layer],
            down_bias[layer][None],
        )
        stored.append((stream, x1, qkv, ctx, ext, swapped, fqkv, fctx, fext, back, u))
        stream = x3.reshape(token_shape)

    reading = stream.astype(bf16)
    projected = jnp.einsum("fsd,dc->fsc", reading, read_weight, preferred_element_type=f32)
    onehot_bins = (bin_index[0].T[..., None] == jnp.arange(BINS)).astype(f32)
    chosen = onehot_bins * sample_mask[None, :, None]
    counted = jnp.maximum(jnp.sum(chosen, axis=1), 1.0)
    bin_sums = jnp.einsum("fsb,fsc->fbc", chosen, projected, precision=highest)
    bin_means = bin_sums / counted[..., None]
    bin_weight = bin_counts[0].astype(f32)
    weight_total = jnp.sum(bin_weight, axis=-1, keepdims=True)
    centre = jnp.sum(bin_weight[..., None] * bin_means, axis=1, keepdims=True) / weight_total[..., None]
    shapes = bin_means - centre
    used_bins = onehot_bins * local_live[:, None, None]
    local_logits = jnp.einsum("fsb,fbc->sc", used_bins, shapes, precision=highest)
    logits = lax.psum(local_logits, "feat")
    row_max = jnp.max(logits, axis=-1, keepdims=True)
    log_total = row_max + jnp.log(jnp.sum(jnp.exp(logits - row_max), axis=-1, keepdims=True))
    label_rows = (class_labels[0][:, None] == jnp.arange(CLASSES)).astype(f32)
    picked = jnp.sum(logits * label_rows, axis=-1)
    live_count = task_sizes[0].astype(f32)
    task_loss = jnp.sum(sample_mask * (log_total[:, 0] - picked)) / live_count
    logit_grad = sample_mask[:, None] * (jnp.exp(logits - log_total) - label_rows) / live_count
    shape_grad = jnp.einsum("fsb,sc->fbc", used_bins, logit_grad, precision=highest)
    means_grad = shape_grad - bin_weight[..., None] / weight_total[..., None] * jnp.sum(
        shape_grad, axis=1, keepdims=True
    )
    sum_grad = means_grad / counted[..., None]
    projected_grad = jnp.einsum("fsb,fbc->fsc", chosen, sum_grad, precision=highest).astype(bf16)
    read_grad = jnp.einsum("fsd,fsc->dc", reading, projected_grad, preferred_element_type=f32)
    stream_grad = output_grad[0].astype(f32).transpose(1, 0, 2) + jnp.einsum(
        "fsc,dc->fsd", projected_grad, read_weight, preferred_element_type=f32
    )

    small = [None] * LAYERS
    big = [None] * LAYERS
    for layer in reversed(range(LAYERS)):
        gain, shift = norm_gain[layer], norm_shift[layer]
        x0, x1, qkv, ctx, ext, swapped, fqkv, fctx, fext, back, u = stored[layer]
        flat = (rows_total, width)
        g2, sent, dup, ddown, dupb, ddownb, dgs2 = call(
            dense_backward,
            "dense_backward",
            [
                (flat, f32),
                (flat, bf16),
                ((hidden_width, width), bf16),
                ((hidden_width, width), bf16),
                ((1, hidden_width), f32),
                ((1, width), f32),
                ((2, width), f32),
            ],
            [
                ((rows_total, hidden_width), bf16),
                ((rows_total, hidden_width), bf16),
                (flat, bf16),
                (flat, bf16),
            ],
            stream_grad.reshape(flat),
            x1.reshape(flat),
            back.reshape(flat),
            u,
            gain,
            shift,
            up_weight[layer],
            down_weight[layer],
        )
        arriving = exchange_out(sent.reshape(token_shape))
        group_shape = (groups, group_rows, width)
        dh, dwf = call(
            functools.partial(feature_backward, size),
            "feature_backward",
            [((all_features, own_samples, width), bf16), ((4, width, width), bf16)],
            [
                ((3,) + group_shape, bf16),
                (group_shape, bf16),
                (group_shape, bf16),
                ((group_rows, width), bf16),
            ],
            arriving,
            swapped,
            feature_weights[layer],
            feature_kcode,
            fqkv,
            fctx,
            fext,
        )
        returned = exchange_back(dh)
        g0, dws, dgs01 = call(
            sample_backward,
            "sample_backward",
            [(token_shape, f32), ((4, width, width), bf16), ((2, 2, width), f32)],
            [
                ((3,) + token_shape, bf16),
                (token_shape, bf16),
                (token_shape, bf16),
                (token_shape, bf16),
                ((features, samples, LANES), bf16),
                ((samples, LANES), f32),
                ((samples, LANES), f32),
            ],
            g2.reshape(token_shape),
            returned,
            x1,
            x0,
            gain,
            shift,
            sample_weights[layer],
            sample_kcode,
            qkv,
            ctx,
            ext,
        )
        stream_grad = g0
        small[layer] = (
            jnp.stack([dgs01[0, 0], dgs01[1, 0], dgs2[0]]),
            jnp.stack([dgs01[0, 1], dgs01[1, 1], dgs2[1]]),
            dupb[0],
            ddownb[0],
        )
        big[layer] = [dws.reshape(4 * width, width), dwf.reshape(4 * width, width), dup, ddown]
    shard_shape = (LAYERS, 4 // task_devices, width // feature_devices, width)
    pieces = [big[layer][member] for member in range(4) for layer in range(LAYERS)]
    rows = [row.reshape(-1, width) for layer in range(LAYERS) for row in small[layer]]
    rows.append(read_grad.T)
    lengths = [row.shape[0] for row in rows]
    fill = -sum(lengths) % 8
    small_rows = jnp.concatenate(rows + [jnp.zeros((fill, width), f32)])
    if (width // feature_devices) % 16 == 0:
        *shares, small_sums = sum_everywhere(pieces, small_rows, task_devices, feature_devices)
    else:
        shares = [
            lax.psum_scatter(piece, ("task", "feat"), scatter_dimension=0, tiled=True).astype(f32)
            for piece in pieces
        ]
        small_sums = lax.psum(small_rows, ("task", "feat"))
    matrices = [jnp.stack(shares[member * LAYERS : member * LAYERS + LAYERS]) for member in range(4)]
    split = []
    at = 0
    for length in lengths:
        split.append(small_sums[at : at + length])
        at += length
    summed = [jnp.stack([split[4 * layer + member] for layer in range(LAYERS)]) for member in range(4)]
    summed[2] = summed[2].reshape(LAYERS, hidden_width)
    summed[3] = summed[3].reshape(LAYERS, width)
    summed.append(split[-1].T)
    return (
        stream.transpose(1, 0, 2)[None],
        shapes[None],
        stream_grad.transpose(1, 0, 2)[None],
        task_loss[None],
        matrices[0].reshape(shard_shape),
        matrices[1].reshape(shard_shape),
        summed[0],
        summed[1],
        matrices[2].transpose(0, 2, 1),
        summed[2],
        matrices[3],
        summed[3],
        summed[4],
    )


def solution(mesh):
    in_specs = (
        P("task", None, "feat", None),
        P(),
        P(),
        P(),
        P(),
        P(),
        P(),
        P(),
        P(),
        P(),
        P("task", None, "feat", None),
        P("task"),
        P("task"),
        P("task", None, "feat"),
        P("task", "feat", None),
        P("task", None),
    )
    out_specs = (
        P("task", None, "feat", None),
        P("task", "feat", None, None),
        P("task", None, "feat", None),
        P("task"),
        P(None, "task", "feat", None),
        P(None, "task", "feat", None),
        P(),
        P(),
        P(None, None, ("task", "feat")),
        P(),
        P(None, ("task", "feat"), None),
        P(),
        P(),
    )
    return jax.shard_map(local, mesh=mesh, in_specs=in_specs, out_specs=out_specs, check_vma=False)
```

```python
import functools

import jax
import jax.numpy as jnp
from jax import lax
from jax.experimental import pallas as pl
from jax.experimental.pallas import tpu as pltpu
from jax.sharding import PartitionSpec as P

HEADS = 8
BINS = 64
CLASSES = 10
LAYERS = 2
LANES = 128
CODE_LANE = 32
ROWS = 256

epsilon = 1e-05
masked_score = -1e30
highest = lax.Precision.HIGHEST
bf16 = jnp.bfloat16
f32 = jnp.float32

NN = (((1,), (0,)), ((), ()))
NT = (((1,), (1,)), ((), ()))
TN = (((0,), (0,)), ((), ()))


def mm(left, right, dims=NN):
    return lax.dot_general(left, right, dims, preferred_element_type=f32)


def lane_row():
    return lax.broadcasted_iota(jnp.int32, (1, LANES), 1)


def half_row(half):
    lanes = lane_row()
    picked = lanes < 64 if half == 0 else lanes >= 64
    return picked.astype(f32).astype(bf16)


def piece_row(pair, half):
    offset = lane_row() - 64 * half - 3 * pair
    return jnp.where((offset >= 0) & (offset < 3), -1.0, 0.0).astype(bf16)


def split_pieces(values, order):
    first = values.astype(bf16).astype(f32)
    rest = values - first
    second = rest.astype(bf16).astype(f32)
    third = rest - second
    return jnp.where(order == 0, first, jnp.where(order == 1, second, third))


def layer_norm(rows, gain, shift):
    centred = rows - jnp.mean(rows, axis=-1, keepdims=True)
    inverse = lax.rsqrt(jnp.mean(centred * centred, axis=-1, keepdims=True) + epsilon)
    normed = centred * inverse
    return normed, inverse, normed * gain + shift


def layer_norm_back(grad_rows, rows, gain):
    centred = rows - jnp.mean(rows, axis=-1, keepdims=True)
    inverse = lax.rsqrt(jnp.mean(centred * centred, axis=-1, keepdims=True) + epsilon)
    normed = centred * inverse
    scaled = grad_rows * gain
    inner = (
        scaled
        - jnp.mean(scaled, axis=-1, keepdims=True)
        - normed * jnp.mean(scaled * normed, axis=-1, keepdims=True)
    )
    gain_part = jnp.sum(grad_rows * normed, axis=0, keepdims=True)
    shift_part = jnp.sum(grad_rows, axis=0, keepdims=True)
    return inverse * inner, gain_part, shift_part


def chunk(index, size):
    return pl.ds(pl.multiple_of(index * size, size), size)


def attend_pair(query, key, value, query_code, key_code, pair, extras):
    query_wide = jnp.concatenate([query, query_code], axis=1)
    total = None
    peaks = []
    for half in range(2):
        mask = half_row(half)
        key_wide = jnp.concatenate([key * mask, key_code], axis=1)
        scores = mm(query_wide, key_wide, NT)
        peak = jnp.max(scores, axis=-1, keepdims=True)
        weights = jnp.exp(scores - peak).astype(bf16)
        ones = jnp.broadcast_to(mask, value.shape)
        part = mm(weights, jnp.concatenate([value * mask, ones], axis=1))
        total = part if total is None else total + part
        peaks.append(peak)
    lanes = lane_row()
    row_total = total[:, LANES:]
    context = total[:, :LANES] / row_total
    log_total = jnp.where(lanes < 64, peaks[0], peaks[1]) + jnp.log(row_total)
    order = lanes % 64 - 3 * pair
    extras = jnp.where((order >= 0) & (order < 3), split_pieces(log_total, order), extras)
    return context.astype(bf16), extras


def attend_pair_back(query, key, value, context_grad, query_extra, grad_extra, key_code, pair):
    query_wide = jnp.concatenate([query, query_extra], axis=1)
    grad_wide = jnp.concatenate([context_grad, grad_extra], axis=1)
    query_grad = key_grad = value_grad = None
    for half in range(2):
        mask = half_row(half)
        pieces = piece_row(pair, half)
        key_half = key * mask
        key_wide = jnp.concatenate([key_half, key_code + pieces], axis=1)
        value_wide = jnp.concatenate(
            [value * mask, jnp.broadcast_to(pieces, value.shape)], axis=1
        )
        attention = jnp.exp(mm(key_wide, query_wide, NT))
        score_grad = (attention * mm(value_wide, grad_wide, NT)).astype(bf16)
        value_part = mm(attention.astype(bf16), context_grad * mask)
        key_part = mm(score_grad, query * mask)
        query_part = mm(score_grad, key_half, TN)
        if half == 0:
            query_grad, key_grad, value_grad = query_part, key_part, value_part
        else:
            query_grad, key_grad, value_grad = (
                query_grad + query_part,
                key_grad + key_part,
                value_grad + value_part,
            )
    return query_grad, key_grad, value_grad


def delta_extra(context, context_grad):
    width = context.shape[1]
    products = context.astype(f32) * context_grad.astype(f32)
    high = products.astype(bf16)
    low = (products - high.astype(f32)).astype(bf16)
    head = lax.broadcasted_iota(jnp.int32, (width, LANES), 0) // (width // HEADS)
    offset = lax.broadcasted_iota(jnp.int32, (width, LANES), 1) - 64 * (head % 2) - 3 * (head // 2)
    spread = jnp.where((offset >= 0) & (offset < 3), 1.0, 0.0).astype(bf16)
    sums = mm(high, spread) + mm(low, spread)
    return split_pieces(sums, lane_row() % 64 % 3).astype(bf16)


def sample_forward(x_ref, gain_ref, shift_ref, w_ref, qcode_ref, kcode_ref, x1_ref, h2_ref, qkv_ref, ctx_ref, ext_ref):
    features, samples, width = x_ref.shape
    steps = samples // ROWS

    def project(unit, carry):
        f, rows = unit // steps, chunk(unit % steps, ROWS)
        _, _, hidden = layer_norm(x_ref[f, rows, :], gain_ref[0:1], shift_ref[0:1])
        hidden = hidden.astype(bf16)
        for member in range(3):
            out = mm(hidden, w_ref[member]).astype(bf16)
            if member == 0:
                out = out * jnp.asarray(0.125, bf16)
            qkv_ref[member, f, rows, :] = out
        return carry

    lax.fori_loop(0, features * steps, project, 0)

    def attend(unit, carry):
        f, rows = unit // steps, chunk(unit % steps, ROWS)
        code = qcode_ref[...]

        def pair_step(pair, extras):
            lanes = chunk(pair, LANES)
            context, extras = attend_pair(
                qkv_ref[0, f, rows, lanes],
                qkv_ref[1, f, :, lanes],
                qkv_ref[2, f, :, lanes],
                code,
                kcode_ref[...],
                pair,
                extras,
            )
            ctx_ref[f, rows, lanes] = context
            return extras

        extras = lax.fori_loop(0, width // LANES, pair_step, code.astype(f32))
        ext_ref[f, rows, :] = extras.astype(bf16)
        x1 = x_ref[f, rows, :] + mm(ctx_ref[f, rows, :], w_ref[3])
        x1_ref[f, rows, :] = x1
        _, _, hidden = layer_norm(x1, gain_ref[1:2], shift_ref[1:2])
        h2_ref[f, rows, :] = hidden.astype(bf16)
        return carry

    lax.fori_loop(0, features * steps, attend, 0)


def load_group(ref, group, size):
    features, _, width = ref.shape
    block = ref[:, chunk(group, size), :]
    if size % 16:
        return block.astype(f32).reshape(features * size, width).astype(bf16)
    return block.reshape(features * size, width)


def store_group(ref, group, size, rows):
    features, _, width = ref.shape
    if size % 16:
        block = rows.astype(f32).reshape(features, size, width).astype(bf16)
    else:
        block = rows.reshape(features, size, width)
    ref[:, chunk(group, size), :] = block


def feature_forward(size, h_ref, w_ref, qcode_ref, kcode_ref, a_ref, qkv_ref, ctx_ref, ext_ref):
    _, samples, width = h_ref.shape

    def step(group, carry):
        hidden = load_group(h_ref, group, size)
        for member in range(3):
            out = mm(hidden, w_ref[member]).astype(bf16)
            if member == 0:
                out = out * jnp.asarray(0.125, bf16)
            qkv_ref[group, member] = out
        code = qcode_ref[...]

        def pair_step(pair, extras):
            lanes = chunk(pair, LANES)
            context, extras = attend_pair(
                qkv_ref[group, 0, :, lanes],
                qkv_ref[group, 1, :, lanes],
                qkv_ref[group, 2, :, lanes],
                code,
                kcode_ref[...],
                pair,
                extras,
            )
            ctx_ref[group, :, lanes] = context
            return extras

        extras = lax.fori_loop(0, width // LANES, pair_step, code.astype(f32))
        ext_ref[group] = extras.astype(bf16)
        store_group(a_ref, group, size, mm(ctx_ref[group], w_ref[3]).astype(bf16))
        return carry

    lax.fori_loop(0, samples // size, step, 0)


def gelu_parts(values):
    cubic = values * values * values
    inside = 0.7978845608028654 * (values + 0.044715 * cubic)
    bent = jnp.tanh(inside)
    return bent


def dense_forward(x_ref, a_ref, gain_ref, shift_ref, up_ref, upb_ref, down_ref, downb_ref, out_ref, u_ref):
    rows_total, width = x_ref.shape
    hidden_width = up_ref.shape[1]

    def step(unit, carry):
        rows = chunk(unit, ROWS)
        x2 = x_ref[rows, :] + a_ref[rows, :].astype(f32)
        _, _, hidden = layer_norm(x2, gain_ref[2:3], shift_ref[2:3])
        hidden = hidden.astype(bf16)
        total = x2 + downb_ref[...]
        for part in range(hidden_width // 512):
            cols = slice(part * 512, part * 512 + 512)
            expanded = mm(hidden, up_ref[:, cols]) + upb_ref[:, cols]
            u_ref[rows, cols] = expanded.astype(bf16)
            active = (0.5 * expanded * (1.0 + gelu_parts(expanded))).astype(bf16)
            total = total + mm(active, down_ref[cols, :])
        out_ref[rows, :] = total
        return carry

    lax.fori_loop(0, rows_total // ROWS, step, 0)


def dense_backward(g_ref, x1_ref, a_ref, u_ref, gain_ref, shift_ref, up_ref, down_ref, out_ref, send_ref, dup_ref, ddown_ref, dupb_ref, ddownb_ref, dgs_ref, active_ref, ugrad_ref, hidden_ref, rowgrad_ref):
    rows_total, width = g_ref.shape
    hidden_width = up_ref.shape[1]
    dupb_ref[...] = jnp.zeros_like(dupb_ref)
    ddownb_ref[...] = jnp.zeros_like(ddownb_ref)
    dgs_ref[...] = jnp.zeros_like(dgs_ref)

    def step(unit, carry):
        rows = chunk(unit, ROWS)
        grad = g_ref[rows, :]
        low = grad.astype(bf16)
        rowgrad_ref[rows, :] = low
        ddownb_ref[...] += jnp.sum(low.astype(f32), axis=0, keepdims=True)
        hidden_grad = None
        for part in range(hidden_width // 512):
            cols = slice(part * 512, part * 512 + 512)
            active_grad = mm(low, down_ref[cols, :], NT).astype(bf16).astype(f32)
            u = u_ref[rows, cols].astype(f32)
            bent = gelu_parts(u)
            slope = 0.5 * (1.0 + bent) + u * (1.0 - bent * bent) * (
                0.3989422804014327 + 0.05351611220146811 * u * u
            )
            active_ref[rows, cols] = (0.5 * u * (1.0 + bent)).astype(bf16)
            ugrad = (active_grad * slope).astype(bf16)
            ugrad_ref[rows, cols] = ugrad
            dupb_ref[:, cols] += jnp.sum(ugrad.astype(f32), axis=0, keepdims=True)
            part_grad = mm(ugrad, up_ref[:, cols], NT)
            hidden_grad = part_grad if hidden_grad is None else hidden_grad + part_grad
        x2 = x1_ref[rows, :] + a_ref[rows, :].astype(f32)
        _, _, hidden = layer_norm(x2, gain_ref[2:3], shift_ref[2:3])
        hidden_ref[rows, :] = hidden.astype(bf16)
        norm_grad, gain_part, shift_part = layer_norm_back(
            hidden_grad.astype(bf16).astype(f32), x2, gain_ref[2:3]
        )
        dgs_ref[0:1] += gain_part
        dgs_ref[1:2] += shift_part
        grad = grad + norm_grad
        out_ref[rows, :] = grad
        send_ref[rows, :] = grad.astype(bf16)
        return carry

    lax.fori_loop(0, rows_total // ROWS, step, 0)

    def weights(part, carry):
        cols = chunk(part, 512)
        dup_ref[cols, :] = mm(ugrad_ref[:, cols], hidden_ref[...], TN).astype(bf16)
        ddown_ref[cols, :] = mm(active_ref[:, cols], rowgrad_ref[...], TN).astype(bf16)
        return carry

    lax.fori_loop(0, hidden_width // 512, weights, 0)


def feature_backward(size, da_ref, h_ref, w_ref, kcode_ref, qkv_ref, ctx_ref, ext_ref, dh_ref, dw_ref, dqkv_ref, hidden_ref, dao_ref, dc_ref):
    _, samples, width = h_ref.shape
    groups = samples // size

    def step(group, carry):
        hidden_ref[group] = load_group(h_ref, group, size)
        dao = load_group(da_ref, group, size)
        dao_ref[group] = dao
        context_grad = mm(dao, w_ref[3], NT).astype(bf16)
        dc_ref[...] = context_grad
        grad_extra = delta_extra(ctx_ref[group], context_grad)

        def pair_step(pair, inner):
            lanes = chunk(pair, LANES)
            query_grad, key_grad, value_grad = attend_pair_back(
                qkv_ref[group, 0, :, lanes],
                qkv_ref[group, 1, :, lanes],
                qkv_ref[group, 2, :, lanes],
                dc_ref[:, lanes],
                ext_ref[group],
                grad_extra,
                kcode_ref[...],
                pair,
            )
            dqkv_ref[0, group, :, lanes] = (query_grad * 0.125).astype(bf16)
            dqkv_ref[1, group, :, lanes] = key_grad.astype(bf16)
            dqkv_ref[2, group, :, lanes] = value_grad.astype(bf16)
            return inner

        lax.fori_loop(0, width // LANES, pair_step, 0)
        total = mm(dqkv_ref[0, group], w_ref[0], NT)
        total = total + mm(dqkv_ref[1, group], w_ref[1], NT)
        total = total + mm(dqkv_ref[2, group], w_ref[2], NT)
        store_group(dh_ref, group, size, total.astype(bf16))
        return carry

    lax.fori_loop(0, groups, step, 0)

    def weights(member, carry):
        total = None
        for group in range(groups):
            part = mm(hidden_ref[group], dqkv_ref[member, group], TN)
            total = part if total is None else total + part
        dw_ref[member] = total.astype(bf16)
        return carry

    lax.fori_loop(0, 3, weights, 0)
    total = None
    for group in range(groups):
        part = mm(ctx_ref[group], dao_ref[group], TN)
        total = part if total is None else total + part
    dw_ref[3] = total.astype(bf16)


def sample_backward(g_ref, dh_ref, x1_ref, x_ref, gain_ref, shift_ref, w_ref, kcode_ref, qkv_ref, ctx_ref, ext_ref, out_ref, dw_ref, dgs_ref, dqkv_ref, hidden_ref, low_ref, dc_ref, gext_ref, kacc_ref, vacc_ref):
    features, samples, width = x_ref.shape
    steps = samples // ROWS
    dgs_ref[...] = jnp.zeros_like(dgs_ref)

    def enter(unit, carry):
        f, rows = unit // steps, chunk(unit % steps, ROWS)
        norm_grad, gain_part, shift_part = layer_norm_back(
            dh_ref[f, rows, :].astype(f32), x1_ref[f, rows, :], gain_ref[1:2]
        )
        dgs_ref[1, 0:1] += gain_part
        dgs_ref[1, 1:2] += shift_part
        grad = g_ref[f, rows, :] + norm_grad
        out_ref[f, rows, :] = grad
        low = grad.astype(bf16)
        low_ref[f, rows, :] = low
        context_grad = mm(low, w_ref[3], NT).astype(bf16)
        dc_ref[f, rows, :] = context_grad
        gext_ref[f, rows, :] = delta_extra(ctx_ref[f, rows, :], context_grad)
        return carry

    lax.fori_loop(0, features * steps, enter, 0)

    def attend(unit, carry):
        f, pair = unit // (width // LANES), unit % (width // LANES)
        lanes = chunk(pair, LANES)

        def query_step(step, inner):
            rows = chunk(step, ROWS)
            query_grad, key_grad, value_grad = attend_pair_back(
                qkv_ref[0, f, rows, lanes],
                qkv_ref[1, f, :, lanes],
                qkv_ref[2, f, :, lanes],
                dc_ref[f, rows, lanes],
                ext_ref[f, rows, :],
                gext_ref[f, rows, :],
                kcode_ref[...],
                pair,
            )
            dqkv_ref[0, f, rows, lanes] = (query_grad * 0.125).astype(bf16)
            first = step == 0
            kacc_ref[...] = jnp.where(first, 0.0, kacc_ref[...]) + key_grad
            vacc_ref[...] = jnp.where(first, 0.0, vacc_ref[...]) + value_grad
            return inner

        lax.fori_loop(0, steps, query_step, 0)
        dqkv_ref[1, f, :, lanes] = kacc_ref[...].astype(bf16)
        dqkv_ref[2, f, :, lanes] = vacc_ref[...].astype(bf16)
        return carry

    kacc_ref[...] = jnp.zeros_like(kacc_ref)
    vacc_ref[...] = jnp.zeros_like(vacc_ref)
    lax.fori_loop(0, features * (width // LANES), attend, 0)

    def leave(unit, carry):
        f, rows = unit // steps, chunk(unit % steps, ROWS)
        total = mm(dqkv_ref[0, f, rows, :], w_ref[0], NT)
        total = total + mm(dqkv_ref[1, f, rows, :], w_ref[1], NT)
        total = total + mm(dqkv_ref[2, f, rows, :], w_ref[2], NT)
        x = x_ref[f, rows, :]
        _, _, hidden = layer_norm(x, gain_ref[0:1], shift_ref[0:1])
        hidden_ref[f, rows, :] = hidden.astype(bf16)
        norm_grad, gain_part, shift_part = layer_norm_back(
            total.astype(bf16).astype(f32), x, gain_ref[0:1]
        )
        dgs_ref[0, 0:1] += gain_part
        dgs_ref[0, 1:2] += shift_part
        out_ref[f, rows, :] += norm_grad
        return carry

    lax.fori_loop(0, features * steps, leave, 0)

    def weights(member, carry):
        total = None
        for f in range(features):
            part = mm(hidden_ref[f], dqkv_ref[member, f], TN)
            total = part if total is None else total + part
        dw_ref[member] = total.astype(bf16)
        return carry

    lax.fori_loop(0, 3, weights, 0)
    total = None
    for f in range(features):
        part = mm(ctx_ref[f], low_ref[f], TN)
        total = part if total is None else total + part
    dw_ref[3] = total.astype(bf16)


def call(body, name, outs, scratch, *operands):
    spec = pl.BlockSpec(memory_space=pltpu.VMEM)
    return pl.pallas_call(
        body,
        name=name,
        out_shape=[jax.ShapeDtypeStruct(shape, kind) for shape, kind in outs],
        in_specs=[spec] * len(operands),
        out_specs=[spec] * len(outs),
        scratch_shapes=[pltpu.VMEM(shape, kind) for shape, kind in scratch],
        compiler_params=pltpu.CompilerParams(vmem_limit_bytes=56 << 20),
    )(*operands)


MESH = pl.DeviceIdType.MESH


def remote(source, target, send_sem, recv_sem, device):
    return pltpu.make_async_remote_copy(
        src_ref=source,
        dst_ref=target,
        send_sem=send_sem,
        recv_sem=recv_sem,
        device_id=device,
        device_id_type=MESH,
    )


def sum_partners(task_devices, feature_devices):
    task, place = lax.axis_index("task"), lax.axis_index("feat")
    chip, core = place // 2, lax.rem(place, 2)
    chips = feature_devices // 2
    pair = [{"feat": place + 1 - 2 * core}]
    tasks = [{"task": lax.rem(task + step, task_devices)} for step in range(1, task_devices)]
    line = [{"feat": 2 * lax.rem(chip + step, chips) + core} for step in range(1, chips)]
    return task, chip, core, pair, tasks, line


def greet(devices):
    barrier = pltpu.get_barrier_semaphore()
    for device in devices:
        pl.semaphore_signal(barrier, inc=1, device_id=device, device_id_type=MESH)


def met(count):
    pl.semaphore_wait(pltpu.get_barrier_semaphore(), count)


def sum_tail(pieces, task_devices, feature_devices, *refs):
    chips = feature_devices // 2
    inputs, small_ref = refs[:pieces], refs[pieces]
    outs, small_out = refs[pieces + 1 : 2 * pieces + 1], refs[2 * pieces + 1]
    own, first, summed, second, third_in, third, sends, recvs, loads, small_got, small_sends, small_recvs = refs[2 * pieces + 2 :]
    task, chip, core, pair, tasks, line = sum_partners(task_devices, feature_devices)
    greet(pair + tasks + line)
    own_loads = [
        pltpu.make_async_copy(inputs[p].at[:, :, core], own.at[p], loads.at[p]) for p in range(pieces)
    ]
    for load in own_loads:
        load.start()
    met(len(pair) + len(tasks) + len(line))

    started = []
    for p in range(pieces):
        copy = remote(inputs[p].at[:, :, 1 - core], first.at[p], sends.at[p, 0], recvs.at[p, 0], pair[0])
        copy.start()
        started.append([copy])
    small_slot = [0]

    def small_exchange(values, devices, index, base):
        copies = []
        for k, device in enumerate(devices):
            copy = remote(values, small_got.at[base + index], small_sends.at[base + k], small_recvs.at[base + k], device)
            copy.start()
            copies.append(copy)
        return copies

    def small_finish(copies, count, base):
        for copy in copies:
            copy.wait()
        total = small_got[base]
        for k in range(1, count):
            total = total + small_got[base + k]
        return total

    small_got[core] = small_ref[...]
    small_copies = small_exchange(small_got.at[core], pair, core, 0)
    for p in range(pieces):
        own_loads[p].wait()
        for copy in started[p]:
            copy.wait()

        def add_core(index, carry, p=p):
            t, z = index // chips, lax.rem(index, chips)
            summed[p, t, z] = (own[p, t, z].astype(f32) + first[p, t, z].astype(f32)).astype(bf16)
            return carry

        lax.fori_loop(0, task_devices * chips, add_core, 0)
        started[p] = []
        for k, device in enumerate(tasks):
            other = lax.rem(task + k + 1, task_devices)
            copy = remote(summed.at[p, other], second.at[p, k], sends.at[p, 1 + k], recvs.at[p, 1 + k], device)
            copy.start()
            started[p].append(copy)
    total = small_finish(small_copies, 2, 0)
    small_got[2 + task] = total
    small_copies = small_exchange(small_got.at[2 + task], tasks, task, 2)
    for p in range(pieces):
        for copy in started[p]:
            copy.wait()

        def add_tasks(z, carry, p=p):
            total = summed[p, task, z].astype(f32)
            for k in range(task_devices - 1):
                total = total + second[p, k, z].astype(f32)
            third_in[p, z] = total.astype(bf16)
            return carry

        lax.fori_loop(0, chips, add_tasks, 0)
        started[p] = []
        for k, device in enumerate(line):
            other = lax.rem(chip + k + 1, chips)
            slot = task_devices + k
            copy = remote(third_in.at[p, other], third.at[p, k], sends.at[p, slot], recvs.at[p, slot], device)
            copy.start()
            started[p].append(copy)
    total = small_finish(small_copies, task_devices, 2)
    base = 2 + task_devices
    small_got[base + chip] = total
    small_copies = small_exchange(small_got.at[base + chip], line, chip, base)
    for p in range(pieces):
        for copy in started[p]:
            copy.wait()
        total = third_in[p, chip].astype(f32)
        for k in range(chips - 1):
            total = total + third[p, k].astype(f32)
        outs[p][...] = total
    small_out[...] = small_finish(small_copies, chips, base)


def sum_everywhere(pieces, small, task_devices, feature_devices):
    chips = feature_devices // 2
    rows, width = pieces[0].shape
    share = rows // (task_devices * feature_devices)
    blocks = [piece.reshape(task_devices, chips, 2, share, width) for piece in pieces]
    count = len(pieces)
    copies = task_devices + chips - 1
    small_copies = 2 + task_devices + chips
    vmem, anywhere = pl.BlockSpec(memory_space=pltpu.VMEM), pl.BlockSpec(memory_space=pl.ANY)
    return pl.pallas_call(
        functools.partial(sum_tail, count, task_devices, feature_devices),
        name="sum_tail",
        out_shape=[jax.ShapeDtypeStruct((share, width), f32)] * count
        + [jax.ShapeDtypeStruct(small.shape, f32)],
        in_specs=[anywhere] * count + [vmem],
        out_specs=[vmem] * (count + 1),
        scratch_shapes=[
            pltpu.VMEM((count, task_devices, chips, share, width), bf16),
            pltpu.VMEM((count, task_devices, chips, share, width), bf16),
            pltpu.VMEM((count, task_devices, chips, share, width), bf16),
            pltpu.VMEM((count, task_devices - 1, chips, share, width), bf16),
            pltpu.VMEM((count, chips, share, width), bf16),
            pltpu.VMEM((count, chips - 1, share, width), bf16),
            pltpu.SemaphoreType.DMA((count, copies)),
            pltpu.SemaphoreType.DMA((count, copies)),
            pltpu.SemaphoreType.DMA((count,)),
            pltpu.VMEM((small_copies,) + small.shape, f32),
            pltpu.SemaphoreType.DMA((small_copies,)),
            pltpu.SemaphoreType.DMA((small_copies,)),
        ],
        compiler_params=pltpu.CompilerParams(
            vmem_limit_bytes=56 << 20, collective_id=0, has_side_effects=True
        ),
    )(*blocks, small)


SIZE = 16


class Place:
    def __init__(self, task_devices, feature_devices):
        self.tasks, self.places = task_devices, feature_devices
        self.chips = feature_devices // 2
        self.task, self.place = lax.axis_index("task"), lax.axis_index("feat")
        self.chip, self.core = self.place // 2, lax.rem(self.place, 2)
        self.far, self.near = self.chip // 2, lax.rem(self.chip, 2)
        self.y, self.x = self.task // 2, lax.rem(self.task, 2)
        self.x_task = {"task": self.task + 1 - 2 * self.x}
        self.y_task = {"task": self.task + 2 - 4 * self.y}
        self.other_core = {"feat": self.place + 1 - 2 * self.core}
        self.near_chip = {"feat": self.place + 2 - 4 * self.near}
        self.far_chip = {"feat": self.place + 4 - 8 * self.far}

    def ring(self, step):
        return lax.rem(self.place + step, self.places)

    def task_partner(self, step):
        return lax.rem(self.task + step, self.tasks)

    def greet(self):
        barrier = pltpu.get_barrier_semaphore()
        for step in range(1, self.places):
            pl.semaphore_signal(barrier, inc=1, device_id={"feat": self.ring(step)}, device_id_type=MESH)
        for step in range(1, self.tasks):
            pl.semaphore_signal(barrier, inc=1, device_id={"task": self.task_partner(step)}, device_id_type=MESH)

    def met(self):
        pl.semaphore_wait(pltpu.get_barrier_semaphore(), self.places - 1 + self.tasks - 1)


class SumStep:
    def __init__(self, step, place, source, own, got, sends, recvs, load):
        self.step = step
        y, x, far, near, core = place.y, place.x, place.far, place.near, place.core
        if step == 1:
            self.mine = [source.at[:, :, :, :, core]]
            parts = [(source.at[:, :, :, :, 1 - core], got, place.other_core)]
        elif step == 2:
            self.mine = [source.at[y, x]]
            parts = []
            for k in range(1, place.tasks):
                other = place.task_partner(k)
                parts.append((source.at[other // 2, lax.rem(other, 2)], got.at[k - 1], {"task": other}))
        elif step == 6:
            self.mine = [source.at[:, x, 0], source.at[y, :, 1]]
            parts = [
                (source.at[:, 1 - x, 0], got.at[0], place.x_task),
                (source.at[1 - y, :, 1], got.at[1], place.y_task),
            ]
        elif step == 7:
            self.mine = [source.at[0, y], source.at[1, x]]
            parts = [
                (source.at[0, 1 - y], got.at[0], place.y_task),
                (source.at[1, 1 - x], got.at[1], place.x_task),
            ]
        elif step == 3:
            self.mine = [source.at[:, near]]
            parts = [(source.at[:, 1 - near], got, place.near_chip)]
        elif step == 4:
            self.mine = [source.at[far]]
            parts = [(source.at[1 - far], got, place.far_chip)]
        else:
            self.mine = [source.at[far, near]]
            parts = []
            for k in range(1, place.chips):
                other = lax.rem(place.chip + k, place.chips)
                parts.append(
                    (source.at[other // 2, lax.rem(other, 2)], got.at[k - 1], {"feat": 2 * other + core})
                )
        self.copies = [
            remote(part, target, sends.at[k], recvs.at[k], device) for k, (part, target, device) in enumerate(parts)
        ]
        self.loads = []
        if own is not None:
            kept = [own] if len(self.mine) == 1 else [own.at[half] for half in range(2)]
            self.loads = [
                pltpu.make_async_copy(part, target, load.at[half])
                for half, (part, target) in enumerate(zip(self.mine, kept))
            ]
            self.mine = kept
        self.got = got

    def start(self):
        for copy in self.copies:
            copy.start()
        for load in self.loads:
            load.start()

    def finish(self, out):
        for load in self.loads:
            load.wait()
        for copy in self.copies:
            copy.wait()
        own, got = self.mine[0], self.got
        if self.step == 1:

            def add_core(index, carry):
                y, x, far = index // 4, lax.rem(index // 2, 2), lax.rem(index, 2)
                out[y, x, far] = own[y, x, far] + got[y, x, far]
                return carry

            lax.fori_loop(0, 8, add_core, 0)
        elif self.step in (2, 5):
            total = own[...].astype(f32)
            for k in range(got.shape[0]):
                total = total + got[k].astype(f32)
            out[...] = total.astype(out.dtype)
        elif self.step in (6, 7):
            for half in range(2):
                out[half] = self.mine[half][...] + got[half]
        elif self.step == 3:
            out[...] = own[...] + got[...]
        else:
            out[...] = own[...].astype(f32) + got[...].astype(f32)


def sum_shapes(step, tasks, share, width):
    block = (share, width)
    if step == 1:
        whole = (2, 2, 2, 2) + block
        return whole, whole, whole, bf16, 1
    if step == 2:
        return (2, 2) + block, (tasks - 1, 2, 2) + block, (2, 2) + block, bf16, tasks - 1
    if step == 6:
        return None, (2, 2, 2) + block, (2, 2, 2) + block, bf16, 2
    if step == 7:
        return (2, 2) + block, (2, 2) + block, (2, 2) + block, bf16, 2
    if step == 3:
        return (2,) + block, (2,) + block, (2,) + block, bf16, 1
    if step == 4:
        return block, block, block, f32, 1
    return block, (3,) + block, block, f32, 3


class Chain:
    def __init__(self, place, steps, points, bufs, source, out):
        self.place, self.steps, self.points, self.bufs, self.out = place, steps, points, bufs, out
        self.at, self.running = 0, False
        self.first = None
        if len(points) > len(steps):
            self.first, self.points = points[0], points[1:]
        self.actions = [None if source is None else self.make(0, source)]
        self.actions += [self.make(at, bufs[at - 1][2]) for at in range(1, len(steps))]

    def make(self, at, source):
        own, got, _, sends, recvs, local_sem = self.bufs[at]
        return SumStep(self.steps[at], self.place, source, own, got, sends, recvs, local_sem)

    def begin(self, source=None):
        if source is not None:
            self.actions[0] = self.make(0, source)
        self.actions[0].start()
        self.running = True

    def reached(self, point):
        if self.first is not None and point == self.first:
            self.begin()
            return
        if not self.running or self.points[self.at] != point:
            return
        self.actions[self.at].finish(self.bufs[self.at][2])
        self.at += 1
        if self.at < len(self.steps):
            self.actions[self.at].start()
            return
        self.running = False
        if self.out is not None:
            self.flush().start()

    def flush(self):
        return pltpu.make_async_copy(self.bufs[-1][2], self.out, self.bufs[-1][5].at[2])


class Box:
    def __init__(self, place, bufs, loads, outs, out_bufs, flush_sem, chains):
        self.place, self.bufs, self.loads = place, bufs, loads
        self.outs, self.out_bufs, self.flush_sem = outs, out_bufs, flush_sem
        self.chains = chains
        self.waited, self.flushed = set(), []

    def start(self, *indices):
        for index in indices:
            if isinstance(index, tuple):
                for part in index[1:]:
                    self.loads[index[0]].one(part).start()
                continue
            for copy in self.loads[index]:
                copy.start()

    def use(self, *indices):
        found = []
        for index in indices:
            if index not in self.waited:
                self.waited.add(index)
                for copy in self.loads[index]:
                    copy.wait()
            found.append(self.bufs[index])
        return found if len(found) > 1 else found[0]

    def part(self, index, part):
        self.waited.add(index)
        self.loads[index].one(part).wait()

    def out(self, *indices):
        found = [self.out_bufs[index] for index in indices]
        return found if len(found) > 1 else found[0]

    def copy_out(self, index, part, view):
        source, target = self.out_bufs[index], self.outs[index]
        if view is not None:
            source, target = view(source, part), view(target, part)
        return pltpu.make_async_copy(source, target, self.flush_sem.at[index, part])

    def flush(self, *indices):
        for index in indices:
            self.copy_out(index, 0, None).start()
            self.flushed.append((index, 0, None))

    def flush_part(self, index, part, view):
        self.copy_out(index, part, view).start()
        if (index, 0, view) not in self.flushed:
            self.flushed += [(index, at, view) for at in range(4)]

    def settle(self, *indices):
        left = []
        for index, part, view in self.flushed:
            if index in indices:
                self.copy_out(index, part, view).wait()
            else:
                left.append((index, part, view))
        self.flushed = left

    def ready(self):
        self.place.met()
        for chain in self.chains:
            if chain.actions[0] is not None and chain.first is None:
                chain.begin()

    def point(self, name):
        for chain in self.chains:
            chain.reached(name)

    def end(self):
        for index, part, view in self.flushed:
            self.copy_out(index, part, view).wait()
        for chain in self.chains:
            if chain.out is not None:
                chain.flush().wait()


class Parts:
    def __init__(self, source, target, view, count, sem):
        self.source, self.target, self.view, self.count, self.sem = source, target, view, count, sem

    def one(self, part):
        if self.view is None:
            return pltpu.make_async_copy(self.source, self.target, self.sem.at[0])
        return pltpu.make_async_copy(self.view(self.source, part), self.view(self.target, part), self.sem.at[part])

    def __iter__(self):
        return iter([self.one(part) for part in range(self.count)])


def fused(body, name, place_sizes, ins, outs, scratch, sums, share_shape, identity):
    tasks, places = place_sizes
    anywhere = pl.BlockSpec(memory_space=pltpu.HBM)
    scalar = pl.BlockSpec(memory_space=pltpu.SMEM)
    buffers = []
    ins = [tuple(item) + (None, 1) if len(item) == 2 else item for item in ins]
    for array, layer, _, _ in ins:
        if layer not in ("scalar", "raw"):
            depth = 0 if layer is None else len(layer) if isinstance(layer, tuple) else 1
            buffers.append(pltpu.VMEM(array.shape[depth:], array.dtype))
    outs = [tuple(item) + (None,) if len(item) == 2 else item for item in outs]
    out_buffers = [pltpu.VMEM(shape, kind) for shape, kind, shared in outs if shared is None]
    sum_results, sum_scratch, sum_arrays = [], [], []
    chain_layout = []
    for steps, _, array, goes_out in sums:
        share, width = share_shape if array is None else array.shape[-2:]
        for at, step in enumerate(steps):
            own, got, result, kind, copies = sum_shapes(step, tasks, share, width)
            loaded = at == 0 and array is not None
            chain_layout.append(loaded)
            sum_scratch += [pltpu.VMEM(own, bf16)] if loaded else []
            sum_scratch += [
                pltpu.VMEM(got, bf16),
                pltpu.VMEM(result, kind),
                pltpu.SemaphoreType.DMA((copies,)),
                pltpu.SemaphoreType.DMA((copies,)),
                pltpu.SemaphoreType.DMA((3,)),
            ]
        if goes_out:
            sum_results.append(jax.ShapeDtypeStruct(result, kind))
        if array is not None:
            sum_arrays.append(array)
    flat_scratch = []
    for item in scratch:
        flat_scratch += list(item) if isinstance(item, tuple) else [item]
    everything = buffers + out_buffers + flat_scratch + sum_scratch
    def kernel(*refs):
        rest = list(refs)

        def pop(count):
            taken = rest[:count]
            del rest[:count]
            return taken

        in_refs, sum_refs = pop(len(ins)), pop(len(sum_arrays))
        out_refs, sum_outs = pop(len(outs)), pop(len(sum_results))
        flat_in = pop(len(buffers))
        fresh, out_bufs = pop(len(out_buffers)), []
        for _, _, shared in outs:
            out_bufs.append(fresh.pop(0) if shared is None else out_bufs[shared])
        user = [tuple(pop(len(item))) if isinstance(item, tuple) else pop(1)[0] for item in scratch]
        layout = list(chain_layout)
        chain_bufs = [
            [pop(6) if layout.pop(0) else [None] + pop(5) for _ in steps] for steps, _, _, _ in sums
        ]
        load_sem, flush_sem = pop(2)
        place = Place(tasks, places)
        loads, bufs = [], []
        for index, (array, layer, view, count) in enumerate(ins):
            if layer in ("scalar", "raw"):
                loads.append([])
                bufs.append(in_refs[index])
                continue
            bufs.append(flat_in.pop(0))
            source = in_refs[index]
            if layer is not None:
                source = source.at[layer]
            loads.append(Parts(source, bufs[-1], view, count, load_sem.at[index]))
        place.greet()
        chains = []
        for (steps, points, array, goes_out), chain_buf in zip(sums, chain_bufs):
            source = None if array is None else sum_refs.pop(0)
            chains.append(Chain(place, steps, points, chain_buf, source, sum_outs.pop(0) if goes_out else None))
        box = Box(place, bufs, loads, out_refs, out_bufs, flush_sem, chains)
        body(box, *user)
        box.end()

    return pl.pallas_call(
        kernel,
        name=name,
        out_shape=[jax.ShapeDtypeStruct(shape, kind) for shape, kind, _ in outs] + sum_results,
        in_specs=[scalar if layer == "scalar" else anywhere for _, layer, _, _ in ins] + [anywhere] * len(sum_arrays),
        out_specs=[anywhere] * (len(outs) + len(sum_results)),
        scratch_shapes=everything
        + [pltpu.SemaphoreType.DMA((len(ins), 8)), pltpu.SemaphoreType.DMA((len(outs), 4))],
        compiler_params=pltpu.CompilerParams(
            vmem_limit_bytes=63 << 20, collective_id=identity, has_side_effects=True
        ),
    )(*[item[0] for item in ins], *sum_arrays)


def cross(ref, unit):
    block = ref[:, :, chunk(unit, SIZE), :]
    return block.reshape(block.shape[0] * block.shape[1] * SIZE, block.shape[3])


def put_cross(ref, unit, rows):
    first, second, _, width = ref.shape
    ref[:, :, chunk(unit, SIZE), :] = rows.reshape(first, second, SIZE, width)


def cross_view(ref, unit):
    return ref.at[:, :, chunk(unit, SIZE), :]


def first_view(ref, unit):
    return ref.at[unit]


def last_view(ref, unit):
    return ref.at[(slice(None),) * (len(ref.shape) - 1) + (chunk(unit, LANES),)]


def own_rows(ref, f, unit, size, lanes=slice(None)):
    block = ref[f, :, chunk(unit, size), lanes]
    return block.reshape(block.shape[0] * size, block.shape[2])


def block_rows(ref, f, unit, per, lanes=slice(None)):
    block = ref[f, chunk(unit, per), :, lanes]
    return block.reshape(per * block.shape[1], block.shape[2])


def all_rows(ref, f, lanes=slice(None)):
    block = ref[f, :, :, lanes]
    return block.reshape(block.shape[0] * block.shape[1], block.shape[2])


def pair_lanes(pair):
    return slice(pair * LANES, pair * LANES + LANES)


def fill_sample_codes(size, query_ref, key_ref):
    if query_ref is not None:
        lanes = lax.broadcasted_iota(jnp.int32, query_ref.shape, 1)
        query_ref[...] = jnp.where(lanes == CODE_LANE, 1.0, 0.0).astype(bf16)
    lanes = lax.broadcasted_iota(jnp.int32, key_ref.shape, 1)
    rows = lax.broadcasted_iota(jnp.int32, key_ref.shape, 0)
    key_ref[...] = jnp.where((lanes == CODE_LANE) & (rows >= size), masked_score, 0.0).astype(bf16)


def fill_feature_codes(count, query_ref, key_ref):
    lanes = lax.broadcasted_iota(jnp.int32, key_ref.shape, 1) - CODE_LANE
    rows = lax.broadcasted_iota(jnp.int32, key_ref.shape, 0)
    own = lanes == (rows & (SIZE - 1))
    inside = (lanes >= 0) & (lanes < SIZE)
    if query_ref is not None:
        query_ref[...] = jnp.where(own, 1.0, 0.0).astype(bf16)
    live = rows < count * SIZE
    key_ref[...] = jnp.where(inside & ~(own & live), masked_score, 0.0).astype(bf16)


def from_rows(raw_ref, out_ref):
    features, blocks, own, width = out_ref.shape
    pairs = width // LANES
    for f in range(features):
        for block in range(pairs):
            rows = raw_ref[pl.ds(block * features + f, blocks * own, stride=features * pairs), :]
            out_ref[f, :, :, pair_lanes(block)] = rows.reshape(blocks, own, LANES).astype(out_ref.dtype)


LAYER_OUTS = 14


def forward_layers(layers, box, sq_ref, sk_ref, fq_ref, fk_ref, raw_ref, *scratch):
    box.start(2, 3, 4, 7)
    size_ref, count_ref = box.use(0, 1)
    fill_sample_codes(size_ref[0], sq_ref, sk_ref)
    fill_feature_codes(count_ref[0], fq_ref, fk_ref)
    x_ref = box.out(LAYER_OUTS * layers)
    raw_ref[...] = box.use(2)[...].astype(f32)
    from_rows(raw_ref, x_ref)
    box.flush(LAYER_OUTS * layers)
    before = None
    for layer in range(layers):
        before = forward_layer(layer, layer == layers - 1, before, box, x_ref, sq_ref, sk_ref, fq_ref, fk_ref, raw_ref, *scratch)
        x_ref = box.out(LAYER_OUTS * layer + 9)


def forward_layer(layer, last, before, box, x_ref, sq_ref, sk_ref, fq_ref, fk_ref, raw_ref, h2_ref, swapped_ref, a_ref, back_ref, all_sends, all_recvs, all_self, all_back_sends, all_back_recvs):
    place = box.place
    first = LAYER_OUTS * layer
    outs = [first + index for index in range(LAYER_OUTS)]
    earlier = [index - LAYER_OUTS for index in outs]
    x1_ref, qkv_ref, ctx_ref, ext_ref, hidden_ref, fqkv_ref, fctx_ref, fext_ref, x2_ref, x3_ref, u_ref, h1_ref, active_ref, h3_ref = box.out(*outs)
    sends, recvs, self_sem = all_sends.at[layer], all_recvs.at[layer], all_self.at[layer]
    back_sends, back_recvs = all_back_sends.at[layer], all_back_recvs.at[layer]
    weights = 7 + 4 * layer
    gain_ref, shift_ref, w_ref = box.use(3, 4, weights)
    if layer > 0:
        box.settle(*[earlier[index] for index in (0, 1, 2, 3, 11)])
    features, blocks, own, width = x_ref.shape
    per = ROWS // own
    steps = blocks // per
    size = ROWS // blocks
    units = own // size
    pairs = width // LANES

    def gain(index):
        return gain_ref[index, layer : layer + 1, :], shift_ref[index, layer : layer + 1, :]

    parts = own // size

    def project(f):
        def rows(part, carry):
            _, _, hidden = layer_norm(block_rows(x_ref, f, part, per), *gain(0))
            hidden = hidden.astype(bf16)
            h1_ref[f, chunk(part, per), :, :] = hidden.reshape(per, own, width)
            for member in range(3):
                out = mm(hidden, w_ref[member]).astype(bf16)
                if member == 0:
                    out = out * jnp.asarray(0.125, bf16)
                qkv_ref[member, f, chunk(part, per), :, :] = out.reshape(per, own, width)
            return carry

        lax.fori_loop(0, steps, rows, 0)

    def copies(unit):
        f, part = unit // parts, lax.rem(unit, parts)
        found = [
            remote(
                h2_ref.at[f, place.ring(k), chunk(part, size), :],
                swapped_ref.at[place.place, f, chunk(part, size), :],
                sends.at[unit, k - 1],
                recvs.at[unit, k - 1],
                {"feat": place.ring(k)},
            )
            for k in range(1, place.places)
        ]
        keep = pltpu.make_async_copy(
            h2_ref.at[f, place.place, chunk(part, size), :],
            swapped_ref.at[place.place, f, chunk(part, size), :],
            self_sem.at[unit],
        )
        return found, keep

    def attend(unit, carry):
        f, part = unit // parts, lax.rem(unit, parts)

        @pl.when(part == 0)
        def _():
            if before is not None:
                before(f)
            project(f)

        code = sq_ref[...]
        extras = code.astype(f32)
        for pair in range(pairs):
            lanes = pair_lanes(pair)
            context, extras = attend_pair(
                own_rows(qkv_ref.at[0], f, part, size, lanes),
                all_rows(qkv_ref.at[1], f, lanes),
                all_rows(qkv_ref.at[2], f, lanes),
                code,
                sk_ref[...],
                pair,
                extras,
            )
            ctx_ref[f, :, chunk(part, size), lanes] = context.reshape(blocks, size, LANES)
        ext_ref[f, :, chunk(part, size), :] = extras.astype(bf16).reshape(blocks, size, LANES)
        x1 = own_rows(x_ref, f, part, size) + mm(own_rows(ctx_ref, f, part, size), w_ref[3])
        x1_ref[f, :, chunk(part, size), :] = x1.reshape(blocks, size, width)
        _, _, hidden = layer_norm(x1, *gain(1))
        h2_ref[f, :, chunk(part, size), :] = hidden.astype(bf16).reshape(blocks, size, width)

        @pl.when(unit == 0)
        def _():
            if layer == 0:
                box.ready()
                box.start(weights + 1, weights + 2, 5, weights + 3, 6)
            if not last:
                box.start(weights + 4, weights + 5, weights + 6, weights + 7)
            else:
                box.start(7 + 4 * (layer + 1))

        found, keep = copies(unit)
        for copy in found:
            copy.start()
        keep.start()
        return carry

    lax.fori_loop(0, features * units, attend, 0)
    box.flush(*[outs[index] for index in (0, 1, 2, 3, 11)])
    if before is not None:
        box.flush(*[earlier[index] for index in (8, 9, 10, 12, 13)])
        before(None)
    fw_ref = box.use(weights + 1)
    if layer > 0:
        box.settle(*earlier[4:8])
    groups = own // SIZE
    shared = size // SIZE

    def back_copies(group, f=None):
        which = slice(None) if f is None else f
        at = 0 if f is None else f
        return [
            remote(
                a_ref.at[place.ring(k), which, chunk(group, SIZE), :],
                back_ref.at[which, place.place, chunk(group, SIZE), :],
                back_sends.at[at, group, k - 1],
                back_recvs.at[at, group, k - 1],
                {"feat": place.ring(k)},
            )
            for k in range(1, place.places)
        ]

    def feature(group, carry):
        @pl.when(lax.rem(group, shared) == 0)
        def _():
            for f in range(features):
                found, keep = copies(f * parts + group // shared)
                for copy in found:
                    copy.wait_recv()
                keep.wait()

        hidden = cross(swapped_ref, group)
        hidden_ref[group] = hidden
        for member in range(3):
            out = mm(hidden, fw_ref[member]).astype(bf16)
            if member == 0:
                out = out * jnp.asarray(0.125, bf16)
            fqkv_ref[group, member] = out
        code = fq_ref[...]
        extras = code.astype(f32)
        for pair in range(pairs):
            lanes = pair_lanes(pair)
            context, extras = attend_pair(
                fqkv_ref[group, 0, :, lanes],
                fqkv_ref[group, 1, :, lanes],
                fqkv_ref[group, 2, :, lanes],
                code,
                fk_ref[...],
                pair,
                extras,
            )
            fctx_ref[group, :, lanes] = context
        fext_ref[group] = extras.astype(bf16)
        put_cross(a_ref, group, mm(fctx_ref[group], fw_ref[3]).astype(bf16))
        for copy in back_copies(group, None if last else 0):
            copy.start()
        back_ref[:, place.place, chunk(group, SIZE), :] = a_ref[place.place, :, chunk(group, SIZE), :]
        return carry

    lax.fori_loop(0, groups, feature, 0)
    if not last:
        for f in range(1, features):

            def send_rest(group, carry, f=f):
                for copy in back_copies(group, f):
                    copy.start()
                return carry

            lax.fori_loop(0, groups, send_rest, 0)
    box.flush(*outs[4:8])

    def settle(unit, carry):
        for copy in copies(unit)[0]:
            copy.wait_send()
        return carry

    lax.fori_loop(0, features * units, settle, 0)
    if last:
        og_ref = box.out(first + LAYER_OUTS + 1)
        raw_ref[...] = box.use(7 + 4 * (layer + 1))[...].astype(f32)
        from_rows(raw_ref, og_ref)
        box.flush(first + LAYER_OUTS + 1)
    up_ref, upb_ref, down_ref, downb_ref = box.use(weights + 2, 5, weights + 3, 6)
    if layer > 0:
        box.settle(*[earlier[index] for index in (8, 9, 10, 12, 13)])
    hidden_width = up_ref.shape[1]

    def feed_forward(x2, keep):
        _, _, hidden = layer_norm(x2, *gain(2))
        hidden = hidden.astype(bf16)
        keep(h3_ref, slice(None), hidden)
        columns = [slice(part * 512, part * 512 + 512) for part in range(hidden_width // 512)]
        actives = []
        for cols in columns:
            u = mm(hidden, up_ref[:, cols]) + upb_ref[layer : layer + 1, cols]
            bent = gelu_parts(u)
            both = 0.5 * (1.0 + bent)
            active = (u * both).astype(bf16)
            keep(active_ref, cols, active)
            slope = both + u * (1.0 - bent * bent) * (0.3989422804014327 + 0.05351611220146811 * u * u)
            keep(u_ref, cols, slope.astype(bf16))
            actives.append(active)
        return x2 + downb_ref[layer : layer + 1, :] + mm(jnp.concatenate(actives, axis=1), down_ref[...])

    def dense(group, carry):
        for copy in back_copies(group):
            copy.wait_recv()
        x2 = cross(x1_ref, group) + cross(back_ref, group).astype(f32)
        put_cross(x2_ref, group, x2)

        def keep(ref, cols, values):
            ref[group, :, cols] = values

        put_cross(x3_ref, group, feed_forward(x2, keep))
        box.flush_part(outs[8], group, cross_view)
        box.flush_part(outs[9], group, cross_view)
        box.flush_part(outs[10], group, first_view)
        box.flush_part(outs[12], group, first_view)
        box.flush_part(outs[13], group, first_view)
        return carry

    def dense_of(f):
        if f is None:

            def settle_back(group, carry):
                for other in range(features):
                    for copy in back_copies(group, other):
                        copy.wait_send()
                return carry

            lax.fori_loop(0, groups, settle_back, 0)
            return

        def arrived(group, carry):
            for copy in back_copies(group, f):
                copy.wait_recv()
            return carry

        lax.fori_loop(0, groups, arrived, 0)

        def rows(unit, carry):
            x2 = own_rows(x1_ref, f, unit, size) + own_rows(back_ref, f, unit, size).astype(f32)
            x2_ref[f, :, chunk(unit, size), :] = x2.reshape(blocks, size, width)
            count = blocks * SIZE

            def keep(ref, cols, values):
                parted = values.reshape(blocks, shared, SIZE, values.shape[1])
                for at in range(shared):
                    ref[unit * shared + at, chunk(f, count), cols] = parted[:, at].reshape(count, values.shape[1])

            x3_ref[f, :, chunk(unit, size), :] = feed_forward(x2, keep).reshape(blocks, size, width)
            return carry

        lax.fori_loop(0, parts, rows, 0)

    if not last:
        return dense_of
    lax.fori_loop(0, groups, dense, 0)

    def settle_back(group, carry):
        for copy in back_copies(group):
            copy.wait_send()
        return carry

    lax.fori_loop(0, groups, settle_back, 0)
    return None


def pieces_of(values):
    first = values.astype(bf16)
    rest = values - first.astype(f32)
    second = rest.astype(bf16)
    return first, second, (rest - second.astype(f32)).astype(bf16)


def exact(left, right, dims):
    first, second, third = pieces_of(right)
    return mm(left, first, dims) + mm(left, second, dims) + mm(left, third, dims)


def exact_left(left, right, dims):
    first, second, third = pieces_of(left)
    return mm(first, right, dims) + mm(second, right, dims) + mm(third, right, dims)


def read_out(box, ins, later, outs, x_ref, x_load, g_ref, reading_ref, got_ref, bins_ref, counted_ref, read_ref, weight_ref, sends, recvs):
    place = box.place
    shapes_ref, loss_ref, rgrad_ref = box.out(*outs)
    read_ref[...] = jnp.zeros_like(read_ref)
    size_ref, count_ref, label_ref, index_ref, population_ref, narrow_ref = box.use(*ins)
    x_load.wait()
    box.start(*later)
    read_ref[0 : narrow_ref.shape[0], :] = narrow_ref[...]
    features, blocks, own, width = x_ref.shape
    samples = blocks * own
    bins = population_ref.shape[1]
    size, count = size_ref[0], count_ref[0]
    mask = (lax.broadcasted_iota(jnp.int32, (1, samples), 1) < size).astype(f32)
    task_size = jnp.zeros((1, samples), f32) + size.astype(f32)
    level = lax.broadcasted_iota(jnp.int32, (bins, bins), 0)
    diagonal = (level == lax.broadcasted_iota(jnp.int32, (bins, bins), 1)).astype(f32)
    live = [
        jnp.where(place.place * features + f < count, 1.0, 0.0) for f in range(features)
    ]
    logits = None
    for f in range(features):
        reading = x_ref[f].reshape(samples, width).astype(bf16)
        reading_ref[f] = reading.reshape(blocks, own, width)
        projected = mm(reading, read_ref[...], NT)
        onehot = (lax.broadcasted_iota(jnp.int32, (bins, samples), 0) == index_ref[f : f + 1, :]).astype(f32)
        bins_ref[f] = onehot.astype(bf16)
        chosen = onehot * mask
        counted = jnp.maximum(jnp.sum(chosen, axis=1, keepdims=True), 1.0)
        counted_ref[f] = jnp.broadcast_to(counted, (bins, LANES))
        means = exact(chosen.astype(bf16), projected, NN) / counted
        weight = jnp.sum(diagonal * population_ref[f : f + 1, :].astype(f32), axis=1, keepdims=True)
        weight_ref[f] = jnp.broadcast_to(weight, (bins, LANES))
        weight = weight_ref[f]
        centre = jnp.sum(weight * means, axis=0, keepdims=True) / jnp.sum(weight, axis=0, keepdims=True)
        shapes = means - centre
        shapes_ref[f] = shapes
        part = exact_left(shapes, bins_ref[f], TN)[:SIZE] * live[f]
        logits = part if logits is None else logits + part
    spans = range(samples // LANES)
    got_ref[place.place] = jnp.concatenate([logits[0:CLASSES, pair_lanes(span)] for span in spans], axis=0)
    box.ready()
    copies = [
        remote(
            got_ref.at[place.place],
            got_ref.at[place.place],
            sends.at[k - 1],
            recvs.at[k - 1],
            {"feat": place.ring(k)},
        )
        for k in range(1, place.places)
    ]
    for copy in copies:
        copy.start()
    for copy in copies:
        copy.wait()
    total = got_ref[0]
    for k in range(1, place.places):
        total = total + got_ref[k]
    rows_left = jnp.zeros((SIZE - CLASSES, LANES), f32)
    logits = jnp.concatenate(
        [
            jnp.concatenate([total[span * CLASSES : span * CLASSES + CLASSES], rows_left], axis=0)
            for span in spans
        ],
        axis=1,
    )
    class_row = lax.broadcasted_iota(jnp.int32, logits.shape, 0)
    inside = class_row < CLASSES
    peak = jnp.max(jnp.where(inside, logits, masked_score), axis=0, keepdims=True)
    weights = jnp.where(inside, jnp.exp(jnp.where(inside, logits - peak, 0.0)), 0.0)
    weight_sum = jnp.sum(weights, axis=0, keepdims=True)
    log_total = peak + jnp.log(weight_sum)
    own_class = (class_row == label_ref[...]).astype(f32)
    picked = jnp.sum(logits * own_class, axis=0, keepdims=True)
    losses = mask * (log_total - picked)
    loss_ref[...] = jnp.broadcast_to(
        jnp.sum(losses, axis=1, keepdims=True) / task_size[:, 0:1], loss_ref.shape
    )
    logit_grad = mask * (weights / weight_sum - own_class) / task_size
    pad = jnp.zeros((LANES - SIZE, samples), f32)
    total = None
    for f in range(features):
        grad_rows = jnp.concatenate([logit_grad * live[f], pad], axis=0)
        shape_grad = exact(bins_ref[f], grad_rows, NT)
        weight = weight_ref[f]
        means_grad = shape_grad - weight / jnp.sum(weight, axis=0, keepdims=True) * jnp.sum(
            shape_grad, axis=0, keepdims=True
        )
        chosen = (bins_ref[f].astype(f32) * mask).astype(bf16)
        proj_grad = exact(chosen, means_grad / counted_ref[f], TN).astype(bf16)
        part = mm(proj_grad, all_rows(reading_ref, f), TN)[:SIZE]
        total = part if total is None else total + part
        if f == 0:
            box.use(1)
        back = mm(proj_grad, read_ref[...]).reshape(blocks, own, width)
        g_ref[f] = g_ref[f] + back
    rgrad_ref[...] = total
    box.flush(*outs)


def dense_feature_backward(layer, box, fk_ref, send_ref, ugrad_ref, rowgrad_ref, dup_ref, ddown_ref, arriving_ref, dc_ref, dh_ref, back_ref, dwf_ref, sends, recvs, self_sem, back_sends, back_recvs, *head):
    place = box.place
    g1_ref, small_ref, sdc_ref, sext_ref, slow_ref = box.out(0, 1, 2, 3, 4)
    if head:
        x_load = pltpu.make_async_copy(box.bufs[18], g1_ref, head[-1])
        box.start(19, 20, 21, 22)
        x_load.start()
    else:
        box.start(6, 7, (1, 0), 2, (3, 0), 4, (5, 0))
    small_ref[...] = jnp.zeros_like(small_ref)
    fill_feature_codes(box.use(0)[0], None, fk_ref)
    if not head:
        box.use(6, 7, 2, 4)
    gain_ref, shift_ref, down_ref, up_ref = box.bufs[6], box.bufs[7], box.bufs[2], box.bufs[4]
    g_ref, slope_ref, x2_ref = box.bufs[1], box.bufs[3], box.bufs[5]
    active_ref, hidden3_ref = box.bufs[16], box.bufs[17]
    if not head:
        box.start((1, 1, 2, 3), (3, 1, 2, 3), (5, 1, 2, 3))
    else:
        later = (1, 6, 7, 2, 3, 4, 5, 17, 16, 8, 9, 10, 11, 12, 13, 14, 15)
        read_out(box, (23, 0, 19, 20, 21, 22), later, (5, 6, 7), g1_ref, x_load, g_ref, send_ref, *head[:-1])
        box.use(6, 7, 2, 4)
    features, blocks, own, width = g_ref.shape
    hidden_width = up_ref.shape[1]
    groups = own // SIZE
    parts = hidden_width // 512
    pairs = width // LANES

    def copies(group):
        found = [
            remote(
                send_ref.at[:, place.ring(k), chunk(group, SIZE), :],
                arriving_ref.at[place.place, :, chunk(group, SIZE), :],
                sends.at[group, k - 1],
                recvs.at[group, k - 1],
                {"feat": place.ring(k)},
            )
            for k in range(1, place.places)
        ]
        keep = pltpu.make_async_copy(
            send_ref.at[:, place.place, chunk(group, SIZE), :],
            arriving_ref.at[place.place, :, chunk(group, SIZE), :],
            self_sem.at[group],
        )
        return found, keep

    def dense(group, carry):
        rows = chunk(group, ROWS)
        if not head:
            box.part(1, group)
        box.part(3, group)
        box.part(5, group)
        grad = cross(g_ref, group)
        low = grad.astype(bf16)
        rowgrad_ref[rows, :] = low
        small_ref[parts : parts + 1] += jnp.sum(low.astype(f32), axis=0, keepdims=True)
        for part in range(parts):
            cols = slice(part * 512, part * 512 + 512)
            active_grad = mm(low, down_ref[cols, :], NT).astype(bf16).astype(f32)
            ugrad = (active_grad * slope_ref[group, :, cols].astype(f32)).astype(bf16)
            ugrad_ref[rows, cols] = ugrad
            small_ref[part : part + 1] += jnp.sum(ugrad.astype(f32), axis=0, keepdims=True)
        hidden_grad = mm(ugrad_ref[rows, :], up_ref[...], NT)
        x2 = cross(x2_ref, group)
        gain = gain_ref[2, layer : layer + 1, :]
        norm_grad, gain_part, shift_part = layer_norm_back(hidden_grad.astype(bf16).astype(f32), x2, gain)
        small_ref[parts + 1 : parts + 2] += gain_part
        small_ref[parts + 2 : parts + 3] += shift_part
        grad = grad + norm_grad
        put_cross(g1_ref, group, grad)
        put_cross(send_ref, group, grad.astype(bf16))
        if not head:

            @pl.when(group == 0)
            def _():
                box.ready()
                box.start(17, 16, 8, 9, 10, 11, 12, 13, 14, 15)

        found, keep = copies(group)
        for copy in found:
            copy.start()
        keep.start()
        return carry

    lax.fori_loop(0, groups, dense, 0)

    def up_weights(part, carry):
        cols = chunk(part, 512)
        out = mm(ugrad_ref[:, cols], hidden3_ref[...], TN)
        dup_ref[part // 2, lax.rem(part, 2)] = out.astype(bf16).reshape(dup_ref.shape[2:])
        return carry

    def down_weights(part, carry):
        cols = chunk(part, 512)
        out = mm(active_ref[:, cols], rowgrad_ref[...], TN)
        ddown_ref[part // 2, lax.rem(part, 2)] = out.astype(bf16).reshape(ddown_ref.shape[2:])
        return carry

    box.use(16, 17)
    lax.fori_loop(0, parts, up_weights, 0)
    box.chains[0].begin(dup_ref)
    lax.fori_loop(0, parts, down_weights, 0)
    box.point("dense")
    box.chains[1].begin(ddown_ref)
    grads_ref = active_ref
    w_ref, qkv_ref, ctx_ref, ext_ref = box.use(8, 9, 10, 11)

    def back_copies(group):
        return [
            remote(
                dh_ref.at[place.ring(k), :, chunk(group, SIZE), :],
                back_ref.at[:, place.place, chunk(group, SIZE), :],
                back_sends.at[group, k - 1],
                back_recvs.at[group, k - 1],
                {"feat": place.ring(k)},
            )
            for k in range(1, place.places)
        ]

    def feature(group, carry):
        found, keep = copies(group)
        for copy in found:
            copy.wait_recv()
        keep.wait()
        rows = chunk(group, ROWS)
        dao = cross(arriving_ref, group)
        grads_ref[rows, 3 * width : 4 * width] = dao
        context_grad = mm(dao, w_ref[3], NT).astype(bf16)
        dc_ref[...] = context_grad
        grad_extra = delta_extra(ctx_ref[group], context_grad)
        for pair in range(pairs):
            lanes = pair_lanes(pair)
            query_grad, key_grad, value_grad = attend_pair_back(
                qkv_ref[group, 0, :, lanes],
                qkv_ref[group, 1, :, lanes],
                qkv_ref[group, 2, :, lanes],
                dc_ref[:, lanes],
                ext_ref[group],
                grad_extra,
                fk_ref[...],
                pair,
            )
            for member, grad in enumerate((query_grad * 0.125, key_grad, value_grad)):
                at = member * width + pair * LANES
                grads_ref[rows, at : at + LANES] = grad.astype(bf16)
        total = mm(grads_ref[rows, 0:width], w_ref[0], NT)
        total = total + mm(grads_ref[rows, width : 2 * width], w_ref[1], NT)
        total = total + mm(grads_ref[rows, 2 * width : 3 * width], w_ref[2], NT)
        put_cross(dh_ref, group, total.astype(bf16))
        for copy in back_copies(group):
            copy.start()
        back_ref[:, place.place, chunk(group, SIZE), :] = dh_ref[place.place, :, chunk(group, SIZE), :]

        for at in range(groups):

            @pl.when(group == at)
            def _(at=at):
                box.point(at)

        return carry

    lax.fori_loop(0, groups, feature, 0)
    hidden_ref = box.use(12)

    def weights(member, carry):
        hidden = hidden_ref[...].reshape(groups * ROWS, width)
        out = mm(hidden, grads_ref[:, chunk(member, width)], TN)
        dwf_ref[member // 2, lax.rem(member, 2)] = out.astype(bf16).reshape(dwf_ref.shape[2:])
        return carry

    lax.fori_loop(0, 3, weights, 0)
    context = ctx_ref[...].reshape(groups * ROWS, width)
    out = mm(context, grads_ref[:, 3 * width : 4 * width], TN)
    dwf_ref[1, 1] = out.astype(bf16).reshape(dwf_ref.shape[2:])
    box.chains[2].begin(dwf_ref)
    box.point("weights")
    x1_ref, wo_ref, sctx_ref = box.use(13, 14, 15)

    def enter(group, carry):
        for copy in back_copies(group):
            copy.wait_recv()
        norm_grad, gain_part, shift_part = layer_norm_back(
            cross(back_ref, group).astype(f32), cross(x1_ref, group), gain_ref[1, layer : layer + 1, :]
        )
        small_ref[parts + 3 : parts + 4] += gain_part
        small_ref[parts + 4 : parts + 5] += shift_part
        grad = cross(g1_ref, group) + norm_grad
        put_cross(g1_ref, group, grad)
        low = grad.astype(bf16)
        put_cross(slow_ref, group, low)
        context_grad = mm(low, wo_ref[...], NT).astype(bf16)
        put_cross(sdc_ref, group, context_grad)
        put_cross(sext_ref, group, delta_extra(cross(sctx_ref, group), context_grad))
        box.flush_part(0, group, cross_view)
        box.flush_part(2, group, cross_view)
        box.flush_part(3, group, cross_view)
        box.flush_part(4, group, cross_view)

        for at in range(groups):

            @pl.when(group == at)
            def _(at=at):
                box.point(10 + at)

        return carry

    lax.fori_loop(0, groups, enter, 0)
    box.flush(1)
    box.point("end")

    def settle(group, carry):
        for copy in copies(group)[0]:
            copy.wait_send()
        for copy in back_copies(group):
            copy.wait_send()
        return carry

    lax.fori_loop(0, groups, settle, 0)


def sample_backward_last(layer, last, box, sk_ref, dqkv_ref, *tail):
    place = box.place
    g0_ref, small_ref = box.out(0, 1)
    box.start((1, 0), (2, 0), 3, 4)
    small_ref[...] = jnp.zeros_like(small_ref)
    fill_sample_codes(box.use(0)[0], None, sk_ref)
    qkv_ref, dc_ref = box.bufs[1], box.bufs[2]
    features, blocks, own, width = dc_ref.shape
    samples = blocks * own
    per = ROWS // own
    steps = blocks // per
    pairs = width // LANES
    total_rows = features * samples
    if last:
        dw_ref, bufs_1, bufs_2, bufs_3, *small_bufs = tail
        share_ref = box.out(3)
    else:
        dw_ref, *small_bufs = tail
    exchange = SmallSums(place, last, *small_bufs)
    ext_ref, gext_ref = box.use(3, 4)
    box.ready()
    box.start((1, 1, 2, 3), (2, 1, 2, 3), 9, 10, 11, 12, 13)

    def step_of(step, pair):
        got_ref, _, sends, recvs = (bufs_1, bufs_2, bufs_3)[step - 1]
        source = dw_ref.at[pair] if step == 1 else (bufs_1, bufs_2)[step - 2][1].at[pair]
        return SumStep(5 if step == 3 else step, place, source, None, got_ref.at[pair], sends.at[pair], recvs.at[pair], None)

    def pass_on(step, pair):
        step_of(step, pair).finish((bufs_1, bufs_2, bufs_3)[step - 1][1].at[pair])
        if step < 3:
            step_of(step + 1, pair).start()

    def attend(pair, carry):
        lanes = chunk(pair, LANES)
        box.part(1, pair)
        box.part(2, pair)
        for f in range(features):
            key_total = value_total = None
            for step in range(steps):
                rows = slice(f * samples + step * ROWS, f * samples + step * ROWS + ROWS)
                query_grad, key_grad, value_grad = attend_pair_back(
                    block_rows(qkv_ref.at[0], f, step, per, lanes),
                    all_rows(qkv_ref.at[1], f, lanes),
                    all_rows(qkv_ref.at[2], f, lanes),
                    block_rows(dc_ref, f, step, per, lanes),
                    block_rows(ext_ref, f, step, per),
                    block_rows(gext_ref, f, step, per),
                    sk_ref[...],
                    pair,
                )
                dqkv_ref[0, rows, lanes] = (query_grad * 0.125).astype(bf16)
                key_total = key_grad if key_total is None else key_total + key_grad
                value_total = value_grad if value_total is None else value_total + value_grad
            rows = slice(f * samples, f * samples + samples)
            dqkv_ref[1, rows, lanes] = key_total.astype(bf16)
            dqkv_ref[2, rows, lanes] = value_total.astype(bf16)

        for at in range(1, pairs):

            @pl.when(pair == at)
            def _(at=at):
                box.point(at)

        @pl.when(pair == 0)
        def _():
            box.start(5, 6, 7, 8)
            dense_rows, other_rows = box.use(12, 13)
            if last:
                exchange.start([(0, 9, dense_rows, 9), (9, 11, other_rows, 2)])
            else:
                exchange.start([(0, 9, dense_rows, 9), (9, 9 + SIZE, other_rows, SIZE)])

        for stage in range(1, 4):

            @pl.when(pair == stage)
            def _(stage=stage):
                exchange.move(stage)

        if not last:
            return carry

        @pl.when(pair == 0)
        def _():
            box.use(9, 10, 11)

        hidden = box.bufs[9][...].reshape(total_rows, width)
        context = box.bufs[10][...].reshape(total_rows, width)
        low_ref = box.bufs[11]
        block = dw_ref.shape[3:]
        for member in range(3):
            out = mm(dqkv_ref[member, :, lanes], hidden, TN).T
            dw_ref[pair, member // 2, member % 2] = out.astype(bf16).reshape(block)
        low = low_ref[:, :, :, lanes].reshape(total_rows, LANES)
        dw_ref[pair, 1, 1] = mm(low, context, TN).T.astype(bf16).reshape(block)
        step_of(1, pair).start()

        @pl.when(pair >= 1)
        def _():
            pass_on(1, pair - 1)

        @pl.when(pair >= 2)
        def _():
            pass_on(2, pair - 2)

        return carry

    lax.fori_loop(0, pairs, attend, 0)
    box.point("attend")
    if not last:
        hidden_ref, context_ref, low_ref = box.use(9, 10, 11)

        def weights(member, carry):
            hidden = hidden_ref[...].reshape(total_rows, width)
            out = mm(hidden, dqkv_ref[member], TN)
            dw_ref[member // 2, lax.rem(member, 2)] = out.astype(bf16).reshape(dw_ref.shape[2:])
            return carry

        lax.fori_loop(0, 3, weights, 0)
        context = context_ref[...].reshape(total_rows, width)
        out = mm(context, low_ref[...].reshape(total_rows, width), TN)
        dw_ref[1, 1] = out.astype(bf16).reshape(dw_ref.shape[2:])
        box.chains[-1].begin(dw_ref)
    w_ref, x_ref, gain_ref, g_ref = box.use(5, 6, 7, 8)
    gain = gain_ref[0, layer : layer + 1, :]

    def leave(unit, carry):
        f, part = unit // steps, lax.rem(unit, steps)
        rows = chunk(unit, ROWS)
        total = mm(dqkv_ref[0, rows, :], w_ref[0], NT)
        total = total + mm(dqkv_ref[1, rows, :], w_ref[1], NT)
        total = total + mm(dqkv_ref[2, rows, :], w_ref[2], NT)
        norm_grad, gain_part, shift_part = layer_norm_back(
            total.astype(bf16).astype(f32), block_rows(x_ref, f, part, per), gain
        )
        small_ref[0:1] += gain_part
        small_ref[1:2] += shift_part
        g0_ref[f, chunk(part, per), :, :] = (block_rows(g_ref, f, part, per) + norm_grad).reshape(per, own, width)
        if last:

            @pl.when(unit == 1)
            def _():
                pass_on(1, pairs - 1)

            @pl.when(unit == 2)
            def _():
                pass_on(2, pairs - 2)

        @pl.when(unit == 2)
        def _():
            box.point("leave")
            box.out(2)[...] = exchange.sum(3)
            box.flush(2)

        return carry

    lax.fori_loop(0, features * steps, leave, 0)
    box.flush(0, 1)
    if last:
        exchange.start_late(small_ref)
        pass_on(2, pairs - 1)
        exchange.move(5)
    box.point("end")
    if last:
        for pair in range(pairs):
            pass_on(3, pair)
            share_ref[:, pair_lanes(pair)] = bufs_3[1][pair]
        box.flush(3)
        box.out(4)[...] = exchange.sum(5)
        box.flush(4)


class SmallSums:
    def __init__(self, place, last, packed, early, late, sends, recvs):
        self.packed, self.early, self.late = packed, early, late
        tasks = [{"task": place.task_partner(k)} for k in range(1, place.tasks)]
        ring = [{"feat": place.ring(k)} for k in range(1, place.places)]
        plan = [
            (early, 0, 2, place.core, [place.other_core]),
            (early, 2, place.tasks, place.task, tasks),
            (early, 2 + place.tasks, 2, place.near, [place.near_chip]),
            (early, 4 + place.tasks, 2, place.far, [place.far_chip]),
            (late, 0, place.places, place.place, ring),
            (late, place.places, place.tasks, place.task, tasks),
        ]
        plan = plan if last else plan[:4]
        self.plan, self.copies, at = plan, [], 0
        for buffer, first, count, mine, devices in plan:
            slot = buffer.at[first + mine]
            self.copies.append(
                [remote(slot, slot, sends.at[at + k], recvs.at[at + k], device) for k, device in enumerate(devices)]
            )
            at += len(devices)

    def send(self, stage, rows):
        buffer, first, _, mine, _ = self.plan[stage]
        buffer[first + mine] = rows
        for copy in self.copies[stage]:
            copy.start()

    def start(self, parts):
        self.packed[...] = jnp.zeros_like(self.packed)
        for begin, end, source, count in parts:
            self.packed[begin:end] = source[0:count]
        self.send(0, self.packed[...])

    def start_late(self, rows_ref):
        blocks = [rows_ref[row : row + 1, pair_lanes(block)] for row in range(2) for block in range(4)]
        self.send(4, jnp.concatenate(blocks, axis=0))

    def sum(self, stage):
        buffer, first, count, _, _ = self.plan[stage]
        for copy in self.copies[stage]:
            copy.wait()
        total = buffer[first]
        for k in range(1, count):
            total = total + buffer[first + k]
        return total

    def move(self, stage):
        self.send(stage, self.sum(stage - 1))


def write_out(dense_rows, x_ref, g_ref, *refs):
    refs = list(refs)
    shares, packed_rows, late, bins, loss, outs = refs[:8], refs[8:10], refs[10], refs[11], refs[12], refs[13:26]
    raw_x, raw_g, x_buf, g_buf, load_sem, out_sem = refs[26:]
    outs[12][0] = loss[0, 0]
    for f in range(bins.shape[0]):
        outs[11][:, f, :] = bins[f].T[0:CLASSES]
    features, blocks, own, width = x_ref.shape
    period = features * (width // LANES)
    per = blocks // 4
    rows_part = per * own

    def load(part, which):
        source, target = ((x_ref, x_buf), (g_ref, g_buf))[which]
        view = (slice(None), pl.ds(part * per, per))
        return pltpu.make_async_copy(source.at[view], target.at[view], load_sem.at[which, part])

    def store(part, which):
        source, target = ((raw_x, outs[0]), (raw_g, outs[1]))[which]
        view = pl.ds(part * rows_part * period, rows_part * period)
        return pltpu.make_async_copy(source.at[view], target.at[view], out_sem.at[which, part])

    for part in range(4):
        load(part, 0).start()
        load(part, 1).start()
    for member in range(4):
        outs[2 + member][0] = shares[2 * member][...]
        outs[2 + member][1] = shares[2 * member + 1][...]
    parts = dense_rows - 5
    for layer in range(2):
        packed, at = packed_rows[layer], 0
        for part in range(parts):
            outs[8][layer : layer + 1, part * width : (part + 1) * width] = packed[at + part : at + part + 1]
        outs[9][layer : layer + 1] = packed[at + parts : at + parts + 1]
        for member, row in ((2, parts + 1), (1, parts + 3)):
            outs[6][member, layer : layer + 1] = packed[at + row : at + row + 1]
            outs[7][member, layer : layer + 1] = packed[at + row + 1 : at + row + 2]
    at = dense_rows
    for block in range(4):
        lanes = pair_lanes(block)
        outs[6][0, 0:1, lanes], outs[7][0, 0:1, lanes] = late[block : block + 1], late[4 + block : 5 + block]
    outs[6][0, 1:2], outs[7][0, 1:2] = packed_rows[0][at : at + 1], packed_rows[0][at + 1 : at + 2]
    outs[10][...] = packed_rows[1][at : at + CLASSES]

    for part in range(4):
        for which, buf, raw in ((0, x_buf, raw_x), (1, g_buf, raw_g)):
            load(part, which).wait()
            for f in range(features):
                for block in range(width // LANES):
                    rows = buf[f, part * per : (part + 1) * per, :, pair_lanes(block)].reshape(rows_part, LANES)
                    start = part * rows_part * period + block * features + f
                    raw[pl.ds(start, rows_part, stride=period), :] = rows
            store(part, which).start()
    for part in range(4):
        store(part, 0).wait()
        store(part, 1).wait()


def codes(item, live, size, rows):
    lanes = jnp.arange(LANES)[None, :] - CODE_LANE
    inside = (lanes >= 0) & (lanes < size)
    own = lanes == item[:, None]
    query_code = (own & inside).astype(bf16)
    key_code = jnp.where(inside & ~(own & live[:, None]), masked_score, 0.0).astype(bf16)
    return query_code, key_code


def local_fused(
    tokens_in,
    sample_weights,
    feature_weights,
    norm_gain,
    norm_shift,
    up_weight,
    up_bias,
    down_weight,
    down_bias,
    read_weight,
    output_grad,
    task_sizes,
    feature_counts,
    bin_index,
    bin_counts,
    class_labels,
):
    samples, features, width = tokens_in.shape[1:]
    hidden_width = up_weight.shape[2]
    tasks, places = lax.axis_size("task"), lax.axis_size("feat")
    own = samples // places
    groups = own // SIZE
    units = features * (own * places // ROWS)
    sizes = (tasks, places)
    shape = (features, places, own, width)
    block_shape = (places, features, own, width)
    group_shape = (groups, ROWS, width)
    share = width // places
    share_shape = (share, width)
    piece_shape = (2, 2, 2, 2, 2, share, width)
    rows_total = groups * ROWS
    vmem = pltpu.VMEM

    def dma(*counts):
        return pltpu.SemaphoreType.DMA(counts)

    def raw_rows(tokens):
        parts = tokens.reshape(samples, features, width // LANES, LANES)
        return parts.transpose(0, 2, 1, 3).reshape(samples * features * (width // LANES), LANES)

    def from_raw(rows):
        parts = rows.reshape(samples, width // LANES, features, LANES)
        return parts.transpose(0, 2, 1, 3).reshape(1, samples, features, width)

    gains = norm_gain.transpose(1, 0, 2)
    shifts = norm_shift.transpose(1, 0, 2)
    layer_outs = [
        (shape, f32),
        ((3,) + shape, bf16),
        (shape, bf16),
        (shape[:3] + (LANES,), bf16),
        (group_shape, bf16),
        ((groups, 3, ROWS, width), bf16),
        (group_shape, bf16),
        ((groups, ROWS, LANES), bf16),
        (shape, f32),
        (shape, f32),
        ((groups, ROWS, hidden_width), bf16),
        (shape, bf16),
        ((groups, ROWS, hidden_width), bf16),
        (group_shape, bf16),
    ]
    ins = [
        (task_sizes, "scalar"),
        (feature_counts, "scalar"),
        (raw_rows(tokens_in), None),
        (gains, None),
        (shifts, None),
        (up_bias, None),
        (down_bias, None),
    ]
    for layer in range(LAYERS):
        ins += [(weight, layer) for weight in (sample_weights, feature_weights, up_weight, down_weight)]
    ins.append((raw_rows(output_grad), None))
    outs = list(layer_outs)
    for layer in range(1, LAYERS):
        outs += [(*item, index) for index, item in enumerate(layer_outs)]
    outs += [(shape, f32), (shape, f32)]
    *kept, first_rows, stream_grad = fused(
        functools.partial(forward_layers, LAYERS),
        "forward_layers",
        sizes,
        ins,
        outs,
        [
            vmem((ROWS, LANES), bf16),
            vmem((samples, LANES), bf16),
            vmem((ROWS, LANES), bf16),
            vmem((ROWS, LANES), bf16),
            vmem((samples * features * (width // LANES), LANES), f32),
            vmem(shape, bf16),
            vmem(block_shape, bf16),
            vmem(block_shape, bf16),
            vmem(shape, bf16),
            dma(LAYERS, units, places - 1),
            dma(LAYERS, units, places - 1),
            dma(LAYERS, units),
            dma(LAYERS, features, groups, places - 1),
            dma(LAYERS, features, groups, places - 1),
        ],
        [],
        share_shape,
        1,
    )
    stored = []
    stream = first_rows
    for layer in range(LAYERS):
        x1, qkv, ctx, ext, hidden, fqkv, fctx, fext, x2, x3, u, h1, act, h3 = kept[14 * layer : 14 * layer + 14]
        stored.append((stream, x1, qkv, ctx, ext, hidden, fqkv, fctx, fext, x2, u, h1, act, h3))
        stream = x3

    finished = {}
    dense_rows = hidden_width // width + 5
    pairs = width // LANES
    flat = (rows_total, width)
    for layer in reversed(range(LAYERS)):
        x0, x1, qkv, ctx, ext, hidden, fqkv, fctx, fext, x2, u, h1, act, h3 = stored[layer]
        last = layer == 0
        ins = [
            (feature_counts, "scalar"),
            (stream_grad, None, cross_view, groups),
            (down_weight, layer),
            (u, None, first_view, groups),
            (up_weight, layer),
            (x2, None, cross_view, groups),
            (gains, None),
            (shifts, None),
            (feature_weights, layer),
            (fqkv, None),
            (fctx, None),
            (fext, None),
            (hidden, None),
            (x1, None),
            (sample_weights, (layer, 3)),
            (ctx, None),
            (act.reshape(rows_total, hidden_width), None),
            (h3.reshape(flat), None),
        ]
        head = []
        if not last:
            ins += [
                (stream, "raw"),
                (class_labels, None),
                (bin_index[0].T, None),
                (bin_counts[0], None),
                (read_weight.T, None),
                (task_sizes, "scalar"),
            ]
            ins[1] = (stream_grad, None)
            head = [
                vmem((places, CLASSES * (samples // LANES), LANES), f32),
                vmem((features, BINS, samples), bf16),
                vmem((features, BINS, LANES), f32),
                vmem((LANES, width), bf16),
                vmem((features, BINS, LANES), f32),
                dma(places - 1),
                dma(places - 1),
                pltpu.SemaphoreType.DMA,
            ]
        sums = [
            ((1, 6, 7, 3), ("dense", 1, 3, 12), None, True),
            ((1, 6, 7, 3), (0, 2, "weights", 12), None, True),
            ((1, 6), (10, 12), None, True),
        ]
        if last:
            sums += [((2, 3), (0, 11), sample_sum, True), ((3,), (0, 11), finished[1][0], True)]
        g1, dense_small, sdc, sext, slow, *results = fused(
            functools.partial(dense_feature_backward, layer),
            "dense_feature_backward",
            sizes,
            ins,
            [
                (shape, f32),
                ((16, width), f32),
                (shape, bf16),
                (shape[:3] + (LANES,), bf16),
                (shape, bf16),
            ]
            + ([] if last else [((features, BINS, LANES), f32), ((8, LANES), f32), ((SIZE, width), f32)]),
            [
                vmem((ROWS, LANES), bf16),
                vmem(shape, bf16),
                vmem((rows_total, hidden_width), bf16),
                vmem(flat, bf16),
                vmem(piece_shape, bf16),
                vmem(piece_shape, bf16),
                vmem(block_shape, bf16),
                vmem((ROWS, width), bf16),
                vmem(block_shape, bf16),
                vmem(shape, bf16),
                vmem(piece_shape, bf16),
                dma(groups, places - 1),
                dma(groups, places - 1),
                dma(groups),
                dma(groups, places - 1),
                dma(groups, places - 1),
            ]
            + head,
            sums,
            share_shape,
            4 + layer,
        )
        if not last:
            shapes, loss, read_grad, *results = results
        up_sum, down_sum, feature_sum, *later_sum = results
        ins = [
            (task_sizes, "scalar"),
            (qkv, None, last_view, pairs),
            (sdc, None, last_view, pairs),
            (ext, None),
            (sext, None),
            (sample_weights, layer),
            (x0, None),
            (gains, None),
            (g1, None),
        ]
        other_small = sample_small if last else read_grad
        ins += [(array, None) for array in (h1, ctx, slow, dense_small, other_small)]
        early_rows = -(-(dense_rows + (2 if last else SIZE)) // 8) * 8
        slots = 6 + tasks
        copies = 1 + (tasks - 1) + 1 + 1 + (places - 1) + (tasks - 1)
        small_scratch = [
            vmem((early_rows, width), f32),
            vmem((slots, early_rows, width), f32),
            vmem((places + tasks, 8, LANES), f32),
            dma(copies),
            dma(copies),
        ]
        outs = [(shape, f32), ((8, width), f32), ((early_rows, width), f32)]
        scratch = [vmem((samples, LANES), bf16), vmem((3,) + flat, bf16)]
        if last:
            outs += [(share_shape, f32), ((8, LANES), f32)]
            scratch.append(vmem((pairs, 2, 2, 2, 2, 2, share, LANES), bf16))
            for step in (1, 2, 5):
                _, got, mine, kind, count = sum_shapes(step, tasks, share, LANES)
                scratch += [
                    (
                        vmem((pairs,) + got, bf16),
                        vmem((pairs,) + mine, kind),
                        dma(pairs, count),
                        dma(pairs, count),
                    )
                ]
            scratch += small_scratch
            sums = [
                ((7, 3, 4), (2, "attend", "end"), feature_sum, True),
                ((4,), ("attend",), up_sum, True),
                ((4,), ("attend",), down_sum, True),
                ((4,), ("attend",), later_sum[0], True),
                ((4,), ("attend",), later_sum[1], True),
            ]
        else:
            scratch += [vmem(piece_shape, bf16), *small_scratch]
            sums = [
                ((7,), (3,), feature_sum, True),
                ((4,), ("attend",), up_sum, True),
                ((4,), ("attend",), down_sum, True),
                ((1,), ("leave",), None, True),
            ]
        stream_grad, sample_small, *more = fused(
            functools.partial(sample_backward_last, layer, last),
            "sample_backward",
            sizes,
            ins,
            outs,
            scratch,
            sums,
            share_shape,
            6 + layer,
        )
        if last:
            packed, share_sum, late, *first = more
            finished[0] = (share_sum, *first[:3])
            finished[1] = (first[3], first[4], *finished[1][1:])
        else:
            later_packed, *finished[1], sample_sum = more

    whole, parked = pl.BlockSpec(memory_space=pltpu.VMEM), pl.BlockSpec(memory_space=pltpu.HBM)
    scalar = pl.BlockSpec(memory_space=pltpu.SMEM)
    matrix = jax.ShapeDtypeStruct((LAYERS, share, width), f32)
    norm = jax.ShapeDtypeStruct((3, LAYERS, width), f32)
    raw_shape = (samples * features * (width // LANES), LANES)
    raw = jax.ShapeDtypeStruct(raw_shape, f32)
    shares = [finished[layer][member] for member in range(4) for layer in range(LAYERS)]
    results = pl.pallas_call(
        functools.partial(write_out, dense_rows),
        name="write_out",
        out_shape=[
            raw,
            raw,
            matrix,
            matrix,
            matrix,
            matrix,
            norm,
            norm,
            jax.ShapeDtypeStruct((LAYERS, hidden_width), f32),
            jax.ShapeDtypeStruct((LAYERS, width), f32),
            jax.ShapeDtypeStruct((CLASSES, width), f32),
            jax.ShapeDtypeStruct((CLASSES, features, BINS), f32),
            jax.ShapeDtypeStruct((1,), f32),
        ],
        in_specs=[parked] * 2 + [whole] * 12 + [scalar],
        out_specs=[parked] * 2 + [whole] * 10 + [scalar],
        scratch_shapes=[
            vmem(raw_shape, f32),
            vmem(raw_shape, f32),
            vmem(shape, f32),
            vmem(shape, f32),
            dma(2, 4),
            dma(2, 4),
        ],
        compiler_params=pltpu.CompilerParams(vmem_limit_bytes=63 << 20),
    )(stream, stream_grad, *shares, packed, later_packed, late, shapes, loss)
    return (
        from_raw(results[0]),
        results[11].transpose(1, 2, 0)[None],
        from_raw(results[1]),
        results[12],
        results[2][:, None],
        results[3][:, None],
        results[6].transpose(1, 0, 2),
        results[7].transpose(1, 0, 2),
        results[4].transpose(0, 2, 1),
        results[8],
        results[5],
        results[9],
        results[10].T,
    )


def local(
    tokens_in,
    sample_weights,
    feature_weights,
    norm_gain,
    norm_shift,
    up_weight,
    up_bias,
    down_weight,
    down_bias,
    read_weight,
    output_grad,
    task_sizes,
    feature_counts,
    bin_index,
    bin_counts,
    class_labels,
):
    samples = tokens_in.shape[1]
    features = tokens_in.shape[2]
    width = tokens_in.shape[3]
    hidden_width = up_weight.shape[2]
    task_devices = lax.axis_size("task")
    feature_devices = lax.axis_size("feat")
    all_features = features * feature_devices
    own_samples = samples // feature_devices
    size = min(16, own_samples)
    groups = own_samples // size
    group_rows = all_features * size
    rows_total = features * samples

    if (
        own_samples % 32 == 0
        and samples % ROWS == 0
        and ROWS % own_samples == 0
        and group_rows == ROWS
        and own_samples == 4 * SIZE
        and task_devices == hidden_width // width == 4
        and feature_devices == 8
    ):
        return local_fused(
            tokens_in,
            sample_weights,
            feature_weights,
            norm_gain,
            norm_shift,
            up_weight,
            up_bias,
            down_weight,
            down_bias,
            read_weight,
            output_grad,
            task_sizes,
            feature_counts,
            bin_index,
            bin_counts,
            class_labels,
        )

    sample_live = jnp.arange(samples) < task_sizes[0]
    feature_live = jnp.arange(all_features) < feature_counts[0]
    sample_mask = sample_live.astype(f32)
    local_index = lax.axis_index("feat") * features + jnp.arange(features)
    local_live = (local_index < feature_counts[0]).astype(f32)
    sample_qcode, sample_kcode = codes(jnp.zeros((samples,), jnp.int32), sample_live, 1, samples)
    sample_qcode = sample_qcode[:ROWS]
    item = jnp.arange(group_rows) % size
    feature_qcode, feature_kcode = codes(item, jnp.repeat(feature_live, size), size, group_rows)

    def exchange_out(rows):
        parts = rows.reshape(features, feature_devices, own_samples, width)
        got = lax.all_to_all(parts, "feat", split_axis=1, concat_axis=0, tiled=True)
        return got.reshape(all_features, own_samples, width)

    def exchange_back(rows):
        parts = rows.reshape(feature_devices, features, own_samples, width)
        got = lax.all_to_all(parts, "feat", split_axis=0, concat_axis=2, tiled=True)
        return got.reshape(features, samples, width)

    stream = tokens_in[0].astype(f32).transpose(1, 0, 2)
    token_shape = (features, samples, width)
    stored = []
    for layer in range(LAYERS):
        gain, shift = norm_gain[layer], norm_shift[layer]
        x1, h2, qkv, ctx, ext = call(
            sample_forward,
            "sample_forward",
            [
                (token_shape, f32),
                (token_shape, bf16),
                ((3,) + token_shape, bf16),
                (token_shape, bf16),
                ((features, samples, LANES), bf16),
            ],
            [],
            stream,
            gain,
            shift,
            sample_weights[layer],
            sample_qcode,
            sample_kcode,
        )
        swapped = exchange_out(h2)
        a, fqkv, fctx, fext = call(
            functools.partial(feature_forward, size),
            "feature_forward",
            [
                ((all_features, own_samples, width), bf16),
                ((groups, 3, group_rows, width), bf16),
                ((groups, group_rows, width), bf16),
                ((groups, group_rows, LANES), bf16),
            ],
            [],
            swapped,
            feature_weights[layer],
            feature_qcode,
            feature_kcode,
        )
        back = exchange_back(a)
        x3, u = call(
            dense_forward,
            "dense_forward",
            [((rows_total, width), f32), ((rows_total, hidden_width), bf16)],
            [],
            x1.reshape(rows_total, width),
            back.reshape(rows_total, width),
            gain,
            shift,
            up_weight[layer],
            up_bias[layer][None],
            down_weight[layer],
            down_bias[layer][None],
        )
        stored.append((stream, x1, qkv, ctx, ext, swapped, fqkv, fctx, fext, back, u))
        stream = x3.reshape(token_shape)

    reading = stream.astype(bf16)
    projected = jnp.einsum("fsd,dc->fsc", reading, read_weight, preferred_element_type=f32)
    onehot_bins = (bin_index[0].T[..., None] == jnp.arange(BINS)).astype(f32)
    chosen = onehot_bins * sample_mask[None, :, None]
    counted = jnp.maximum(jnp.sum(chosen, axis=1), 1.0)
    bin_sums = jnp.einsum("fsb,fsc->fbc", chosen, projected, precision=highest)
    bin_means = bin_sums / counted[..., None]
    bin_weight = bin_counts[0].astype(f32)
    weight_total = jnp.sum(bin_weight, axis=-1, keepdims=True)
    centre = jnp.sum(bin_weight[..., None] * bin_means, axis=1, keepdims=True) / weight_total[..., None]
    shapes = bin_means - centre
    used_bins = onehot_bins * local_live[:, None, None]
    local_logits = jnp.einsum("fsb,fbc->sc", used_bins, shapes, precision=highest)
    logits = lax.psum(local_logits, "feat")
    row_max = jnp.max(logits, axis=-1, keepdims=True)
    log_total = row_max + jnp.log(jnp.sum(jnp.exp(logits - row_max), axis=-1, keepdims=True))
    label_rows = (class_labels[0][:, None] == jnp.arange(CLASSES)).astype(f32)
    picked = jnp.sum(logits * label_rows, axis=-1)
    live_count = task_sizes[0].astype(f32)
    task_loss = jnp.sum(sample_mask * (log_total[:, 0] - picked)) / live_count
    logit_grad = sample_mask[:, None] * (jnp.exp(logits - log_total) - label_rows) / live_count
    shape_grad = jnp.einsum("fsb,sc->fbc", used_bins, logit_grad, precision=highest)
    means_grad = shape_grad - bin_weight[..., None] / weight_total[..., None] * jnp.sum(
        shape_grad, axis=1, keepdims=True
    )
    sum_grad = means_grad / counted[..., None]
    projected_grad = jnp.einsum("fsb,fbc->fsc", chosen, sum_grad, precision=highest).astype(bf16)
    read_grad = jnp.einsum("fsd,fsc->dc", reading, projected_grad, preferred_element_type=f32)
    stream_grad = output_grad[0].astype(f32).transpose(1, 0, 2) + jnp.einsum(
        "fsc,dc->fsd", projected_grad, read_weight, preferred_element_type=f32
    )

    small = [None] * LAYERS
    big = [None] * LAYERS
    for layer in reversed(range(LAYERS)):
        gain, shift = norm_gain[layer], norm_shift[layer]
        x0, x1, qkv, ctx, ext, swapped, fqkv, fctx, fext, back, u = stored[layer]
        flat = (rows_total, width)
        g2, sent, dup, ddown, dupb, ddownb, dgs2 = call(
            dense_backward,
            "dense_backward",
            [
                (flat, f32),
                (flat, bf16),
                ((hidden_width, width), bf16),
                ((hidden_width, width), bf16),
                ((1, hidden_width), f32),
                ((1, width), f32),
                ((2, width), f32),
            ],
            [
                ((rows_total, hidden_width), bf16),
                ((rows_total, hidden_width), bf16),
                (flat, bf16),
                (flat, bf16),
            ],
            stream_grad.reshape(flat),
            x1.reshape(flat),
            back.reshape(flat),
            u,
            gain,
            shift,
            up_weight[layer],
            down_weight[layer],
        )
        arriving = exchange_out(sent.reshape(token_shape))
        group_shape = (groups, group_rows, width)
        dh, dwf = call(
            functools.partial(feature_backward, size),
            "feature_backward",
            [((all_features, own_samples, width), bf16), ((4, width, width), bf16)],
            [
                ((3,) + group_shape, bf16),
                (group_shape, bf16),
                (group_shape, bf16),
                ((group_rows, width), bf16),
            ],
            arriving,
            swapped,
            feature_weights[layer],
            feature_kcode,
            fqkv,
            fctx,
            fext,
        )
        returned = exchange_back(dh)
        g0, dws, dgs01 = call(
            sample_backward,
            "sample_backward",
            [(token_shape, f32), ((4, width, width), bf16), ((2, 2, width), f32)],
            [
                ((3,) + token_shape, bf16),
                (token_shape, bf16),
                (token_shape, bf16),
                (token_shape, bf16),
                ((features, samples, LANES), bf16),
                ((samples, LANES), f32),
                ((samples, LANES), f32),
            ],
            g2.reshape(token_shape),
            returned,
            x1,
            x0,
            gain,
            shift,
            sample_weights[layer],
            sample_kcode,
            qkv,
            ctx,
            ext,
        )
        stream_grad = g0
        small[layer] = (
            jnp.stack([dgs01[0, 0], dgs01[1, 0], dgs2[0]]),
            jnp.stack([dgs01[0, 1], dgs01[1, 1], dgs2[1]]),
            dupb[0],
            ddownb[0],
        )
        big[layer] = [dws.reshape(4 * width, width), dwf.reshape(4 * width, width), dup, ddown]
    shard_shape = (LAYERS, 4 // task_devices, width // feature_devices, width)
    pieces = [big[layer][member] for member in range(4) for layer in range(LAYERS)]
    rows = [row.reshape(-1, width) for layer in range(LAYERS) for row in small[layer]]
    rows.append(read_grad.T)
    lengths = [row.shape[0] for row in rows]
    fill = -sum(lengths) % 8
    small_rows = jnp.concatenate(rows + [jnp.zeros((fill, width), f32)])
    if (width // feature_devices) % 16 == 0:
        *shares, small_sums = sum_everywhere(pieces, small_rows, task_devices, feature_devices)
    else:
        shares = [
            lax.psum_scatter(piece, ("task", "feat"), scatter_dimension=0, tiled=True).astype(f32)
            for piece in pieces
        ]
        small_sums = lax.psum(small_rows, ("task", "feat"))
    matrices = [jnp.stack(shares[member * LAYERS : member * LAYERS + LAYERS]) for member in range(4)]
    split = []
    at = 0
    for length in lengths:
        split.append(small_sums[at : at + length])
        at += length
    summed = [jnp.stack([split[4 * layer + member] for layer in range(LAYERS)]) for member in range(4)]
    summed[2] = summed[2].reshape(LAYERS, hidden_width)
    summed[3] = summed[3].reshape(LAYERS, width)
    summed.append(split[-1].T)
    return (
        stream.transpose(1, 0, 2)[None],
        shapes[None],
        stream_grad.transpose(1, 0, 2)[None],
        task_loss[None],
        matrices[0].reshape(shard_shape),
        matrices[1].reshape(shard_shape),
        summed[0],
        summed[1],
        matrices[2].transpose(0, 2, 1),
        summed[2],
        matrices[3],
        summed[3],
        summed[4],
    )


def solution(mesh):
    in_specs = (
        P("task", None, "feat", None),
        P(),
        P(),
        P(),
        P(),
        P(),
        P(),
        P(),
        P(),
        P(),
        P("task", None, "feat", None),
        P("task"),
        P("task"),
        P("task", None, "feat"),
        P("task", "feat", None),
        P("task", None),
    )
    out_specs = (
        P("task", None, "feat", None),
        P("task", "feat", None, None),
        P("task", None, "feat", None),
        P("task"),
        P(None, "task", "feat", None),
        P(None, "task", "feat", None),
        P(),
        P(),
        P(None, None, ("task", "feat")),
        P(),
        P(None, ("task", "feat"), None),
        P(),
        P(),
    )
    return jax.shard_map(local, mesh=mesh, in_specs=in_specs, out_specs=out_specs, check_vma=False)
```

```python
import functools

import jax
import jax.numpy as jnp
from jax import lax
from jax.experimental import pallas as pl
from jax.experimental.pallas import tpu as pltpu
from jax.sharding import PartitionSpec as P

HEADS = 8
BINS = 64
CLASSES = 10
LAYERS = 2
LANES = 128
CODE_LANE = 32
ROWS = 256

epsilon = 1e-05
masked_score = -1e30
highest = lax.Precision.HIGHEST
bf16 = jnp.bfloat16
f32 = jnp.float32

NN = (((1,), (0,)), ((), ()))
NT = (((1,), (1,)), ((), ()))
TN = (((0,), (0,)), ((), ()))


def mm(left, right, dims=NN):
    return lax.dot_general(left, right, dims, preferred_element_type=f32)


def lane_row():
    return lax.broadcasted_iota(jnp.int32, (1, LANES), 1)


def half_row(half):
    lanes = lane_row()
    picked = lanes < 64 if half == 0 else lanes >= 64
    return picked.astype(f32).astype(bf16)


def piece_row(pair, half):
    offset = lane_row() - 64 * half - 3 * pair
    return jnp.where((offset >= 0) & (offset < 3), -1.0, 0.0).astype(bf16)


def split_pieces(values, order):
    first = values.astype(bf16).astype(f32)
    rest = values - first
    second = rest.astype(bf16).astype(f32)
    third = rest - second
    return jnp.where(order == 0, first, jnp.where(order == 1, second, third))


def layer_norm(rows, gain, shift):
    centred = rows - jnp.mean(rows, axis=-1, keepdims=True)
    inverse = lax.rsqrt(jnp.mean(centred * centred, axis=-1, keepdims=True) + epsilon)
    normed = centred * inverse
    return normed, inverse, normed * gain + shift


def layer_norm_back(grad_rows, rows, gain):
    centred = rows - jnp.mean(rows, axis=-1, keepdims=True)
    inverse = lax.rsqrt(jnp.mean(centred * centred, axis=-1, keepdims=True) + epsilon)
    normed = centred * inverse
    scaled = grad_rows * gain
    inner = (
        scaled
        - jnp.mean(scaled, axis=-1, keepdims=True)
        - normed * jnp.mean(scaled * normed, axis=-1, keepdims=True)
    )
    gain_part = jnp.sum(grad_rows * normed, axis=0, keepdims=True)
    shift_part = jnp.sum(grad_rows, axis=0, keepdims=True)
    return inverse * inner, gain_part, shift_part


def chunk(index, size):
    return pl.ds(pl.multiple_of(index * size, size), size)


def attend_pair(query, key, value, query_code, key_code, pair, extras):
    query_wide = jnp.concatenate([query, query_code], axis=1)
    total = None
    peaks = []
    for half in range(2):
        mask = half_row(half)
        key_wide = jnp.concatenate([key * mask, key_code], axis=1)
        scores = mm(query_wide, key_wide, NT)
        peak = jnp.max(scores, axis=-1, keepdims=True)
        weights = jnp.exp(scores - peak).astype(bf16)
        ones = jnp.broadcast_to(mask, value.shape)
        part = mm(weights, jnp.concatenate([value * mask, ones], axis=1))
        total = part if total is None else total + part
        peaks.append(peak)
    lanes = lane_row()
    row_total = total[:, LANES:]
    context = total[:, :LANES] / row_total
    log_total = jnp.where(lanes < 64, peaks[0], peaks[1]) + jnp.log(row_total)
    order = lanes % 64 - 3 * pair
    extras = jnp.where((order >= 0) & (order < 3), split_pieces(log_total, order), extras)
    return context.astype(bf16), extras


def attend_pair_back(query, key, value, context_grad, query_extra, grad_extra, key_code, pair):
    query_wide = jnp.concatenate([query, query_extra], axis=1)
    grad_wide = jnp.concatenate([context_grad, grad_extra], axis=1)
    query_grad = key_grad = value_grad = None
    for half in range(2):
        mask = half_row(half)
        pieces = piece_row(pair, half)
        key_half = key * mask
        key_wide = jnp.concatenate([key_half, key_code + pieces], axis=1)
        value_wide = jnp.concatenate(
            [value * mask, jnp.broadcast_to(pieces, value.shape)], axis=1
        )
        attention = jnp.exp(mm(key_wide, query_wide, NT))
        score_grad = (attention * mm(value_wide, grad_wide, NT)).astype(bf16)
        value_part = mm(attention.astype(bf16), context_grad * mask)
        key_part = mm(score_grad, query * mask)
        query_part = mm(score_grad, key_half, TN)
        if half == 0:
            query_grad, key_grad, value_grad = query_part, key_part, value_part
        else:
            query_grad, key_grad, value_grad = (
                query_grad + query_part,
                key_grad + key_part,
                value_grad + value_part,
            )
    return query_grad, key_grad, value_grad


def delta_extra(context, context_grad):
    width = context.shape[1]
    products = context.astype(f32) * context_grad.astype(f32)
    high = products.astype(bf16)
    low = (products - high.astype(f32)).astype(bf16)
    head = lax.broadcasted_iota(jnp.int32, (width, LANES), 0) // (width // HEADS)
    offset = lax.broadcasted_iota(jnp.int32, (width, LANES), 1) - 64 * (head % 2) - 3 * (head // 2)
    spread = jnp.where((offset >= 0) & (offset < 3), 1.0, 0.0).astype(bf16)
    sums = mm(high, spread) + mm(low, spread)
    return split_pieces(sums, lane_row() % 64 % 3).astype(bf16)


def sample_forward(x_ref, gain_ref, shift_ref, w_ref, qcode_ref, kcode_ref, x1_ref, h2_ref, qkv_ref, ctx_ref, ext_ref):
    features, samples, width = x_ref.shape
    steps = samples // ROWS

    def project(unit, carry):
        f, rows = unit // steps, chunk(unit % steps, ROWS)
        _, _, hidden = layer_norm(x_ref[f, rows, :], gain_ref[0:1], shift_ref[0:1])
        hidden = hidden.astype(bf16)
        for member in range(3):
            out = mm(hidden, w_ref[member]).astype(bf16)
            if member == 0:
                out = out * jnp.asarray(0.125, bf16)
            qkv_ref[member, f, rows, :] = out
        return carry

    lax.fori_loop(0, features * steps, project, 0)

    def attend(unit, carry):
        f, rows = unit // steps, chunk(unit % steps, ROWS)
        code = qcode_ref[...]

        def pair_step(pair, extras):
            lanes = chunk(pair, LANES)
            context, extras = attend_pair(
                qkv_ref[0, f, rows, lanes],
                qkv_ref[1, f, :, lanes],
                qkv_ref[2, f, :, lanes],
                code,
                kcode_ref[...],
                pair,
                extras,
            )
            ctx_ref[f, rows, lanes] = context
            return extras

        extras = lax.fori_loop(0, width // LANES, pair_step, code.astype(f32))
        ext_ref[f, rows, :] = extras.astype(bf16)
        x1 = x_ref[f, rows, :] + mm(ctx_ref[f, rows, :], w_ref[3])
        x1_ref[f, rows, :] = x1
        _, _, hidden = layer_norm(x1, gain_ref[1:2], shift_ref[1:2])
        h2_ref[f, rows, :] = hidden.astype(bf16)
        return carry

    lax.fori_loop(0, features * steps, attend, 0)


def load_group(ref, group, size):
    features, _, width = ref.shape
    block = ref[:, chunk(group, size), :]
    if size % 16:
        return block.astype(f32).reshape(features * size, width).astype(bf16)
    return block.reshape(features * size, width)


def store_group(ref, group, size, rows):
    features, _, width = ref.shape
    if size % 16:
        block = rows.astype(f32).reshape(features, size, width).astype(bf16)
    else:
        block = rows.reshape(features, size, width)
    ref[:, chunk(group, size), :] = block


def feature_forward(size, h_ref, w_ref, qcode_ref, kcode_ref, a_ref, qkv_ref, ctx_ref, ext_ref):
    _, samples, width = h_ref.shape

    def step(group, carry):
        hidden = load_group(h_ref, group, size)
        for member in range(3):
            out = mm(hidden, w_ref[member]).astype(bf16)
            if member == 0:
                out = out * jnp.asarray(0.125, bf16)
            qkv_ref[group, member] = out
        code = qcode_ref[...]

        def pair_step(pair, extras):
            lanes = chunk(pair, LANES)
            context, extras = attend_pair(
                qkv_ref[group, 0, :, lanes],
                qkv_ref[group, 1, :, lanes],
                qkv_ref[group, 2, :, lanes],
                code,
                kcode_ref[...],
                pair,
                extras,
            )
            ctx_ref[group, :, lanes] = context
            return extras

        extras = lax.fori_loop(0, width // LANES, pair_step, code.astype(f32))
        ext_ref[group] = extras.astype(bf16)
        store_group(a_ref, group, size, mm(ctx_ref[group], w_ref[3]).astype(bf16))
        return carry

    lax.fori_loop(0, samples // size, step, 0)


def gelu_parts(values):
    cubic = values * values * values
    inside = 0.7978845608028654 * (values + 0.044715 * cubic)
    bent = jnp.tanh(inside)
    return bent


def dense_forward(x_ref, a_ref, gain_ref, shift_ref, up_ref, upb_ref, down_ref, downb_ref, out_ref, u_ref):
    rows_total, width = x_ref.shape
    hidden_width = up_ref.shape[1]

    def step(unit, carry):
        rows = chunk(unit, ROWS)
        x2 = x_ref[rows, :] + a_ref[rows, :].astype(f32)
        _, _, hidden = layer_norm(x2, gain_ref[2:3], shift_ref[2:3])
        hidden = hidden.astype(bf16)
        total = x2 + downb_ref[...]
        for part in range(hidden_width // 512):
            cols = slice(part * 512, part * 512 + 512)
            expanded = mm(hidden, up_ref[:, cols]) + upb_ref[:, cols]
            u_ref[rows, cols] = expanded.astype(bf16)
            active = (0.5 * expanded * (1.0 + gelu_parts(expanded))).astype(bf16)
            total = total + mm(active, down_ref[cols, :])
        out_ref[rows, :] = total
        return carry

    lax.fori_loop(0, rows_total // ROWS, step, 0)


def dense_backward(g_ref, x1_ref, a_ref, u_ref, gain_ref, shift_ref, up_ref, down_ref, out_ref, send_ref, dup_ref, ddown_ref, dupb_ref, ddownb_ref, dgs_ref, active_ref, ugrad_ref, hidden_ref, rowgrad_ref):
    rows_total, width = g_ref.shape
    hidden_width = up_ref.shape[1]
    dupb_ref[...] = jnp.zeros_like(dupb_ref)
    ddownb_ref[...] = jnp.zeros_like(ddownb_ref)
    dgs_ref[...] = jnp.zeros_like(dgs_ref)

    def step(unit, carry):
        rows = chunk(unit, ROWS)
        grad = g_ref[rows, :]
        low = grad.astype(bf16)
        rowgrad_ref[rows, :] = low
        ddownb_ref[...] += jnp.sum(low.astype(f32), axis=0, keepdims=True)
        hidden_grad = None
        for part in range(hidden_width // 512):
            cols = slice(part * 512, part * 512 + 512)
            active_grad = mm(low, down_ref[cols, :], NT).astype(bf16).astype(f32)
            u = u_ref[rows, cols].astype(f32)
            bent = gelu_parts(u)
            slope = 0.5 * (1.0 + bent) + u * (1.0 - bent * bent) * (
                0.3989422804014327 + 0.05351611220146811 * u * u
            )
            active_ref[rows, cols] = (0.5 * u * (1.0 + bent)).astype(bf16)
            ugrad = (active_grad * slope).astype(bf16)
            ugrad_ref[rows, cols] = ugrad
            dupb_ref[:, cols] += jnp.sum(ugrad.astype(f32), axis=0, keepdims=True)
            part_grad = mm(ugrad, up_ref[:, cols], NT)
            hidden_grad = part_grad if hidden_grad is None else hidden_grad + part_grad
        x2 = x1_ref[rows, :] + a_ref[rows, :].astype(f32)
        _, _, hidden = layer_norm(x2, gain_ref[2:3], shift_ref[2:3])
        hidden_ref[rows, :] = hidden.astype(bf16)
        norm_grad, gain_part, shift_part = layer_norm_back(
            hidden_grad.astype(bf16).astype(f32), x2, gain_ref[2:3]
        )
        dgs_ref[0:1] += gain_part
        dgs_ref[1:2] += shift_part
        grad = grad + norm_grad
        out_ref[rows, :] = grad
        send_ref[rows, :] = grad.astype(bf16)
        return carry

    lax.fori_loop(0, rows_total // ROWS, step, 0)

    def weights(part, carry):
        cols = chunk(part, 512)
        dup_ref[cols, :] = mm(ugrad_ref[:, cols], hidden_ref[...], TN).astype(bf16)
        ddown_ref[cols, :] = mm(active_ref[:, cols], rowgrad_ref[...], TN).astype(bf16)
        return carry

    lax.fori_loop(0, hidden_width // 512, weights, 0)


def feature_backward(size, da_ref, h_ref, w_ref, kcode_ref, qkv_ref, ctx_ref, ext_ref, dh_ref, dw_ref, dqkv_ref, hidden_ref, dao_ref, dc_ref):
    _, samples, width = h_ref.shape
    groups = samples // size

    def step(group, carry):
        hidden_ref[group] = load_group(h_ref, group, size)
        dao = load_group(da_ref, group, size)
        dao_ref[group] = dao
        context_grad = mm(dao, w_ref[3], NT).astype(bf16)
        dc_ref[...] = context_grad
        grad_extra = delta_extra(ctx_ref[group], context_grad)

        def pair_step(pair, inner):
            lanes = chunk(pair, LANES)
            query_grad, key_grad, value_grad = attend_pair_back(
                qkv_ref[group, 0, :, lanes],
                qkv_ref[group, 1, :, lanes],
                qkv_ref[group, 2, :, lanes],
                dc_ref[:, lanes],
                ext_ref[group],
                grad_extra,
                kcode_ref[...],
                pair,
            )
            dqkv_ref[0, group, :, lanes] = (query_grad * 0.125).astype(bf16)
            dqkv_ref[1, group, :, lanes] = key_grad.astype(bf16)
            dqkv_ref[2, group, :, lanes] = value_grad.astype(bf16)
            return inner

        lax.fori_loop(0, width // LANES, pair_step, 0)
        total = mm(dqkv_ref[0, group], w_ref[0], NT)
        total = total + mm(dqkv_ref[1, group], w_ref[1], NT)
        total = total + mm(dqkv_ref[2, group], w_ref[2], NT)
        store_group(dh_ref, group, size, total.astype(bf16))
        return carry

    lax.fori_loop(0, groups, step, 0)

    def weights(member, carry):
        total = None
        for group in range(groups):
            part = mm(hidden_ref[group], dqkv_ref[member, group], TN)
            total = part if total is None else total + part
        dw_ref[member] = total.astype(bf16)
        return carry

    lax.fori_loop(0, 3, weights, 0)
    total = None
    for group in range(groups):
        part = mm(ctx_ref[group], dao_ref[group], TN)
        total = part if total is None else total + part
    dw_ref[3] = total.astype(bf16)


def sample_backward(g_ref, dh_ref, x1_ref, x_ref, gain_ref, shift_ref, w_ref, kcode_ref, qkv_ref, ctx_ref, ext_ref, out_ref, dw_ref, dgs_ref, dqkv_ref, hidden_ref, low_ref, dc_ref, gext_ref, kacc_ref, vacc_ref):
    features, samples, width = x_ref.shape
    steps = samples // ROWS
    dgs_ref[...] = jnp.zeros_like(dgs_ref)

    def enter(unit, carry):
        f, rows = unit // steps, chunk(unit % steps, ROWS)
        norm_grad, gain_part, shift_part = layer_norm_back(
            dh_ref[f, rows, :].astype(f32), x1_ref[f, rows, :], gain_ref[1:2]
        )
        dgs_ref[1, 0:1] += gain_part
        dgs_ref[1, 1:2] += shift_part
        grad = g_ref[f, rows, :] + norm_grad
        out_ref[f, rows, :] = grad
        low = grad.astype(bf16)
        low_ref[f, rows, :] = low
        context_grad = mm(low, w_ref[3], NT).astype(bf16)
        dc_ref[f, rows, :] = context_grad
        gext_ref[f, rows, :] = delta_extra(ctx_ref[f, rows, :], context_grad)
        return carry

    lax.fori_loop(0, features * steps, enter, 0)

    def attend(unit, carry):
        f, pair = unit // (width // LANES), unit % (width // LANES)
        lanes = chunk(pair, LANES)

        def query_step(step, inner):
            rows = chunk(step, ROWS)
            query_grad, key_grad, value_grad = attend_pair_back(
                qkv_ref[0, f, rows, lanes],
                qkv_ref[1, f, :, lanes],
                qkv_ref[2, f, :, lanes],
                dc_ref[f, rows, lanes],
                ext_ref[f, rows, :],
                gext_ref[f, rows, :],
                kcode_ref[...],
                pair,
            )
            dqkv_ref[0, f, rows, lanes] = (query_grad * 0.125).astype(bf16)
            first = step == 0
            kacc_ref[...] = jnp.where(first, 0.0, kacc_ref[...]) + key_grad
            vacc_ref[...] = jnp.where(first, 0.0, vacc_ref[...]) + value_grad
            return inner

        lax.fori_loop(0, steps, query_step, 0)
        dqkv_ref[1, f, :, lanes] = kacc_ref[...].astype(bf16)
        dqkv_ref[2, f, :, lanes] = vacc_ref[...].astype(bf16)
        return carry

    kacc_ref[...] = jnp.zeros_like(kacc_ref)
    vacc_ref[...] = jnp.zeros_like(vacc_ref)
    lax.fori_loop(0, features * (width // LANES), attend, 0)

    def leave(unit, carry):
        f, rows = unit // steps, chunk(unit % steps, ROWS)
        total = mm(dqkv_ref[0, f, rows, :], w_ref[0], NT)
        total = total + mm(dqkv_ref[1, f, rows, :], w_ref[1], NT)
        total = total + mm(dqkv_ref[2, f, rows, :], w_ref[2], NT)
        x = x_ref[f, rows, :]
        _, _, hidden = layer_norm(x, gain_ref[0:1], shift_ref[0:1])
        hidden_ref[f, rows, :] = hidden.astype(bf16)
        norm_grad, gain_part, shift_part = layer_norm_back(
            total.astype(bf16).astype(f32), x, gain_ref[0:1]
        )
        dgs_ref[0, 0:1] += gain_part
        dgs_ref[0, 1:2] += shift_part
        out_ref[f, rows, :] += norm_grad
        return carry

    lax.fori_loop(0, features * steps, leave, 0)

    def weights(member, carry):
        total = None
        for f in range(features):
            part = mm(hidden_ref[f], dqkv_ref[member, f], TN)
            total = part if total is None else total + part
        dw_ref[member] = total.astype(bf16)
        return carry

    lax.fori_loop(0, 3, weights, 0)
    total = None
    for f in range(features):
        part = mm(ctx_ref[f], low_ref[f], TN)
        total = part if total is None else total + part
    dw_ref[3] = total.astype(bf16)


def call(body, name, outs, scratch, *operands):
    spec = pl.BlockSpec(memory_space=pltpu.VMEM)
    return pl.pallas_call(
        body,
        name=name,
        out_shape=[jax.ShapeDtypeStruct(shape, kind) for shape, kind in outs],
        in_specs=[spec] * len(operands),
        out_specs=[spec] * len(outs),
        scratch_shapes=[pltpu.VMEM(shape, kind) for shape, kind in scratch],
        compiler_params=pltpu.CompilerParams(vmem_limit_bytes=56 << 20),
    )(*operands)


MESH = pl.DeviceIdType.MESH


def remote(source, target, send_sem, recv_sem, device):
    return pltpu.make_async_remote_copy(
        src_ref=source,
        dst_ref=target,
        send_sem=send_sem,
        recv_sem=recv_sem,
        device_id=device,
        device_id_type=MESH,
    )


def sum_partners(task_devices, feature_devices):
    task, place = lax.axis_index("task"), lax.axis_index("feat")
    chip, core = place // 2, lax.rem(place, 2)
    chips = feature_devices // 2
    pair = [{"feat": place + 1 - 2 * core}]
    tasks = [{"task": lax.rem(task + step, task_devices)} for step in range(1, task_devices)]
    line = [{"feat": 2 * lax.rem(chip + step, chips) + core} for step in range(1, chips)]
    return task, chip, core, pair, tasks, line


def greet(devices):
    barrier = pltpu.get_barrier_semaphore()
    for device in devices:
        pl.semaphore_signal(barrier, inc=1, device_id=device, device_id_type=MESH)


def met(count):
    pl.semaphore_wait(pltpu.get_barrier_semaphore(), count)


def sum_tail(pieces, task_devices, feature_devices, *refs):
    chips = feature_devices // 2
    inputs, small_ref = refs[:pieces], refs[pieces]
    outs, small_out = refs[pieces + 1 : 2 * pieces + 1], refs[2 * pieces + 1]
    own, first, summed, second, third_in, third, sends, recvs, loads, small_got, small_sends, small_recvs = refs[2 * pieces + 2 :]
    task, chip, core, pair, tasks, line = sum_partners(task_devices, feature_devices)
    greet(pair + tasks + line)
    own_loads = [
        pltpu.make_async_copy(inputs[p].at[:, :, core], own.at[p], loads.at[p]) for p in range(pieces)
    ]
    for load in own_loads:
        load.start()
    met(len(pair) + len(tasks) + len(line))

    started = []
    for p in range(pieces):
        copy = remote(inputs[p].at[:, :, 1 - core], first.at[p], sends.at[p, 0], recvs.at[p, 0], pair[0])
        copy.start()
        started.append([copy])
    small_slot = [0]

    def small_exchange(values, devices, index, base):
        copies = []
        for k, device in enumerate(devices):
            copy = remote(values, small_got.at[base + index], small_sends.at[base + k], small_recvs.at[base + k], device)
            copy.start()
            copies.append(copy)
        return copies

    def small_finish(copies, count, base):
        for copy in copies:
            copy.wait()
        total = small_got[base]
        for k in range(1, count):
            total = total + small_got[base + k]
        return total

    small_got[core] = small_ref[...]
    small_copies = small_exchange(small_got.at[core], pair, core, 0)
    for p in range(pieces):
        own_loads[p].wait()
        for copy in started[p]:
            copy.wait()

        def add_core(index, carry, p=p):
            t, z = index // chips, lax.rem(index, chips)
            summed[p, t, z] = (own[p, t, z].astype(f32) + first[p, t, z].astype(f32)).astype(bf16)
            return carry

        lax.fori_loop(0, task_devices * chips, add_core, 0)
        started[p] = []
        for k, device in enumerate(tasks):
            other = lax.rem(task + k + 1, task_devices)
            copy = remote(summed.at[p, other], second.at[p, k], sends.at[p, 1 + k], recvs.at[p, 1 + k], device)
            copy.start()
            started[p].append(copy)
    total = small_finish(small_copies, 2, 0)
    small_got[2 + task] = total
    small_copies = small_exchange(small_got.at[2 + task], tasks, task, 2)
    for p in range(pieces):
        for copy in started[p]:
            copy.wait()

        def add_tasks(z, carry, p=p):
            total = summed[p, task, z].astype(f32)
            for k in range(task_devices - 1):
                total = total + second[p, k, z].astype(f32)
            third_in[p, z] = total.astype(bf16)
            return carry

        lax.fori_loop(0, chips, add_tasks, 0)
        started[p] = []
        for k, device in enumerate(line):
            other = lax.rem(chip + k + 1, chips)
            slot = task_devices + k
            copy = remote(third_in.at[p, other], third.at[p, k], sends.at[p, slot], recvs.at[p, slot], device)
            copy.start()
            started[p].append(copy)
    total = small_finish(small_copies, task_devices, 2)
    base = 2 + task_devices
    small_got[base + chip] = total
    small_copies = small_exchange(small_got.at[base + chip], line, chip, base)
    for p in range(pieces):
        for copy in started[p]:
            copy.wait()
        total = third_in[p, chip].astype(f32)
        for k in range(chips - 1):
            total = total + third[p, k].astype(f32)
        outs[p][...] = total
    small_out[...] = small_finish(small_copies, chips, base)


def sum_everywhere(pieces, small, task_devices, feature_devices):
    chips = feature_devices // 2
    rows, width = pieces[0].shape
    share = rows // (task_devices * feature_devices)
    blocks = [piece.reshape(task_devices, chips, 2, share, width) for piece in pieces]
    count = len(pieces)
    copies = task_devices + chips - 1
    small_copies = 2 + task_devices + chips
    vmem, anywhere = pl.BlockSpec(memory_space=pltpu.VMEM), pl.BlockSpec(memory_space=pl.ANY)
    return pl.pallas_call(
        functools.partial(sum_tail, count, task_devices, feature_devices),
        name="sum_tail",
        out_shape=[jax.ShapeDtypeStruct((share, width), f32)] * count
        + [jax.ShapeDtypeStruct(small.shape, f32)],
        in_specs=[anywhere] * count + [vmem],
        out_specs=[vmem] * (count + 1),
        scratch_shapes=[
            pltpu.VMEM((count, task_devices, chips, share, width), bf16),
            pltpu.VMEM((count, task_devices, chips, share, width), bf16),
            pltpu.VMEM((count, task_devices, chips, share, width), bf16),
            pltpu.VMEM((count, task_devices - 1, chips, share, width), bf16),
            pltpu.VMEM((count, chips, share, width), bf16),
            pltpu.VMEM((count, chips - 1, share, width), bf16),
            pltpu.SemaphoreType.DMA((count, copies)),
            pltpu.SemaphoreType.DMA((count, copies)),
            pltpu.SemaphoreType.DMA((count,)),
            pltpu.VMEM((small_copies,) + small.shape, f32),
            pltpu.SemaphoreType.DMA((small_copies,)),
            pltpu.SemaphoreType.DMA((small_copies,)),
        ],
        compiler_params=pltpu.CompilerParams(
            vmem_limit_bytes=56 << 20, collective_id=0, has_side_effects=True
        ),
    )(*blocks, small)


SIZE = 16


class Place:
    def __init__(self, task_devices, feature_devices):
        self.tasks, self.places = task_devices, feature_devices
        self.chips = feature_devices // 2
        self.task, self.place = lax.axis_index("task"), lax.axis_index("feat")
        self.chip, self.core = self.place // 2, lax.rem(self.place, 2)
        self.far, self.near = self.chip // 2, lax.rem(self.chip, 2)
        self.y, self.x = self.task // 2, lax.rem(self.task, 2)
        self.x_task = {"task": self.task + 1 - 2 * self.x}
        self.y_task = {"task": self.task + 2 - 4 * self.y}
        self.other_core = {"feat": self.place + 1 - 2 * self.core}
        self.near_chip = {"feat": self.place + 2 - 4 * self.near}
        self.far_chip = {"feat": self.place + 4 - 8 * self.far}

    def ring(self, step):
        return lax.rem(self.place + step, self.places)

    def task_partner(self, step):
        return lax.rem(self.task + step, self.tasks)

    def greet(self):
        barrier = pltpu.get_barrier_semaphore()
        for step in range(1, self.places):
            pl.semaphore_signal(barrier, inc=1, device_id={"feat": self.ring(step)}, device_id_type=MESH)
        for step in range(1, self.tasks):
            pl.semaphore_signal(barrier, inc=1, device_id={"task": self.task_partner(step)}, device_id_type=MESH)

    def met(self):
        pl.semaphore_wait(pltpu.get_barrier_semaphore(), self.places - 1 + self.tasks - 1)


class SumStep:
    def __init__(self, step, place, source, own, got, sends, recvs, load):
        self.step = step
        y, x, far, near, core = place.y, place.x, place.far, place.near, place.core
        if step == 1:
            self.mine = [source.at[:, :, :, :, core]]
            parts = [(source.at[:, :, :, :, 1 - core], got, place.other_core)]
        elif step == 2:
            self.mine = [source.at[y, x]]
            parts = []
            for k in range(1, place.tasks):
                other = place.task_partner(k)
                parts.append((source.at[other // 2, lax.rem(other, 2)], got.at[k - 1], {"task": other}))
        elif step == 6:
            self.mine = [source.at[:, x, 0], source.at[y, :, 1]]
            parts = [
                (source.at[:, 1 - x, 0], got.at[0], place.x_task),
                (source.at[1 - y, :, 1], got.at[1], place.y_task),
            ]
        elif step == 7:
            self.mine = [source.at[0, y], source.at[1, x]]
            parts = [
                (source.at[0, 1 - y], got.at[0], place.y_task),
                (source.at[1, 1 - x], got.at[1], place.x_task),
            ]
        elif step == 3:
            self.mine = [source.at[:, near]]
            parts = [(source.at[:, 1 - near], got, place.near_chip)]
        elif step == 4:
            self.mine = [source.at[far]]
            parts = [(source.at[1 - far], got, place.far_chip)]
        else:
            self.mine = [source.at[far, near]]
            parts = []
            for k in range(1, place.chips):
                other = lax.rem(place.chip + k, place.chips)
                parts.append(
                    (source.at[other // 2, lax.rem(other, 2)], got.at[k - 1], {"feat": 2 * other + core})
                )
        self.copies = [
            remote(part, target, sends.at[k], recvs.at[k], device) for k, (part, target, device) in enumerate(parts)
        ]
        self.loads = []
        if own is not None:
            kept = [own] if len(self.mine) == 1 else [own.at[half] for half in range(2)]
            self.loads = [
                pltpu.make_async_copy(part, target, load.at[half])
                for half, (part, target) in enumerate(zip(self.mine, kept))
            ]
            self.mine = kept
        self.got = got

    def start(self):
        for copy in self.copies:
            copy.start()
        for load in self.loads:
            load.start()

    def finish(self, out):
        for load in self.loads:
            load.wait()
        for copy in self.copies:
            copy.wait()
        own, got = self.mine[0], self.got
        if self.step == 1:

            def add_core(index, carry):
                y, x, far = index // 4, lax.rem(index // 2, 2), lax.rem(index, 2)
                out[y, x, far] = own[y, x, far] + got[y, x, far]
                return carry

            lax.fori_loop(0, 8, add_core, 0)
        elif self.step in (2, 5):
            total = own[...].astype(f32)
            for k in range(got.shape[0]):
                total = total + got[k].astype(f32)
            out[...] = total.astype(out.dtype)
        elif self.step in (6, 7):
            for half in range(2):
                out[half] = self.mine[half][...] + got[half]
        elif self.step == 3:
            out[...] = own[...] + got[...]
        else:
            out[...] = own[...].astype(f32) + got[...].astype(f32)


def sum_shapes(step, tasks, share, width):
    block = (share, width)
    if step == 1:
        whole = (2, 2, 2, 2) + block
        return whole, whole, whole, bf16, 1
    if step == 2:
        return (2, 2) + block, (tasks - 1, 2, 2) + block, (2, 2) + block, bf16, tasks - 1
    if step == 6:
        return None, (2, 2, 2) + block, (2, 2, 2) + block, bf16, 2
    if step == 7:
        return (2, 2) + block, (2, 2) + block, (2, 2) + block, bf16, 2
    if step == 3:
        return (2,) + block, (2,) + block, (2,) + block, bf16, 1
    if step == 4:
        return block, block, block, f32, 1
    return block, (3,) + block, block, f32, 3


class Chain:
    def __init__(self, place, steps, points, bufs, source, out):
        self.place, self.steps, self.points, self.bufs, self.out = place, steps, points, bufs, out
        self.at, self.running = 0, False
        self.first = None
        if len(points) > len(steps):
            self.first, self.points = points[0], points[1:]
        self.actions = [None if source is None else self.make(0, source)]
        self.actions += [self.make(at, bufs[at - 1][2]) for at in range(1, len(steps))]

    def make(self, at, source):
        own, got, _, sends, recvs, local_sem = self.bufs[at]
        return SumStep(self.steps[at], self.place, source, own, got, sends, recvs, local_sem)

    def begin(self, source=None):
        if source is not None:
            self.actions[0] = self.make(0, source)
        self.actions[0].start()
        self.running = True

    def reached(self, point):
        if self.first is not None and point == self.first:
            self.begin()
            return
        if not self.running or self.points[self.at] != point:
            return
        self.actions[self.at].finish(self.bufs[self.at][2])
        self.at += 1
        if self.at < len(self.steps):
            self.actions[self.at].start()
            return
        self.running = False
        if self.out is not None:
            self.flush().start()

    def flush(self):
        return pltpu.make_async_copy(self.bufs[-1][2], self.out, self.bufs[-1][5].at[2])


class Box:
    def __init__(self, place, bufs, loads, outs, out_bufs, flush_sem, chains):
        self.place, self.bufs, self.loads = place, bufs, loads
        self.outs, self.out_bufs, self.flush_sem = outs, out_bufs, flush_sem
        self.chains = chains
        self.waited, self.flushed = set(), []

    def start(self, *indices):
        for index in indices:
            if isinstance(index, tuple):
                for part in index[1:]:
                    self.loads[index[0]].one(part).start()
                continue
            for copy in self.loads[index]:
                copy.start()

    def use(self, *indices):
        found = []
        for index in indices:
            if index not in self.waited:
                self.waited.add(index)
                for copy in self.loads[index]:
                    copy.wait()
            found.append(self.bufs[index])
        return found if len(found) > 1 else found[0]

    def part(self, index, part):
        self.waited.add(index)
        self.loads[index].one(part).wait()

    def out(self, *indices):
        found = [self.out_bufs[index] for index in indices]
        return found if len(found) > 1 else found[0]

    def copy_out(self, index, part, view):
        source, target = self.out_bufs[index], self.outs[index]
        if view is not None:
            source, target = view(source, part), view(target, part)
        return pltpu.make_async_copy(source, target, self.flush_sem.at[index, part])

    def flush(self, *indices):
        for index in indices:
            self.copy_out(index, 0, None).start()
            self.flushed.append((index, 0, None))

    def flush_part(self, index, part, view):
        self.copy_out(index, part, view).start()
        if (index, 0, view) not in self.flushed:
            self.flushed += [(index, at, view) for at in range(4)]

    def settle(self, *indices):
        left = []
        for index, part, view in self.flushed:
            if index in indices:
                self.copy_out(index, part, view).wait()
            else:
                left.append((index, part, view))
        self.flushed = left

    def ready(self):
        self.place.met()
        for chain in self.chains:
            if chain.actions[0] is not None and chain.first is None:
                chain.begin()

    def point(self, name):
        for chain in self.chains:
            chain.reached(name)

    def end(self):
        for index, part, view in self.flushed:
            self.copy_out(index, part, view).wait()
        for chain in self.chains:
            if chain.out is not None:
                chain.flush().wait()


class Parts:
    def __init__(self, source, target, view, count, sem):
        self.source, self.target, self.view, self.count, self.sem = source, target, view, count, sem

    def one(self, part):
        if self.view is None:
            return pltpu.make_async_copy(self.source, self.target, self.sem.at[0])
        return pltpu.make_async_copy(self.view(self.source, part), self.view(self.target, part), self.sem.at[part])

    def __iter__(self):
        return iter([self.one(part) for part in range(self.count)])


def fused(body, name, place_sizes, ins, outs, scratch, sums, share_shape, identity):
    tasks, places = place_sizes
    anywhere = pl.BlockSpec(memory_space=pltpu.HBM)
    scalar = pl.BlockSpec(memory_space=pltpu.SMEM)
    buffers = []
    ins = [tuple(item) + (None, 1) if len(item) == 2 else item for item in ins]
    for array, layer, _, _ in ins:
        if layer not in ("scalar", "raw"):
            depth = 0 if layer is None else len(layer) if isinstance(layer, tuple) else 1
            buffers.append(pltpu.VMEM(array.shape[depth:], array.dtype))
    outs = [tuple(item) + (None,) if len(item) == 2 else item for item in outs]
    out_buffers = [pltpu.VMEM(shape, kind) for shape, kind, shared in outs if shared is None]
    sum_results, sum_scratch, sum_arrays = [], [], []
    chain_layout = []
    for steps, _, array, goes_out in sums:
        share, width = share_shape if array is None else array.shape[-2:]
        for at, step in enumerate(steps):
            own, got, result, kind, copies = sum_shapes(step, tasks, share, width)
            loaded = at == 0 and array is not None
            chain_layout.append(loaded)
            sum_scratch += [pltpu.VMEM(own, bf16)] if loaded else []
            sum_scratch += [
                pltpu.VMEM(got, bf16),
                pltpu.VMEM(result, kind),
                pltpu.SemaphoreType.DMA((copies,)),
                pltpu.SemaphoreType.DMA((copies,)),
                pltpu.SemaphoreType.DMA((3,)),
            ]
        if goes_out:
            sum_results.append(jax.ShapeDtypeStruct(result, kind))
        if array is not None:
            sum_arrays.append(array)
    flat_scratch = []
    for item in scratch:
        flat_scratch += list(item) if isinstance(item, tuple) else [item]
    everything = buffers + out_buffers + flat_scratch + sum_scratch
    def kernel(*refs):
        rest = list(refs)

        def pop(count):
            taken = rest[:count]
            del rest[:count]
            return taken

        in_refs, sum_refs = pop(len(ins)), pop(len(sum_arrays))
        out_refs, sum_outs = pop(len(outs)), pop(len(sum_results))
        flat_in = pop(len(buffers))
        fresh, out_bufs = pop(len(out_buffers)), []
        for _, _, shared in outs:
            out_bufs.append(fresh.pop(0) if shared is None else out_bufs[shared])
        user = [tuple(pop(len(item))) if isinstance(item, tuple) else pop(1)[0] for item in scratch]
        layout = list(chain_layout)
        chain_bufs = [
            [pop(6) if layout.pop(0) else [None] + pop(5) for _ in steps] for steps, _, _, _ in sums
        ]
        load_sem, flush_sem = pop(2)
        place = Place(tasks, places)
        loads, bufs = [], []
        for index, (array, layer, view, count) in enumerate(ins):
            if layer in ("scalar", "raw"):
                loads.append([])
                bufs.append(in_refs[index])
                continue
            bufs.append(flat_in.pop(0))
            source = in_refs[index]
            if layer is not None:
                source = source.at[layer]
            loads.append(Parts(source, bufs[-1], view, count, load_sem.at[index]))
        place.greet()
        chains = []
        for (steps, points, array, goes_out), chain_buf in zip(sums, chain_bufs):
            source = None if array is None else sum_refs.pop(0)
            chains.append(Chain(place, steps, points, chain_buf, source, sum_outs.pop(0) if goes_out else None))
        box = Box(place, bufs, loads, out_refs, out_bufs, flush_sem, chains)
        body(box, *user)
        box.end()

    return pl.pallas_call(
        kernel,
        name=name,
        out_shape=[jax.ShapeDtypeStruct(shape, kind) for shape, kind, _ in outs] + sum_results,
        in_specs=[scalar if layer == "scalar" else anywhere for _, layer, _, _ in ins] + [anywhere] * len(sum_arrays),
        out_specs=[anywhere] * (len(outs) + len(sum_results)),
        scratch_shapes=everything
        + [pltpu.SemaphoreType.DMA((len(ins), 8)), pltpu.SemaphoreType.DMA((len(outs), 4))],
        compiler_params=pltpu.CompilerParams(
            vmem_limit_bytes=63 << 20, collective_id=identity, has_side_effects=True
        ),
    )(*[item[0] for item in ins], *sum_arrays)


def cross(ref, unit):
    block = ref[:, :, chunk(unit, SIZE), :]
    return block.reshape(block.shape[0] * block.shape[1] * SIZE, block.shape[3])


def put_cross(ref, unit, rows):
    first, second, _, width = ref.shape
    ref[:, :, chunk(unit, SIZE), :] = rows.reshape(first, second, SIZE, width)


def cross_view(ref, unit):
    return ref.at[:, :, chunk(unit, SIZE), :]


def first_view(ref, unit):
    return ref.at[unit]


def last_view(ref, unit):
    return ref.at[(slice(None),) * (len(ref.shape) - 1) + (chunk(unit, LANES),)]


def own_rows(ref, f, unit, size, lanes=slice(None)):
    block = ref[f, :, chunk(unit, size), lanes]
    return block.reshape(block.shape[0] * size, block.shape[2])


def block_rows(ref, f, unit, per, lanes=slice(None)):
    block = ref[f, chunk(unit, per), :, lanes]
    return block.reshape(per * block.shape[1], block.shape[2])


def all_rows(ref, f, lanes=slice(None)):
    block = ref[f, :, :, lanes]
    return block.reshape(block.shape[0] * block.shape[1], block.shape[2])


def pair_lanes(pair):
    return slice(pair * LANES, pair * LANES + LANES)


def fill_sample_codes(size, query_ref, key_ref):
    if query_ref is not None:
        lanes = lax.broadcasted_iota(jnp.int32, query_ref.shape, 1)
        query_ref[...] = jnp.where(lanes == CODE_LANE, 1.0, 0.0).astype(bf16)
    lanes = lax.broadcasted_iota(jnp.int32, key_ref.shape, 1)
    rows = lax.broadcasted_iota(jnp.int32, key_ref.shape, 0)
    key_ref[...] = jnp.where((lanes == CODE_LANE) & (rows >= size), masked_score, 0.0).astype(bf16)


def fill_feature_codes(count, query_ref, key_ref):
    lanes = lax.broadcasted_iota(jnp.int32, key_ref.shape, 1) - CODE_LANE
    rows = lax.broadcasted_iota(jnp.int32, key_ref.shape, 0)
    own = lanes == (rows & (SIZE - 1))
    inside = (lanes >= 0) & (lanes < SIZE)
    if query_ref is not None:
        query_ref[...] = jnp.where(own, 1.0, 0.0).astype(bf16)
    live = rows < count * SIZE
    key_ref[...] = jnp.where(inside & ~(own & live), masked_score, 0.0).astype(bf16)


def from_rows(raw_ref, out_ref):
    features, blocks, own, width = out_ref.shape
    pairs = width // LANES
    for f in range(features):
        for block in range(pairs):
            rows = raw_ref[pl.ds(block * features + f, blocks * own, stride=features * pairs), :]
            out_ref[f, :, :, pair_lanes(block)] = rows.reshape(blocks, own, LANES).astype(out_ref.dtype)


LAYER_OUTS = 14


def forward_layers(layers, box, sq_ref, sk_ref, fq_ref, fk_ref, raw_ref, *scratch):
    box.start(2, 3, 4, 7)
    size_ref, count_ref = box.use(0, 1)
    fill_sample_codes(size_ref[0], sq_ref, sk_ref)
    fill_feature_codes(count_ref[0], fq_ref, fk_ref)
    x_ref = box.out(LAYER_OUTS * layers)
    raw_ref[...] = box.use(2)[...].astype(f32)
    from_rows(raw_ref, x_ref)
    box.flush(LAYER_OUTS * layers)
    before = None
    for layer in range(layers):
        before = forward_layer(layer, layer == layers - 1, before, box, x_ref, sq_ref, sk_ref, fq_ref, fk_ref, raw_ref, *scratch)
        x_ref = box.out(LAYER_OUTS * layer + 9)


def forward_layer(layer, last, before, box, x_ref, sq_ref, sk_ref, fq_ref, fk_ref, raw_ref, h2_ref, swapped_ref, a_ref, back_ref, all_sends, all_recvs, all_self, all_back_sends, all_back_recvs):
    place = box.place
    first = LAYER_OUTS * layer
    outs = [first + index for index in range(LAYER_OUTS)]
    earlier = [index - LAYER_OUTS for index in outs]
    x1_ref, qkv_ref, ctx_ref, ext_ref, hidden_ref, fqkv_ref, fctx_ref, fext_ref, x2_ref, x3_ref, u_ref, h1_ref, active_ref, h3_ref = box.out(*outs)
    sends, recvs, self_sem = all_sends.at[layer], all_recvs.at[layer], all_self.at[layer]
    back_sends, back_recvs = all_back_sends.at[layer], all_back_recvs.at[layer]
    weights = 7 + 4 * layer
    gain_ref, shift_ref, w_ref = box.use(3, 4, weights)
    if layer > 0:
        box.settle(*[earlier[index] for index in (0, 1, 2, 3, 11)])
    features, blocks, own, width = x_ref.shape
    per = ROWS // own
    steps = blocks // per
    size = ROWS // blocks
    units = own // size
    pairs = width // LANES

    def gain(index):
        return gain_ref[index, layer : layer + 1, :], shift_ref[index, layer : layer + 1, :]

    parts = own // size

    def project(f):
        def rows(part, carry):
            _, _, hidden = layer_norm(block_rows(x_ref, f, part, per), *gain(0))
            hidden = hidden.astype(bf16)
            h1_ref[f, chunk(part, per), :, :] = hidden.reshape(per, own, width)
            for member in range(3):
                out = mm(hidden, w_ref[member]).astype(bf16)
                if member == 0:
                    out = out * jnp.asarray(0.125, bf16)
                qkv_ref[member, f, chunk(part, per), :, :] = out.reshape(per, own, width)
            return carry

        lax.fori_loop(0, steps, rows, 0)

    def copies(unit):
        f, part = unit // parts, lax.rem(unit, parts)
        found = [
            remote(
                h2_ref.at[f, place.ring(k), chunk(part, size), :],
                swapped_ref.at[place.place, f, chunk(part, size), :],
                sends.at[unit, k - 1],
                recvs.at[unit, k - 1],
                {"feat": place.ring(k)},
            )
            for k in range(1, place.places)
        ]
        keep = pltpu.make_async_copy(
            h2_ref.at[f, place.place, chunk(part, size), :],
            swapped_ref.at[place.place, f, chunk(part, size), :],
            self_sem.at[unit],
        )
        return found, keep

    def attend(unit, carry):
        f, part = unit // parts, lax.rem(unit, parts)

        @pl.when(part == 0)
        def _():
            if before is not None:
                before(f)
            project(f)

        code = sq_ref[...]
        extras = code.astype(f32)
        for pair in range(pairs):
            lanes = pair_lanes(pair)
            context, extras = attend_pair(
                own_rows(qkv_ref.at[0], f, part, size, lanes),
                all_rows(qkv_ref.at[1], f, lanes),
                all_rows(qkv_ref.at[2], f, lanes),
                code,
                sk_ref[...],
                pair,
                extras,
            )
            ctx_ref[f, :, chunk(part, size), lanes] = context.reshape(blocks, size, LANES)
        ext_ref[f, :, chunk(part, size), :] = extras.astype(bf16).reshape(blocks, size, LANES)
        x1 = own_rows(x_ref, f, part, size) + mm(own_rows(ctx_ref, f, part, size), w_ref[3])
        x1_ref[f, :, chunk(part, size), :] = x1.reshape(blocks, size, width)
        _, _, hidden = layer_norm(x1, *gain(1))
        h2_ref[f, :, chunk(part, size), :] = hidden.astype(bf16).reshape(blocks, size, width)

        @pl.when(unit == 0)
        def _():
            if layer == 0:
                box.ready()
                box.start(weights + 1, weights + 2, 5, weights + 3, 6)
            if not last:
                box.start(weights + 4, weights + 5, weights + 6, weights + 7)
            else:
                box.start(7 + 4 * (layer + 1))

        found, keep = copies(unit)
        for copy in found:
            copy.start()
        keep.start()
        return carry

    lax.fori_loop(0, features * units, attend, 0)
    box.flush(*[outs[index] for index in (0, 1, 2, 3, 11)])
    if before is not None:
        box.flush(*[earlier[index] for index in (8, 9, 10, 12, 13)])
        before(None)
    fw_ref = box.use(weights + 1)
    if layer > 0:
        box.settle(*earlier[4:8])
    groups = own // SIZE
    shared = size // SIZE

    def back_copies(group, f=None):
        which = slice(None) if f is None else f
        at = 0 if f is None else f
        return [
            remote(
                a_ref.at[place.ring(k), which, chunk(group, SIZE), :],
                back_ref.at[which, place.place, chunk(group, SIZE), :],
                back_sends.at[at, group, k - 1],
                back_recvs.at[at, group, k - 1],
                {"feat": place.ring(k)},
            )
            for k in range(1, place.places)
        ]

    def feature(group, carry):
        @pl.when(lax.rem(group, shared) == 0)
        def _():
            for f in range(features):
                found, keep = copies(f * parts + group // shared)
                for copy in found:
                    copy.wait_recv()
                keep.wait()

        hidden = cross(swapped_ref, group)
        hidden_ref[group] = hidden
        for member in range(3):
            out = mm(hidden, fw_ref[member]).astype(bf16)
            if member == 0:
                out = out * jnp.asarray(0.125, bf16)
            fqkv_ref[group, member] = out
        code = fq_ref[...]
        extras = code.astype(f32)
        for pair in range(pairs):
            lanes = pair_lanes(pair)
            context, extras = attend_pair(
                fqkv_ref[group, 0, :, lanes],
                fqkv_ref[group, 1, :, lanes],
                fqkv_ref[group, 2, :, lanes],
                code,
                fk_ref[...],
                pair,
                extras,
            )
            fctx_ref[group, :, lanes] = context
        fext_ref[group] = extras.astype(bf16)
        put_cross(a_ref, group, mm(fctx_ref[group], fw_ref[3]).astype(bf16))
        for copy in back_copies(group, None if last else 0):
            copy.start()
        back_ref[:, place.place, chunk(group, SIZE), :] = a_ref[place.place, :, chunk(group, SIZE), :]
        return carry

    lax.fori_loop(0, groups, feature, 0)
    if not last:
        for f in range(1, features):

            def send_rest(group, carry, f=f):
                for copy in back_copies(group, f):
                    copy.start()
                return carry

            lax.fori_loop(0, groups, send_rest, 0)
    box.flush(*outs[4:8])

    def settle(unit, carry):
        for copy in copies(unit)[0]:
            copy.wait_send()
        return carry

    lax.fori_loop(0, features * units, settle, 0)
    if last:
        og_ref = box.out(first + LAYER_OUTS + 1)
        raw_ref[...] = box.use(7 + 4 * (layer + 1))[...].astype(f32)
        from_rows(raw_ref, og_ref)
        box.flush(first + LAYER_OUTS + 1)
    up_ref, upb_ref, down_ref, downb_ref = box.use(weights + 2, 5, weights + 3, 6)
    if layer > 0:
        box.settle(*[earlier[index] for index in (8, 9, 10, 12, 13)])
    hidden_width = up_ref.shape[1]

    def feed_forward(x2, keep):
        _, _, hidden = layer_norm(x2, *gain(2))
        hidden = hidden.astype(bf16)
        keep(h3_ref, slice(None), hidden)
        columns = [slice(part * 512, part * 512 + 512) for part in range(hidden_width // 512)]
        actives = []
        for cols in columns:
            u = mm(hidden, up_ref[:, cols]) + upb_ref[layer : layer + 1, cols]
            bent = gelu_parts(u)
            both = 0.5 * (1.0 + bent)
            active = (u * both).astype(bf16)
            keep(active_ref, cols, active)
            slope = both + u * (1.0 - bent * bent) * (0.3989422804014327 + 0.05351611220146811 * u * u)
            keep(u_ref, cols, slope.astype(bf16))
            actives.append(active)
        return x2 + downb_ref[layer : layer + 1, :] + mm(jnp.concatenate(actives, axis=1), down_ref[...])

    def dense(group, carry):
        for copy in back_copies(group):
            copy.wait_recv()
        x2 = cross(x1_ref, group) + cross(back_ref, group).astype(f32)
        put_cross(x2_ref, group, x2)

        def keep(ref, cols, values):
            ref[group, :, cols] = values

        put_cross(x3_ref, group, feed_forward(x2, keep))
        box.flush_part(outs[8], group, cross_view)
        box.flush_part(outs[9], group, cross_view)
        box.flush_part(outs[10], group, first_view)
        box.flush_part(outs[12], group, first_view)
        box.flush_part(outs[13], group, first_view)
        return carry

    def dense_of(f):
        if f is None:

            def settle_back(group, carry):
                for other in range(features):
                    for copy in back_copies(group, other):
                        copy.wait_send()
                return carry

            lax.fori_loop(0, groups, settle_back, 0)
            return

        def arrived(group, carry):
            for copy in back_copies(group, f):
                copy.wait_recv()
            return carry

        lax.fori_loop(0, groups, arrived, 0)

        def rows(unit, carry):
            x2 = own_rows(x1_ref, f, unit, size) + own_rows(back_ref, f, unit, size).astype(f32)
            x2_ref[f, :, chunk(unit, size), :] = x2.reshape(blocks, size, width)
            count = blocks * SIZE

            def keep(ref, cols, values):
                parted = values.reshape(blocks, shared, SIZE, values.shape[1])
                for at in range(shared):
                    ref[unit * shared + at, chunk(f, count), cols] = parted[:, at].reshape(count, values.shape[1])

            x3_ref[f, :, chunk(unit, size), :] = feed_forward(x2, keep).reshape(blocks, size, width)
            return carry

        lax.fori_loop(0, parts, rows, 0)

    if not last:
        return dense_of
    lax.fori_loop(0, groups, dense, 0)

    def settle_back(group, carry):
        for copy in back_copies(group):
            copy.wait_send()
        return carry

    lax.fori_loop(0, groups, settle_back, 0)
    return None


def pieces_of(values):
    first = values.astype(bf16)
    rest = values - first.astype(f32)
    second = rest.astype(bf16)
    return first, second, (rest - second.astype(f32)).astype(bf16)


def exact(left, right, dims):
    first, second, third = pieces_of(right)
    return mm(left, first, dims) + mm(left, second, dims) + mm(left, third, dims)


def exact_left(left, right, dims):
    first, second, third = pieces_of(left)
    return mm(first, right, dims) + mm(second, right, dims) + mm(third, right, dims)


def read_out(box, ins, later, outs, x_ref, x_load, g_ref, reading_ref, got_ref, bins_ref, counted_ref, read_ref, weight_ref, sends, recvs):
    place = box.place
    shapes_ref, loss_ref, rgrad_ref = box.out(*outs)
    read_ref[...] = jnp.zeros_like(read_ref)
    size_ref, count_ref, label_ref, index_ref, population_ref, narrow_ref = box.use(*ins)
    x_load.wait()
    box.start(*later)
    read_ref[0 : narrow_ref.shape[0], :] = narrow_ref[...]
    features, blocks, own, width = x_ref.shape
    samples = blocks * own
    bins = population_ref.shape[1]
    size, count = size_ref[0], count_ref[0]
    mask = (lax.broadcasted_iota(jnp.int32, (1, samples), 1) < size).astype(f32)
    task_size = jnp.zeros((1, samples), f32) + size.astype(f32)
    level = lax.broadcasted_iota(jnp.int32, (bins, bins), 0)
    diagonal = (level == lax.broadcasted_iota(jnp.int32, (bins, bins), 1)).astype(f32)
    live = [
        jnp.where(place.place * features + f < count, 1.0, 0.0) for f in range(features)
    ]
    logits = None
    for f in range(features):
        reading = x_ref[f].reshape(samples, width).astype(bf16)
        reading_ref[f] = reading.reshape(blocks, own, width)
        projected = mm(reading, read_ref[...], NT)
        onehot = (lax.broadcasted_iota(jnp.int32, (bins, samples), 0) == index_ref[f : f + 1, :]).astype(f32)
        bins_ref[f] = onehot.astype(bf16)
        chosen = onehot * mask
        counted = jnp.maximum(jnp.sum(chosen, axis=1, keepdims=True), 1.0)
        counted_ref[f] = jnp.broadcast_to(counted, (bins, LANES))
        means = exact(chosen.astype(bf16), projected, NN) / counted
        weight = jnp.sum(diagonal * population_ref[f : f + 1, :].astype(f32), axis=1, keepdims=True)
        weight_ref[f] = jnp.broadcast_to(weight, (bins, LANES))
        weight = weight_ref[f]
        centre = jnp.sum(weight * means, axis=0, keepdims=True) / jnp.sum(weight, axis=0, keepdims=True)
        shapes = means - centre
        shapes_ref[f] = shapes
        part = exact_left(shapes, bins_ref[f], TN)[:SIZE] * live[f]
        logits = part if logits is None else logits + part
    spans = range(samples // LANES)
    got_ref[place.place] = jnp.concatenate([logits[0:CLASSES, pair_lanes(span)] for span in spans], axis=0)
    box.ready()
    copies = [
        remote(
            got_ref.at[place.place],
            got_ref.at[place.place],
            sends.at[k - 1],
            recvs.at[k - 1],
            {"feat": place.ring(k)},
        )
        for k in range(1, place.places)
    ]
    for copy in copies:
        copy.start()
    for copy in copies:
        copy.wait()
    total = got_ref[0]
    for k in range(1, place.places):
        total = total + got_ref[k]
    rows_left = jnp.zeros((SIZE - CLASSES, LANES), f32)
    logits = jnp.concatenate(
        [
            jnp.concatenate([total[span * CLASSES : span * CLASSES + CLASSES], rows_left], axis=0)
            for span in spans
        ],
        axis=1,
    )
    class_row = lax.broadcasted_iota(jnp.int32, logits.shape, 0)
    inside = class_row < CLASSES
    peak = jnp.max(jnp.where(inside, logits, masked_score), axis=0, keepdims=True)
    weights = jnp.where(inside, jnp.exp(jnp.where(inside, logits - peak, 0.0)), 0.0)
    weight_sum = jnp.sum(weights, axis=0, keepdims=True)
    log_total = peak + jnp.log(weight_sum)
    own_class = (class_row == label_ref[...]).astype(f32)
    picked = jnp.sum(logits * own_class, axis=0, keepdims=True)
    losses = mask * (log_total - picked)
    loss_ref[...] = jnp.broadcast_to(
        jnp.sum(losses, axis=1, keepdims=True) / task_size[:, 0:1], loss_ref.shape
    )
    logit_grad = mask * (weights / weight_sum - own_class) / task_size
    pad = jnp.zeros((LANES - SIZE, samples), f32)
    total = None
    for f in range(features):
        grad_rows = jnp.concatenate([logit_grad * live[f], pad], axis=0)
        shape_grad = exact(bins_ref[f], grad_rows, NT)
        weight = weight_ref[f]
        means_grad = shape_grad - weight / jnp.sum(weight, axis=0, keepdims=True) * jnp.sum(
            shape_grad, axis=0, keepdims=True
        )
        chosen = (bins_ref[f].astype(f32) * mask).astype(bf16)
        proj_grad = exact(chosen, means_grad / counted_ref[f], TN).astype(bf16)
        part = mm(proj_grad, all_rows(reading_ref, f), TN)[:SIZE]
        total = part if total is None else total + part
        if f == 0:
            box.use(1)
        back = mm(proj_grad, read_ref[...]).reshape(blocks, own, width)
        g_ref[f] = g_ref[f] + back
    rgrad_ref[...] = total
    box.flush(*outs)


def dense_feature_backward(layer, box, fk_ref, send_ref, ugrad_ref, rowgrad_ref, dup_ref, ddown_ref, arriving_ref, dc_ref, dh_ref, back_ref, dwf_ref, sends, recvs, self_sem, back_sends, back_recvs, *head):
    place = box.place
    g1_ref, small_ref, sdc_ref, sext_ref, slow_ref = box.out(0, 1, 2, 3, 4)
    if head:
        x_load = pltpu.make_async_copy(box.bufs[18], g1_ref, head[-1])
        box.start(19, 20, 21, 22)
        x_load.start()
    else:
        box.start(6, 7, (1, 0), 2, (3, 0), 4, (5, 0))
    small_ref[...] = jnp.zeros_like(small_ref)
    fill_feature_codes(box.use(0)[0], None, fk_ref)
    if not head:
        box.use(6, 7, 2, 4)
    gain_ref, shift_ref, down_ref, up_ref = box.bufs[6], box.bufs[7], box.bufs[2], box.bufs[4]
    g_ref, slope_ref, x2_ref = box.bufs[1], box.bufs[3], box.bufs[5]
    active_ref, hidden3_ref = box.bufs[16], box.bufs[17]
    if not head:
        box.start((1, 1, 2, 3), (3, 1, 2, 3), (5, 1, 2, 3))
    else:
        later = (1, 6, 7, 2, 3, 4, 5, 17, 16, 8, 9, 10, 11, 12, 13, 14, 15)
        read_out(box, (23, 0, 19, 20, 21, 22), later, (5, 6, 7), g1_ref, x_load, g_ref, send_ref, *head[:-1])
        box.use(6, 7, 2, 4)
    features, blocks, own, width = g_ref.shape
    hidden_width = up_ref.shape[1]
    groups = own // SIZE
    parts = hidden_width // 512
    pairs = width // LANES

    def copies(group):
        found = [
            remote(
                send_ref.at[:, place.ring(k), chunk(group, SIZE), :],
                arriving_ref.at[place.place, :, chunk(group, SIZE), :],
                sends.at[group, k - 1],
                recvs.at[group, k - 1],
                {"feat": place.ring(k)},
            )
            for k in range(1, place.places)
        ]
        keep = pltpu.make_async_copy(
            send_ref.at[:, place.place, chunk(group, SIZE), :],
            arriving_ref.at[place.place, :, chunk(group, SIZE), :],
            self_sem.at[group],
        )
        return found, keep

    def dense(group, carry):
        rows = chunk(group, ROWS)
        if not head:
            box.part(1, group)
        box.part(3, group)
        box.part(5, group)
        grad = cross(g_ref, group)
        low = grad.astype(bf16)
        rowgrad_ref[rows, :] = low
        small_ref[parts : parts + 1] += jnp.sum(low.astype(f32), axis=0, keepdims=True)
        for part in range(parts):
            cols = slice(part * 512, part * 512 + 512)
            active_grad = mm(low, down_ref[cols, :], NT).astype(bf16).astype(f32)
            ugrad = (active_grad * slope_ref[group, :, cols].astype(f32)).astype(bf16)
            ugrad_ref[rows, cols] = ugrad
            small_ref[part : part + 1] += jnp.sum(ugrad.astype(f32), axis=0, keepdims=True)
        hidden_grad = mm(ugrad_ref[rows, :], up_ref[...], NT)
        x2 = cross(x2_ref, group)
        gain = gain_ref[2, layer : layer + 1, :]
        norm_grad, gain_part, shift_part = layer_norm_back(hidden_grad.astype(bf16).astype(f32), x2, gain)
        small_ref[parts + 1 : parts + 2] += gain_part
        small_ref[parts + 2 : parts + 3] += shift_part
        grad = grad + norm_grad
        put_cross(g1_ref, group, grad)
        put_cross(send_ref, group, grad.astype(bf16))
        if not head:

            @pl.when(group == 0)
            def _():
                box.ready()
                box.start(17, 16, 8, 9, 10, 11, 12, 13, 14, 15)

        found, keep = copies(group)
        for copy in found:
            copy.start()
        keep.start()
        return carry

    lax.fori_loop(0, groups, dense, 0)

    def up_weights(part, carry):
        cols = chunk(part, 512)
        out = mm(ugrad_ref[:, cols], hidden3_ref[...], TN)
        dup_ref[part // 2, lax.rem(part, 2)] = out.astype(bf16).reshape(dup_ref.shape[2:])
        return carry

    def down_weights(part, carry):
        cols = chunk(part, 512)
        out = mm(active_ref[:, cols], rowgrad_ref[...], TN)
        ddown_ref[part // 2, lax.rem(part, 2)] = out.astype(bf16).reshape(ddown_ref.shape[2:])
        return carry

    box.use(16, 17)
    lax.fori_loop(0, parts, up_weights, 0)
    box.chains[0].begin(dup_ref)
    lax.fori_loop(0, parts, down_weights, 0)
    box.point("dense")
    box.chains[1].begin(ddown_ref)
    grads_ref = active_ref
    w_ref, qkv_ref, ctx_ref, ext_ref = box.use(8, 9, 10, 11)

    def back_copies(group):
        return [
            remote(
                dh_ref.at[place.ring(k), :, chunk(group, SIZE), :],
                back_ref.at[:, place.place, chunk(group, SIZE), :],
                back_sends.at[group, k - 1],
                back_recvs.at[group, k - 1],
                {"feat": place.ring(k)},
            )
            for k in range(1, place.places)
        ]

    def feature(group, carry):
        found, keep = copies(group)
        for copy in found:
            copy.wait_recv()
        keep.wait()
        rows = chunk(group, ROWS)
        dao = cross(arriving_ref, group)
        grads_ref[rows, 3 * width : 4 * width] = dao
        context_grad = mm(dao, w_ref[3], NT).astype(bf16)
        dc_ref[...] = context_grad
        grad_extra = delta_extra(ctx_ref[group], context_grad)
        for pair in range(pairs):
            lanes = pair_lanes(pair)
            query_grad, key_grad, value_grad = attend_pair_back(
                qkv_ref[group, 0, :, lanes],
                qkv_ref[group, 1, :, lanes],
                qkv_ref[group, 2, :, lanes],
                dc_ref[:, lanes],
                ext_ref[group],
                grad_extra,
                fk_ref[...],
                pair,
            )
            for member, grad in enumerate((query_grad * 0.125, key_grad, value_grad)):
                at = member * width + pair * LANES
                grads_ref[rows, at : at + LANES] = grad.astype(bf16)
        total = mm(grads_ref[rows, 0:width], w_ref[0], NT)
        total = total + mm(grads_ref[rows, width : 2 * width], w_ref[1], NT)
        total = total + mm(grads_ref[rows, 2 * width : 3 * width], w_ref[2], NT)
        put_cross(dh_ref, group, total.astype(bf16))
        for copy in back_copies(group):
            copy.start()
        back_ref[:, place.place, chunk(group, SIZE), :] = dh_ref[place.place, :, chunk(group, SIZE), :]

        for at in range(groups):

            @pl.when(group == at)
            def _(at=at):
                box.point(at)

        return carry

    lax.fori_loop(0, groups, feature, 0)
    hidden_ref = box.use(12)

    def weights(member, carry):
        hidden = hidden_ref[...].reshape(groups * ROWS, width)
        out = mm(hidden, grads_ref[:, chunk(member, width)], TN)
        dwf_ref[member // 2, lax.rem(member, 2)] = out.astype(bf16).reshape(dwf_ref.shape[2:])
        return carry

    lax.fori_loop(0, 3, weights, 0)
    context = ctx_ref[...].reshape(groups * ROWS, width)
    out = mm(context, grads_ref[:, 3 * width : 4 * width], TN)
    dwf_ref[1, 1] = out.astype(bf16).reshape(dwf_ref.shape[2:])
    box.chains[2].begin(dwf_ref)
    box.point("weights")
    x1_ref, wo_ref, sctx_ref = box.use(13, 14, 15)

    def enter(group, carry):
        for copy in back_copies(group):
            copy.wait_recv()
        norm_grad, gain_part, shift_part = layer_norm_back(
            cross(back_ref, group).astype(f32), cross(x1_ref, group), gain_ref[1, layer : layer + 1, :]
        )
        small_ref[parts + 3 : parts + 4] += gain_part
        small_ref[parts + 4 : parts + 5] += shift_part
        grad = cross(g1_ref, group) + norm_grad
        put_cross(g1_ref, group, grad)
        low = grad.astype(bf16)
        put_cross(slow_ref, group, low)
        context_grad = mm(low, wo_ref[...], NT).astype(bf16)
        put_cross(sdc_ref, group, context_grad)
        put_cross(sext_ref, group, delta_extra(cross(sctx_ref, group), context_grad))
        box.flush_part(0, group, cross_view)
        box.flush_part(2, group, cross_view)
        box.flush_part(3, group, cross_view)
        box.flush_part(4, group, cross_view)

        for at in range(groups):

            @pl.when(group == at)
            def _(at=at):
                box.point(10 + at)

        return carry

    lax.fori_loop(0, groups, enter, 0)
    box.flush(1)
    box.point("end")

    def settle(group, carry):
        for copy in copies(group)[0]:
            copy.wait_send()
        for copy in back_copies(group):
            copy.wait_send()
        return carry

    lax.fori_loop(0, groups, settle, 0)


def sample_backward_last(layer, last, box, sk_ref, dqkv_ref, *tail):
    place = box.place
    g0_ref, small_ref = box.out(0, 1)
    box.start((1, 0), (2, 0), 3, 4)
    small_ref[...] = jnp.zeros_like(small_ref)
    fill_sample_codes(box.use(0)[0], None, sk_ref)
    qkv_ref, dc_ref = box.bufs[1], box.bufs[2]
    features, blocks, own, width = dc_ref.shape
    samples = blocks * own
    per = ROWS // own
    steps = blocks // per
    pairs = width // LANES
    total_rows = features * samples
    if last:
        dw_ref, bufs_1, bufs_2, bufs_3, *small_bufs = tail
        share_ref = box.out(3)
    else:
        dw_ref, *small_bufs = tail
    exchange = SmallSums(place, last, *small_bufs)
    ext_ref, gext_ref = box.use(3, 4)
    box.ready()
    box.start((1, 1, 2, 3), (2, 1, 2, 3), 9, 10, 11, 12, 13)

    def step_of(step, pair):
        got_ref, _, sends, recvs = (bufs_1, bufs_2, bufs_3)[step - 1]
        source = dw_ref.at[pair] if step == 1 else (bufs_1, bufs_2)[step - 2][1].at[pair]
        return SumStep(5 if step == 3 else step, place, source, None, got_ref.at[pair], sends.at[pair], recvs.at[pair], None)

    def pass_on(step, pair):
        step_of(step, pair).finish((bufs_1, bufs_2, bufs_3)[step - 1][1].at[pair])
        if step < 3:
            step_of(step + 1, pair).start()

    def attend(pair, carry):
        lanes = chunk(pair, LANES)
        box.part(1, pair)
        box.part(2, pair)
        for f in range(features):
            key_total = value_total = None
            for step in range(steps):
                rows = slice(f * samples + step * ROWS, f * samples + step * ROWS + ROWS)
                query_grad, key_grad, value_grad = attend_pair_back(
                    block_rows(qkv_ref.at[0], f, step, per, lanes),
                    all_rows(qkv_ref.at[1], f, lanes),
                    all_rows(qkv_ref.at[2], f, lanes),
                    block_rows(dc_ref, f, step, per, lanes),
                    block_rows(ext_ref, f, step, per),
                    block_rows(gext_ref, f, step, per),
                    sk_ref[...],
                    pair,
                )
                dqkv_ref[0, rows, lanes] = (query_grad * 0.125).astype(bf16)
                key_total = key_grad if key_total is None else key_total + key_grad
                value_total = value_grad if value_total is None else value_total + value_grad
            rows = slice(f * samples, f * samples + samples)
            dqkv_ref[1, rows, lanes] = key_total.astype(bf16)
            dqkv_ref[2, rows, lanes] = value_total.astype(bf16)

        for at in range(1, pairs):

            @pl.when(pair == at)
            def _(at=at):
                box.point(at)

        @pl.when(pair == 0)
        def _():
            box.start(5, 6, 7, 8)
            dense_rows, other_rows = box.use(12, 13)
            if last:
                exchange.start([(0, 9, dense_rows, 9), (9, 11, other_rows, 2)])
            else:
                exchange.start([(0, 9, dense_rows, 9), (9, 9 + SIZE, other_rows, SIZE)])

        for stage in range(1, 4):

            @pl.when(pair == stage)
            def _(stage=stage):
                exchange.move(stage)

        if not last:
            return carry

        @pl.when(pair == 0)
        def _():
            box.use(9, 10, 11)

        hidden = box.bufs[9][...].reshape(total_rows, width)
        context = box.bufs[10][...].reshape(total_rows, width)
        low_ref = box.bufs[11]
        block = dw_ref.shape[3:]
        for member in range(3):
            out = mm(dqkv_ref[member, :, lanes], hidden, TN).T
            dw_ref[pair, member // 2, member % 2] = out.astype(bf16).reshape(block)
        low = low_ref[:, :, :, lanes].reshape(total_rows, LANES)
        dw_ref[pair, 1, 1] = mm(low, context, TN).T.astype(bf16).reshape(block)
        step_of(1, pair).start()

        @pl.when(pair >= 1)
        def _():
            pass_on(1, pair - 1)

        @pl.when(pair >= 2)
        def _():
            pass_on(2, pair - 2)

        return carry

    lax.fori_loop(0, pairs, attend, 0)
    box.point("attend")
    if not last:
        hidden_ref, context_ref, low_ref = box.use(9, 10, 11)

        def weights(member, carry):
            hidden = hidden_ref[...].reshape(total_rows, width)
            out = mm(hidden, dqkv_ref[member], TN)
            dw_ref[member // 2, lax.rem(member, 2)] = out.astype(bf16).reshape(dw_ref.shape[2:])
            return carry

        lax.fori_loop(0, 3, weights, 0)
        context = context_ref[...].reshape(total_rows, width)
        out = mm(context, low_ref[...].reshape(total_rows, width), TN)
        dw_ref[1, 1] = out.astype(bf16).reshape(dw_ref.shape[2:])
        box.chains[-1].begin(dw_ref)
    w_ref, x_ref, gain_ref, g_ref = box.use(5, 6, 7, 8)
    gain = gain_ref[0, layer : layer + 1, :]

    def leave(unit, carry):
        f, part = unit // steps, lax.rem(unit, steps)
        rows = chunk(unit, ROWS)
        total = mm(dqkv_ref[0, rows, :], w_ref[0], NT)
        total = total + mm(dqkv_ref[1, rows, :], w_ref[1], NT)
        total = total + mm(dqkv_ref[2, rows, :], w_ref[2], NT)
        norm_grad, gain_part, shift_part = layer_norm_back(
            total.astype(bf16).astype(f32), block_rows(x_ref, f, part, per), gain
        )
        small_ref[0:1] += gain_part
        small_ref[1:2] += shift_part
        g0_ref[f, chunk(part, per), :, :] = (block_rows(g_ref, f, part, per) + norm_grad).reshape(per, own, width)
        if last:

            @pl.when(unit == 1)
            def _():
                pass_on(1, pairs - 1)

            @pl.when(unit == 2)
            def _():
                pass_on(2, pairs - 2)

        @pl.when(unit == 2)
        def _():
            box.point("leave")
            box.out(2)[...] = exchange.sum(3)
            box.flush(2)

        return carry

    lax.fori_loop(0, features * steps, leave, 0)
    box.flush(0, 1)
    if last:
        exchange.start_late(small_ref)
        pass_on(2, pairs - 1)
        exchange.move(5)
    box.point("end")
    if last:
        for pair in range(pairs):
            pass_on(3, pair)
            share_ref[:, pair_lanes(pair)] = bufs_3[1][pair]
        box.flush(3)
        box.out(4)[...] = exchange.sum(5)
        box.flush(4)


class SmallSums:
    def __init__(self, place, last, packed, early, late, sends, recvs):
        self.packed, self.early, self.late = packed, early, late
        tasks = [{"task": place.task_partner(k)} for k in range(1, place.tasks)]
        ring = [{"feat": place.ring(k)} for k in range(1, place.places)]
        plan = [
            (early, 0, 2, place.core, [place.other_core]),
            (early, 2, place.tasks, place.task, tasks),
            (early, 2 + place.tasks, 2, place.near, [place.near_chip]),
            (early, 4 + place.tasks, 2, place.far, [place.far_chip]),
            (late, 0, place.places, place.place, ring),
            (late, place.places, place.tasks, place.task, tasks),
        ]
        plan = plan if last else plan[:4]
        self.plan, self.copies, at = plan, [], 0
        for buffer, first, count, mine, devices in plan:
            slot = buffer.at[first + mine]
            self.copies.append(
                [remote(slot, slot, sends.at[at + k], recvs.at[at + k], device) for k, device in enumerate(devices)]
            )
            at += len(devices)

    def send(self, stage, rows):
        buffer, first, _, mine, _ = self.plan[stage]
        buffer[first + mine] = rows
        for copy in self.copies[stage]:
            copy.start()

    def start(self, parts):
        self.packed[...] = jnp.zeros_like(self.packed)
        for begin, end, source, count in parts:
            self.packed[begin:end] = source[0:count]
        self.send(0, self.packed[...])

    def start_late(self, rows_ref):
        blocks = [rows_ref[row : row + 1, pair_lanes(block)] for row in range(2) for block in range(4)]
        self.send(4, jnp.concatenate(blocks, axis=0))

    def sum(self, stage):
        buffer, first, count, _, _ = self.plan[stage]
        for copy in self.copies[stage]:
            copy.wait()
        total = buffer[first]
        for k in range(1, count):
            total = total + buffer[first + k]
        return total

    def move(self, stage):
        self.send(stage, self.sum(stage - 1))


def write_out(dense_rows, x_ref, g_ref, *refs):
    refs = list(refs)
    shares, packed_rows, late, bins, loss, outs = refs[:8], refs[8:10], refs[10], refs[11], refs[12], refs[13:26]
    raw_x, raw_g, x_buf, g_buf, load_sem, out_sem = refs[26:]
    outs[12][0] = loss[0, 0]
    for f in range(bins.shape[0]):
        outs[11][:, f, :] = bins[f].T[0:CLASSES]
    features, blocks, own, width = x_ref.shape
    period = features * (width // LANES)
    per = blocks // 4
    rows_part = per * own

    def load(part, which):
        source, target = ((x_ref, x_buf), (g_ref, g_buf))[which]
        view = (slice(None), pl.ds(part * per, per))
        return pltpu.make_async_copy(source.at[view], target.at[view], load_sem.at[which, part])

    def store(part, which):
        source, target = ((raw_x, outs[0]), (raw_g, outs[1]))[which]
        view = pl.ds(part * rows_part * period, rows_part * period)
        return pltpu.make_async_copy(source.at[view], target.at[view], out_sem.at[which, part])

    for part in range(4):
        load(part, 0).start()
        load(part, 1).start()
    for member in range(4):
        outs[2 + member][0] = shares[2 * member][...]
        outs[2 + member][1] = shares[2 * member + 1][...]
    parts = dense_rows - 5
    for layer in range(2):
        packed, at = packed_rows[layer], 0
        for part in range(parts):
            outs[8][layer : layer + 1, part * width : (part + 1) * width] = packed[at + part : at + part + 1]
        outs[9][layer : layer + 1] = packed[at + parts : at + parts + 1]
        for member, row in ((2, parts + 1), (1, parts + 3)):
            outs[6][member, layer : layer + 1] = packed[at + row : at + row + 1]
            outs[7][member, layer : layer + 1] = packed[at + row + 1 : at + row + 2]
    at = dense_rows
    for block in range(4):
        lanes = pair_lanes(block)
        outs[6][0, 0:1, lanes], outs[7][0, 0:1, lanes] = late[block : block + 1], late[4 + block : 5 + block]
    outs[6][0, 1:2], outs[7][0, 1:2] = packed_rows[0][at : at + 1], packed_rows[0][at + 1 : at + 2]
    outs[10][...] = packed_rows[1][at : at + CLASSES]

    for part in range(4):
        for which, buf, raw in ((0, x_buf, raw_x), (1, g_buf, raw_g)):
            load(part, which).wait()
            for f in range(features):
                for block in range(width // LANES):
                    rows = buf[f, part * per : (part + 1) * per, :, pair_lanes(block)].reshape(rows_part, LANES)
                    start = part * rows_part * period + block * features + f
                    raw[pl.ds(start, rows_part, stride=period), :] = rows
            store(part, which).start()
    for part in range(4):
        store(part, 0).wait()
        store(part, 1).wait()


def codes(item, live, size, rows):
    lanes = jnp.arange(LANES)[None, :] - CODE_LANE
    inside = (lanes >= 0) & (lanes < size)
    own = lanes == item[:, None]
    query_code = (own & inside).astype(bf16)
    key_code = jnp.where(inside & ~(own & live[:, None]), masked_score, 0.0).astype(bf16)
    return query_code, key_code


def local_fused(
    tokens_in,
    sample_weights,
    feature_weights,
    norm_gain,
    norm_shift,
    up_weight,
    up_bias,
    down_weight,
    down_bias,
    read_weight,
    output_grad,
    task_sizes,
    feature_counts,
    bin_index,
    bin_counts,
    class_labels,
):
    samples, features, width = tokens_in.shape[1:]
    hidden_width = up_weight.shape[2]
    tasks, places = lax.axis_size("task"), lax.axis_size("feat")
    own = samples // places
    groups = own // SIZE
    units = features * (own * places // ROWS)
    sizes = (tasks, places)
    shape = (features, places, own, width)
    block_shape = (places, features, own, width)
    group_shape = (groups, ROWS, width)
    share = width // places
    share_shape = (share, width)
    piece_shape = (2, 2, 2, 2, 2, share, width)
    rows_total = groups * ROWS
    vmem = pltpu.VMEM

    def dma(*counts):
        return pltpu.SemaphoreType.DMA(counts)

    def raw_rows(tokens):
        parts = tokens.reshape(samples, features, width // LANES, LANES)
        return parts.transpose(0, 2, 1, 3).reshape(samples * features * (width // LANES), LANES)

    def from_raw(rows):
        parts = rows.reshape(samples, width // LANES, features, LANES)
        return parts.transpose(0, 2, 1, 3).reshape(1, samples, features, width)

    gains = norm_gain.transpose(1, 0, 2)
    shifts = norm_shift.transpose(1, 0, 2)
    layer_outs = [
        (shape, f32),
        ((3,) + shape, bf16),
        (shape, bf16),
        (shape[:3] + (LANES,), bf16),
        (group_shape, bf16),
        ((groups, 3, ROWS, width), bf16),
        (group_shape, bf16),
        ((groups, ROWS, LANES), bf16),
        (shape, f32),
        (shape, f32),
        ((groups, ROWS, hidden_width), bf16),
        (shape, bf16),
        ((groups, ROWS, hidden_width), bf16),
        (group_shape, bf16),
    ]
    ins = [
        (task_sizes, "scalar"),
        (feature_counts, "scalar"),
        (raw_rows(tokens_in), None),
        (gains, None),
        (shifts, None),
        (up_bias, None),
        (down_bias, None),
    ]
    for layer in range(LAYERS):
        ins += [(weight, layer) for weight in (sample_weights, feature_weights, up_weight, down_weight)]
    ins.append((raw_rows(output_grad), None))
    outs = list(layer_outs)
    for layer in range(1, LAYERS):
        outs += [(*item, index) for index, item in enumerate(layer_outs)]
    outs += [(shape, f32), (shape, f32)]
    *kept, first_rows, stream_grad = fused(
        functools.partial(forward_layers, LAYERS),
        "forward_layers",
        sizes,
        ins,
        outs,
        [
            vmem((ROWS, LANES), bf16),
            vmem((samples, LANES), bf16),
            vmem((ROWS, LANES), bf16),
            vmem((ROWS, LANES), bf16),
            vmem((samples * features * (width // LANES), LANES), f32),
            vmem(shape, bf16),
            vmem(block_shape, bf16),
            vmem(block_shape, bf16),
            vmem(shape, bf16),
            dma(LAYERS, units, places - 1),
            dma(LAYERS, units, places - 1),
            dma(LAYERS, units),
            dma(LAYERS, features, groups, places - 1),
            dma(LAYERS, features, groups, places - 1),
        ],
        [],
        share_shape,
        1,
    )
    stored = []
    stream = first_rows
    for layer in range(LAYERS):
        x1, qkv, ctx, ext, hidden, fqkv, fctx, fext, x2, x3, u, h1, act, h3 = kept[14 * layer : 14 * layer + 14]
        stored.append((stream, x1, qkv, ctx, ext, hidden, fqkv, fctx, fext, x2, u, h1, act, h3))
        stream = x3

    finished = {}
    dense_rows = hidden_width // width + 5
    pairs = width // LANES
    flat = (rows_total, width)
    for layer in reversed(range(LAYERS)):
        x0, x1, qkv, ctx, ext, hidden, fqkv, fctx, fext, x2, u, h1, act, h3 = stored[layer]
        last = layer == 0
        ins = [
            (feature_counts, "scalar"),
            (stream_grad, None, cross_view, groups),
            (down_weight, layer),
            (u, None, first_view, groups),
            (up_weight, layer),
            (x2, None, cross_view, groups),
            (gains, None),
            (shifts, None),
            (feature_weights, layer),
            (fqkv, None),
            (fctx, None),
            (fext, None),
            (hidden, None),
            (x1, None),
            (sample_weights, (layer, 3)),
            (ctx, None),
            (act.reshape(rows_total, hidden_width), None),
            (h3.reshape(flat), None),
        ]
        head = []
        if not last:
            ins += [
                (stream, "raw"),
                (class_labels, None),
                (bin_index[0].T, None),
                (bin_counts[0], None),
                (jnp.pad(read_weight.T, ((0, SIZE - CLASSES), (0, 0))), None),
                (task_sizes, "scalar"),
            ]
            ins[1] = (stream_grad, None)
            head = [
                vmem((places, CLASSES * (samples // LANES), LANES), f32),
                vmem((features, BINS, samples), bf16),
                vmem((features, BINS, LANES), f32),
                vmem((LANES, width), bf16),
                vmem((features, BINS, LANES), f32),
                dma(places - 1),
                dma(places - 1),
                pltpu.SemaphoreType.DMA,
            ]
        sums = [
            ((1, 6, 7, 3), ("dense", 2, "weights", 12), None, True),
            ((1, 6, 7, 3), (0, 3, 10, 12), None, True),
            ((1, 6), (10, 12), None, True),
        ]
        if last:
            sums += [((2, 3), (0, 11), sample_sum, True), ((3,), (0, 11), finished[1][0], True)]
        g1, dense_small, sdc, sext, slow, *results = fused(
            functools.partial(dense_feature_backward, layer),
            "dense_feature_backward",
            sizes,
            ins,
            [
                (shape, f32),
                ((16, width), f32),
                (shape, bf16),
                (shape[:3] + (LANES,), bf16),
                (shape, bf16),
            ]
            + ([] if last else [((features, BINS, LANES), f32), ((8, LANES), f32), ((SIZE, width), f32)]),
            [
                vmem((ROWS, LANES), bf16),
                vmem(shape, bf16),
                vmem((rows_total, hidden_width), bf16),
                vmem(flat, bf16),
                vmem(piece_shape, bf16),
                vmem(piece_shape, bf16),
                vmem(block_shape, bf16),
                vmem((ROWS, width), bf16),
                vmem(block_shape, bf16),
                vmem(shape, bf16),
                vmem(piece_shape, bf16),
                dma(groups, places - 1),
                dma(groups, places - 1),
                dma(groups),
                dma(groups, places - 1),
                dma(groups, places - 1),
            ]
            + head,
            sums,
            share_shape,
            4 + layer,
        )
        if not last:
            shapes, loss, read_grad, *results = results
        up_sum, down_sum, feature_sum, *later_sum = results
        ins = [
            (task_sizes, "scalar"),
            (qkv, None, last_view, pairs),
            (sdc, None, last_view, pairs),
            (ext, None),
            (sext, None),
            (sample_weights, layer),
            (x0, None),
            (gains, None),
            (g1, None),
        ]
        other_small = sample_small if last else read_grad
        ins += [(array, None) for array in (h1, ctx, slow, dense_small, other_small)]
        early_rows = -(-(dense_rows + (2 if last else SIZE)) // 8) * 8
        slots = 6 + tasks
        copies = 1 + (tasks - 1) + 1 + 1 + (places - 1) + (tasks - 1)
        small_scratch = [
            vmem((early_rows, width), f32),
            vmem((slots, early_rows, width), f32),
            vmem((places + tasks, 8, LANES), f32),
            dma(copies),
            dma(copies),
        ]
        outs = [(shape, f32), ((8, width), f32), ((early_rows, width), f32)]
        scratch = [vmem((samples, LANES), bf16), vmem((3,) + flat, bf16)]
        if last:
            outs += [(share_shape, f32), ((8, LANES), f32)]
            scratch.append(vmem((pairs, 2, 2, 2, 2, 2, share, LANES), bf16))
            for step in (1, 2, 5):
                _, got, mine, kind, count = sum_shapes(step, tasks, share, LANES)
                scratch += [
                    (
                        vmem((pairs,) + got, bf16),
                        vmem((pairs,) + mine, kind),
                        dma(pairs, count),
                        dma(pairs, count),
                    )
                ]
            scratch += small_scratch
            sums = [
                ((7, 3, 4), (2, "attend", "end"), feature_sum, True),
                ((4,), ("attend",), up_sum, True),
                ((4,), ("attend",), down_sum, True),
                ((4,), ("attend",), later_sum[0], True),
                ((4,), ("attend",), later_sum[1], True),
            ]
        else:
            scratch += [vmem(piece_shape, bf16), *small_scratch]
            sums = [
                ((7,), (3,), feature_sum, True),
                ((4,), ("attend",), up_sum, True),
                ((4,), ("attend",), down_sum, True),
                ((1,), ("leave",), None, True),
            ]
        stream_grad, sample_small, *more = fused(
            functools.partial(sample_backward_last, layer, last),
            "sample_backward",
            sizes,
            ins,
            outs,
            scratch,
            sums,
            share_shape,
            6 + layer,
        )
        if last:
            packed, share_sum, late, *first = more
            finished[0] = (share_sum, *first[:3])
            finished[1] = (first[3], first[4], *finished[1][1:])
        else:
            later_packed, *finished[1], sample_sum = more

    whole, parked = pl.BlockSpec(memory_space=pltpu.VMEM), pl.BlockSpec(memory_space=pltpu.HBM)
    scalar = pl.BlockSpec(memory_space=pltpu.SMEM)
    matrix = jax.ShapeDtypeStruct((LAYERS, share, width), f32)
    norm = jax.ShapeDtypeStruct((3, LAYERS, width), f32)
    raw_shape = (samples * features * (width // LANES), LANES)
    raw = jax.ShapeDtypeStruct(raw_shape, f32)
    shares = [finished[layer][member] for member in range(4) for layer in range(LAYERS)]
    results = pl.pallas_call(
        functools.partial(write_out, dense_rows),
        name="write_out",
        out_shape=[
            raw,
            raw,
            matrix,
            matrix,
            matrix,
            matrix,
            norm,
            norm,
            jax.ShapeDtypeStruct((LAYERS, hidden_width), f32),
            jax.ShapeDtypeStruct((LAYERS, width), f32),
            jax.ShapeDtypeStruct((CLASSES, width), f32),
            jax.ShapeDtypeStruct((CLASSES, features, BINS), f32),
            jax.ShapeDtypeStruct((1,), f32),
        ],
        in_specs=[parked] * 2 + [whole] * 12 + [scalar],
        out_specs=[parked] * 2 + [whole] * 10 + [scalar],
        scratch_shapes=[
            vmem(raw_shape, f32),
            vmem(raw_shape, f32),
            vmem(shape, f32),
            vmem(shape, f32),
            dma(2, 4),
            dma(2, 4),
        ],
        compiler_params=pltpu.CompilerParams(vmem_limit_bytes=63 << 20),
    )(stream, stream_grad, *shares, packed, later_packed, late, shapes, loss)
    return (
        from_raw(results[0]),
        results[11].transpose(1, 2, 0)[None],
        from_raw(results[1]),
        results[12],
        results[2][:, None],
        results[3][:, None],
        results[6].transpose(1, 0, 2),
        results[7].transpose(1, 0, 2),
        results[4].transpose(0, 2, 1),
        results[8],
        results[5],
        results[9],
        results[10].T,
    )


def local(
    tokens_in,
    sample_weights,
    feature_weights,
    norm_gain,
    norm_shift,
    up_weight,
    up_bias,
    down_weight,
    down_bias,
    read_weight,
    output_grad,
    task_sizes,
    feature_counts,
    bin_index,
    bin_counts,
    class_labels,
):
    samples = tokens_in.shape[1]
    features = tokens_in.shape[2]
    width = tokens_in.shape[3]
    hidden_width = up_weight.shape[2]
    task_devices = lax.axis_size("task")
    feature_devices = lax.axis_size("feat")
    all_features = features * feature_devices
    own_samples = samples // feature_devices
    size = min(16, own_samples)
    groups = own_samples // size
    group_rows = all_features * size
    rows_total = features * samples

    if (
        own_samples % 32 == 0
        and samples % ROWS == 0
        and ROWS % own_samples == 0
        and group_rows == ROWS
        and own_samples == 4 * SIZE
        and task_devices == hidden_width // width == 4
        and feature_devices == 8
    ):
        return local_fused(
            tokens_in,
            sample_weights,
            feature_weights,
            norm_gain,
            norm_shift,
            up_weight,
            up_bias,
            down_weight,
            down_bias,
            read_weight,
            output_grad,
            task_sizes,
            feature_counts,
            bin_index,
            bin_counts,
            class_labels,
        )

    sample_live = jnp.arange(samples) < task_sizes[0]
    feature_live = jnp.arange(all_features) < feature_counts[0]
    sample_mask = sample_live.astype(f32)
    local_index = lax.axis_index("feat") * features + jnp.arange(features)
    local_live = (local_index < feature_counts[0]).astype(f32)
    sample_qcode, sample_kcode = codes(jnp.zeros((samples,), jnp.int32), sample_live, 1, samples)
    sample_qcode = sample_qcode[:ROWS]
    item = jnp.arange(group_rows) % size
    feature_qcode, feature_kcode = codes(item, jnp.repeat(feature_live, size), size, group_rows)

    def exchange_out(rows):
        parts = rows.reshape(features, feature_devices, own_samples, width)
        got = lax.all_to_all(parts, "feat", split_axis=1, concat_axis=0, tiled=True)
        return got.reshape(all_features, own_samples, width)

    def exchange_back(rows):
        parts = rows.reshape(feature_devices, features, own_samples, width)
        got = lax.all_to_all(parts, "feat", split_axis=0, concat_axis=2, tiled=True)
        return got.reshape(features, samples, width)

    stream = tokens_in[0].astype(f32).transpose(1, 0, 2)
    token_shape = (features, samples, width)
    stored = []
    for layer in range(LAYERS):
        gain, shift = norm_gain[layer], norm_shift[layer]
        x1, h2, qkv, ctx, ext = call(
            sample_forward,
            "sample_forward",
            [
                (token_shape, f32),
                (token_shape, bf16),
                ((3,) + token_shape, bf16),
                (token_shape, bf16),
                ((features, samples, LANES), bf16),
            ],
            [],
            stream,
            gain,
            shift,
            sample_weights[layer],
            sample_qcode,
            sample_kcode,
        )
        swapped = exchange_out(h2)
        a, fqkv, fctx, fext = call(
            functools.partial(feature_forward, size),
            "feature_forward",
            [
                ((all_features, own_samples, width), bf16),
                ((groups, 3, group_rows, width), bf16),
                ((groups, group_rows, width), bf16),
                ((groups, group_rows, LANES), bf16),
            ],
            [],
            swapped,
            feature_weights[layer],
            feature_qcode,
            feature_kcode,
        )
        back = exchange_back(a)
        x3, u = call(
            dense_forward,
            "dense_forward",
            [((rows_total, width), f32), ((rows_total, hidden_width), bf16)],
            [],
            x1.reshape(rows_total, width),
            back.reshape(rows_total, width),
            gain,
            shift,
            up_weight[layer],
            up_bias[layer][None],
            down_weight[layer],
            down_bias[layer][None],
        )
        stored.append((stream, x1, qkv, ctx, ext, swapped, fqkv, fctx, fext, back, u))
        stream = x3.reshape(token_shape)

    reading = stream.astype(bf16)
    projected = jnp.einsum("fsd,dc->fsc", reading, read_weight, preferred_element_type=f32)
    onehot_bins = (bin_index[0].T[..., None] == jnp.arange(BINS)).astype(f32)
    chosen = onehot_bins * sample_mask[None, :, None]
    counted = jnp.maximum(jnp.sum(chosen, axis=1), 1.0)
    bin_sums = jnp.einsum("fsb,fsc->fbc", chosen, projected, precision=highest)
    bin_means = bin_sums / counted[..., None]
    bin_weight = bin_counts[0].astype(f32)
    weight_total = jnp.sum(bin_weight, axis=-1, keepdims=True)
    centre = jnp.sum(bin_weight[..., None] * bin_means, axis=1, keepdims=True) / weight_total[..., None]
    shapes = bin_means - centre
    used_bins = onehot_bins * local_live[:, None, None]
    local_logits = jnp.einsum("fsb,fbc->sc", used_bins, shapes, precision=highest)
    logits = lax.psum(local_logits, "feat")
    row_max = jnp.max(logits, axis=-1, keepdims=True)
    log_total = row_max + jnp.log(jnp.sum(jnp.exp(logits - row_max), axis=-1, keepdims=True))
    label_rows = (class_labels[0][:, None] == jnp.arange(CLASSES)).astype(f32)
    picked = jnp.sum(logits * label_rows, axis=-1)
    live_count = task_sizes[0].astype(f32)
    task_loss = jnp.sum(sample_mask * (log_total[:, 0] - picked)) / live_count
    logit_grad = sample_mask[:, None] * (jnp.exp(logits - log_total) - label_rows) / live_count
    shape_grad = jnp.einsum("fsb,sc->fbc", used_bins, logit_grad, precision=highest)
    means_grad = shape_grad - bin_weight[..., None] / weight_total[..., None] * jnp.sum(
        shape_grad, axis=1, keepdims=True
    )
    sum_grad = means_grad / counted[..., None]
    projected_grad = jnp.einsum("fsb,fbc->fsc", chosen, sum_grad, precision=highest).astype(bf16)
    read_grad = jnp.einsum("fsd,fsc->dc", reading, projected_grad, preferred_element_type=f32)
    stream_grad = output_grad[0].astype(f32).transpose(1, 0, 2) + jnp.einsum(
        "fsc,dc->fsd", projected_grad, read_weight, preferred_element_type=f32
    )

    small = [None] * LAYERS
    big = [None] * LAYERS
    for layer in reversed(range(LAYERS)):
        gain, shift = norm_gain[layer], norm_shift[layer]
        x0, x1, qkv, ctx, ext, swapped, fqkv, fctx, fext, back, u = stored[layer]
        flat = (rows_total, width)
        g2, sent, dup, ddown, dupb, ddownb, dgs2 = call(
            dense_backward,
            "dense_backward",
            [
                (flat, f32),
                (flat, bf16),
                ((hidden_width, width), bf16),
                ((hidden_width, width), bf16),
                ((1, hidden_width), f32),
                ((1, width), f32),
                ((2, width), f32),
            ],
            [
                ((rows_total, hidden_width), bf16),
                ((rows_total, hidden_width), bf16),
                (flat, bf16),
                (flat, bf16),
            ],
            stream_grad.reshape(flat),
            x1.reshape(flat),
            back.reshape(flat),
            u,
            gain,
            shift,
            up_weight[layer],
            down_weight[layer],
        )
        arriving = exchange_out(sent.reshape(token_shape))
        group_shape = (groups, group_rows, width)
        dh, dwf = call(
            functools.partial(feature_backward, size),
            "feature_backward",
            [((all_features, own_samples, width), bf16), ((4, width, width), bf16)],
            [
                ((3,) + group_shape, bf16),
                (group_shape, bf16),
                (group_shape, bf16),
                ((group_rows, width), bf16),
            ],
            arriving,
            swapped,
            feature_weights[layer],
            feature_kcode,
            fqkv,
            fctx,
            fext,
        )
        returned = exchange_back(dh)
        g0, dws, dgs01 = call(
            sample_backward,
            "sample_backward",
            [(token_shape, f32), ((4, width, width), bf16), ((2, 2, width), f32)],
            [
                ((3,) + token_shape, bf16),
                (token_shape, bf16),
                (token_shape, bf16),
                (token_shape, bf16),
                ((features, samples, LANES), bf16),
                ((samples, LANES), f32),
                ((samples, LANES), f32),
            ],
            g2.reshape(token_shape),
            returned,
            x1,
            x0,
            gain,
            shift,
            sample_weights[layer],
            sample_kcode,
            qkv,
            ctx,
            ext,
        )
        stream_grad = g0
        small[layer] = (
            jnp.stack([dgs01[0, 0], dgs01[1, 0], dgs2[0]]),
            jnp.stack([dgs01[0, 1], dgs01[1, 1], dgs2[1]]),
            dupb[0],
            ddownb[0],
        )
        big[layer] = [dws.reshape(4 * width, width), dwf.reshape(4 * width, width), dup, ddown]
    shard_shape = (LAYERS, 4 // task_devices, width // feature_devices, width)
    pieces = [big[layer][member] for member in range(4) for layer in range(LAYERS)]
    rows = [row.reshape(-1, width) for layer in range(LAYERS) for row in small[layer]]
    rows.append(read_grad.T)
    lengths = [row.shape[0] for row in rows]
    fill = -sum(lengths) % 8
    small_rows = jnp.concatenate(rows + [jnp.zeros((fill, width), f32)])
    if (width // feature_devices) % 16 == 0:
        *shares, small_sums = sum_everywhere(pieces, small_rows, task_devices, feature_devices)
    else:
        shares = [
            lax.psum_scatter(piece, ("task", "feat"), scatter_dimension=0, tiled=True).astype(f32)
            for piece in pieces
        ]
        small_sums = lax.psum(small_rows, ("task", "feat"))
    matrices = [jnp.stack(shares[member * LAYERS : member * LAYERS + LAYERS]) for member in range(4)]
    split = []
    at = 0
    for length in lengths:
        split.append(small_sums[at : at + length])
        at += length
    summed = [jnp.stack([split[4 * layer + member] for layer in range(LAYERS)]) for member in range(4)]
    summed[2] = summed[2].reshape(LAYERS, hidden_width)
    summed[3] = summed[3].reshape(LAYERS, width)
    summed.append(split[-1].T)
    return (
        stream.transpose(1, 0, 2)[None],
        shapes[None],
        stream_grad.transpose(1, 0, 2)[None],
        task_loss[None],
        matrices[0].reshape(shard_shape),
        matrices[1].reshape(shard_shape),
        summed[0],
        summed[1],
        matrices[2].transpose(0, 2, 1),
        summed[2],
        matrices[3],
        summed[3],
        summed[4],
    )


def solution(mesh):
    in_specs = (
        P("task", None, "feat", None),
        P(),
        P(),
        P(),
        P(),
        P(),
        P(),
        P(),
        P(),
        P(),
        P("task", None, "feat", None),
        P("task"),
        P("task"),
        P("task", None, "feat"),
        P("task", "feat", None),
        P("task", None),
    )
    out_specs = (
        P("task", None, "feat", None),
        P("task", "feat", None, None),
        P("task", None, "feat", None),
        P("task"),
        P(None, "task", "feat", None),
        P(None, "task", "feat", None),
        P(),
        P(),
        P(None, None, ("task", "feat")),
        P(),
        P(None, ("task", "feat"), None),
        P(),
        P(),
    )
    return jax.shard_map(local, mesh=mesh, in_specs=in_specs, out_specs=out_specs, check_vma=False)
```

```python
import functools

import jax
import jax.numpy as jnp
from jax import lax
from jax.experimental import pallas as pl
from jax.experimental.pallas import tpu as pltpu
from jax.sharding import PartitionSpec as P

HEADS = 8
BINS = 64
CLASSES = 10
LAYERS = 2
LANES = 128
CODE_LANE = 32
ROWS = 256

epsilon = 1e-05
masked_score = -1e30
highest = lax.Precision.HIGHEST
bf16 = jnp.bfloat16
f32 = jnp.float32

NN = (((1,), (0,)), ((), ()))
NT = (((1,), (1,)), ((), ()))
TN = (((0,), (0,)), ((), ()))


def mm(left, right, dims=NN):
    return lax.dot_general(left, right, dims, preferred_element_type=f32)


def lane_row():
    return lax.broadcasted_iota(jnp.int32, (1, LANES), 1)


def half_row(half):
    lanes = lane_row()
    picked = lanes < 64 if half == 0 else lanes >= 64
    return picked.astype(f32).astype(bf16)


def piece_row(pair, half):
    offset = lane_row() - 64 * half - 3 * pair
    return jnp.where((offset >= 0) & (offset < 3), -1.0, 0.0).astype(bf16)


def split_pieces(values, order):
    first = values.astype(bf16).astype(f32)
    rest = values - first
    second = rest.astype(bf16).astype(f32)
    third = rest - second
    return jnp.where(order == 0, first, jnp.where(order == 1, second, third))


def layer_norm(rows, gain, shift):
    centred = rows - jnp.mean(rows, axis=-1, keepdims=True)
    inverse = lax.rsqrt(jnp.mean(centred * centred, axis=-1, keepdims=True) + epsilon)
    normed = centred * inverse
    return normed, inverse, normed * gain + shift


def layer_norm_back(grad_rows, rows, gain):
    centred = rows - jnp.mean(rows, axis=-1, keepdims=True)
    inverse = lax.rsqrt(jnp.mean(centred * centred, axis=-1, keepdims=True) + epsilon)
    normed = centred * inverse
    scaled = grad_rows * gain
    inner = (
        scaled
        - jnp.mean(scaled, axis=-1, keepdims=True)
        - normed * jnp.mean(scaled * normed, axis=-1, keepdims=True)
    )
    gain_part = jnp.sum(grad_rows * normed, axis=0, keepdims=True)
    shift_part = jnp.sum(grad_rows, axis=0, keepdims=True)
    return inverse * inner, gain_part, shift_part


def chunk(index, size):
    return pl.ds(pl.multiple_of(index * size, size), size)


def attend_pair(query, key, value, query_code, key_code, pair, extras):
    query_wide = jnp.concatenate([query, query_code], axis=1)
    total = None
    peaks = []
    for half in range(2):
        mask = half_row(half)
        key_wide = jnp.concatenate([key * mask, key_code], axis=1)
        scores = mm(query_wide, key_wide, NT)
        peak = jnp.max(scores, axis=-1, keepdims=True)
        weights = jnp.exp(scores - peak).astype(bf16)
        ones = jnp.broadcast_to(mask, value.shape)
        part = mm(weights, jnp.concatenate([value * mask, ones], axis=1))
        total = part if total is None else total + part
        peaks.append(peak)
    lanes = lane_row()
    row_total = total[:, LANES:]
    context = total[:, :LANES] / row_total
    log_total = jnp.where(lanes < 64, peaks[0], peaks[1]) + jnp.log(row_total)
    order = lanes % 64 - 3 * pair
    extras = jnp.where((order >= 0) & (order < 3), split_pieces(log_total, order), extras)
    return context.astype(bf16), extras


def attend_pair_back(query, key, value, context_grad, query_extra, grad_extra, key_code, pair):
    query_wide = jnp.concatenate([query, query_extra], axis=1)
    grad_wide = jnp.concatenate([context_grad, grad_extra], axis=1)
    query_grad = key_grad = value_grad = None
    for half in range(2):
        mask = half_row(half)
        pieces = piece_row(pair, half)
        key_half = key * mask
        key_wide = jnp.concatenate([key_half, key_code + pieces], axis=1)
        value_wide = jnp.concatenate(
            [value * mask, jnp.broadcast_to(pieces, value.shape)], axis=1
        )
        attention = jnp.exp(mm(key_wide, query_wide, NT))
        score_grad = (attention * mm(value_wide, grad_wide, NT)).astype(bf16)
        value_part = mm(attention.astype(bf16), context_grad * mask)
        key_part = mm(score_grad, query * mask)
        query_part = mm(score_grad, key_half, TN)
        if half == 0:
            query_grad, key_grad, value_grad = query_part, key_part, value_part
        else:
            query_grad, key_grad, value_grad = (
                query_grad + query_part,
                key_grad + key_part,
                value_grad + value_part,
            )
    return query_grad, key_grad, value_grad


def delta_extra(context, context_grad):
    width = context.shape[1]
    products = context.astype(f32) * context_grad.astype(f32)
    high = products.astype(bf16)
    low = (products - high.astype(f32)).astype(bf16)
    head = lax.broadcasted_iota(jnp.int32, (width, LANES), 0) // (width // HEADS)
    offset = lax.broadcasted_iota(jnp.int32, (width, LANES), 1) - 64 * (head % 2) - 3 * (head // 2)
    spread = jnp.where((offset >= 0) & (offset < 3), 1.0, 0.0).astype(bf16)
    sums = mm(high, spread) + mm(low, spread)
    return split_pieces(sums, lane_row() % 64 % 3).astype(bf16)


def sample_forward(x_ref, gain_ref, shift_ref, w_ref, qcode_ref, kcode_ref, x1_ref, h2_ref, qkv_ref, ctx_ref, ext_ref):
    features, samples, width = x_ref.shape
    steps = samples // ROWS

    def project(unit, carry):
        f, rows = unit // steps, chunk(unit % steps, ROWS)
        _, _, hidden = layer_norm(x_ref[f, rows, :], gain_ref[0:1], shift_ref[0:1])
        hidden = hidden.astype(bf16)
        for member in range(3):
            out = mm(hidden, w_ref[member]).astype(bf16)
            if member == 0:
                out = out * jnp.asarray(0.125, bf16)
            qkv_ref[member, f, rows, :] = out
        return carry

    lax.fori_loop(0, features * steps, project, 0)

    def attend(unit, carry):
        f, rows = unit // steps, chunk(unit % steps, ROWS)
        code = qcode_ref[...]

        def pair_step(pair, extras):
            lanes = chunk(pair, LANES)
            context, extras = attend_pair(
                qkv_ref[0, f, rows, lanes],
                qkv_ref[1, f, :, lanes],
                qkv_ref[2, f, :, lanes],
                code,
                kcode_ref[...],
                pair,
                extras,
            )
            ctx_ref[f, rows, lanes] = context
            return extras

        extras = lax.fori_loop(0, width // LANES, pair_step, code.astype(f32))
        ext_ref[f, rows, :] = extras.astype(bf16)
        x1 = x_ref[f, rows, :] + mm(ctx_ref[f, rows, :], w_ref[3])
        x1_ref[f, rows, :] = x1
        _, _, hidden = layer_norm(x1, gain_ref[1:2], shift_ref[1:2])
        h2_ref[f, rows, :] = hidden.astype(bf16)
        return carry

    lax.fori_loop(0, features * steps, attend, 0)


def load_group(ref, group, size):
    features, _, width = ref.shape
    block = ref[:, chunk(group, size), :]
    if size % 16:
        return block.astype(f32).reshape(features * size, width).astype(bf16)
    return block.reshape(features * size, width)


def store_group(ref, group, size, rows):
    features, _, width = ref.shape
    if size % 16:
        block = rows.astype(f32).reshape(features, size, width).astype(bf16)
    else:
        block = rows.reshape(features, size, width)
    ref[:, chunk(group, size), :] = block


def feature_forward(size, h_ref, w_ref, qcode_ref, kcode_ref, a_ref, qkv_ref, ctx_ref, ext_ref):
    _, samples, width = h_ref.shape

    def step(group, carry):
        hidden = load_group(h_ref, group, size)
        for member in range(3):
            out = mm(hidden, w_ref[member]).astype(bf16)
            if member == 0:
                out = out * jnp.asarray(0.125, bf16)
            qkv_ref[group, member] = out
        code = qcode_ref[...]

        def pair_step(pair, extras):
            lanes = chunk(pair, LANES)
            context, extras = attend_pair(
                qkv_ref[group, 0, :, lanes],
                qkv_ref[group, 1, :, lanes],
                qkv_ref[group, 2, :, lanes],
                code,
                kcode_ref[...],
                pair,
                extras,
            )
            ctx_ref[group, :, lanes] = context
            return extras

        extras = lax.fori_loop(0, width // LANES, pair_step, code.astype(f32))
        ext_ref[group] = extras.astype(bf16)
        store_group(a_ref, group, size, mm(ctx_ref[group], w_ref[3]).astype(bf16))
        return carry

    lax.fori_loop(0, samples // size, step, 0)


def gelu_parts(values):
    cubic = values * values * values
    inside = 0.7978845608028654 * (values + 0.044715 * cubic)
    bent = jnp.tanh(inside)
    return bent


def dense_forward(x_ref, a_ref, gain_ref, shift_ref, up_ref, upb_ref, down_ref, downb_ref, out_ref, u_ref):
    rows_total, width = x_ref.shape
    hidden_width = up_ref.shape[1]

    def step(unit, carry):
        rows = chunk(unit, ROWS)
        x2 = x_ref[rows, :] + a_ref[rows, :].astype(f32)
        _, _, hidden = layer_norm(x2, gain_ref[2:3], shift_ref[2:3])
        hidden = hidden.astype(bf16)
        total = x2 + downb_ref[...]
        for part in range(hidden_width // 512):
            cols = slice(part * 512, part * 512 + 512)
            expanded = mm(hidden, up_ref[:, cols]) + upb_ref[:, cols]
            u_ref[rows, cols] = expanded.astype(bf16)
            active = (0.5 * expanded * (1.0 + gelu_parts(expanded))).astype(bf16)
            total = total + mm(active, down_ref[cols, :])
        out_ref[rows, :] = total
        return carry

    lax.fori_loop(0, rows_total // ROWS, step, 0)


def dense_backward(g_ref, x1_ref, a_ref, u_ref, gain_ref, shift_ref, up_ref, down_ref, out_ref, send_ref, dup_ref, ddown_ref, dupb_ref, ddownb_ref, dgs_ref, active_ref, ugrad_ref, hidden_ref, rowgrad_ref):
    rows_total, width = g_ref.shape
    hidden_width = up_ref.shape[1]
    dupb_ref[...] = jnp.zeros_like(dupb_ref)
    ddownb_ref[...] = jnp.zeros_like(ddownb_ref)
    dgs_ref[...] = jnp.zeros_like(dgs_ref)

    def step(unit, carry):
        rows = chunk(unit, ROWS)
        grad = g_ref[rows, :]
        low = grad.astype(bf16)
        rowgrad_ref[rows, :] = low
        ddownb_ref[...] += jnp.sum(low.astype(f32), axis=0, keepdims=True)
        hidden_grad = None
        for part in range(hidden_width // 512):
            cols = slice(part * 512, part * 512 + 512)
            active_grad = mm(low, down_ref[cols, :], NT).astype(bf16).astype(f32)
            u = u_ref[rows, cols].astype(f32)
            bent = gelu_parts(u)
            slope = 0.5 * (1.0 + bent) + u * (1.0 - bent * bent) * (
                0.3989422804014327 + 0.05351611220146811 * u * u
            )
            active_ref[rows, cols] = (0.5 * u * (1.0 + bent)).astype(bf16)
            ugrad = (active_grad * slope).astype(bf16)
            ugrad_ref[rows, cols] = ugrad
            dupb_ref[:, cols] += jnp.sum(ugrad.astype(f32), axis=0, keepdims=True)
            part_grad = mm(ugrad, up_ref[:, cols], NT)
            hidden_grad = part_grad if hidden_grad is None else hidden_grad + part_grad
        x2 = x1_ref[rows, :] + a_ref[rows, :].astype(f32)
        _, _, hidden = layer_norm(x2, gain_ref[2:3], shift_ref[2:3])
        hidden_ref[rows, :] = hidden.astype(bf16)
        norm_grad, gain_part, shift_part = layer_norm_back(
            hidden_grad.astype(bf16).astype(f32), x2, gain_ref[2:3]
        )
        dgs_ref[0:1] += gain_part
        dgs_ref[1:2] += shift_part
        grad = grad + norm_grad
        out_ref[rows, :] = grad
        send_ref[rows, :] = grad.astype(bf16)
        return carry

    lax.fori_loop(0, rows_total // ROWS, step, 0)

    def weights(part, carry):
        cols = chunk(part, 512)
        dup_ref[cols, :] = mm(ugrad_ref[:, cols], hidden_ref[...], TN).astype(bf16)
        ddown_ref[cols, :] = mm(active_ref[:, cols], rowgrad_ref[...], TN).astype(bf16)
        return carry

    lax.fori_loop(0, hidden_width // 512, weights, 0)


def feature_backward(size, da_ref, h_ref, w_ref, kcode_ref, qkv_ref, ctx_ref, ext_ref, dh_ref, dw_ref, dqkv_ref, hidden_ref, dao_ref, dc_ref):
    _, samples, width = h_ref.shape
    groups = samples // size

    def step(group, carry):
        hidden_ref[group] = load_group(h_ref, group, size)
        dao = load_group(da_ref, group, size)
        dao_ref[group] = dao
        context_grad = mm(dao, w_ref[3], NT).astype(bf16)
        dc_ref[...] = context_grad
        grad_extra = delta_extra(ctx_ref[group], context_grad)

        def pair_step(pair, inner):
            lanes = chunk(pair, LANES)
            query_grad, key_grad, value_grad = attend_pair_back(
                qkv_ref[group, 0, :, lanes],
                qkv_ref[group, 1, :, lanes],
                qkv_ref[group, 2, :, lanes],
                dc_ref[:, lanes],
                ext_ref[group],
                grad_extra,
                kcode_ref[...],
                pair,
            )
            dqkv_ref[0, group, :, lanes] = (query_grad * 0.125).astype(bf16)
            dqkv_ref[1, group, :, lanes] = key_grad.astype(bf16)
            dqkv_ref[2, group, :, lanes] = value_grad.astype(bf16)
            return inner

        lax.fori_loop(0, width // LANES, pair_step, 0)
        total = mm(dqkv_ref[0, group], w_ref[0], NT)
        total = total + mm(dqkv_ref[1, group], w_ref[1], NT)
        total = total + mm(dqkv_ref[2, group], w_ref[2], NT)
        store_group(dh_ref, group, size, total.astype(bf16))
        return carry

    lax.fori_loop(0, groups, step, 0)

    def weights(member, carry):
        total = None
        for group in range(groups):
            part = mm(hidden_ref[group], dqkv_ref[member, group], TN)
            total = part if total is None else total + part
        dw_ref[member] = total.astype(bf16)
        return carry

    lax.fori_loop(0, 3, weights, 0)
    total = None
    for group in range(groups):
        part = mm(ctx_ref[group], dao_ref[group], TN)
        total = part if total is None else total + part
    dw_ref[3] = total.astype(bf16)


def sample_backward(g_ref, dh_ref, x1_ref, x_ref, gain_ref, shift_ref, w_ref, kcode_ref, qkv_ref, ctx_ref, ext_ref, out_ref, dw_ref, dgs_ref, dqkv_ref, hidden_ref, low_ref, dc_ref, gext_ref, kacc_ref, vacc_ref):
    features, samples, width = x_ref.shape
    steps = samples // ROWS
    dgs_ref[...] = jnp.zeros_like(dgs_ref)

    def enter(unit, carry):
        f, rows = unit // steps, chunk(unit % steps, ROWS)
        norm_grad, gain_part, shift_part = layer_norm_back(
            dh_ref[f, rows, :].astype(f32), x1_ref[f, rows, :], gain_ref[1:2]
        )
        dgs_ref[1, 0:1] += gain_part
        dgs_ref[1, 1:2] += shift_part
        grad = g_ref[f, rows, :] + norm_grad
        out_ref[f, rows, :] = grad
        low = grad.astype(bf16)
        low_ref[f, rows, :] = low
        context_grad = mm(low, w_ref[3], NT).astype(bf16)
        dc_ref[f, rows, :] = context_grad
        gext_ref[f, rows, :] = delta_extra(ctx_ref[f, rows, :], context_grad)
        return carry

    lax.fori_loop(0, features * steps, enter, 0)

    def attend(unit, carry):
        f, pair = unit // (width // LANES), unit % (width // LANES)
        lanes = chunk(pair, LANES)

        def query_step(step, inner):
            rows = chunk(step, ROWS)
            query_grad, key_grad, value_grad = attend_pair_back(
                qkv_ref[0, f, rows, lanes],
                qkv_ref[1, f, :, lanes],
                qkv_ref[2, f, :, lanes],
                dc_ref[f, rows, lanes],
                ext_ref[f, rows, :],
                gext_ref[f, rows, :],
                kcode_ref[...],
                pair,
            )
            dqkv_ref[0, f, rows, lanes] = (query_grad * 0.125).astype(bf16)
            first = step == 0
            kacc_ref[...] = jnp.where(first, 0.0, kacc_ref[...]) + key_grad
            vacc_ref[...] = jnp.where(first, 0.0, vacc_ref[...]) + value_grad
            return inner

        lax.fori_loop(0, steps, query_step, 0)
        dqkv_ref[1, f, :, lanes] = kacc_ref[...].astype(bf16)
        dqkv_ref[2, f, :, lanes] = vacc_ref[...].astype(bf16)
        return carry

    kacc_ref[...] = jnp.zeros_like(kacc_ref)
    vacc_ref[...] = jnp.zeros_like(vacc_ref)
    lax.fori_loop(0, features * (width // LANES), attend, 0)

    def leave(unit, carry):
        f, rows = unit // steps, chunk(unit % steps, ROWS)
        total = mm(dqkv_ref[0, f, rows, :], w_ref[0], NT)
        total = total + mm(dqkv_ref[1, f, rows, :], w_ref[1], NT)
        total = total + mm(dqkv_ref[2, f, rows, :], w_ref[2], NT)
        x = x_ref[f, rows, :]
        _, _, hidden = layer_norm(x, gain_ref[0:1], shift_ref[0:1])
        hidden_ref[f, rows, :] = hidden.astype(bf16)
        norm_grad, gain_part, shift_part = layer_norm_back(
            total.astype(bf16).astype(f32), x, gain_ref[0:1]
        )
        dgs_ref[0, 0:1] += gain_part
        dgs_ref[0, 1:2] += shift_part
        out_ref[f, rows, :] += norm_grad
        return carry

    lax.fori_loop(0, features * steps, leave, 0)

    def weights(member, carry):
        total = None
        for f in range(features):
            part = mm(hidden_ref[f], dqkv_ref[member, f], TN)
            total = part if total is None else total + part
        dw_ref[member] = total.astype(bf16)
        return carry

    lax.fori_loop(0, 3, weights, 0)
    total = None
    for f in range(features):
        part = mm(ctx_ref[f], low_ref[f], TN)
        total = part if total is None else total + part
    dw_ref[3] = total.astype(bf16)


def call(body, name, outs, scratch, *operands):
    spec = pl.BlockSpec(memory_space=pltpu.VMEM)
    return pl.pallas_call(
        body,
        name=name,
        out_shape=[jax.ShapeDtypeStruct(shape, kind) for shape, kind in outs],
        in_specs=[spec] * len(operands),
        out_specs=[spec] * len(outs),
        scratch_shapes=[pltpu.VMEM(shape, kind) for shape, kind in scratch],
        compiler_params=pltpu.CompilerParams(vmem_limit_bytes=56 << 20),
    )(*operands)


MESH = pl.DeviceIdType.MESH


def remote(source, target, send_sem, recv_sem, device):
    return pltpu.make_async_remote_copy(
        src_ref=source,
        dst_ref=target,
        send_sem=send_sem,
        recv_sem=recv_sem,
        device_id=device,
        device_id_type=MESH,
    )


def sum_partners(task_devices, feature_devices):
    task, place = lax.axis_index("task"), lax.axis_index("feat")
    chip, core = place // 2, lax.rem(place, 2)
    chips = feature_devices // 2
    pair = [{"feat": place + 1 - 2 * core}]
    tasks = [{"task": lax.rem(task + step, task_devices)} for step in range(1, task_devices)]
    line = [{"feat": 2 * lax.rem(chip + step, chips) + core} for step in range(1, chips)]
    return task, chip, core, pair, tasks, line


def greet(devices):
    barrier = pltpu.get_barrier_semaphore()
    for device in devices:
        pl.semaphore_signal(barrier, inc=1, device_id=device, device_id_type=MESH)


def met(count):
    pl.semaphore_wait(pltpu.get_barrier_semaphore(), count)


def sum_tail(pieces, task_devices, feature_devices, *refs):
    chips = feature_devices // 2
    inputs, small_ref = refs[:pieces], refs[pieces]
    outs, small_out = refs[pieces + 1 : 2 * pieces + 1], refs[2 * pieces + 1]
    own, first, summed, second, third_in, third, sends, recvs, loads, small_got, small_sends, small_recvs = refs[2 * pieces + 2 :]
    task, chip, core, pair, tasks, line = sum_partners(task_devices, feature_devices)
    greet(pair + tasks + line)
    own_loads = [
        pltpu.make_async_copy(inputs[p].at[:, :, core], own.at[p], loads.at[p]) for p in range(pieces)
    ]
    for load in own_loads:
        load.start()
    met(len(pair) + len(tasks) + len(line))

    started = []
    for p in range(pieces):
        copy = remote(inputs[p].at[:, :, 1 - core], first.at[p], sends.at[p, 0], recvs.at[p, 0], pair[0])
        copy.start()
        started.append([copy])
    small_slot = [0]

    def small_exchange(values, devices, index, base):
        copies = []
        for k, device in enumerate(devices):
            copy = remote(values, small_got.at[base + index], small_sends.at[base + k], small_recvs.at[base + k], device)
            copy.start()
            copies.append(copy)
        return copies

    def small_finish(copies, count, base):
        for copy in copies:
            copy.wait()
        total = small_got[base]
        for k in range(1, count):
            total = total + small_got[base + k]
        return total

    small_got[core] = small_ref[...]
    small_copies = small_exchange(small_got.at[core], pair, core, 0)
    for p in range(pieces):
        own_loads[p].wait()
        for copy in started[p]:
            copy.wait()

        def add_core(index, carry, p=p):
            t, z = index // chips, lax.rem(index, chips)
            summed[p, t, z] = (own[p, t, z].astype(f32) + first[p, t, z].astype(f32)).astype(bf16)
            return carry

        lax.fori_loop(0, task_devices * chips, add_core, 0)
        started[p] = []
        for k, device in enumerate(tasks):
            other = lax.rem(task + k + 1, task_devices)
            copy = remote(summed.at[p, other], second.at[p, k], sends.at[p, 1 + k], recvs.at[p, 1 + k], device)
            copy.start()
            started[p].append(copy)
    total = small_finish(small_copies, 2, 0)
    small_got[2 + task] = total
    small_copies = small_exchange(small_got.at[2 + task], tasks, task, 2)
    for p in range(pieces):
        for copy in started[p]:
            copy.wait()

        def add_tasks(z, carry, p=p):
            total = summed[p, task, z].astype(f32)
            for k in range(task_devices - 1):
                total = total + second[p, k, z].astype(f32)
            third_in[p, z] = total.astype(bf16)
            return carry

        lax.fori_loop(0, chips, add_tasks, 0)
        started[p] = []
        for k, device in enumerate(line):
            other = lax.rem(chip + k + 1, chips)
            slot = task_devices + k
            copy = remote(third_in.at[p, other], third.at[p, k], sends.at[p, slot], recvs.at[p, slot], device)
            copy.start()
            started[p].append(copy)
    total = small_finish(small_copies, task_devices, 2)
    base = 2 + task_devices
    small_got[base + chip] = total
    small_copies = small_exchange(small_got.at[base + chip], line, chip, base)
    for p in range(pieces):
        for copy in started[p]:
            copy.wait()
        total = third_in[p, chip].astype(f32)
        for k in range(chips - 1):
            total = total + third[p, k].astype(f32)
        outs[p][...] = total
    small_out[...] = small_finish(small_copies, chips, base)


def sum_everywhere(pieces, small, task_devices, feature_devices):
    chips = feature_devices // 2
    rows, width = pieces[0].shape
    share = rows // (task_devices * feature_devices)
    blocks = [piece.reshape(task_devices, chips, 2, share, width) for piece in pieces]
    count = len(pieces)
    copies = task_devices + chips - 1
    small_copies = 2 + task_devices + chips
    vmem, anywhere = pl.BlockSpec(memory_space=pltpu.VMEM), pl.BlockSpec(memory_space=pl.ANY)
    return pl.pallas_call(
        functools.partial(sum_tail, count, task_devices, feature_devices),
        name="sum_tail",
        out_shape=[jax.ShapeDtypeStruct((share, width), f32)] * count
        + [jax.ShapeDtypeStruct(small.shape, f32)],
        in_specs=[anywhere] * count + [vmem],
        out_specs=[vmem] * (count + 1),
        scratch_shapes=[
            pltpu.VMEM((count, task_devices, chips, share, width), bf16),
            pltpu.VMEM((count, task_devices, chips, share, width), bf16),
            pltpu.VMEM((count, task_devices, chips, share, width), bf16),
            pltpu.VMEM((count, task_devices - 1, chips, share, width), bf16),
            pltpu.VMEM((count, chips, share, width), bf16),
            pltpu.VMEM((count, chips - 1, share, width), bf16),
            pltpu.SemaphoreType.DMA((count, copies)),
            pltpu.SemaphoreType.DMA((count, copies)),
            pltpu.SemaphoreType.DMA((count,)),
            pltpu.VMEM((small_copies,) + small.shape, f32),
            pltpu.SemaphoreType.DMA((small_copies,)),
            pltpu.SemaphoreType.DMA((small_copies,)),
        ],
        compiler_params=pltpu.CompilerParams(
            vmem_limit_bytes=56 << 20, collective_id=0, has_side_effects=True
        ),
    )(*blocks, small)


SIZE = 16


class Place:
    def __init__(self, task_devices, feature_devices):
        self.tasks, self.places = task_devices, feature_devices
        self.chips = feature_devices // 2
        self.task, self.place = lax.axis_index("task"), lax.axis_index("feat")
        self.chip, self.core = self.place // 2, lax.rem(self.place, 2)
        self.far, self.near = self.chip // 2, lax.rem(self.chip, 2)
        self.y, self.x = self.task // 2, lax.rem(self.task, 2)
        self.x_task = {"task": self.task + 1 - 2 * self.x}
        self.y_task = {"task": self.task + 2 - 4 * self.y}
        self.other_core = {"feat": self.place + 1 - 2 * self.core}
        self.near_chip = {"feat": self.place + 2 - 4 * self.near}
        self.far_chip = {"feat": self.place + 4 - 8 * self.far}

    def ring(self, step):
        return lax.rem(self.place + step, self.places)

    def task_partner(self, step):
        return lax.rem(self.task + step, self.tasks)

    def greet(self):
        barrier = pltpu.get_barrier_semaphore()
        for step in range(1, self.places):
            pl.semaphore_signal(barrier, inc=1, device_id={"feat": self.ring(step)}, device_id_type=MESH)
        for step in range(1, self.tasks):
            pl.semaphore_signal(barrier, inc=1, device_id={"task": self.task_partner(step)}, device_id_type=MESH)

    def met(self):
        pl.semaphore_wait(pltpu.get_barrier_semaphore(), self.places - 1 + self.tasks - 1)


class SumStep:
    def __init__(self, step, place, source, own, got, sends, recvs, load):
        self.step = step
        y, x, far, near, core = place.y, place.x, place.far, place.near, place.core
        if step == 1:
            self.mine = [source.at[:, :, :, :, core]]
            parts = [(source.at[:, :, :, :, 1 - core], got, place.other_core)]
        elif step == 2:
            self.mine = [source.at[y, x]]
            parts = []
            for k in range(1, place.tasks):
                other = place.task_partner(k)
                parts.append((source.at[other // 2, lax.rem(other, 2)], got.at[k - 1], {"task": other}))
        elif step == 6:
            self.mine = [source.at[:, x, 0], source.at[y, :, 1]]
            parts = [
                (source.at[:, 1 - x, 0], got.at[0], place.x_task),
                (source.at[1 - y, :, 1], got.at[1], place.y_task),
            ]
        elif step == 7:
            self.mine = [source.at[0, y], source.at[1, x]]
            parts = [
                (source.at[0, 1 - y], got.at[0], place.y_task),
                (source.at[1, 1 - x], got.at[1], place.x_task),
            ]
        elif step == 3:
            self.mine = [source.at[:, near]]
            parts = [(source.at[:, 1 - near], got, place.near_chip)]
        elif step == 4:
            self.mine = [source.at[far]]
            parts = [(source.at[1 - far], got, place.far_chip)]
        else:
            self.mine = [source.at[far, near]]
            parts = []
            for k in range(1, place.chips):
                other = lax.rem(place.chip + k, place.chips)
                parts.append(
                    (source.at[other // 2, lax.rem(other, 2)], got.at[k - 1], {"feat": 2 * other + core})
                )
        self.copies = [
            remote(part, target, sends.at[k], recvs.at[k], device) for k, (part, target, device) in enumerate(parts)
        ]
        self.loads = []
        if own is not None:
            kept = [own] if len(self.mine) == 1 else [own.at[half] for half in range(2)]
            self.loads = [
                pltpu.make_async_copy(part, target, load.at[half])
                for half, (part, target) in enumerate(zip(self.mine, kept))
            ]
            self.mine = kept
        self.got = got

    def start(self):
        for copy in self.copies:
            copy.start()
        for load in self.loads:
            load.start()

    def finish(self, out):
        for load in self.loads:
            load.wait()
        for copy in self.copies:
            copy.wait()
        own, got = self.mine[0], self.got
        if self.step == 1:

            def add_core(index, carry):
                y, x, far = index // 4, lax.rem(index // 2, 2), lax.rem(index, 2)
                out[y, x, far] = own[y, x, far] + got[y, x, far]
                return carry

            lax.fori_loop(0, 8, add_core, 0)
        elif self.step in (2, 5):
            total = own[...].astype(f32)
            for k in range(got.shape[0]):
                total = total + got[k].astype(f32)
            out[...] = total.astype(out.dtype)
        elif self.step in (6, 7):
            for half in range(2):
                out[half] = self.mine[half][...] + got[half]
        elif self.step == 3:
            out[...] = own[...] + got[...]
        else:
            out[...] = own[...].astype(f32) + got[...].astype(f32)


def sum_shapes(step, tasks, share, width):
    block = (share, width)
    if step == 1:
        whole = (2, 2, 2, 2) + block
        return whole, whole, whole, bf16, 1
    if step == 2:
        return (2, 2) + block, (tasks - 1, 2, 2) + block, (2, 2) + block, bf16, tasks - 1
    if step == 6:
        return None, (2, 2, 2) + block, (2, 2, 2) + block, bf16, 2
    if step == 7:
        return (2, 2) + block, (2, 2) + block, (2, 2) + block, bf16, 2
    if step == 3:
        return (2,) + block, (2,) + block, (2,) + block, bf16, 1
    if step == 4:
        return block, block, block, f32, 1
    return block, (3,) + block, block, f32, 3


class Chain:
    def __init__(self, place, steps, points, bufs, source, out):
        self.place, self.steps, self.points, self.bufs, self.out = place, steps, points, bufs, out
        self.at, self.running = 0, False
        self.first = None
        if len(points) > len(steps):
            self.first, self.points = points[0], points[1:]
        self.actions = [None if source is None else self.make(0, source)]
        self.actions += [self.make(at, bufs[at - 1][2]) for at in range(1, len(steps))]

    def make(self, at, source):
        own, got, _, sends, recvs, local_sem = self.bufs[at]
        return SumStep(self.steps[at], self.place, source, own, got, sends, recvs, local_sem)

    def begin(self, source=None):
        if source is not None:
            self.actions[0] = self.make(0, source)
        self.actions[0].start()
        self.running = True

    def reached(self, point):
        if self.first is not None and point == self.first:
            self.begin()
            return
        if not self.running or self.points[self.at] != point:
            return
        self.actions[self.at].finish(self.bufs[self.at][2])
        self.at += 1
        if self.at < len(self.steps):
            self.actions[self.at].start()
            return
        self.running = False
        if self.out is not None:
            self.flush().start()

    def flush(self):
        return pltpu.make_async_copy(self.bufs[-1][2], self.out, self.bufs[-1][5].at[2])


class Box:
    def __init__(self, place, bufs, loads, outs, out_bufs, flush_sem, chains):
        self.place, self.bufs, self.loads = place, bufs, loads
        self.outs, self.out_bufs, self.flush_sem = outs, out_bufs, flush_sem
        self.chains = chains
        self.waited, self.flushed = set(), []

    def start(self, *indices):
        for index in indices:
            if isinstance(index, tuple):
                for part in index[1:]:
                    self.loads[index[0]].one(part).start()
                continue
            for copy in self.loads[index]:
                copy.start()

    def use(self, *indices):
        found = []
        for index in indices:
            if index not in self.waited:
                self.waited.add(index)
                for copy in self.loads[index]:
                    copy.wait()
            found.append(self.bufs[index])
        return found if len(found) > 1 else found[0]

    def part(self, index, part):
        self.waited.add(index)
        self.loads[index].one(part).wait()

    def out(self, *indices):
        found = [self.out_bufs[index] for index in indices]
        return found if len(found) > 1 else found[0]

    def copy_out(self, index, part, view):
        source, target = self.out_bufs[index], self.outs[index]
        if view is not None:
            source, target = view(source, part), view(target, part)
        return pltpu.make_async_copy(source, target, self.flush_sem.at[index, part])

    def flush(self, *indices):
        for index in indices:
            self.copy_out(index, 0, None).start()
            self.flushed.append((index, 0, None))

    def flush_part(self, index, part, view):
        self.copy_out(index, part, view).start()
        if (index, 0, view) not in self.flushed:
            self.flushed += [(index, at, view) for at in range(4)]

    def settle(self, *indices):
        left = []
        for index, part, view in self.flushed:
            if index in indices:
                self.copy_out(index, part, view).wait()
            else:
                left.append((index, part, view))
        self.flushed = left

    def ready(self):
        self.place.met()
        for chain in self.chains:
            if chain.actions[0] is not None and chain.first is None:
                chain.begin()

    def point(self, name):
        for chain in self.chains:
            chain.reached(name)

    def end(self):
        for index, part, view in self.flushed:
            self.copy_out(index, part, view).wait()
        for chain in self.chains:
            if chain.out is not None:
                chain.flush().wait()


class Parts:
    def __init__(self, source, target, view, count, sem):
        self.source, self.target, self.view, self.count, self.sem = source, target, view, count, sem

    def one(self, part):
        if self.view is None:
            return pltpu.make_async_copy(self.source, self.target, self.sem.at[0])
        return pltpu.make_async_copy(self.view(self.source, part), self.view(self.target, part), self.sem.at[part])

    def __iter__(self):
        return iter([self.one(part) for part in range(self.count)])


def fused(body, name, place_sizes, ins, outs, scratch, sums, share_shape, identity):
    tasks, places = place_sizes
    anywhere = pl.BlockSpec(memory_space=pltpu.HBM)
    scalar = pl.BlockSpec(memory_space=pltpu.SMEM)
    buffers = []
    ins = [tuple(item) + (None, 1) if len(item) == 2 else item for item in ins]
    for array, layer, _, _ in ins:
        if layer not in ("scalar", "raw"):
            depth = 0 if layer is None else len(layer) if isinstance(layer, tuple) else 1
            buffers.append(pltpu.VMEM(array.shape[depth:], array.dtype))
    outs = [tuple(item) + (None,) if len(item) == 2 else item for item in outs]
    out_buffers = [pltpu.VMEM(shape, kind) for shape, kind, shared in outs if shared is None]
    sum_results, sum_scratch, sum_arrays = [], [], []
    chain_layout = []
    for steps, _, array, goes_out in sums:
        share, width = share_shape if array is None else array.shape[-2:]
        for at, step in enumerate(steps):
            own, got, result, kind, copies = sum_shapes(step, tasks, share, width)
            loaded = at == 0 and array is not None
            chain_layout.append(loaded)
            sum_scratch += [pltpu.VMEM(own, bf16)] if loaded else []
            sum_scratch += [
                pltpu.VMEM(got, bf16),
                pltpu.VMEM(result, kind),
                pltpu.SemaphoreType.DMA((copies,)),
                pltpu.SemaphoreType.DMA((copies,)),
                pltpu.SemaphoreType.DMA((3,)),
            ]
        if goes_out:
            sum_results.append(jax.ShapeDtypeStruct(result, kind))
        if array is not None:
            sum_arrays.append(array)
    flat_scratch = []
    for item in scratch:
        flat_scratch += list(item) if isinstance(item, tuple) else [item]
    everything = buffers + out_buffers + flat_scratch + sum_scratch
    def kernel(*refs):
        rest = list(refs)

        def pop(count):
            taken = rest[:count]
            del rest[:count]
            return taken

        in_refs, sum_refs = pop(len(ins)), pop(len(sum_arrays))
        out_refs, sum_outs = pop(len(outs)), pop(len(sum_results))
        flat_in = pop(len(buffers))
        fresh, out_bufs = pop(len(out_buffers)), []
        for _, _, shared in outs:
            out_bufs.append(fresh.pop(0) if shared is None else out_bufs[shared])
        user = [tuple(pop(len(item))) if isinstance(item, tuple) else pop(1)[0] for item in scratch]
        layout = list(chain_layout)
        chain_bufs = [
            [pop(6) if layout.pop(0) else [None] + pop(5) for _ in steps] for steps, _, _, _ in sums
        ]
        load_sem, flush_sem = pop(2)
        place = Place(tasks, places)
        loads, bufs = [], []
        for index, (array, layer, view, count) in enumerate(ins):
            if layer in ("scalar", "raw"):
                loads.append([])
                bufs.append(in_refs[index])
                continue
            bufs.append(flat_in.pop(0))
            source = in_refs[index]
            if layer is not None:
                source = source.at[layer]
            loads.append(Parts(source, bufs[-1], view, count, load_sem.at[index]))
        place.greet()
        chains = []
        for (steps, points, array, goes_out), chain_buf in zip(sums, chain_bufs):
            source = None if array is None else sum_refs.pop(0)
            chains.append(Chain(place, steps, points, chain_buf, source, sum_outs.pop(0) if goes_out else None))
        box = Box(place, bufs, loads, out_refs, out_bufs, flush_sem, chains)
        body(box, *user)
        box.end()

    return pl.pallas_call(
        kernel,
        name=name,
        out_shape=[jax.ShapeDtypeStruct(shape, kind) for shape, kind, _ in outs] + sum_results,
        in_specs=[scalar if layer == "scalar" else anywhere for _, layer, _, _ in ins] + [anywhere] * len(sum_arrays),
        out_specs=[anywhere] * (len(outs) + len(sum_results)),
        scratch_shapes=everything
        + [pltpu.SemaphoreType.DMA((len(ins), 8)), pltpu.SemaphoreType.DMA((len(outs), 4))],
        compiler_params=pltpu.CompilerParams(
            vmem_limit_bytes=63 << 20, collective_id=identity, has_side_effects=True
        ),
    )(*[item[0] for item in ins], *sum_arrays)


def cross(ref, unit):
    block = ref[:, :, chunk(unit, SIZE), :]
    return block.reshape(block.shape[0] * block.shape[1] * SIZE, block.shape[3])


def put_cross(ref, unit, rows):
    first, second, _, width = ref.shape
    ref[:, :, chunk(unit, SIZE), :] = rows.reshape(first, second, SIZE, width)


def cross_view(ref, unit):
    return ref.at[:, :, chunk(unit, SIZE), :]


def first_view(ref, unit):
    return ref.at[unit]


def last_view(ref, unit):
    return ref.at[(slice(None),) * (len(ref.shape) - 1) + (chunk(unit, LANES),)]


def own_rows(ref, f, unit, size, lanes=slice(None)):
    block = ref[f, :, chunk(unit, size), lanes]
    return block.reshape(block.shape[0] * size, block.shape[2])


def block_rows(ref, f, unit, per, lanes=slice(None)):
    block = ref[f, chunk(unit, per), :, lanes]
    return block.reshape(per * block.shape[1], block.shape[2])


def all_rows(ref, f, lanes=slice(None)):
    block = ref[f, :, :, lanes]
    return block.reshape(block.shape[0] * block.shape[1], block.shape[2])


def pair_lanes(pair):
    return slice(pair * LANES, pair * LANES + LANES)


def fill_sample_codes(size, query_ref, key_ref):
    if query_ref is not None:
        lanes = lax.broadcasted_iota(jnp.int32, query_ref.shape, 1)
        query_ref[...] = jnp.where(lanes == CODE_LANE, 1.0, 0.0).astype(bf16)
    lanes = lax.broadcasted_iota(jnp.int32, key_ref.shape, 1)
    rows = lax.broadcasted_iota(jnp.int32, key_ref.shape, 0)
    key_ref[...] = jnp.where((lanes == CODE_LANE) & (rows >= size), masked_score, 0.0).astype(bf16)


def fill_feature_codes(count, query_ref, key_ref):
    lanes = lax.broadcasted_iota(jnp.int32, key_ref.shape, 1) - CODE_LANE
    rows = lax.broadcasted_iota(jnp.int32, key_ref.shape, 0)
    own = lanes == (rows & (SIZE - 1))
    inside = (lanes >= 0) & (lanes < SIZE)
    if query_ref is not None:
        query_ref[...] = jnp.where(own, 1.0, 0.0).astype(bf16)
    live = rows < count * SIZE
    key_ref[...] = jnp.where(inside & ~(own & live), masked_score, 0.0).astype(bf16)


def from_rows(raw_ref, out_ref):
    features, blocks, own, width = out_ref.shape
    pairs = width // LANES
    for f in range(features):
        for block in range(pairs):
            rows = raw_ref[pl.ds(block * features + f, blocks * own, stride=features * pairs), :]
            out_ref[f, :, :, pair_lanes(block)] = rows.reshape(blocks, own, LANES).astype(out_ref.dtype)


LAYER_OUTS = 14


def forward_layers(layers, box, sq_ref, sk_ref, fq_ref, fk_ref, raw_ref, *scratch):
    box.start(2, 3, 4, 7)
    size_ref, count_ref = box.use(0, 1)
    fill_sample_codes(size_ref[0], sq_ref, sk_ref)
    fill_feature_codes(count_ref[0], fq_ref, fk_ref)
    x_ref = box.out(LAYER_OUTS * layers)
    raw_ref[...] = box.use(2)[...].astype(f32)
    from_rows(raw_ref, x_ref)
    box.flush(LAYER_OUTS * layers)
    before = None
    for layer in range(layers):
        before = forward_layer(layer, layer == layers - 1, before, box, x_ref, sq_ref, sk_ref, fq_ref, fk_ref, raw_ref, *scratch)
        x_ref = box.out(LAYER_OUTS * layer + 9)


def forward_layer(layer, last, before, box, x_ref, sq_ref, sk_ref, fq_ref, fk_ref, raw_ref, h2_ref, swapped_ref, a_ref, back_ref, all_sends, all_recvs, all_self, all_back_sends, all_back_recvs):
    place = box.place
    first = LAYER_OUTS * layer
    outs = [first + index for index in range(LAYER_OUTS)]
    earlier = [index - LAYER_OUTS for index in outs]
    x1_ref, qkv_ref, ctx_ref, ext_ref, hidden_ref, fqkv_ref, fctx_ref, fext_ref, x2_ref, x3_ref, u_ref, h1_ref, active_ref, h3_ref = box.out(*outs)
    sends, recvs, self_sem = all_sends.at[layer], all_recvs.at[layer], all_self.at[layer]
    back_sends, back_recvs = all_back_sends.at[layer], all_back_recvs.at[layer]
    weights = 7 + 4 * layer
    gain_ref, shift_ref, w_ref = box.use(3, 4, weights)
    if layer > 0:
        box.settle(*[earlier[index] for index in (0, 1, 2, 3, 11)])
    features, blocks, own, width = x_ref.shape
    per = ROWS // own
    steps = blocks // per
    size = ROWS // blocks
    units = own // size
    pairs = width // LANES

    def gain(index):
        return gain_ref[index, layer : layer + 1, :], shift_ref[index, layer : layer + 1, :]

    parts = own // size

    def project(f):
        def rows(part, carry):
            _, _, hidden = layer_norm(block_rows(x_ref, f, part, per), *gain(0))
            hidden = hidden.astype(bf16)
            h1_ref[f, chunk(part, per), :, :] = hidden.reshape(per, own, width)
            for member in range(3):
                out = mm(hidden, w_ref[member]).astype(bf16)
                if member == 0:
                    out = out * jnp.asarray(0.125, bf16)
                qkv_ref[member, f, chunk(part, per), :, :] = out.reshape(per, own, width)
            return carry

        lax.fori_loop(0, steps, rows, 0)

    def copies(unit):
        f, part = unit // parts, lax.rem(unit, parts)
        found = [
            remote(
                h2_ref.at[f, place.ring(k), chunk(part, size), :],
                swapped_ref.at[place.place, f, chunk(part, size), :],
                sends.at[unit, k - 1],
                recvs.at[unit, k - 1],
                {"feat": place.ring(k)},
            )
            for k in range(1, place.places)
        ]
        keep = pltpu.make_async_copy(
            h2_ref.at[f, place.place, chunk(part, size), :],
            swapped_ref.at[place.place, f, chunk(part, size), :],
            self_sem.at[unit],
        )
        return found, keep

    def attend(unit, carry):
        f, part = unit // parts, lax.rem(unit, parts)

        @pl.when(part == 0)
        def _():
            if before is not None:
                before(f)
            project(f)

        code = sq_ref[...]
        extras = code.astype(f32)
        for pair in range(pairs):
            lanes = pair_lanes(pair)
            context, extras = attend_pair(
                own_rows(qkv_ref.at[0], f, part, size, lanes),
                all_rows(qkv_ref.at[1], f, lanes),
                all_rows(qkv_ref.at[2], f, lanes),
                code,
                sk_ref[...],
                pair,
                extras,
            )
            ctx_ref[f, :, chunk(part, size), lanes] = context.reshape(blocks, size, LANES)
        ext_ref[f, :, chunk(part, size), :] = extras.astype(bf16).reshape(blocks, size, LANES)
        x1 = own_rows(x_ref, f, part, size) + mm(own_rows(ctx_ref, f, part, size), w_ref[3])
        x1_ref[f, :, chunk(part, size), :] = x1.reshape(blocks, size, width)
        _, _, hidden = layer_norm(x1, *gain(1))
        h2_ref[f, :, chunk(part, size), :] = hidden.astype(bf16).reshape(blocks, size, width)

        @pl.when(unit == 0)
        def _():
            if layer == 0:
                box.ready()
                box.start(weights + 1, weights + 2, 5, weights + 3, 6)
            if not last:
                box.start(weights + 4, weights + 5, weights + 6, weights + 7)
            else:
                box.start(7 + 4 * (layer + 1))

        found, keep = copies(unit)
        for copy in found:
            copy.start()
        keep.start()
        return carry

    lax.fori_loop(0, features * units, attend, 0)
    box.flush(*[outs[index] for index in (0, 1, 2, 3, 11)])
    if before is not None:
        box.flush(*[earlier[index] for index in (8, 9, 10, 12, 13)])
        before(None)
    fw_ref = box.use(weights + 1)
    if layer > 0:
        box.settle(*earlier[4:8])
    groups = own // SIZE
    shared = size // SIZE

    def back_copies(group, f=None):
        which = slice(None) if f is None else f
        at = 0 if f is None else f
        return [
            remote(
                a_ref.at[place.ring(k), which, chunk(group, SIZE), :],
                back_ref.at[which, place.place, chunk(group, SIZE), :],
                back_sends.at[at, group, k - 1],
                back_recvs.at[at, group, k - 1],
                {"feat": place.ring(k)},
            )
            for k in range(1, place.places)
        ]

    def feature(group, carry):
        @pl.when(lax.rem(group, shared) == 0)
        def _():
            for f in range(features):
                found, keep = copies(f * parts + group // shared)
                for copy in found:
                    copy.wait_recv()
                keep.wait()

        hidden = cross(swapped_ref, group)
        hidden_ref[group] = hidden
        for member in range(3):
            out = mm(hidden, fw_ref[member]).astype(bf16)
            if member == 0:
                out = out * jnp.asarray(0.125, bf16)
            fqkv_ref[group, member] = out
        code = fq_ref[...]
        extras = code.astype(f32)
        for pair in range(pairs):
            lanes = pair_lanes(pair)
            context, extras = attend_pair(
                fqkv_ref[group, 0, :, lanes],
                fqkv_ref[group, 1, :, lanes],
                fqkv_ref[group, 2, :, lanes],
                code,
                fk_ref[...],
                pair,
                extras,
            )
            fctx_ref[group, :, lanes] = context
        fext_ref[group] = extras.astype(bf16)
        put_cross(a_ref, group, mm(fctx_ref[group], fw_ref[3]).astype(bf16))
        for copy in back_copies(group, None if last else 0):
            copy.start()
        back_ref[:, place.place, chunk(group, SIZE), :] = a_ref[place.place, :, chunk(group, SIZE), :]
        return carry

    lax.fori_loop(0, groups, feature, 0)
    if not last:
        for f in range(1, features):

            def send_rest(group, carry, f=f):
                for copy in back_copies(group, f):
                    copy.start()
                return carry

            lax.fori_loop(0, groups, send_rest, 0)
    box.flush(*outs[4:8])

    def settle(unit, carry):
        for copy in copies(unit)[0]:
            copy.wait_send()
        return carry

    lax.fori_loop(0, features * units, settle, 0)
    if last:
        og_ref = box.out(first + LAYER_OUTS + 1)
        raw_ref[...] = box.use(7 + 4 * (layer + 1))[...].astype(f32)
        from_rows(raw_ref, og_ref)
        box.flush(first + LAYER_OUTS + 1)
    up_ref, upb_ref, down_ref, downb_ref = box.use(weights + 2, 5, weights + 3, 6)
    if layer > 0:
        box.settle(*[earlier[index] for index in (8, 9, 10, 12, 13)])
    hidden_width = up_ref.shape[1]

    def feed_forward(x2, keep):
        _, _, hidden = layer_norm(x2, *gain(2))
        hidden = hidden.astype(bf16)
        keep(h3_ref, slice(None), hidden)
        columns = [slice(part * 512, part * 512 + 512) for part in range(hidden_width // 512)]
        actives = []
        for cols in columns:
            u = mm(hidden, up_ref[:, cols]) + upb_ref[layer : layer + 1, cols]
            bent = gelu_parts(u)
            both = 0.5 * (1.0 + bent)
            active = (u * both).astype(bf16)
            keep(active_ref, cols, active)
            slope = both + u * (1.0 - bent * bent) * (0.3989422804014327 + 0.05351611220146811 * u * u)
            keep(u_ref, cols, slope.astype(bf16))
            actives.append(active)
        return x2 + downb_ref[layer : layer + 1, :] + mm(jnp.concatenate(actives, axis=1), down_ref[...])

    def dense(group, carry):
        for copy in back_copies(group):
            copy.wait_recv()
        x2 = cross(x1_ref, group) + cross(back_ref, group).astype(f32)
        put_cross(x2_ref, group, x2)

        def keep(ref, cols, values):
            ref[group, :, cols] = values

        put_cross(x3_ref, group, feed_forward(x2, keep))
        box.flush_part(outs[8], group, cross_view)
        box.flush_part(outs[9], group, cross_view)
        box.flush_part(outs[10], group, first_view)
        box.flush_part(outs[12], group, first_view)
        box.flush_part(outs[13], group, first_view)
        return carry

    def dense_of(f):
        if f is None:

            def settle_back(group, carry):
                for other in range(features):
                    for copy in back_copies(group, other):
                        copy.wait_send()
                return carry

            lax.fori_loop(0, groups, settle_back, 0)
            return

        def arrived(group, carry):
            for copy in back_copies(group, f):
                copy.wait_recv()
            return carry

        lax.fori_loop(0, groups, arrived, 0)

        def rows(unit, carry):
            x2 = own_rows(x1_ref, f, unit, size) + own_rows(back_ref, f, unit, size).astype(f32)
            x2_ref[f, :, chunk(unit, size), :] = x2.reshape(blocks, size, width)
            count = blocks * SIZE

            def keep(ref, cols, values):
                parted = values.reshape(blocks, shared, SIZE, values.shape[1])
                for at in range(shared):
                    ref[unit * shared + at, chunk(f, count), cols] = parted[:, at].reshape(count, values.shape[1])

            x3_ref[f, :, chunk(unit, size), :] = feed_forward(x2, keep).reshape(blocks, size, width)
            return carry

        lax.fori_loop(0, parts, rows, 0)

    if not last:
        return dense_of
    lax.fori_loop(0, groups, dense, 0)

    def settle_back(group, carry):
        for copy in back_copies(group):
            copy.wait_send()
        return carry

    lax.fori_loop(0, groups, settle_back, 0)
    return None


def pieces_of(values):
    first = values.astype(bf16)
    rest = values - first.astype(f32)
    second = rest.astype(bf16)
    return first, second, (rest - second.astype(f32)).astype(bf16)


def exact(left, right, dims):
    first, second, third = pieces_of(right)
    return mm(left, first, dims) + mm(left, second, dims) + mm(left, third, dims)


def exact_left(left, right, dims):
    first, second, third = pieces_of(left)
    return mm(first, right, dims) + mm(second, right, dims) + mm(third, right, dims)


def read_out(box, ins, later, outs, x_ref, x_load, g_ref, reading_ref, got_ref, bins_ref, counted_ref, read_ref, weight_ref, sends, recvs):
    place = box.place
    shapes_ref, loss_ref, rgrad_ref = box.out(*outs)
    read_ref[...] = jnp.zeros_like(read_ref)
    size_ref, count_ref, label_ref, index_ref, population_ref, narrow_ref = box.use(*ins)
    x_load.wait()
    box.start(*later)
    read_ref[0 : narrow_ref.shape[0], :] = narrow_ref[...]
    features, blocks, own, width = x_ref.shape
    samples = blocks * own
    bins = population_ref.shape[1]
    size, count = size_ref[0], count_ref[0]
    mask = (lax.broadcasted_iota(jnp.int32, (1, samples), 1) < size).astype(f32)
    task_size = jnp.zeros((1, samples), f32) + size.astype(f32)
    level = lax.broadcasted_iota(jnp.int32, (bins, bins), 0)
    diagonal = (level == lax.broadcasted_iota(jnp.int32, (bins, bins), 1)).astype(f32)
    live = [
        jnp.where(place.place * features + f < count, 1.0, 0.0) for f in range(features)
    ]
    logits = None
    for f in range(features):
        reading = x_ref[f].reshape(samples, width).astype(bf16)
        reading_ref[f] = reading.reshape(blocks, own, width)
        projected = mm(reading, read_ref[...], NT)
        onehot = (lax.broadcasted_iota(jnp.int32, (bins, samples), 0) == index_ref[f : f + 1, :]).astype(f32)
        bins_ref[f] = onehot.astype(bf16)
        chosen = onehot * mask
        counted = jnp.maximum(jnp.sum(chosen, axis=1, keepdims=True), 1.0)
        counted_ref[f] = jnp.broadcast_to(counted, (bins, LANES))
        means = exact(chosen.astype(bf16), projected, NN) / counted
        weight = jnp.sum(diagonal * population_ref[f : f + 1, :].astype(f32), axis=1, keepdims=True)
        weight_ref[f] = jnp.broadcast_to(weight, (bins, LANES))
        weight = weight_ref[f]
        centre = jnp.sum(weight * means, axis=0, keepdims=True) / jnp.sum(weight, axis=0, keepdims=True)
        shapes = means - centre
        shapes_ref[f] = shapes
        part = exact_left(shapes, bins_ref[f], TN)[:SIZE] * live[f]
        logits = part if logits is None else logits + part
    spans = range(samples // LANES)
    got_ref[place.place] = jnp.concatenate([logits[0:CLASSES, pair_lanes(span)] for span in spans], axis=0)
    box.ready()
    copies = [
        remote(
            got_ref.at[place.place],
            got_ref.at[place.place],
            sends.at[k - 1],
            recvs.at[k - 1],
            {"feat": place.ring(k)},
        )
        for k in range(1, place.places)
    ]
    for copy in copies:
        copy.start()
    for copy in copies:
        copy.wait()
    total = got_ref[0]
    for k in range(1, place.places):
        total = total + got_ref[k]
    rows_left = jnp.zeros((SIZE - CLASSES, LANES), f32)
    logits = jnp.concatenate(
        [
            jnp.concatenate([total[span * CLASSES : span * CLASSES + CLASSES], rows_left], axis=0)
            for span in spans
        ],
        axis=1,
    )
    class_row = lax.broadcasted_iota(jnp.int32, logits.shape, 0)
    inside = class_row < CLASSES
    peak = jnp.max(jnp.where(inside, logits, masked_score), axis=0, keepdims=True)
    weights = jnp.where(inside, jnp.exp(jnp.where(inside, logits - peak, 0.0)), 0.0)
    weight_sum = jnp.sum(weights, axis=0, keepdims=True)
    log_total = peak + jnp.log(weight_sum)
    own_class = (class_row == label_ref[...]).astype(f32)
    picked = jnp.sum(logits * own_class, axis=0, keepdims=True)
    losses = mask * (log_total - picked)
    loss_ref[...] = jnp.broadcast_to(
        jnp.sum(losses, axis=1, keepdims=True) / task_size[:, 0:1], loss_ref.shape
    )
    logit_grad = mask * (weights / weight_sum - own_class) / task_size
    pad = jnp.zeros((LANES - SIZE, samples), f32)
    total = None
    for f in range(features):
        grad_rows = jnp.concatenate([logit_grad * live[f], pad], axis=0)
        shape_grad = exact(bins_ref[f], grad_rows, NT)
        weight = weight_ref[f]
        means_grad = shape_grad - weight / jnp.sum(weight, axis=0, keepdims=True) * jnp.sum(
            shape_grad, axis=0, keepdims=True
        )
        chosen = (bins_ref[f].astype(f32) * mask).astype(bf16)
        proj_grad = exact(chosen, means_grad / counted_ref[f], TN).astype(bf16)
        part = mm(proj_grad, all_rows(reading_ref, f), TN)[:SIZE]
        total = part if total is None else total + part
        if f == 0:
            box.use(1)
        back = mm(proj_grad, read_ref[...]).reshape(blocks, own, width)
        g_ref[f] = g_ref[f] + back
    rgrad_ref[...] = total
    box.flush(*outs)


def dense_feature_backward(layer, box, fk_ref, send_ref, ugrad_ref, rowgrad_ref, dup_ref, ddown_ref, arriving_ref, dc_ref, dh_ref, back_ref, dwf_ref, sends, recvs, self_sem, back_sends, back_recvs, *head):
    place = box.place
    g1_ref, small_ref, sdc_ref, sext_ref, slow_ref = box.out(0, 1, 2, 3, 4)
    if head:
        x_load = pltpu.make_async_copy(box.bufs[18], g1_ref, head[-1])
        box.start(19, 20, 21, 22)
        x_load.start()
    else:
        box.start(6, 7, (1, 0), 2, (3, 0), 4, (5, 0))
    small_ref[...] = jnp.zeros_like(small_ref)
    fill_feature_codes(box.use(0)[0], None, fk_ref)
    if not head:
        box.use(6, 7, 2, 4)
    gain_ref, shift_ref, down_ref, up_ref = box.bufs[6], box.bufs[7], box.bufs[2], box.bufs[4]
    g_ref, slope_ref, x2_ref = box.bufs[1], box.bufs[3], box.bufs[5]
    active_ref, hidden3_ref = box.bufs[16], box.bufs[17]
    if not head:
        box.start((1, 1, 2, 3), (3, 1, 2, 3), (5, 1, 2, 3))
    else:
        later = (1, 6, 7, 2, 3, 4, 5, 17, 16, 8, 9, 10, 11, 12, 13, 14, 15)
        read_out(box, (23, 0, 19, 20, 21, 22), later, (5, 6, 7), g1_ref, x_load, g_ref, send_ref, *head[:-1])
        box.use(6, 7, 2, 4)
    features, blocks, own, width = g_ref.shape
    hidden_width = up_ref.shape[1]
    groups = own // SIZE
    parts = hidden_width // 512
    pairs = width // LANES

    def copies(group):
        found = [
            remote(
                send_ref.at[:, place.ring(k), chunk(group, SIZE), :],
                arriving_ref.at[place.place, :, chunk(group, SIZE), :],
                sends.at[group, k - 1],
                recvs.at[group, k - 1],
                {"feat": place.ring(k)},
            )
            for k in range(1, place.places)
        ]
        keep = pltpu.make_async_copy(
            send_ref.at[:, place.place, chunk(group, SIZE), :],
            arriving_ref.at[place.place, :, chunk(group, SIZE), :],
            self_sem.at[group],
        )
        return found, keep

    def dense(group, carry):
        rows = chunk(group, ROWS)
        if not head:
            box.part(1, group)
        box.part(3, group)
        box.part(5, group)
        grad = cross(g_ref, group)
        low = grad.astype(bf16)
        rowgrad_ref[rows, :] = low
        small_ref[parts : parts + 1] += jnp.sum(low.astype(f32), axis=0, keepdims=True)
        for part in range(parts):
            cols = slice(part * 512, part * 512 + 512)
            active_grad = mm(low, down_ref[cols, :], NT).astype(bf16).astype(f32)
            ugrad = (active_grad * slope_ref[group, :, cols].astype(f32)).astype(bf16)
            ugrad_ref[rows, cols] = ugrad
            small_ref[part : part + 1] += jnp.sum(ugrad.astype(f32), axis=0, keepdims=True)
        hidden_grad = mm(ugrad_ref[rows, :], up_ref[...], NT)
        x2 = cross(x2_ref, group)
        gain = gain_ref[2, layer : layer + 1, :]
        norm_grad, gain_part, shift_part = layer_norm_back(hidden_grad.astype(bf16).astype(f32), x2, gain)
        small_ref[parts + 1 : parts + 2] += gain_part
        small_ref[parts + 2 : parts + 3] += shift_part
        grad = grad + norm_grad
        put_cross(g1_ref, group, grad)
        put_cross(send_ref, group, grad.astype(bf16))
        if not head:

            @pl.when(group == 0)
            def _():
                box.ready()
                box.start(17, 16, 8, 9, 10, 11, 12, 13, 14, 15)

        found, keep = copies(group)
        for copy in found:
            copy.start()
        keep.start()
        return carry

    lax.fori_loop(0, groups, dense, 0)

    def up_weights(part, carry):
        cols = chunk(part, 512)
        out = mm(ugrad_ref[:, cols], hidden3_ref[...], TN)
        dup_ref[part // 2, lax.rem(part, 2)] = out.astype(bf16).reshape(dup_ref.shape[2:])
        return carry

    def down_weights(part, carry):
        cols = chunk(part, 512)
        out = mm(active_ref[:, cols], rowgrad_ref[...], TN)
        ddown_ref[part // 2, lax.rem(part, 2)] = out.astype(bf16).reshape(ddown_ref.shape[2:])
        return carry

    box.use(16, 17)
    lax.fori_loop(0, parts, up_weights, 0)
    box.chains[0].begin(dup_ref)
    lax.fori_loop(0, parts, down_weights, 0)
    box.point("dense")
    box.chains[1].begin(ddown_ref)
    grads_ref = active_ref
    w_ref, qkv_ref, ctx_ref, ext_ref = box.use(8, 9, 10, 11)

    def back_copies(group):
        return [
            remote(
                dh_ref.at[place.ring(k), :, chunk(group, SIZE), :],
                back_ref.at[:, place.place, chunk(group, SIZE), :],
                back_sends.at[group, k - 1],
                back_recvs.at[group, k - 1],
                {"feat": place.ring(k)},
            )
            for k in range(1, place.places)
        ]

    def feature(group, carry):
        found, keep = copies(group)
        for copy in found:
            copy.wait_recv()
        keep.wait()
        rows = chunk(group, ROWS)
        dao = cross(arriving_ref, group)
        grads_ref[rows, 3 * width : 4 * width] = dao
        context_grad = mm(dao, w_ref[3], NT).astype(bf16)
        dc_ref[...] = context_grad
        grad_extra = delta_extra(ctx_ref[group], context_grad)
        for pair in range(pairs):
            lanes = pair_lanes(pair)
            query_grad, key_grad, value_grad = attend_pair_back(
                qkv_ref[group, 0, :, lanes],
                qkv_ref[group, 1, :, lanes],
                qkv_ref[group, 2, :, lanes],
                dc_ref[:, lanes],
                ext_ref[group],
                grad_extra,
                fk_ref[...],
                pair,
            )
            for member, grad in enumerate((query_grad * 0.125, key_grad, value_grad)):
                at = member * width + pair * LANES
                grads_ref[rows, at : at + LANES] = grad.astype(bf16)
        total = mm(grads_ref[rows, 0:width], w_ref[0], NT)
        total = total + mm(grads_ref[rows, width : 2 * width], w_ref[1], NT)
        total = total + mm(grads_ref[rows, 2 * width : 3 * width], w_ref[2], NT)
        put_cross(dh_ref, group, total.astype(bf16))
        for copy in back_copies(group):
            copy.start()
        back_ref[:, place.place, chunk(group, SIZE), :] = dh_ref[place.place, :, chunk(group, SIZE), :]

        for at in range(groups):

            @pl.when(group == at)
            def _(at=at):
                box.point(at)

        return carry

    lax.fori_loop(0, groups, feature, 0)
    hidden_ref = box.use(12)

    def weights(member, carry):
        hidden = hidden_ref[...].reshape(groups * ROWS, width)
        out = mm(hidden, grads_ref[:, chunk(member, width)], TN)
        dwf_ref[member // 2, lax.rem(member, 2)] = out.astype(bf16).reshape(dwf_ref.shape[2:])
        return carry

    lax.fori_loop(0, 3, weights, 0)
    context = ctx_ref[...].reshape(groups * ROWS, width)
    out = mm(context, grads_ref[:, 3 * width : 4 * width], TN)
    dwf_ref[1, 1] = out.astype(bf16).reshape(dwf_ref.shape[2:])
    box.chains[2].begin(dwf_ref)
    box.point("weights")
    x1_ref, wo_ref, sctx_ref = box.use(13, 14, 15)

    def enter(group, carry):
        for copy in back_copies(group):
            copy.wait_recv()
        norm_grad, gain_part, shift_part = layer_norm_back(
            cross(back_ref, group).astype(f32), cross(x1_ref, group), gain_ref[1, layer : layer + 1, :]
        )
        small_ref[parts + 3 : parts + 4] += gain_part
        small_ref[parts + 4 : parts + 5] += shift_part
        grad = cross(g1_ref, group) + norm_grad
        put_cross(g1_ref, group, grad)
        low = grad.astype(bf16)
        put_cross(slow_ref, group, low)
        context_grad = mm(low, wo_ref[...], NT).astype(bf16)
        put_cross(sdc_ref, group, context_grad)
        put_cross(sext_ref, group, delta_extra(cross(sctx_ref, group), context_grad))
        box.flush_part(0, group, cross_view)
        box.flush_part(2, group, cross_view)
        box.flush_part(3, group, cross_view)
        box.flush_part(4, group, cross_view)

        for at in range(groups):

            @pl.when(group == at)
            def _(at=at):
                box.point(10 + at)

        return carry

    lax.fori_loop(0, groups, enter, 0)
    box.flush(1)
    box.point("end")

    def settle(group, carry):
        for copy in copies(group)[0]:
            copy.wait_send()
        for copy in back_copies(group):
            copy.wait_send()
        return carry

    lax.fori_loop(0, groups, settle, 0)


def sample_backward_last(layer, last, box, sk_ref, dqkv_ref, *tail):
    place = box.place
    g0_ref, small_ref = box.out(0, 1)
    box.start((1, 0), (2, 0), 3, 4)
    small_ref[...] = jnp.zeros_like(small_ref)
    fill_sample_codes(box.use(0)[0], None, sk_ref)
    qkv_ref, dc_ref = box.bufs[1], box.bufs[2]
    features, blocks, own, width = dc_ref.shape
    samples = blocks * own
    per = ROWS // own
    steps = blocks // per
    pairs = width // LANES
    total_rows = features * samples
    if last:
        dw_ref, bufs_1, bufs_2, bufs_3, *small_bufs = tail
        share_ref = box.out(3)
    else:
        dw_ref, *small_bufs = tail
    exchange = SmallSums(place, last, *small_bufs)
    ext_ref, gext_ref = box.use(3, 4)
    if last:
        box.ready()
    box.start((1, 1, 2, 3), (2, 1, 2, 3), 9, 10, 11, 12, 13)

    def step_of(step, pair):
        got_ref, _, sends, recvs = (bufs_1, bufs_2, bufs_3)[step - 1]
        source = dw_ref.at[pair] if step == 1 else (bufs_1, bufs_2)[step - 2][1].at[pair]
        return SumStep(5 if step == 3 else step, place, source, None, got_ref.at[pair], sends.at[pair], recvs.at[pair], None)

    def pass_on(step, pair):
        step_of(step, pair).finish((bufs_1, bufs_2, bufs_3)[step - 1][1].at[pair])
        if step < 3:
            step_of(step + 1, pair).start()

    def attend(pair, carry):
        lanes = chunk(pair, LANES)
        box.part(1, pair)
        box.part(2, pair)
        for f in range(features):
            key_total = value_total = None
            for step in range(steps):
                rows = slice(f * samples + step * ROWS, f * samples + step * ROWS + ROWS)
                query_grad, key_grad, value_grad = attend_pair_back(
                    block_rows(qkv_ref.at[0], f, step, per, lanes),
                    all_rows(qkv_ref.at[1], f, lanes),
                    all_rows(qkv_ref.at[2], f, lanes),
                    block_rows(dc_ref, f, step, per, lanes),
                    block_rows(ext_ref, f, step, per),
                    block_rows(gext_ref, f, step, per),
                    sk_ref[...],
                    pair,
                )
                dqkv_ref[0, rows, lanes] = (query_grad * 0.125).astype(bf16)
                key_total = key_grad if key_total is None else key_total + key_grad
                value_total = value_grad if value_total is None else value_total + value_grad
            rows = slice(f * samples, f * samples + samples)
            dqkv_ref[1, rows, lanes] = key_total.astype(bf16)
            dqkv_ref[2, rows, lanes] = value_total.astype(bf16)

        if not last:

            @pl.when(pair == 0)
            def _():
                box.ready()

        for at in range(1, pairs):

            @pl.when(pair == at)
            def _(at=at):
                box.point(at)

        @pl.when(pair == 0)
        def _():
            box.start(5, 6, 7, 8)
            dense_rows, other_rows = box.use(12, 13)
            if last:
                exchange.start([(0, 9, dense_rows, 9), (9, 11, other_rows, 2)])
            else:
                exchange.start([(0, 9, dense_rows, 9), (9, 9 + SIZE, other_rows, SIZE)])

        for stage in range(1, 4):

            @pl.when(pair == stage)
            def _(stage=stage):
                exchange.move(stage)

        if not last:
            return carry

        @pl.when(pair == 0)
        def _():
            box.use(9, 10, 11)

        hidden = box.bufs[9][...].reshape(total_rows, width)
        context = box.bufs[10][...].reshape(total_rows, width)
        low_ref = box.bufs[11]
        block = dw_ref.shape[3:]
        for member in range(3):
            out = mm(dqkv_ref[member, :, lanes], hidden, TN).T
            dw_ref[pair, member // 2, member % 2] = out.astype(bf16).reshape(block)
        low = low_ref[:, :, :, lanes].reshape(total_rows, LANES)
        dw_ref[pair, 1, 1] = mm(low, context, TN).T.astype(bf16).reshape(block)
        step_of(1, pair).start()

        @pl.when(pair >= 1)
        def _():
            pass_on(1, pair - 1)

        @pl.when(pair >= 2)
        def _():
            pass_on(2, pair - 2)

        return carry

    lax.fori_loop(0, pairs, attend, 0)
    box.point("attend")
    if not last:
        hidden_ref, context_ref, low_ref = box.use(9, 10, 11)

        def weights(member, carry):
            hidden = hidden_ref[...].reshape(total_rows, width)
            out = mm(hidden, dqkv_ref[member], TN)
            dw_ref[member // 2, lax.rem(member, 2)] = out.astype(bf16).reshape(dw_ref.shape[2:])
            return carry

        lax.fori_loop(0, 3, weights, 0)
        context = context_ref[...].reshape(total_rows, width)
        out = mm(context, low_ref[...].reshape(total_rows, width), TN)
        dw_ref[1, 1] = out.astype(bf16).reshape(dw_ref.shape[2:])
        box.chains[-1].begin(dw_ref)
    w_ref, x_ref, gain_ref, g_ref = box.use(5, 6, 7, 8)
    gain = gain_ref[0, layer : layer + 1, :]

    def leave(unit, carry):
        f, part = unit // steps, lax.rem(unit, steps)
        rows = chunk(unit, ROWS)
        total = mm(dqkv_ref[0, rows, :], w_ref[0], NT)
        total = total + mm(dqkv_ref[1, rows, :], w_ref[1], NT)
        total = total + mm(dqkv_ref[2, rows, :], w_ref[2], NT)
        norm_grad, gain_part, shift_part = layer_norm_back(
            total.astype(bf16).astype(f32), block_rows(x_ref, f, part, per), gain
        )
        small_ref[0:1] += gain_part
        small_ref[1:2] += shift_part
        g0_ref[f, chunk(part, per), :, :] = (block_rows(g_ref, f, part, per) + norm_grad).reshape(per, own, width)
        if last:

            @pl.when(unit == 1)
            def _():
                pass_on(1, pairs - 1)

            @pl.when(unit == 2)
            def _():
                pass_on(2, pairs - 2)

        @pl.when(unit == 2)
        def _():
            box.point("leave")
            box.out(2)[...] = exchange.sum(3)
            box.flush(2)

        return carry

    lax.fori_loop(0, features * steps, leave, 0)
    box.flush(0, 1)
    if last:
        exchange.start_late(small_ref)
        pass_on(2, pairs - 1)
        exchange.move(5)
    box.point("end")
    if last:
        for pair in range(pairs):
            pass_on(3, pair)
            share_ref[:, pair_lanes(pair)] = bufs_3[1][pair]
        box.flush(3)
        box.out(4)[...] = exchange.sum(5)
        box.flush(4)


class SmallSums:
    def __init__(self, place, last, packed, early, late, sends, recvs):
        self.packed, self.early, self.late = packed, early, late
        tasks = [{"task": place.task_partner(k)} for k in range(1, place.tasks)]
        ring = [{"feat": place.ring(k)} for k in range(1, place.places)]
        plan = [
            (early, 0, 2, place.core, [place.other_core]),
            (early, 2, place.tasks, place.task, tasks),
            (early, 2 + place.tasks, 2, place.near, [place.near_chip]),
            (early, 4 + place.tasks, 2, place.far, [place.far_chip]),
            (late, 0, place.places, place.place, ring),
            (late, place.places, place.tasks, place.task, tasks),
        ]
        plan = plan if last else plan[:4]
        self.plan, self.copies, at = plan, [], 0
        for buffer, first, count, mine, devices in plan:
            slot = buffer.at[first + mine]
            self.copies.append(
                [remote(slot, slot, sends.at[at + k], recvs.at[at + k], device) for k, device in enumerate(devices)]
            )
            at += len(devices)

    def send(self, stage, rows):
        buffer, first, _, mine, _ = self.plan[stage]
        buffer[first + mine] = rows
        for copy in self.copies[stage]:
            copy.start()

    def start(self, parts):
        self.packed[...] = jnp.zeros_like(self.packed)
        for begin, end, source, count in parts:
            self.packed[begin:end] = source[0:count]
        self.send(0, self.packed[...])

    def start_late(self, rows_ref):
        blocks = [rows_ref[row : row + 1, pair_lanes(block)] for row in range(2) for block in range(4)]
        self.send(4, jnp.concatenate(blocks, axis=0))

    def sum(self, stage):
        buffer, first, count, _, _ = self.plan[stage]
        for copy in self.copies[stage]:
            copy.wait()
        total = buffer[first]
        for k in range(1, count):
            total = total + buffer[first + k]
        return total

    def move(self, stage):
        self.send(stage, self.sum(stage - 1))


def write_out(dense_rows, x_ref, g_ref, *refs):
    refs = list(refs)
    shares, packed_rows, late, bins, loss, outs = refs[:8], refs[8:10], refs[10], refs[11], refs[12], refs[13:26]
    raw_x, raw_g, x_buf, g_buf, load_sem, out_sem = refs[26:]
    outs[12][0] = loss[0, 0]
    for f in range(bins.shape[0]):
        outs[11][:, f, :] = bins[f].T[0:CLASSES]
    features, blocks, own, width = x_ref.shape
    period = features * (width // LANES)
    per = blocks // 4
    rows_part = per * own

    def load(part, which):
        source, target = ((x_ref, x_buf), (g_ref, g_buf))[which]
        view = (slice(None), pl.ds(part * per, per))
        return pltpu.make_async_copy(source.at[view], target.at[view], load_sem.at[which, part])

    def store(part, which):
        source, target = ((raw_x, outs[0]), (raw_g, outs[1]))[which]
        view = pl.ds(part * rows_part * period, rows_part * period)
        return pltpu.make_async_copy(source.at[view], target.at[view], out_sem.at[which, part])

    for part in range(4):
        load(part, 0).start()
        load(part, 1).start()
    for member in range(4):
        outs[2 + member][0] = shares[2 * member][...]
        outs[2 + member][1] = shares[2 * member + 1][...]
    parts = dense_rows - 5
    for layer in range(2):
        packed, at = packed_rows[layer], 0
        for part in range(parts):
            outs[8][layer : layer + 1, part * width : (part + 1) * width] = packed[at + part : at + part + 1]
        outs[9][layer : layer + 1] = packed[at + parts : at + parts + 1]
        for member, row in ((2, parts + 1), (1, parts + 3)):
            outs[6][member, layer : layer + 1] = packed[at + row : at + row + 1]
            outs[7][member, layer : layer + 1] = packed[at + row + 1 : at + row + 2]
    at = dense_rows
    for block in range(4):
        lanes = pair_lanes(block)
        outs[6][0, 0:1, lanes], outs[7][0, 0:1, lanes] = late[block : block + 1], late[4 + block : 5 + block]
    outs[6][0, 1:2], outs[7][0, 1:2] = packed_rows[0][at : at + 1], packed_rows[0][at + 1 : at + 2]
    outs[10][...] = packed_rows[1][at : at + CLASSES]

    for part in range(4):
        for which, buf, raw in ((0, x_buf, raw_x), (1, g_buf, raw_g)):
            load(part, which).wait()
            for f in range(features):
                for block in range(width // LANES):
                    rows = buf[f, part * per : (part + 1) * per, :, pair_lanes(block)].reshape(rows_part, LANES)
                    start = part * rows_part * period + block * features + f
                    raw[pl.ds(start, rows_part, stride=period), :] = rows
            store(part, which).start()
    for part in range(4):
        store(part, 0).wait()
        store(part, 1).wait()


def codes(item, live, size, rows):
    lanes = jnp.arange(LANES)[None, :] - CODE_LANE
    inside = (lanes >= 0) & (lanes < size)
    own = lanes == item[:, None]
    query_code = (own & inside).astype(bf16)
    key_code = jnp.where(inside & ~(own & live[:, None]), masked_score, 0.0).astype(bf16)
    return query_code, key_code


def local_fused(
    tokens_in,
    sample_weights,
    feature_weights,
    norm_gain,
    norm_shift,
    up_weight,
    up_bias,
    down_weight,
    down_bias,
    read_weight,
    output_grad,
    task_sizes,
    feature_counts,
    bin_index,
    bin_counts,
    class_labels,
):
    samples, features, width = tokens_in.shape[1:]
    hidden_width = up_weight.shape[2]
    tasks, places = lax.axis_size("task"), lax.axis_size("feat")
    own = samples // places
    groups = own // SIZE
    units = features * (own * places // ROWS)
    sizes = (tasks, places)
    shape = (features, places, own, width)
    block_shape = (places, features, own, width)
    group_shape = (groups, ROWS, width)
    share = width // places
    share_shape = (share, width)
    piece_shape = (2, 2, 2, 2, 2, share, width)
    rows_total = groups * ROWS
    vmem = pltpu.VMEM

    def dma(*counts):
        return pltpu.SemaphoreType.DMA(counts)

    def raw_rows(tokens):
        parts = tokens.reshape(samples, features, width // LANES, LANES)
        return parts.transpose(0, 2, 1, 3).reshape(samples * features * (width // LANES), LANES)

    def from_raw(rows):
        parts = rows.reshape(samples, width // LANES, features, LANES)
        return parts.transpose(0, 2, 1, 3).reshape(1, samples, features, width)

    gains = norm_gain.transpose(1, 0, 2)
    shifts = norm_shift.transpose(1, 0, 2)
    layer_outs = [
        (shape, f32),
        ((3,) + shape, bf16),
        (shape, bf16),
        (shape[:3] + (LANES,), bf16),
        (group_shape, bf16),
        ((groups, 3, ROWS, width), bf16),
        (group_shape, bf16),
        ((groups, ROWS, LANES), bf16),
        (shape, f32),
        (shape, f32),
        ((groups, ROWS, hidden_width), bf16),
        (shape, bf16),
        ((groups, ROWS, hidden_width), bf16),
        (group_shape, bf16),
    ]
    ins = [
        (task_sizes, "scalar"),
        (feature_counts, "scalar"),
        (raw_rows(tokens_in), None),
        (gains, None),
        (shifts, None),
        (up_bias, None),
        (down_bias, None),
    ]
    for layer in range(LAYERS):
        ins += [(weight, layer) for weight in (sample_weights, feature_weights, up_weight, down_weight)]
    ins.append((raw_rows(output_grad), None))
    outs = list(layer_outs)
    for layer in range(1, LAYERS):
        outs += [(*item, index) for index, item in enumerate(layer_outs)]
    outs += [(shape, f32), (shape, f32)]
    *kept, first_rows, stream_grad = fused(
        functools.partial(forward_layers, LAYERS),
        "forward_layers",
        sizes,
        ins,
        outs,
        [
            vmem((ROWS, LANES), bf16),
            vmem((samples, LANES), bf16),
            vmem((ROWS, LANES), bf16),
            vmem((ROWS, LANES), bf16),
            vmem((samples * features * (width // LANES), LANES), f32),
            vmem(shape, bf16),
            vmem(block_shape, bf16),
            vmem(block_shape, bf16),
            vmem(shape, bf16),
            dma(LAYERS, units, places - 1),
            dma(LAYERS, units, places - 1),
            dma(LAYERS, units),
            dma(LAYERS, features, groups, places - 1),
            dma(LAYERS, features, groups, places - 1),
        ],
        [],
        share_shape,
        1,
    )
    stored = []
    stream = first_rows
    for layer in range(LAYERS):
        x1, qkv, ctx, ext, hidden, fqkv, fctx, fext, x2, x3, u, h1, act, h3 = kept[14 * layer : 14 * layer + 14]
        stored.append((stream, x1, qkv, ctx, ext, hidden, fqkv, fctx, fext, x2, u, h1, act, h3))
        stream = x3

    finished = {}
    dense_rows = hidden_width // width + 5
    pairs = width // LANES
    flat = (rows_total, width)
    for layer in reversed(range(LAYERS)):
        x0, x1, qkv, ctx, ext, hidden, fqkv, fctx, fext, x2, u, h1, act, h3 = stored[layer]
        last = layer == 0
        ins = [
            (feature_counts, "scalar"),
            (stream_grad, None, cross_view, groups),
            (down_weight, layer),
            (u, None, first_view, groups),
            (up_weight, layer),
            (x2, None, cross_view, groups),
            (gains, None),
            (shifts, None),
            (feature_weights, layer),
            (fqkv, None),
            (fctx, None),
            (fext, None),
            (hidden, None),
            (x1, None),
            (sample_weights, (layer, 3)),
            (ctx, None),
            (act.reshape(rows_total, hidden_width), None),
            (h3.reshape(flat), None),
        ]
        head = []
        if not last:
            ins += [
                (stream, "raw"),
                (class_labels, None),
                (bin_index[0].T, None),
                (bin_counts[0], None),
                (read_weight.T, None),
                (task_sizes, "scalar"),
            ]
            ins[1] = (stream_grad, None)
            head = [
                vmem((places, CLASSES * (samples // LANES), LANES), f32),
                vmem((features, BINS, samples), bf16),
                vmem((features, BINS, LANES), f32),
                vmem((LANES, width), bf16),
                vmem((features, BINS, LANES), f32),
                dma(places - 1),
                dma(places - 1),
                pltpu.SemaphoreType.DMA,
            ]
        sums = [
            ((1, 6, 7, 3), ("dense", 2, "weights", 12), None, True),
            ((1, 6, 7, 3), (0, 3, 10, 12), None, True),
            ((1, 6), (10, 12), None, True),
        ]
        if last:
            sums += [((2, 3), (0, 11), sample_sum, True), ((3,), (0, 11), finished[1][0], True)]
        g1, dense_small, sdc, sext, slow, *results = fused(
            functools.partial(dense_feature_backward, layer),
            "dense_feature_backward",
            sizes,
            ins,
            [
                (shape, f32),
                ((16, width), f32),
                (shape, bf16),
                (shape[:3] + (LANES,), bf16),
                (shape, bf16),
            ]
            + ([] if last else [((features, BINS, LANES), f32), ((8, LANES), f32), ((SIZE, width), f32)]),
            [
                vmem((ROWS, LANES), bf16),
                vmem(shape, bf16),
                vmem((rows_total, hidden_width), bf16),
                vmem(flat, bf16),
                vmem(piece_shape, bf16),
                vmem(piece_shape, bf16),
                vmem(block_shape, bf16),
                vmem((ROWS, width), bf16),
                vmem(block_shape, bf16),
                vmem(shape, bf16),
                vmem(piece_shape, bf16),
                dma(groups, places - 1),
                dma(groups, places - 1),
                dma(groups),
                dma(groups, places - 1),
                dma(groups, places - 1),
            ]
            + head,
            sums,
            share_shape,
            4 + layer,
        )
        if not last:
            shapes, loss, read_grad, *results = results
        up_sum, down_sum, feature_sum, *later_sum = results
        ins = [
            (task_sizes, "scalar"),
            (qkv, None, last_view, pairs),
            (sdc, None, last_view, pairs),
            (ext, None),
            (sext, None),
            (sample_weights, layer),
            (x0, None),
            (gains, None),
            (g1, None),
        ]
        other_small = sample_small if last else read_grad
        ins += [(array, None) for array in (h1, ctx, slow, dense_small, other_small)]
        early_rows = -(-(dense_rows + (2 if last else SIZE)) // 8) * 8
        slots = 6 + tasks
        copies = 1 + (tasks - 1) + 1 + 1 + (places - 1) + (tasks - 1)
        small_scratch = [
            vmem((early_rows, width), f32),
            vmem((slots, early_rows, width), f32),
            vmem((places + tasks, 8, LANES), f32),
            dma(copies),
            dma(copies),
        ]
        outs = [(shape, f32), ((8, width), f32), ((early_rows, width), f32)]
        scratch = [vmem((samples, LANES), bf16), vmem((3,) + flat, bf16)]
        if last:
            outs += [(share_shape, f32), ((8, LANES), f32)]
            scratch.append(vmem((pairs, 2, 2, 2, 2, 2, share, LANES), bf16))
            for step in (1, 2, 5):
                _, got, mine, kind, count = sum_shapes(step, tasks, share, LANES)
                scratch += [
                    (
                        vmem((pairs,) + got, bf16),
                        vmem((pairs,) + mine, kind),
                        dma(pairs, count),
                        dma(pairs, count),
                    )
                ]
            scratch += small_scratch
            sums = [
                ((7, 3, 4), (2, "attend", "end"), feature_sum, True),
                ((4,), ("attend",), up_sum, True),
                ((4,), ("attend",), down_sum, True),
                ((4,), ("attend",), later_sum[0], True),
                ((4,), ("attend",), later_sum[1], True),
            ]
        else:
            scratch += [vmem(piece_shape, bf16), *small_scratch]
            sums = [
                ((7,), (3,), feature_sum, True),
                ((4,), ("attend",), up_sum, True),
                ((4,), ("attend",), down_sum, True),
                ((1,), ("leave",), None, True),
            ]
        stream_grad, sample_small, *more = fused(
            functools.partial(sample_backward_last, layer, last),
            "sample_backward",
            sizes,
            ins,
            outs,
            scratch,
            sums,
            share_shape,
            6 + layer,
        )
        if last:
            packed, share_sum, late, *first = more
            finished[0] = (share_sum, *first[:3])
            finished[1] = (first[3], first[4], *finished[1][1:])
        else:
            later_packed, *finished[1], sample_sum = more

    whole, parked = pl.BlockSpec(memory_space=pltpu.VMEM), pl.BlockSpec(memory_space=pltpu.HBM)
    scalar = pl.BlockSpec(memory_space=pltpu.SMEM)
    matrix = jax.ShapeDtypeStruct((LAYERS, share, width), f32)
    norm = jax.ShapeDtypeStruct((3, LAYERS, width), f32)
    raw_shape = (samples * features * (width // LANES), LANES)
    raw = jax.ShapeDtypeStruct(raw_shape, f32)
    shares = [finished[layer][member] for member in range(4) for layer in range(LAYERS)]
    results = pl.pallas_call(
        functools.partial(write_out, dense_rows),
        name="write_out",
        out_shape=[
            raw,
            raw,
            matrix,
            matrix,
            matrix,
            matrix,
            norm,
            norm,
            jax.ShapeDtypeStruct((LAYERS, hidden_width), f32),
            jax.ShapeDtypeStruct((LAYERS, width), f32),
            jax.ShapeDtypeStruct((CLASSES, width), f32),
            jax.ShapeDtypeStruct((CLASSES, features, BINS), f32),
            jax.ShapeDtypeStruct((1,), f32),
        ],
        in_specs=[parked] * 2 + [whole] * 12 + [scalar],
        out_specs=[parked] * 2 + [whole] * 10 + [scalar],
        scratch_shapes=[
            vmem(raw_shape, f32),
            vmem(raw_shape, f32),
            vmem(shape, f32),
            vmem(shape, f32),
            dma(2, 4),
            dma(2, 4),
        ],
        compiler_params=pltpu.CompilerParams(vmem_limit_bytes=63 << 20),
    )(stream, stream_grad, *shares, packed, later_packed, late, shapes, loss)
    return (
        from_raw(results[0]),
        results[11].transpose(1, 2, 0)[None],
        from_raw(results[1]),
        results[12],
        results[2][:, None],
        results[3][:, None],
        results[6].transpose(1, 0, 2),
        results[7].transpose(1, 0, 2),
        results[4].transpose(0, 2, 1),
        results[8],
        results[5],
        results[9],
        results[10].T,
    )


def local(
    tokens_in,
    sample_weights,
    feature_weights,
    norm_gain,
    norm_shift,
    up_weight,
    up_bias,
    down_weight,
    down_bias,
    read_weight,
    output_grad,
    task_sizes,
    feature_counts,
    bin_index,
    bin_counts,
    class_labels,
):
    samples = tokens_in.shape[1]
    features = tokens_in.shape[2]
    width = tokens_in.shape[3]
    hidden_width = up_weight.shape[2]
    task_devices = lax.axis_size("task")
    feature_devices = lax.axis_size("feat")
    all_features = features * feature_devices
    own_samples = samples // feature_devices
    size = min(16, own_samples)
    groups = own_samples // size
    group_rows = all_features * size
    rows_total = features * samples

    if (
        own_samples % 32 == 0
        and samples % ROWS == 0
        and ROWS % own_samples == 0
        and group_rows == ROWS
        and own_samples == 4 * SIZE
        and task_devices == hidden_width // width == 4
        and feature_devices == 8
    ):
        return local_fused(
            tokens_in,
            sample_weights,
            feature_weights,
            norm_gain,
            norm_shift,
            up_weight,
            up_bias,
            down_weight,
            down_bias,
            read_weight,
            output_grad,
            task_sizes,
            feature_counts,
            bin_index,
            bin_counts,
            class_labels,
        )

    sample_live = jnp.arange(samples) < task_sizes[0]
    feature_live = jnp.arange(all_features) < feature_counts[0]
    sample_mask = sample_live.astype(f32)
    local_index = lax.axis_index("feat") * features + jnp.arange(features)
    local_live = (local_index < feature_counts[0]).astype(f32)
    sample_qcode, sample_kcode = codes(jnp.zeros((samples,), jnp.int32), sample_live, 1, samples)
    sample_qcode = sample_qcode[:ROWS]
    item = jnp.arange(group_rows) % size
    feature_qcode, feature_kcode = codes(item, jnp.repeat(feature_live, size), size, group_rows)

    def exchange_out(rows):
        parts = rows.reshape(features, feature_devices, own_samples, width)
        got = lax.all_to_all(parts, "feat", split_axis=1, concat_axis=0, tiled=True)
        return got.reshape(all_features, own_samples, width)

    def exchange_back(rows):
        parts = rows.reshape(feature_devices, features, own_samples, width)
        got = lax.all_to_all(parts, "feat", split_axis=0, concat_axis=2, tiled=True)
        return got.reshape(features, samples, width)

    stream = tokens_in[0].astype(f32).transpose(1, 0, 2)
    token_shape = (features, samples, width)
    stored = []
    for layer in range(LAYERS):
        gain, shift = norm_gain[layer], norm_shift[layer]
        x1, h2, qkv, ctx, ext = call(
            sample_forward,
            "sample_forward",
            [
                (token_shape, f32),
                (token_shape, bf16),
                ((3,) + token_shape, bf16),
                (token_shape, bf16),
                ((features, samples, LANES), bf16),
            ],
            [],
            stream,
            gain,
            shift,
            sample_weights[layer],
            sample_qcode,
            sample_kcode,
        )
        swapped = exchange_out(h2)
        a, fqkv, fctx, fext = call(
            functools.partial(feature_forward, size),
            "feature_forward",
            [
                ((all_features, own_samples, width), bf16),
                ((groups, 3, group_rows, width), bf16),
                ((groups, group_rows, width), bf16),
                ((groups, group_rows, LANES), bf16),
            ],
            [],
            swapped,
            feature_weights[layer],
            feature_qcode,
            feature_kcode,
        )
        back = exchange_back(a)
        x3, u = call(
            dense_forward,
            "dense_forward",
            [((rows_total, width), f32), ((rows_total, hidden_width), bf16)],
            [],
            x1.reshape(rows_total, width),
            back.reshape(rows_total, width),
            gain,
            shift,
            up_weight[layer],
            up_bias[layer][None],
            down_weight[layer],
            down_bias[layer][None],
        )
        stored.append((stream, x1, qkv, ctx, ext, swapped, fqkv, fctx, fext, back, u))
        stream = x3.reshape(token_shape)

    reading = stream.astype(bf16)
    projected = jnp.einsum("fsd,dc->fsc", reading, read_weight, preferred_element_type=f32)
    onehot_bins = (bin_index[0].T[..., None] == jnp.arange(BINS)).astype(f32)
    chosen = onehot_bins * sample_mask[None, :, None]
    counted = jnp.maximum(jnp.sum(chosen, axis=1), 1.0)
    bin_sums = jnp.einsum("fsb,fsc->fbc", chosen, projected, precision=highest)
    bin_means = bin_sums / counted[..., None]
    bin_weight = bin_counts[0].astype(f32)
    weight_total = jnp.sum(bin_weight, axis=-1, keepdims=True)
    centre = jnp.sum(bin_weight[..., None] * bin_means, axis=1, keepdims=True) / weight_total[..., None]
    shapes = bin_means - centre
    used_bins = onehot_bins * local_live[:, None, None]
    local_logits = jnp.einsum("fsb,fbc->sc", used_bins, shapes, precision=highest)
    logits = lax.psum(local_logits, "feat")
    row_max = jnp.max(logits, axis=-1, keepdims=True)
    log_total = row_max + jnp.log(jnp.sum(jnp.exp(logits - row_max), axis=-1, keepdims=True))
    label_rows = (class_labels[0][:, None] == jnp.arange(CLASSES)).astype(f32)
    picked = jnp.sum(logits * label_rows, axis=-1)
    live_count = task_sizes[0].astype(f32)
    task_loss = jnp.sum(sample_mask * (log_total[:, 0] - picked)) / live_count
    logit_grad = sample_mask[:, None] * (jnp.exp(logits - log_total) - label_rows) / live_count
    shape_grad = jnp.einsum("fsb,sc->fbc", used_bins, logit_grad, precision=highest)
    means_grad = shape_grad - bin_weight[..., None] / weight_total[..., None] * jnp.sum(
        shape_grad, axis=1, keepdims=True
    )
    sum_grad = means_grad / counted[..., None]
    projected_grad = jnp.einsum("fsb,fbc->fsc", chosen, sum_grad, precision=highest).astype(bf16)
    read_grad = jnp.einsum("fsd,fsc->dc", reading, projected_grad, preferred_element_type=f32)
    stream_grad = output_grad[0].astype(f32).transpose(1, 0, 2) + jnp.einsum(
        "fsc,dc->fsd", projected_grad, read_weight, preferred_element_type=f32
    )

    small = [None] * LAYERS
    big = [None] * LAYERS
    for layer in reversed(range(LAYERS)):
        gain, shift = norm_gain[layer], norm_shift[layer]
        x0, x1, qkv, ctx, ext, swapped, fqkv, fctx, fext, back, u = stored[layer]
        flat = (rows_total, width)
        g2, sent, dup, ddown, dupb, ddownb, dgs2 = call(
            dense_backward,
            "dense_backward",
            [
                (flat, f32),
                (flat, bf16),
                ((hidden_width, width), bf16),
                ((hidden_width, width), bf16),
                ((1, hidden_width), f32),
                ((1, width), f32),
                ((2, width), f32),
            ],
            [
                ((rows_total, hidden_width), bf16),
                ((rows_total, hidden_width), bf16),
                (flat, bf16),
                (flat, bf16),
            ],
            stream_grad.reshape(flat),
            x1.reshape(flat),
            back.reshape(flat),
            u,
            gain,
            shift,
            up_weight[layer],
            down_weight[layer],
        )
        arriving = exchange_out(sent.reshape(token_shape))
        group_shape = (groups, group_rows, width)
        dh, dwf = call(
            functools.partial(feature_backward, size),
            "feature_backward",
            [((all_features, own_samples, width), bf16), ((4, width, width), bf16)],
            [
                ((3,) + group_shape, bf16),
                (group_shape, bf16),
                (group_shape, bf16),
                ((group_rows, width), bf16),
            ],
            arriving,
            swapped,
            feature_weights[layer],
            feature_kcode,
            fqkv,
            fctx,
            fext,
        )
        returned = exchange_back(dh)
        g0, dws, dgs01 = call(
            sample_backward,
            "sample_backward",
            [(token_shape, f32), ((4, width, width), bf16), ((2, 2, width), f32)],
            [
                ((3,) + token_shape, bf16),
                (token_shape, bf16),
                (token_shape, bf16),
                (token_shape, bf16),
                ((features, samples, LANES), bf16),
                ((samples, LANES), f32),
                ((samples, LANES), f32),
            ],
            g2.reshape(token_shape),
            returned,
            x1,
            x0,
            gain,
            shift,
            sample_weights[layer],
            sample_kcode,
            qkv,
            ctx,
            ext,
        )
        stream_grad = g0
        small[layer] = (
            jnp.stack([dgs01[0, 0], dgs01[1, 0], dgs2[0]]),
            jnp.stack([dgs01[0, 1], dgs01[1, 1], dgs2[1]]),
            dupb[0],
            ddownb[0],
        )
        big[layer] = [dws.reshape(4 * width, width), dwf.reshape(4 * width, width), dup, ddown]
    shard_shape = (LAYERS, 4 // task_devices, width // feature_devices, width)
    pieces = [big[layer][member] for member in range(4) for layer in range(LAYERS)]
    rows = [row.reshape(-1, width) for layer in range(LAYERS) for row in small[layer]]
    rows.append(read_grad.T)
    lengths = [row.shape[0] for row in rows]
    fill = -sum(lengths) % 8
    small_rows = jnp.concatenate(rows + [jnp.zeros((fill, width), f32)])
    if (width // feature_devices) % 16 == 0:
        *shares, small_sums = sum_everywhere(pieces, small_rows, task_devices, feature_devices)
    else:
        shares = [
            lax.psum_scatter(piece, ("task", "feat"), scatter_dimension=0, tiled=True).astype(f32)
            for piece in pieces
        ]
        small_sums = lax.psum(small_rows, ("task", "feat"))
    matrices = [jnp.stack(shares[member * LAYERS : member * LAYERS + LAYERS]) for member in range(4)]
    split = []
    at = 0
    for length in lengths:
        split.append(small_sums[at : at + length])
        at += length
    summed = [jnp.stack([split[4 * layer + member] for layer in range(LAYERS)]) for member in range(4)]
    summed[2] = summed[2].reshape(LAYERS, hidden_width)
    summed[3] = summed[3].reshape(LAYERS, width)
    summed.append(split[-1].T)
    return (
        stream.transpose(1, 0, 2)[None],
        shapes[None],
        stream_grad.transpose(1, 0, 2)[None],
        task_loss[None],
        matrices[0].reshape(shard_shape),
        matrices[1].reshape(shard_shape),
        summed[0],
        summed[1],
        matrices[2].transpose(0, 2, 1),
        summed[2],
        matrices[3],
        summed[3],
        summed[4],
    )


def solution(mesh):
    in_specs = (
        P("task", None, "feat", None),
        P(),
        P(),
        P(),
        P(),
        P(),
        P(),
        P(),
        P(),
        P(),
        P("task", None, "feat", None),
        P("task"),
        P("task"),
        P("task", None, "feat"),
        P("task", "feat", None),
        P("task", None),
    )
    out_specs = (
        P("task", None, "feat", None),
        P("task", "feat", None, None),
        P("task", None, "feat", None),
        P("task"),
        P(None, "task", "feat", None),
        P(None, "task", "feat", None),
        P(),
        P(),
        P(None, None, ("task", "feat")),
        P(),
        P(None, ("task", "feat"), None),
        P(),
        P(),
    )
    return jax.shard_map(local, mesh=mesh, in_specs=in_specs, out_specs=out_specs, check_vma=False)
```
